32 devices in a mesh: ty: 8 (over z, core), tx: 4 (over y, x).
Axes of the slice: x: 2, y: 2, z: 4, core: 2. Of those that a mesh axis runs over, the one named last changes fastest.
Arguments:
- image: float32 [4096, 4096], P('ty', 'tx'), may hold values from -6 to 6
- noise: float32 [2, 4096, 4096], P(None, 'ty', 'tx'), may hold values from -6 to 6
- offsets: int32 [2, 2], replicated, may hold values from 1 to 7, as said below
- key_mask: int32 [256, 256], P('ty', 'tx'), may hold values 0 or 1
- gains: float32 [2, 4096, 4096], P(None, ('ty', 'tx')), may hold values from -1 to 1
- observed: float32 [2, 4096, 4096], P(None, ('ty', 'tx')), may hold values from -6 to 6
- vis_weight: float32 [4096, 4096], P(('ty', 'tx')), may hold values from 0.05 to 1
- w_embed: bfloat16 [256, 512], replicated, may hold values from -0.375 to 0.375
- w_qkv: bfloat16 [2, 512, 1536], replicated, as said below
- w_proj: bfloat16 [2, 512, 512], replicated, may hold values from -0.25 to 0.25
- w_up: bfloat16 [2, 512, 2048], replicated, may hold values from -0.25 to 0.25
- w_down: bfloat16 [2, 2048, 512], replicated, may hold values from -0.125 to 0.125
- w_unembed: bfloat16 [512, 256], replicated, may hold values from -0.25 to 0.25
- norm_gains: float32 [2, 2, 512], replicated, may hold values from 0.1 to 1.9
Outputs:
- sampled: float32 [4096, 4096], P('ty', 'tx')
The draws below stay inside these ranges and needn't reach their ends.
Inputs may be any that keep to these rules, and one draw needn't show every extreme that they name: `offsets`: each entry lies in 1 to 7, and some entry equals 7. `w_qkv`: columns ordered by query, key or value, then head, then feature of the head.
All inputs are finite; a program needn't handle non-finite values. No bound on the sum of `key_mask` on one device may be relied on, other than what follows from the above.
Results may differ from the reference program's by a relative error of at most 0.04.
Values may be sent and summed in bfloat16 or wider, within the bound.
No kernel may reach another device: no remote copies, remote signals or barrier semaphores. Data moves between devices by JAX's collectives and lax.ppermute only.
A program may use at most 192 MiB of HBM per device.

```python
import math
import jax
import jax.numpy as jnp
from jax import lax

N = 4096
PATCH = 16
WIN = 8
D = 512
HEADS = 8
FF = 2048
STEPS = 2
BLOCKS = 2
TOK = 256
PIXELS = 256


def draw_offsets(key, part):
    key = jax.random.fold_in(key, 5)
    drawn = jax.random.randint(key, (STEPS * 2,), 1, WIN)
    chosen = jax.random.randint(jax.random.fold_in(key, 1), (), 0, STEPS * 2)
    flat = jnp.where(jnp.arange(STEPS * 2) == chosen, WIN - 1, drawn)
    return flat.reshape(STEPS, 2).astype(jnp.int32)


def draw_w_qkv(key, part):
    key = jax.random.fold_in(key, 11)
    base = jax.random.normal(key, (BLOCKS, D, 3, HEADS, D // HEADS), jnp.float32) * D ** (-0.5)
    return base.reshape(BLOCKS, D, 3 * D).astype(jnp.bfloat16)


def touch_ends(values, rng, smallest, high):
    longest = values.shape.index(max(values.shape))
    spots = []
    for shift in (0, 1):
        where = [jax.random.randint(jax.random.fold_in(rng, axis), (), 0, length) for axis, length in enumerate(values.shape)]
        where[longest] = (where[longest] + shift) % values.shape[longest]
        spots.append(tuple(where))
    return values.at[spots[0]].set(smallest).at[spots[1]].set(high)


def level_of(stream_key, dims, cuts, smallest, top_value):
    factor_of, own = 1.0, jax.random.fold_in(stream_key, 6)
    for dim, shards_of in cuts:
        heights = jnp.exp(jax.random.uniform(jax.random.fold_in(own, dim), (shards_of,), jnp.float32, smallest / len(cuts), top_value / len(cuts)))
        factor_of = factor_of * jnp.repeat(heights, dims[dim] // shards_of).reshape([-1 if axis == dim else 1 for axis in range(len(dims))])
    return factor_of


def gaussian(own_key, shape, scale, limit, cuts=(), kind=jnp.bfloat16):
    entries = jax.random.normal(own_key, shape, jnp.float32) * scale
    if len(cuts) > 0:
        entries = level_of(own_key, shape, cuts, -0.22, 0.18) * entries
    return jnp.clip(entries, min=-limit, max=limit).astype(kind)


def setup_inputs(seed: int = 0) -> dict:
    arg_keys = jax.random.split(jax.random.key(seed), 15)
    image = gaussian(arg_keys[0], (N, N), 1.0, 6.0, ((0, 8), (1, 4)), jnp.float32)
    noise = gaussian(arg_keys[1], (STEPS, N, N), 1.0, 6.0, ((1, 8), (2, 4)), jnp.float32)
    offsets = draw_offsets(jax.random.fold_in(arg_keys[14], 71), 0)
    key_mask = touch_ends((jax.random.randint(arg_keys[3], (TOK, TOK), 0, 8) < 7).astype(jnp.int32), jax.random.fold_in(arg_keys[3], 1), 0, 1)
    gains = jnp.clip(jax.random.uniform(arg_keys[4], (2, N, N), jnp.float32, -1.0, 1.0) * level_of(arg_keys[4], (2, N, N), ((1, 32),), -0.4, 0.0), -1.0, 1.0)
    observed = gaussian(arg_keys[5], (2, N, N), 1.0, 6.0, ((1, 32),), jnp.float32)
    vis_weight = jnp.clip(jnp.exp(math.log(1.0) - 2.9957323 * jax.random.uniform(arg_keys[6], (N, N), jnp.float32) ** level_of(arg_keys[6], (N, N), ((0, 32),), -0.2, 0.2)), 0.05, 1.0)
    w_embed = gaussian(arg_keys[7], (PIXELS, D), PIXELS ** -0.5, 0.375)
    w_qkv = draw_w_qkv(jax.random.fold_in(arg_keys[14], 71), 0)
    w_proj = gaussian(arg_keys[9], (BLOCKS, D, D), D ** -0.5, 0.25)
    w_up = gaussian(arg_keys[10], (BLOCKS, D, FF), D ** -0.5, 0.25)
    w_down = gaussian(arg_keys[11], (BLOCKS, FF, D), FF ** -0.5, 0.125)
    w_unembed = gaussian(arg_keys[12], (D, PIXELS), D ** -0.5, 0.25)
    norm_gains = jnp.clip(1.0 + 0.18 * jax.random.normal(arg_keys[13], (BLOCKS, 2, D), jnp.float32), 0.1, 1.9)
    return {"image": image, "noise": noise, "offsets": offsets, "key_mask": key_mask, "gains": gains, "observed": observed, "vis_weight": vis_weight, "w_embed": w_embed, "w_qkv": w_qkv, "w_proj": w_proj, "w_up": w_up, "w_down": w_down, "w_unembed": w_unembed, "norm_gains": norm_gains}


SIGMAS = (0.8, 0.5, 0.3)
STEP_SIZES = (0.9, 0.7)
EPSILON = 1e-05

def layer_norm(values, gain):
    centre = lax.optimization_barrier(jnp.mean(values, axis=-1, keepdims=True))
    shifted = values - centre
    spread = lax.optimization_barrier(jnp.mean(shifted * shifted, axis=-1, keepdims=True))
    return shifted * lax.rsqrt(spread + EPSILON) * gain

def to_windows(grid):
    rows, cols, feats = grid.shape
    shaped = grid.reshape(rows // WIN, WIN, cols // WIN, WIN, feats).transpose(0, 2, 1, 3, 4)
    return shaped.reshape(rows // WIN * (cols // WIN), WIN * WIN, feats)

def from_windows(windows, rows, cols):
    feats = windows.shape[-1]
    shaped = windows.reshape(rows // WIN, cols // WIN, WIN, WIN, feats).transpose(0, 2, 1, 3, 4)
    return shaped.reshape(rows, cols, feats)

def attention(normed, labels, keep, w_qkv, w_proj):
    rows, cols = (normed.shape[0], normed.shape[1])
    mixed = jnp.dot(normed.reshape(rows * cols, D), w_qkv, preferred_element_type=jnp.float32)
    mixed = to_windows(mixed.astype(jnp.bfloat16).reshape(rows, cols, 3 * D))
    number = mixed.shape[0]
    parts = mixed.reshape(number, WIN * WIN, 3, HEADS, D // HEADS).astype(jnp.float32)
    scores = jnp.einsum('wqhe,wkhe->whqk', parts[:, :, 0], parts[:, :, 1]) / math.sqrt(D // HEADS)
    label_win = to_windows(labels[:, :, None])[:, :, 0]
    keep_win = to_windows(keep[:, :, None])[:, :, 0]
    same = label_win[:, :, None] == label_win[:, None, :]
    visible = (keep_win[:, None, :] == 1) | jnp.eye(WIN * WIN, dtype=bool)[None]
    allowed = (same & visible)[:, None]
    scores = jnp.where(allowed, scores, -1e+30)
    largest = lax.optimization_barrier(jnp.max(scores, axis=-1, keepdims=True))
    weights = jnp.exp(scores - largest)
    probs = (weights / lax.optimization_barrier(jnp.sum(weights, axis=-1, keepdims=True))).astype(jnp.bfloat16)
    attended = jnp.einsum('whqk,wkhe->wqhe', probs.astype(jnp.float32), parts[:, :, 2]).astype(jnp.bfloat16)
    attended = from_windows(attended.reshape(number, WIN * WIN, D), rows, cols)
    projected = jnp.dot(attended.reshape(rows * cols, D), w_proj, preferred_element_type=jnp.float32)
    return projected.reshape(rows, cols, D)

def swin_block(grid, labels, keep, w_qkv, w_proj, w_up, w_down, gains):
    rows, cols = (grid.shape[0], grid.shape[1])
    flow = grid.astype(jnp.float32)
    normed = layer_norm(flow, gains[0]).astype(jnp.bfloat16)
    flow = flow + attention(normed, labels, keep, w_qkv, w_proj)
    normed = layer_norm(flow, gains[1]).astype(jnp.bfloat16).reshape(rows * cols, D)
    hidden = jax.nn.gelu(jnp.dot(normed, w_up, preferred_element_type=jnp.float32), approximate=True)
    hidden = hidden.astype(jnp.bfloat16)
    flow = flow + jnp.dot(hidden, w_down, preferred_element_type=jnp.float32).reshape(rows, cols, D)
    return flow.astype(jnp.bfloat16)

def banded(grid, labels, keep, w_qkv, w_proj, w_up, w_down, gains):
    side = grid.shape[0]
    bands = side // WIN

    def one_band(band):
        return swin_block(band[0], band[1], band[2], w_qkv, w_proj, w_up, w_down, gains)
    stacked = lax.map(one_band, (grid.reshape(bands, WIN, side, D), labels.reshape(bands, WIN, side), keep.reshape(bands, WIN, side)))
    return stacked.reshape(side, side, D)

def patches_of(picture):
    rows, cols = picture.shape
    shaped = picture.reshape(rows // PATCH, PATCH, cols // PATCH, PATCH).transpose(0, 2, 1, 3)
    return shaped.reshape(rows // PATCH, cols // PATCH, PATCH * PATCH).astype(jnp.bfloat16)

def image_of(pieces):
    rows, cols = (pieces.shape[0], pieces.shape[1])
    shaped = pieces.reshape(rows, cols, PATCH, PATCH).transpose(0, 2, 1, 3)
    return shaped.reshape(rows * PATCH, cols * PATCH)

def region(index, shift):
    side = N // PATCH
    return jnp.where(index < side - WIN, 0, jnp.where(index < side - shift, 1, 2)).astype(jnp.int32)

def likelihood(state, gains, observed, vis_weight):
    spectrum = jnp.fft.fft2(state).T / N
    gain = lax.complex(gains[0], gains[1])
    seen = lax.complex(observed[0], observed[1])
    back = jnp.conj(gain) * (vis_weight * (gain * spectrum - seen))
    return jnp.real(jnp.fft.ifft2(back.T)) * N

def reference(image, noise, offsets, key_mask, gains, observed, vis_weight, w_embed, w_qkv, w_proj, w_up, w_down, w_unembed, norm_gains):
    side = N // PATCH
    state = image
    plain = jnp.zeros((side, side), jnp.int32)
    all_keep = jnp.ones((side, side), jnp.int32)
    index = jnp.arange(side, dtype=jnp.int32)
    for step in range(STEPS):
        grad = likelihood(state, gains, observed, vis_weight)
        half = state - STEP_SIZES[step] * grad
        patches = patches_of(half)
        tokens = jnp.dot(patches.reshape(side * side, PATCH * PATCH), w_embed, preferred_element_type=jnp.float32)
        tokens = tokens.astype(jnp.bfloat16).reshape(side, side, D)
        first = banded(tokens, plain, key_mask, w_qkv[0], w_proj[0], w_up[0], w_down[0], norm_gains[0])
        shift_rows = offsets[step, 0]
        shift_cols = offsets[step, 1]
        rolled = jnp.roll(first, -shift_rows, axis=0)
        rolled = jnp.roll(rolled, -shift_cols, axis=1)
        regions = 3 * region(index, shift_rows)[:, None] + region(index, shift_cols)[None, :]
        second = banded(rolled, regions, all_keep, w_qkv[1], w_proj[1], w_up[1], w_down[1], norm_gains[1])
        restored = jnp.roll(second, shift_rows, axis=0)
        restored = jnp.roll(restored, shift_cols, axis=1)
        estimate = jnp.dot(restored.reshape(side * side, D), w_unembed, preferred_element_type=jnp.float32)
        estimate = image_of(estimate.reshape(side, side, PATCH * PATCH))
        state = half - SIGMAS[step] * estimate + SIGMAS[step + 1] * noise[step]
    return state
```

```python
import functools
import math

import jax
import jax.numpy as jnp
import ml_dtypes
import numpy as np
from jax import lax
from jax.experimental import pallas as pl
from jax.experimental.pallas import tpu as pltpu
from jax.sharding import PartitionSpec as P

N = 4096
PATCH = 16
PIXELS = PATCH * PATCH
WIN = 8
D = 512
HEADS = 8
STEPS = 2
SPAN = WIN * WIN
TOK = N // PATCH

SIGMAS = (0.8, 0.5, 0.3)
STEP_SIZES = (0.9, 0.7)
EPSILON = 1e-05
HIGHEST = lax.Precision.HIGHEST
BF16 = jnp.bfloat16
F32 = jnp.float32
VMEM_LIMIT = 56 * 1024 * 1024
PARAMS = pltpu.CompilerParams(vmem_limit_bytes=VMEM_LIMIT)
TN = (((0,), (0,)), ((), ()))
NT = (((1,), (1,)), ((), ()))
NN = (((1,), (0,)), ((), ()))


def mm(left, right, dims=NN):
    return lax.dot_general(left, right, dims, preferred_element_type=F32)


def counting(length):
    return jnp.arange(length, dtype=jnp.int32)


def roots(length, outer, inner, sign):
    product = outer[:, None] * inner[None, :] % length
    angle = 2.0 * math.pi / length * product.astype(F32)
    return (jnp.cos(angle), sign * jnp.sin(angle))


def complex_einsum(form, left, right):
    real = jnp.einsum(form, left[0], right[0], precision=HIGHEST) - jnp.einsum(
        form, left[1], right[1], precision=HIGHEST
    )
    imag = jnp.einsum(form, left[0], right[1], precision=HIGHEST) + jnp.einsum(
        form, left[1], right[0], precision=HIGHEST
    )
    return (real, imag)


def complex_times(left, right):
    return (left[0] * right[0] - left[1] * right[1], left[0] * right[1] + left[1] * right[0])


def along_last(real_part, imag_part, groups, sign):
    rows, length = real_part.shape
    inner = length // groups
    first = roots(groups, counting(groups), counting(groups), sign)
    twist = roots(length, counting(inner), counting(groups), sign)
    second = roots(inner, counting(inner), counting(inner), sign)
    shaped = real_part.reshape(rows, groups, inner)
    if imag_part is None:
        partial_value = (
            jnp.einsum("mab,ka->mbk", shaped, first[0], precision=HIGHEST),
            jnp.einsum("mab,ka->mbk", shaped, first[1], precision=HIGHEST),
        )
    else:
        partial_value = complex_einsum(
            "mab,ka->mbk", (shaped, imag_part.reshape(rows, groups, inner)), first
        )
    partial_value = complex_times(partial_value, twist)
    result = complex_einsum("jb,mbk->mjk", second, partial_value)
    return (result[0].reshape(rows, length), result[1].reshape(rows, length))


def across_groups(pair, groups, sign):
    inner, cols = pair[0].shape
    width = cols // groups
    length = groups * inner
    first = roots(groups, counting(groups), counting(groups), sign)
    twist = roots(length, counting(inner), counting(groups), sign)
    second = roots(inner, counting(inner), counting(inner), sign)
    shaped = (pair[0].reshape(inner, groups, width), pair[1].reshape(inner, groups, width))
    partial_value = complex_einsum("bhc,kh->cbk", shaped, first)
    partial_value = complex_times(partial_value, twist)
    result = complex_einsum("jb,cbk->cjk", second, partial_value)
    return (result[0].reshape(width, length), result[1].reshape(width, length))


def exchange_pair(pair):
    return tuple(
        lax.all_to_all(
            part.astype(BF16), ("ty", "tx"), split_axis=1, concat_axis=1, tiled=True
        ).astype(F32)
        for part in pair
    )


def plain_gradient(tile, gains, observed, vis_weight):
    devices = lax.axis_size("ty") * lax.axis_size("tx")
    slab = lax.all_to_all(tile.astype(BF16), "tx", split_axis=0, concat_axis=1, tiled=True)
    moved = exchange_pair(along_last(slab.astype(F32), None, devices, -1.0))
    spectrum = across_groups(moved, devices, -1.0)
    spectrum = (spectrum[0] * (1.0 / N), spectrum[1] * (1.0 / N))
    model = complex_times((gains[0], gains[1]), spectrum)
    misfit = (vis_weight * (model[0] - observed[0]), vis_weight * (model[1] - observed[1]))
    back = complex_times((gains[0], -gains[1]), misfit)
    returned = exchange_pair(along_last(back[0], back[1], devices, 1.0))
    slab_grad = across_groups(returned, devices, 1.0)[0] * (1.0 / N)
    return lax.all_to_all(slab_grad.astype(BF16), "tx", split_axis=1, concat_axis=0, tiled=True)


def embed_complex(angle, row_axis, col_axis):
    cos, sin = np.cos(angle), np.sin(angle)
    top = np.stack([cos, sin], axis=col_axis)
    bottom = np.stack([-sin, cos], axis=col_axis)
    return np.stack([top, bottom], axis=row_axis)


def wheel(length, product):
    return 2.0 * math.pi / length * (product % length)


@functools.lru_cache(maxsize=None)
def row_constants():
    k = np.arange(TOK)
    angle = wheel(TOK, k[:, None] * k[None, :])
    first = np.concatenate([np.cos(angle), -np.sin(angle)], axis=1)
    b = np.tile(np.arange(PATCH), PATCH)
    angle = wheel(N, b[:, None] * k[None, :])
    twist = np.stack([np.cos(angle), -np.sin(angle)])
    p = np.arange(PATCH)
    small = embed_complex(wheel(PATCH, p[:, None] * p[None, :]), 1, 1)
    second = np.einsum("kpqb,xy->kpxqyb", small, np.eye(PATCH)).reshape(2 * PIXELS, 2 * PIXELS)
    return (
        first.astype(ml_dtypes.bfloat16),
        twist.astype(np.float32),
        second.astype(ml_dtypes.bfloat16),
        np.ascontiguousarray(second.T).astype(ml_dtypes.bfloat16),
    )


@functools.lru_cache(maxsize=None)
def column_constants(devices, rows):
    s = np.arange(devices)
    small = embed_complex(wheel(devices, s[:, None] * s[None, :]), 1, 2)
    wide = devices * 2 * PATCH
    outer = np.einsum("qpsr,xy->qpxsry", small, np.eye(PATCH)).reshape(wide, wide)
    kr = s[:, None] + devices * np.arange(rows)[None, :]
    angle = wheel(N, kr[:, :, None] * np.arange(rows)[None, None, :])
    inner = embed_complex(angle, 1, 2).reshape(devices, 2 * rows, 2 * rows) / N
    return tuple(
        np.ascontiguousarray(value).astype(ml_dtypes.bfloat16)
        for value in (outer, outer.T, inner, inner.transpose(0, 2, 1))
    )


def row_forward(x_ref, first_ref, twist_ref, second_ref, out_ref):
    count = x_ref.shape[1]

    def step(i, carry):
        band = x_ref[:, i].reshape(TOK, PIXELS)
        mixed = mm(band, first_ref[...], TN)
        real, imag = mixed[:, :TOK], mixed[:, TOK:]
        tr, ti = twist_ref[0], twist_ref[1]
        turned = jnp.concatenate(
            [(real * tr - imag * ti).astype(BF16), (real * ti + imag * tr).astype(BF16)], axis=0
        )
        result = mm(second_ref[...], turned).astype(BF16).reshape(PATCH, 2, PATCH, TOK)
        half = TOK // 2
        rows = pl.ds(pl.multiple_of(i * PATCH, PATCH), PATCH)
        out_ref[:, 0, :, rows, :] = result[..., :half]
        out_ref[:, 1, :, rows, :] = result[..., half:]
        return carry

    lax.fori_loop(0, count, step, 0)


def row_inverse(v_ref, first_ref, twist_ref, second_ref, out_ref):
    parts, count, cols, _ = out_ref.shape

    def step(i, carry):
        rows = pl.ds(pl.multiple_of(i * PATCH, PATCH), PATCH)
        wide = jnp.concatenate(
            [
                v_ref[:, 0, :, rows, :].reshape(2 * PIXELS, TOK // 2),
                v_ref[:, 1, :, rows, :].reshape(2 * PIXELS, TOK // 2),
            ],
            axis=1,
        )
        mixed = mm(second_ref[...], wide)
        real, imag = mixed[:PIXELS], mixed[PIXELS:]
        tr, ti = twist_ref[0], twist_ref[1]
        turned = jnp.concatenate(
            [(real * tr + imag * ti).astype(BF16), (imag * tr - real * ti).astype(BF16)], axis=1
        )
        result = mm(first_ref[...], turned, NT).astype(BF16)
        out_ref[:, i] = result.reshape(parts, cols, PIXELS)
        return carry

    lax.fori_loop(0, count, step, 0)


def column_both(
    x_ref, scale_ref, data_ref, outer_ref, outer_t_ref, inner_ref, inner_t_ref, out_ref, mid_ref
):
    devices, _, rows, width = x_ref.shape
    wide = devices * 2 * PATCH

    def turn(source, target, matrix):
        for pair in range(rows // (2 * PATCH)):
            first = slice(pair * 2 * PATCH, pair * 2 * PATCH + PATCH)
            second = slice(pair * 2 * PATCH + PATCH, (pair + 1) * 2 * PATCH)
            both = jnp.concatenate(
                [
                    source[:, :, first, :].reshape(wide, width),
                    source[:, :, second, :].reshape(wide, width),
                ],
                axis=1,
            )
            result = mm(matrix[...], both).astype(BF16)
            target[:, :, first, :] = result[:, :width].reshape(devices, 2, PATCH, width)
            target[:, :, second, :] = result[:, width:].reshape(devices, 2, PATCH, width)

    turn(x_ref, mid_ref, outer_ref)

    def step(q, carry):
        spectrum = mm(inner_ref[q], mid_ref[q].reshape(2 * rows, width)).reshape(2, rows, width)
        scale = scale_ref[q].astype(F32)
        back = spectrum * scale[None] - data_ref[:, q].astype(F32)
        wave = mm(inner_t_ref[q], back.astype(BF16).reshape(2 * rows, width))
        mid_ref[q] = wave.astype(BF16).reshape(2, rows, width)
        return carry

    lax.fori_loop(0, devices, step, 0, unroll=4)
    turn(mid_ref, out_ref, outer_t_ref)


def spectrum_inputs(gains, observed, vis_weight, devices):
    width = vis_weight.shape[0]

    def turned(value):
        shaped = value.astype(BF16).reshape(width, N // devices, devices)
        return shaped.transpose(2, 1, 0)

    gr, gi = gains[0], gains[1]
    scale = turned(vis_weight * (gr * gr + gi * gi))
    data = jnp.stack(
        [
            turned(vis_weight * (gr * observed[0] + gi * observed[1])),
            turned(vis_weight * (gr * observed[1] - gi * observed[0])),
        ]
    )
    return scale, data


def patch_gradient(state, scale, data):
    ty, tx = lax.axis_size("ty"), lax.axis_size("tx")
    devices = ty * tx
    rows, cols, _ = state.shape
    own = rows // tx
    slab = N // devices
    first, twist, second, second_t = (jnp.asarray(value) for value in row_constants())
    outer, outer_t, inner, inner_t = (
        jnp.asarray(value) for value in column_constants(devices, slab)
    )
    gathered = lax.all_to_all(
        state.reshape(tx, own, cols, PIXELS), "tx", split_axis=0, concat_axis=0, tiled=True
    )
    sent = pl.pallas_call(
        row_forward,
        out_shape=jax.ShapeDtypeStruct((PATCH, devices // PATCH, 2, slab, slab), BF16),
        compiler_params=PARAMS,
    )(gathered, first, twist, second)
    moved = lax.all_to_all(
        sent.reshape(devices, 2, slab, slab), ("ty", "tx"), split_axis=0, concat_axis=0, tiled=True
    )
    waves = pl.pallas_call(
        column_both,
        out_shape=jax.ShapeDtypeStruct((devices, 2, slab, slab), BF16),
        scratch_shapes=[pltpu.VMEM((devices, 2, slab, slab), BF16)],
        compiler_params=PARAMS,
    )(moved, scale, data, outer, outer_t, inner, inner_t)
    returned = lax.all_to_all(waves, ("ty", "tx"), split_axis=0, concat_axis=0, tiled=True)
    slabs = pl.pallas_call(
        row_inverse,
        out_shape=jax.ShapeDtypeStruct((tx, own, cols, PIXELS), BF16),
        compiler_params=PARAMS,
    )(returned.reshape(PATCH, devices // PATCH, 2, slab, slab), first, twist, second_t)
    grad = lax.all_to_all(slabs, "tx", split_axis=0, concat_axis=0, tiled=True)
    return grad.reshape(rows, cols, PIXELS)


def layer_norm(values, gain):
    centre = jnp.mean(values, axis=-1, keepdims=True)
    shifted = values - centre
    spread = jnp.mean(shifted * shifted, axis=-1, keepdims=True)
    return (shifted * lax.rsqrt(spread + EPSILON) * gain).astype(BF16)


def to_windows(band):
    rows, cols, feats = band.shape
    pieces = [
        band[:, w * WIN : (w + 1) * WIN, :].reshape(SPAN, feats) for w in range(cols // WIN)
    ]
    return jnp.concatenate(pieces, axis=0)


def from_windows(tokens, cols):
    feats = tokens.shape[-1]
    pieces = [
        tokens[w * SPAN : (w + 1) * SPAN].reshape(WIN, WIN, feats) for w in range(cols // WIN)
    ]
    return jnp.concatenate(pieces, axis=1)


def swin_band(flow, bias_ref, qkv_ref, proj_ref, up_ref, down_ref, gain_ref, mixed_ref, att_ref):
    tokens = flow.shape[0]
    normed = layer_norm(flow, gain_ref[0:1, :])
    depth = D // HEADS
    scale = 1.0 / math.sqrt(depth)
    mixed_ref[:, :D] = (mm(normed, qkv_ref[:, :D]) * scale).astype(BF16)
    mixed_ref[:, D:] = mm(normed, qkv_ref[:, D:]).astype(BF16)
    lane = lax.broadcasted_iota(jnp.int32, (SPAN, 2 * depth), 1)
    lower = lane < depth
    for w in range(tokens // SPAN):
        rows = slice(w * SPAN, (w + 1) * SPAN)
        bias = bias_ref[w]
        for p in range(HEADS // 2):
            lanes = slice(p * 2 * depth, (p + 1) * 2 * depth)
            query = mixed_ref[rows, lanes]
            key = mixed_ref[rows, D + p * 2 * depth : D + (p + 1) * 2 * depth]
            value = mixed_ref[rows, 2 * D + p * 2 * depth : 2 * D + (p + 1) * 2 * depth]
            zero = jnp.zeros_like(query)
            split = jnp.concatenate(
                [jnp.where(lower, query, zero), jnp.where(lower, zero, query)], axis=0
            )
            scores = mm(key, split, NT) + bias
            weights = jnp.exp(scores - jnp.max(scores, axis=0, keepdims=True))
            probs = weights * (1.0 / jnp.sum(weights, axis=0, keepdims=True))
            mixture = mm(probs.astype(BF16), value, TN)
            att_ref[rows, lanes] = jnp.where(lower, mixture[:SPAN], mixture[SPAN:]).astype(BF16)
    flow = flow + mm(att_ref[...], proj_ref[...])
    normed = layer_norm(flow, gain_ref[1:2, :])
    hidden_size = up_ref.shape[1]
    for c in range(hidden_size // D):
        part = slice(c * D, (c + 1) * D)
        hidden = jax.nn.gelu(mm(normed, up_ref[:, part]), approximate=True)
        flow = flow + mm(hidden.astype(BF16), down_ref[part, :])
    return flow


def first_kernel(
    zeta, state_ref, grad_ref, bias_ref, embed_ref, qkv_ref, proj_ref, up_ref, down_ref, gain_ref,
    half_ref, out_ref, mixed_ref, att_ref,
):
    half = state_ref[...] - zeta * grad_ref[...].astype(F32)
    half_ref[...] = half
    tokens = mm(to_windows(half).astype(BF16), embed_ref[...]).astype(BF16).astype(F32)
    flow = swin_band(
        tokens, bias_ref, qkv_ref, proj_ref, up_ref, down_ref, gain_ref, mixed_ref, att_ref
    )
    out_ref[...] = from_windows(flow, half.shape[1]).astype(BF16)


def second_kernel(
    shift_ref, grid_ref, bias_ref, qkv_ref, proj_ref, up_ref, down_ref, gain_ref, unembed_ref,
    out_ref, mixed_ref, att_ref,
):
    cols = out_ref.shape[1]
    top = pl.program_id(0) * WIN + shift_ref[0]
    wide = grid_ref[pl.ds(top, WIN)]
    place = lax.broadcasted_iota(jnp.int32, (cols, wide.shape[1]), 1)
    target = lax.broadcasted_iota(jnp.int32, (cols, wide.shape[1]), 0) + shift_ref[1]
    pick = jnp.where(place == target, 1.0, 0.0).astype(BF16)
    band = jnp.stack([mm(pick, wide[n]) for n in range(WIN)])
    flow = swin_band(
        to_windows(band), bias_ref, qkv_ref, proj_ref, up_ref, down_ref, gain_ref, mixed_ref, att_ref
    )
    estimate = mm(flow.astype(BF16), unembed_ref[...])
    out_ref[...] = from_windows(estimate, cols).astype(BF16)


def whole(array):
    zeros = (0,) * array.ndim
    return pl.BlockSpec(array.shape, lambda *_: zeros)


def band_spec(cols, feats):
    return pl.BlockSpec((WIN, cols, feats), lambda n, *_: (n, 0, 0))


def bias_spec(cols):
    return pl.BlockSpec((cols // WIN, SPAN, 2 * SPAN), lambda n, *_: (n, 0, 0))


def band_scratch(cols):
    return [pltpu.VMEM((WIN * cols, 3 * D), BF16), pltpu.VMEM((WIN * cols, D), BF16)]


def first_block(zeta, state, grad, bias, w_embed, weights):
    rows, cols, _ = state.shape
    return pl.pallas_call(
        functools.partial(first_kernel, zeta),
        grid=(rows // WIN,),
        in_specs=[band_spec(cols, PIXELS), band_spec(cols, PIXELS), bias_spec(cols), whole(w_embed)]
        + [whole(value) for value in weights],
        out_specs=[band_spec(cols, PIXELS), band_spec(cols, D)],
        out_shape=[
            jax.ShapeDtypeStruct((rows, cols, PIXELS), F32),
            jax.ShapeDtypeStruct((rows, cols, D), BF16),
        ],
        scratch_shapes=band_scratch(cols),
        compiler_params=PARAMS,
    )(state, grad, bias, w_embed, *weights)


def second_block(shift, grid, bias, w_unembed, weights, rows, cols):
    return pl.pallas_call(
        second_kernel,
        grid_spec=pltpu.PrefetchScalarGridSpec(
            num_scalar_prefetch=1,
            grid=(rows // WIN,),
            in_specs=[whole(grid), bias_spec(cols)]
            + [whole(value) for value in weights]
            + [whole(w_unembed)],
            out_specs=band_spec(cols, PIXELS),
            scratch_shapes=band_scratch(cols),
        ),
        out_shape=jax.ShapeDtypeStruct((rows, cols, PIXELS), BF16),
        compiler_params=PARAMS,
    )(shift, grid, bias, *weights, w_unembed)


def from_behind(shard, axis, by):
    size = lax.axis_size(axis)
    return lax.ppermute(shard, axis, [(i, (i + by) % size) for i in range(size)])


def with_next(grid):
    wide = jnp.concatenate([grid, from_behind(grid[:, :WIN], "tx", -1)], axis=1)
    return jnp.concatenate([wide, from_behind(wide[:WIN], "ty", -1)], axis=0)


def with_previous(grid):
    wide = jnp.concatenate([from_behind(grid[:, -WIN:], "tx", 1), grid], axis=1)
    return jnp.concatenate([from_behind(wide[-WIN:], "ty", 1), wide], axis=0)


def windows_of(grid):
    rows, cols = grid.shape
    shaped = grid.reshape(rows // WIN, WIN, cols // WIN, WIN).transpose(0, 2, 1, 3)
    return shaped.reshape(rows // WIN * (cols // WIN), SPAN)


def bias_of(labels, keep):
    allowed = jnp.ones((1, SPAN, SPAN), bool)
    if labels is not None:
        label = windows_of(labels)
        allowed = label[:, :, None] == label[:, None, :]
    if keep is not None:
        kept = windows_of(keep)[:, :, None] == 1
        allowed = allowed & (kept | jnp.eye(SPAN, dtype=bool)[None])
    bias = jnp.where(allowed, 0.0, -1e30).astype(F32)
    return jnp.concatenate([bias, bias], axis=2)


def region(index, shift):
    return jnp.where(index < TOK - WIN, 0, jnp.where(index < TOK - shift, 1, 2)).astype(jnp.int32)


def patches_of(picture):
    rows, cols = picture.shape
    shaped = picture.reshape(rows // PATCH, PATCH, cols // PATCH, PATCH).transpose(0, 2, 1, 3)
    return shaped.reshape(rows // PATCH, cols // PATCH, PIXELS)


def image_of(pieces):
    rows, cols = (pieces.shape[0], pieces.shape[1])
    shaped = pieces.reshape(rows, cols, PATCH, PATCH).transpose(0, 2, 1, 3)
    return shaped.reshape(rows * PATCH, cols * PATCH)


def per_device(
    image, noise, offsets, key_mask, gains, observed, vis_weight,
    w_embed, w_qkv, w_proj, w_up, w_down, w_unembed, norm_gains,
):
    rows = image.shape[0] // PATCH
    cols = image.shape[1] // PATCH
    devices = lax.axis_size("ty") * lax.axis_size("tx")
    fast = N // devices == TOK // 2
    row_index = lax.axis_index("ty") * rows + counting(rows)
    col_index = lax.axis_index("tx") * cols + counting(cols)
    weights = [
        (w_qkv[j], w_proj[j], w_up[j], w_down[j], norm_gains[j]) for j in range(w_qkv.shape[0])
    ]
    state = patches_of(image)
    if fast:
        scale, data = spectrum_inputs(gains, observed, vis_weight, devices)
    first_bias = bias_of(None, key_mask)
    for step in range(STEPS):
        if fast:
            grad = patch_gradient(state.astype(BF16), scale, data)
        else:
            grad = patches_of(plain_gradient(image_of(state), gains, observed, vis_weight))
        half, first = first_block(STEP_SIZES[step], state, grad, first_bias, w_embed, weights[0])
        shift_rows = offsets[step, 0]
        shift_cols = offsets[step, 1]
        labels = 3 * region(row_index, shift_rows)[:, None] + region(col_index, shift_cols)[None, :]
        second_bias = bias_of(labels, None)
        rolled = second_block(
            offsets[step], with_next(first), second_bias, w_unembed, weights[1], rows, cols
        )
        estimate = lax.dynamic_slice(
            with_previous(rolled),
            (WIN - shift_rows, WIN - shift_cols, jnp.zeros((), jnp.int32)),
            (rows, cols, PIXELS),
        )
        state = half - SIGMAS[step] * estimate.astype(F32)
        if step + 1 < STEPS:
            state = state + SIGMAS[step + 1] * patches_of(noise[step])
    return image_of(state) + SIGMAS[STEPS] * noise[STEPS - 1]


def solution(mesh):
    in_specs = (
        P("ty", "tx"),
        P(None, "ty", "tx"),
        P(),
        P("ty", "tx"),
        P(None, ("ty", "tx"), None),
        P(None, ("ty", "tx"), None),
        P(("ty", "tx"), None),
        P(),
        P(),
        P(),
        P(),
        P(),
        P(),
        P(),
    )
    out_specs = P("ty", "tx")
    return jax.shard_map(
        per_device, mesh=mesh, in_specs=in_specs, out_specs=out_specs, check_vma=False
    )
```

```python
import functools
import math

import jax
import jax.numpy as jnp
import ml_dtypes
import numpy as np
from jax import lax
from jax.experimental import pallas as pl
from jax.experimental.pallas import tpu as pltpu
from jax.sharding import PartitionSpec as P

N = 4096
PATCH = 16
PIXELS = PATCH * PATCH
WIN = 8
D = 512
HEADS = 8
STEPS = 2
SPAN = WIN * WIN
LANES = 128
TOK = N // PATCH

SIGMAS = (0.8, 0.5, 0.3)
STEP_SIZES = (0.9, 0.7)
EPSILON = 1e-05
HIGHEST = lax.Precision.HIGHEST
BF16 = jnp.bfloat16
F32 = jnp.float32
GELU_IN = math.sqrt(2.0 / math.pi)
GELU_CUBE = 0.044715 * GELU_IN
VMEM_LIMIT = 56 * 1024 * 1024
PARAMS = pltpu.CompilerParams(vmem_limit_bytes=VMEM_LIMIT)
TN = (((0,), (0,)), ((), ()))
NT = (((1,), (1,)), ((), ()))
NN = (((1,), (0,)), ((), ()))


def mm(left, right, dims=NN):
    return lax.dot_general(left, right, dims, preferred_element_type=F32)


def counting(length):
    return jnp.arange(length, dtype=jnp.int32)


def roots(length, outer, inner, sign):
    product = outer[:, None] * inner[None, :] % length
    angle = 2.0 * math.pi / length * product.astype(F32)
    return (jnp.cos(angle), sign * jnp.sin(angle))


def complex_einsum(form, left, right):
    real = jnp.einsum(form, left[0], right[0], precision=HIGHEST) - jnp.einsum(
        form, left[1], right[1], precision=HIGHEST
    )
    imag = jnp.einsum(form, left[0], right[1], precision=HIGHEST) + jnp.einsum(
        form, left[1], right[0], precision=HIGHEST
    )
    return (real, imag)


def complex_times(left, right):
    return (left[0] * right[0] - left[1] * right[1], left[0] * right[1] + left[1] * right[0])


def along_last(real_part, imag_part, groups, sign):
    rows, length = real_part.shape
    inner = length // groups
    first = roots(groups, counting(groups), counting(groups), sign)
    twist = roots(length, counting(inner), counting(groups), sign)
    second = roots(inner, counting(inner), counting(inner), sign)
    shaped = real_part.reshape(rows, groups, inner)
    if imag_part is None:
        partial_value = (
            jnp.einsum("mab,ka->mbk", shaped, first[0], precision=HIGHEST),
            jnp.einsum("mab,ka->mbk", shaped, first[1], precision=HIGHEST),
        )
    else:
        partial_value = complex_einsum(
            "mab,ka->mbk", (shaped, imag_part.reshape(rows, groups, inner)), first
        )
    partial_value = complex_times(partial_value, twist)
    result = complex_einsum("jb,mbk->mjk", second, partial_value)
    return (result[0].reshape(rows, length), result[1].reshape(rows, length))


def across_groups(pair, groups, sign):
    inner, cols = pair[0].shape
    width = cols // groups
    length = groups * inner
    first = roots(groups, counting(groups), counting(groups), sign)
    twist = roots(length, counting(inner), counting(groups), sign)
    second = roots(inner, counting(inner), counting(inner), sign)
    shaped = (pair[0].reshape(inner, groups, width), pair[1].reshape(inner, groups, width))
    partial_value = complex_einsum("bhc,kh->cbk", shaped, first)
    partial_value = complex_times(partial_value, twist)
    result = complex_einsum("jb,cbk->cjk", second, partial_value)
    return (result[0].reshape(width, length), result[1].reshape(width, length))


def exchange_pair(pair):
    return tuple(
        lax.all_to_all(
            part.astype(BF16), ("ty", "tx"), split_axis=1, concat_axis=1, tiled=True
        ).astype(F32)
        for part in pair
    )


def plain_gradient(tile, gains, observed, vis_weight):
    devices = lax.axis_size("ty") * lax.axis_size("tx")
    slab = lax.all_to_all(tile.astype(BF16), "tx", split_axis=0, concat_axis=1, tiled=True)
    moved = exchange_pair(along_last(slab.astype(F32), None, devices, -1.0))
    spectrum = across_groups(moved, devices, -1.0)
    spectrum = (spectrum[0] * (1.0 / N), spectrum[1] * (1.0 / N))
    model = complex_times((gains[0], gains[1]), spectrum)
    misfit = (vis_weight * (model[0] - observed[0]), vis_weight * (model[1] - observed[1]))
    back = complex_times((gains[0], -gains[1]), misfit)
    returned = exchange_pair(along_last(back[0], back[1], devices, 1.0))
    slab_grad = across_groups(returned, devices, 1.0)[0] * (1.0 / N)
    return lax.all_to_all(slab_grad.astype(BF16), "tx", split_axis=1, concat_axis=0, tiled=True)


def embed_complex(angle, row_axis, col_axis):
    cos, sin = np.cos(angle), np.sin(angle)
    top = np.stack([cos, sin], axis=col_axis)
    bottom = np.stack([-sin, cos], axis=col_axis)
    return np.stack([top, bottom], axis=row_axis)


def wheel(length, product):
    return 2.0 * math.pi / length * (product % length)


@functools.lru_cache(maxsize=None)
def row_constants():
    k = np.arange(TOK)
    angle = wheel(TOK, k[:, None] * k[None, :])
    first = np.concatenate([np.cos(angle), -np.sin(angle)], axis=1)
    b = np.repeat(np.arange(PATCH), PATCH)
    angle = wheel(N, b[:, None] * k[None, :])
    twist = np.stack([np.cos(angle), -np.sin(angle)])
    p = np.arange(PATCH)
    small = embed_complex(wheel(PATCH, p[:, None] * p[None, :]), 1, 1)
    second = np.einsum("kpqb,xy->kpxqby", small, np.eye(PATCH)).reshape(2 * PIXELS, 2 * PIXELS)
    return (
        first.astype(ml_dtypes.bfloat16),
        twist.astype(np.float32),
        second.astype(ml_dtypes.bfloat16),
        np.ascontiguousarray(second.T).astype(ml_dtypes.bfloat16),
    )


@functools.lru_cache(maxsize=None)
def column_constants(devices, rows):
    s = np.arange(devices)
    small = embed_complex(wheel(devices, s[:, None] * s[None, :]), 1, 2)
    wide = devices * 2 * PATCH
    outer = np.einsum("qpsr,xy->qpxsry", small, np.eye(PATCH)).reshape(wide, wide)
    kr = s[:, None] + devices * np.arange(rows)[None, :]
    angle = wheel(N, kr[:, :, None] * np.arange(rows)[None, None, :])
    inner = embed_complex(angle, 1, 2).reshape(devices, 2 * rows, 2 * rows) / N
    return tuple(
        np.ascontiguousarray(value).astype(ml_dtypes.bfloat16)
        for value in (outer, outer.T, inner, inner.transpose(0, 2, 1))
    )


def row_forward(x_ref, first_ref, twist_ref, second_ref, out_ref):
    count = x_ref.shape[1]

    def step(i, carry):
        band = x_ref[:, i].reshape(TOK, PIXELS)
        mixed = mm(band, first_ref[...], TN)
        real, imag = mixed[:, :TOK], mixed[:, TOK:]
        tr, ti = twist_ref[0], twist_ref[1]
        turned = jnp.concatenate(
            [(real * tr - imag * ti).astype(BF16), (real * ti + imag * tr).astype(BF16)], axis=0
        )
        result = mm(second_ref[...], turned).astype(BF16).reshape(PATCH, 2, PATCH, TOK)
        half = TOK // 2
        rows = pl.ds(pl.multiple_of(i * PATCH, PATCH), PATCH)
        out_ref[:, 0, :, rows, :] = result[..., :half]
        out_ref[:, 1, :, rows, :] = result[..., half:]
        return carry

    lax.fori_loop(0, count, step, 0)


def row_inverse(v_ref, first_ref, twist_ref, second_ref, out_ref):
    parts, count, cols, _ = out_ref.shape

    def step(i, carry):
        rows = pl.ds(pl.multiple_of(i * PATCH, PATCH), PATCH)
        wide = jnp.concatenate(
            [
                v_ref[:, 0, :, rows, :].reshape(2 * PIXELS, TOK // 2),
                v_ref[:, 1, :, rows, :].reshape(2 * PIXELS, TOK // 2),
            ],
            axis=1,
        )
        mixed = mm(second_ref[...], wide)
        real, imag = mixed[:PIXELS], mixed[PIXELS:]
        tr, ti = twist_ref[0], twist_ref[1]
        turned = jnp.concatenate(
            [(real * tr + imag * ti).astype(BF16), (imag * tr - real * ti).astype(BF16)], axis=1
        )
        result = mm(first_ref[...], turned, NT).astype(BF16)
        out_ref[:, i] = result.reshape(parts, cols, PIXELS)
        return carry

    lax.fori_loop(0, count, step, 0)


def column_both(
    x_ref, scale_ref, data_ref, outer_ref, outer_t_ref, inner_ref, inner_t_ref, out_ref, mid_ref
):
    devices, _, rows, width = x_ref.shape
    wide = devices * 2 * PATCH

    def turn(source, target, matrix):
        for pair in range(rows // (2 * PATCH)):
            first = slice(pair * 2 * PATCH, pair * 2 * PATCH + PATCH)
            second = slice(pair * 2 * PATCH + PATCH, (pair + 1) * 2 * PATCH)
            both = jnp.concatenate(
                [
                    source[:, :, first, :].reshape(wide, width),
                    source[:, :, second, :].reshape(wide, width),
                ],
                axis=1,
            )
            result = mm(matrix[...], both).astype(BF16)
            target[:, :, first, :] = result[:, :width].reshape(devices, 2, PATCH, width)
            target[:, :, second, :] = result[:, width:].reshape(devices, 2, PATCH, width)

    turn(x_ref, mid_ref, outer_ref)

    def step(q, carry):
        spectrum = mm(inner_ref[q], mid_ref[q].reshape(2 * rows, width)).reshape(2, rows, width)
        scale = scale_ref[q].astype(F32)
        back = spectrum * scale[None] - data_ref[:, q].astype(F32)
        wave = mm(inner_t_ref[q], back.astype(BF16).reshape(2 * rows, width))
        mid_ref[q] = wave.astype(BF16).reshape(2, rows, width)
        return carry

    lax.fori_loop(0, devices, step, 0, unroll=4)
    turn(mid_ref, out_ref, outer_t_ref)


def spectrum_inputs(gains, observed, vis_weight, devices):
    width = vis_weight.shape[0]

    def turned(value):
        shaped = value.astype(BF16).reshape(width, N // devices, devices)
        return shaped.transpose(2, 1, 0)

    gr, gi = gains[0], gains[1]
    scale = turned(vis_weight * (gr * gr + gi * gi))
    data = jnp.stack(
        [
            turned(vis_weight * (gr * observed[0] + gi * observed[1])),
            turned(vis_weight * (gr * observed[1] - gi * observed[0])),
        ]
    )
    return scale, data


def patch_gradient(state, scale, data):
    ty, tx = lax.axis_size("ty"), lax.axis_size("tx")
    devices = ty * tx
    rows, cols, _ = state.shape
    own = rows // tx
    slab = N // devices
    first, twist, second, second_t = (jnp.asarray(value) for value in row_constants())
    outer, outer_t, inner, inner_t = (
        jnp.asarray(value) for value in column_constants(devices, slab)
    )
    gathered = lax.all_to_all(
        state.reshape(tx, own, cols, PIXELS), "tx", split_axis=0, concat_axis=0, tiled=True
    )
    sent = pl.pallas_call(
        row_forward,
        out_shape=jax.ShapeDtypeStruct((PATCH, devices // PATCH, 2, slab, slab), BF16),
        compiler_params=PARAMS,
    )(gathered, first, twist, second)
    moved = lax.all_to_all(
        sent.reshape(devices, 2, slab, slab), ("ty", "tx"), split_axis=0, concat_axis=0, tiled=True
    )
    waves = pl.pallas_call(
        column_both,
        out_shape=jax.ShapeDtypeStruct((devices, 2, slab, slab), BF16),
        scratch_shapes=[pltpu.VMEM((devices, 2, slab, slab), BF16)],
        compiler_params=PARAMS,
    )(moved, scale, data, outer, outer_t, inner, inner_t)
    returned = lax.all_to_all(waves, ("ty", "tx"), split_axis=0, concat_axis=0, tiled=True)
    slabs = pl.pallas_call(
        row_inverse,
        out_shape=jax.ShapeDtypeStruct((tx, own, cols, PIXELS), BF16),
        compiler_params=PARAMS,
    )(returned.reshape(PATCH, devices // PATCH, 2, slab, slab), first, twist, second_t)
    grad = lax.all_to_all(slabs, "tx", split_axis=0, concat_axis=0, tiled=True)
    return grad.reshape(rows, cols, PIXELS)


def layer_norm(values, gain):
    centre = jnp.mean(values, axis=-1, keepdims=True)
    shifted = values - centre
    spread = jnp.mean(shifted * shifted, axis=-1, keepdims=True)
    return (shifted * lax.rsqrt(spread + EPSILON) * gain).astype(BF16)


def to_windows(band):
    rows, cols, feats = band.shape
    pieces = [
        band[:, w * WIN : (w + 1) * WIN, :].reshape(SPAN, feats) for w in range(cols // WIN)
    ]
    return jnp.concatenate(pieces, axis=0)


def from_windows(tokens, cols):
    feats = tokens.shape[-1]
    pieces = [
        tokens[w * SPAN : (w + 1) * SPAN].reshape(WIN, WIN, feats) for w in range(cols // WIN)
    ]
    return jnp.concatenate(pieces, axis=1)


def swin_band(
    flow, bias_ref, qkv_ref, proj_ref, up_ref, down_ref, gain_ref, mixed_ref, score_ref, prob_ref
):
    count = flow.shape[0] // SPAN
    pairs = HEADS // 2
    depth = D // HEADS
    wide = 2 * depth
    normed = layer_norm(flow, gain_ref[0:1, :])
    scale = 1.0 / math.sqrt(depth)
    mixed_ref[:, :D] = (mm(normed, qkv_ref[:, :D]) * scale).astype(BF16)
    mixed_ref[:, D : 2 * D] = mm(normed, qkv_ref[:, D : 2 * D]).astype(BF16)
    mixed_ref[:, 2 * D :] = mm(normed, qkv_ref[:, 2 * D :]).astype(BF16)
    lower = lax.broadcasted_iota(jnp.int32, (SPAN, wide), 1) < depth
    for w in range(count):
        rows = slice(w * SPAN, (w + 1) * SPAN)
        for p in range(pairs):
            query = mixed_ref[rows, p * wide : (p + 1) * wide]
            key = mixed_ref[rows, D + p * wide : D + (p + 1) * wide]
            zero = jnp.zeros_like(query)
            split = jnp.concatenate(
                [jnp.where(lower, query, zero), jnp.where(lower, zero, query)], axis=0
            )
            score_ref[w, :, p * wide : (p + 1) * wide] = mm(key, split, NT)
    for w in range(count):
        bias = bias_ref[w]
        for p in range(pairs):
            lanes = slice(p * wide, (p + 1) * wide)
            scores = score_ref[w, :, lanes] + bias
            weights = jnp.exp(scores - jnp.max(scores, axis=0, keepdims=True))
            share = 1.0 / jnp.sum(weights, axis=0, keepdims=True)
            prob_ref[w, :, lanes] = (weights * share).astype(BF16)
    for w in range(count):
        rows = slice(w * SPAN, (w + 1) * SPAN)
        for p in range(pairs):
            lanes = slice(p * wide, (p + 1) * wide)
            value = mixed_ref[rows, 2 * D + p * wide : 2 * D + (p + 1) * wide]
            mixture = mm(prob_ref[w, :, lanes], value, TN)
            mixed_ref[rows, lanes] = jnp.where(lower, mixture[:SPAN], mixture[SPAN:]).astype(BF16)
    flow = flow + mm(mixed_ref[:, :D], proj_ref[...])
    normed = layer_norm(flow, gain_ref[1:2, :])
    chunks = up_ref.shape[1] // D
    total = jnp.zeros_like(flow)
    ahead = mm(normed, up_ref[:, :D])
    for c in range(chunks):
        value = ahead
        if c + 1 < chunks:
            ahead = mm(normed, up_ref[:, (c + 1) * D : (c + 2) * D])
        inside = value * (GELU_IN + GELU_CUBE * (value * value))
        active = (value + value * jnp.tanh(inside)).astype(BF16)
        total = total + mm(active, down_ref[c * D : (c + 1) * D, :])
    return flow + 0.5 * total


def first_kernel(
    zeta, state_ref, grad_ref, bias_ref, embed_ref, qkv_ref, proj_ref, up_ref, down_ref, gain_ref,
    half_ref, out_ref, mixed_ref, score_ref, prob_ref,
):
    half = state_ref[...] - zeta * grad_ref[...].astype(F32)
    half_ref[...] = half
    tokens = mm(to_windows(half).astype(BF16), embed_ref[...]).astype(BF16).astype(F32)
    flow = swin_band(
        tokens, bias_ref, qkv_ref, proj_ref, up_ref, down_ref, gain_ref, mixed_ref, score_ref,
        prob_ref,
    )
    out_ref[...] = from_windows(flow, half.shape[1]).astype(BF16)


def second_kernel(
    shift_ref, grid_ref, bias_ref, qkv_ref, proj_ref, up_ref, down_ref, gain_ref, unembed_ref,
    out_ref, mixed_ref, score_ref, prob_ref,
):
    cols = out_ref.shape[1]
    top = pl.program_id(0) * WIN + shift_ref[0]
    wide = grid_ref[pl.ds(top, WIN)]
    place = lax.broadcasted_iota(jnp.int32, (cols, wide.shape[1]), 1)
    target = lax.broadcasted_iota(jnp.int32, (cols, wide.shape[1]), 0) + shift_ref[1]
    pick = jnp.where(place == target, 1.0, 0.0).astype(BF16)
    band = jnp.stack([mm(pick, wide[n]) for n in range(WIN)])
    flow = swin_band(
        to_windows(band), bias_ref, qkv_ref, proj_ref, up_ref, down_ref, gain_ref, mixed_ref,
        score_ref, prob_ref,
    )
    estimate = mm(flow.astype(BF16), unembed_ref[...])
    out_ref[...] = from_windows(estimate, cols).astype(BF16)


def whole(array):
    zeros = (0,) * array.ndim
    return pl.BlockSpec(array.shape, lambda *_: zeros)


def member(array, j):
    place = (j,) + (0,) * (array.ndim - 1)
    return pl.BlockSpec((None,) + array.shape[1:], lambda *_: place)


def band_spec(cols, feats):
    return pl.BlockSpec((WIN, cols, feats), lambda n, *_: (n, 0, 0))


def bias_spec(cols):
    return pl.BlockSpec((cols // WIN, SPAN, 2 * SPAN), lambda n, *_: (n, 0, 0))


def band_scratch(cols):
    count = cols // WIN
    return [
        pltpu.VMEM((WIN * cols, 3 * D), BF16),
        pltpu.VMEM((count, SPAN, HEADS * SPAN), F32),
        pltpu.VMEM((count, SPAN, HEADS * SPAN), BF16),
    ]


def first_block(zeta, state, grad, bias, w_embed, weights):
    rows, cols, _ = state.shape
    return pl.pallas_call(
        functools.partial(first_kernel, zeta),
        grid=(rows // WIN,),
        in_specs=[band_spec(cols, PIXELS), band_spec(cols, PIXELS), bias_spec(cols), whole(w_embed)]
        + [member(value, 0) for value in weights],
        out_specs=[band_spec(cols, PIXELS), band_spec(cols, D)],
        out_shape=[
            jax.ShapeDtypeStruct((rows, cols, PIXELS), F32),
            jax.ShapeDtypeStruct((rows, cols, D), BF16),
        ],
        scratch_shapes=band_scratch(cols),
        compiler_params=PARAMS,
    )(state, grad, bias, w_embed, *weights)


def second_block(shift, grid, bias, w_unembed, weights, rows, cols):
    return pl.pallas_call(
        second_kernel,
        grid_spec=pltpu.PrefetchScalarGridSpec(
            num_scalar_prefetch=1,
            grid=(rows // WIN,),
            in_specs=[whole(grid), bias_spec(cols)]
            + [member(value, 1) for value in weights]
            + [whole(w_unembed)],
            out_specs=band_spec(cols, PIXELS),
            scratch_shapes=band_scratch(cols),
        ),
        out_shape=jax.ShapeDtypeStruct((rows, cols, PIXELS), BF16),
        compiler_params=PARAMS,
    )(shift, grid, bias, *weights, w_unembed)


def from_behind(shard, axis, by):
    size = lax.axis_size(axis)
    return lax.ppermute(shard, axis, [(i, (i + by) % size) for i in range(size)])


def with_next(grid):
    wide = jnp.concatenate([grid, from_behind(grid[:, :WIN], "tx", -1)], axis=1)
    return jnp.concatenate([wide, from_behind(wide[:WIN], "ty", -1)], axis=0)


def with_previous(grid):
    wide = jnp.concatenate([from_behind(grid[:, -WIN:], "tx", 1), grid], axis=1)
    return jnp.concatenate([from_behind(wide[-WIN:], "ty", 1), wide], axis=0)


def windows_of(grid):
    rows, cols = grid.shape
    shaped = grid.reshape(rows // WIN, WIN, cols // WIN, WIN).transpose(0, 2, 1, 3)
    return shaped.reshape(rows // WIN * (cols // WIN), SPAN)


def bias_of(labels, keep):
    allowed = jnp.ones((1, SPAN, SPAN), bool)
    if labels is not None:
        label = windows_of(labels)
        allowed = label[:, :, None] == label[:, None, :]
    if keep is not None:
        kept = windows_of(keep)[:, :, None] == 1
        allowed = allowed & (kept | jnp.eye(SPAN, dtype=bool)[None])
    bias = jnp.where(allowed, 0.0, -1e30).astype(F32)
    return jnp.concatenate([bias, bias], axis=2)


def region(index, shift):
    return jnp.where(index < TOK - WIN, 0, jnp.where(index < TOK - shift, 1, 2)).astype(jnp.int32)


@functools.lru_cache(maxsize=None)
def lane_order(cols):
    parts = LANES // cols
    groups = PATCH // parts
    lane = np.arange(PATCH * cols)
    g, h, k = lane // LANES, lane % LANES // cols, lane % cols
    source = PATCH * k + h * groups + g
    matrix = np.zeros((PATCH * cols, PATCH * cols), np.float32)
    matrix[source, lane] = 1.0
    return matrix.astype(ml_dtypes.bfloat16), np.ascontiguousarray(matrix.T).astype(
        ml_dtypes.bfloat16
    )


def move_lanes(values, matrix):
    high = values.astype(BF16)
    low = (values - high.astype(F32)).astype(BF16)
    return mm(high, matrix) + mm(low, matrix)


def to_patches_kernel(tile_ref, order_ref, out_ref):
    count, cols, _ = out_ref.shape
    parts = LANES // cols
    groups = PATCH // parts
    ordered = move_lanes(tile_ref[...], order_ref[...])
    for i in range(count):
        band = ordered[i * PATCH : (i + 1) * PATCH]
        stacked = jnp.concatenate(
            [band[:, g * LANES : (g + 1) * LANES] for g in range(groups)], axis=0
        )
        turned = stacked.T
        out_ref[i] = jnp.concatenate(
            [turned[h * cols : (h + 1) * cols] for h in range(parts)], axis=1
        )


def to_tile_kernel(scale, patch_ref, noise_ref, order_ref, out_ref):
    count, cols, _ = patch_ref.shape
    parts = LANES // cols
    groups = PATCH // parts
    width = groups * PATCH
    bands = []
    for i in range(count):
        patch = patch_ref[i]
        stacked = jnp.concatenate(
            [patch[:, h * width : (h + 1) * width] for h in range(parts)], axis=0
        )
        turned = stacked.T
        bands.append(
            jnp.concatenate([turned[g * PATCH : (g + 1) * PATCH] for g in range(groups)], axis=1)
        )
    moved = move_lanes(jnp.concatenate(bands, axis=0), order_ref[...])
    out_ref[...] = moved + scale * noise_ref[...]


def patches_of(tiles, j):
    rows, cols = tiles.shape[1] // PATCH, tiles.shape[2] // PATCH
    order = jnp.asarray(lane_order(cols)[0])
    step = rows // 4
    return pl.pallas_call(
        to_patches_kernel,
        grid=(rows // step,),
        in_specs=[
            pl.BlockSpec((None, step * PATCH, cols * PATCH), lambda n: (j, n, 0)),
            whole(order),
        ],
        out_specs=pl.BlockSpec((step, cols, PIXELS), lambda n: (n, 0, 0)),
        out_shape=jax.ShapeDtypeStruct((rows, cols, PIXELS), F32),
        compiler_params=PARAMS,
    )(tiles, order)


def tile_of(patches, scale, noise, j):
    rows, cols, _ = patches.shape
    order = jnp.asarray(lane_order(cols)[1])
    step = rows // 4
    return pl.pallas_call(
        functools.partial(to_tile_kernel, scale),
        grid=(rows // step,),
        in_specs=[
            pl.BlockSpec((step, cols, PIXELS), lambda n: (n, 0, 0)),
            pl.BlockSpec((None, step * PATCH, cols * PATCH), lambda n: (j, n, 0)),
            whole(order),
        ],
        out_specs=pl.BlockSpec((step * PATCH, cols * PATCH), lambda n: (n, 0)),
        out_shape=jax.ShapeDtypeStruct((rows * PATCH, cols * PATCH), F32),
        compiler_params=PARAMS,
    )(patches, noise, order)


def per_device(
    image, noise, offsets, key_mask, gains, observed, vis_weight,
    w_embed, w_qkv, w_proj, w_up, w_down, w_unembed, norm_gains,
):
    rows = image.shape[0] // PATCH
    cols = image.shape[1] // PATCH
    devices = lax.axis_size("ty") * lax.axis_size("tx")
    fast = N // devices == TOK // 2
    row_index = lax.axis_index("ty") * rows + counting(rows)
    col_index = lax.axis_index("tx") * cols + counting(cols)
    weights = (w_qkv, w_proj, w_up, w_down, norm_gains)
    w_embed = w_embed.reshape(PATCH, PATCH, D).transpose(1, 0, 2).reshape(PIXELS, D)
    w_unembed = w_unembed.reshape(D, PATCH, PATCH).transpose(0, 2, 1).reshape(D, PIXELS)
    state = patches_of(image[None], 0)
    if fast:
        scale, data = spectrum_inputs(gains, observed, vis_weight, devices)
    first_bias = bias_of(None, key_mask)
    for step in range(STEPS):
        if fast:
            grad = patch_gradient(state.astype(BF16), scale, data)
        else:
            grad = plain_gradient(tile_of(state, 0.0, noise, 0), gains, observed, vis_weight)
            grad = patches_of(grad.astype(F32)[None], 0).astype(BF16)
        half, first = first_block(STEP_SIZES[step], state, grad, first_bias, w_embed, weights)
        shift_rows = offsets[step, 0]
        shift_cols = offsets[step, 1]
        labels = 3 * region(row_index, shift_rows)[:, None] + region(col_index, shift_cols)[None, :]
        second_bias = bias_of(labels, None)
        rolled = second_block(
            offsets[step], with_next(first), second_bias, w_unembed, weights, rows, cols
        )
        estimate = lax.dynamic_slice(
            with_previous(rolled),
            (WIN - shift_rows, WIN - shift_cols, jnp.zeros((), jnp.int32)),
            (rows, cols, PIXELS),
        )
        state = half - SIGMAS[step] * estimate.astype(F32)
        if step + 1 < STEPS:
            state = state + SIGMAS[step + 1] * patches_of(noise, step)
    return tile_of(state, SIGMAS[STEPS], noise, STEPS - 1)


def solution(mesh):
    in_specs = (
        P("ty", "tx"),
        P(None, "ty", "tx"),
        P(),
        P("ty", "tx"),
        P(None, ("ty", "tx"), None),
        P(None, ("ty", "tx"), None),
        P(("ty", "tx"), None),
        P(),
        P(),
        P(),
        P(),
        P(),
        P(),
        P(),
    )
    out_specs = P("ty", "tx")
    return jax.shard_map(
        per_device, mesh=mesh, in_specs=in_specs, out_specs=out_specs, check_vma=False
    )
```

```python
import functools
import math

import jax
import jax.numpy as jnp
import ml_dtypes
import numpy as np
from jax import lax
from jax.experimental import pallas as pl
from jax.experimental.pallas import tpu as pltpu
from jax.sharding import PartitionSpec as P

N = 4096
PATCH = 16
PIXELS = PATCH * PATCH
WIN = 8
D = 512
HEADS = 8
STEPS = 2
SPAN = WIN * WIN
LANES = 128
CHUNKS = 2
TOK = N // PATCH

SIGMAS = (0.8, 0.5, 0.3)
STEP_SIZES = (0.9, 0.7)
EPSILON = 1e-05
HIGHEST = lax.Precision.HIGHEST
BF16 = jnp.bfloat16
F32 = jnp.float32
GELU_IN = math.sqrt(2.0 / math.pi)
GELU_CUBE = 0.044715 * GELU_IN
VMEM_LIMIT = 56 * 1024 * 1024
PARAMS = pltpu.CompilerParams(vmem_limit_bytes=VMEM_LIMIT)
TN = (((0,), (0,)), ((), ()))
NT = (((1,), (1,)), ((), ()))
NN = (((1,), (0,)), ((), ()))


def mm(left, right, dims=NN):
    return lax.dot_general(left, right, dims, preferred_element_type=F32)


def counting(length):
    return jnp.arange(length, dtype=jnp.int32)


def roots(length, outer, inner, sign):
    product = outer[:, None] * inner[None, :] % length
    angle = 2.0 * math.pi / length * product.astype(F32)
    return (jnp.cos(angle), sign * jnp.sin(angle))


def complex_einsum(form, left, right):
    real = jnp.einsum(form, left[0], right[0], precision=HIGHEST) - jnp.einsum(
        form, left[1], right[1], precision=HIGHEST
    )
    imag = jnp.einsum(form, left[0], right[1], precision=HIGHEST) + jnp.einsum(
        form, left[1], right[0], precision=HIGHEST
    )
    return (real, imag)


def complex_times(left, right):
    return (left[0] * right[0] - left[1] * right[1], left[0] * right[1] + left[1] * right[0])


def along_last(real_part, imag_part, groups, sign):
    rows, length = real_part.shape
    inner = length // groups
    first = roots(groups, counting(groups), counting(groups), sign)
    twist = roots(length, counting(inner), counting(groups), sign)
    second = roots(inner, counting(inner), counting(inner), sign)
    shaped = real_part.reshape(rows, groups, inner)
    if imag_part is None:
        partial_value = (
            jnp.einsum("mab,ka->mbk", shaped, first[0], precision=HIGHEST),
            jnp.einsum("mab,ka->mbk", shaped, first[1], precision=HIGHEST),
        )
    else:
        partial_value = complex_einsum(
            "mab,ka->mbk", (shaped, imag_part.reshape(rows, groups, inner)), first
        )
    partial_value = complex_times(partial_value, twist)
    result = complex_einsum("jb,mbk->mjk", second, partial_value)
    return (result[0].reshape(rows, length), result[1].reshape(rows, length))


def across_groups(pair, groups, sign):
    inner, cols = pair[0].shape
    width = cols // groups
    length = groups * inner
    first = roots(groups, counting(groups), counting(groups), sign)
    twist = roots(length, counting(inner), counting(groups), sign)
    second = roots(inner, counting(inner), counting(inner), sign)
    shaped = (pair[0].reshape(inner, groups, width), pair[1].reshape(inner, groups, width))
    partial_value = complex_einsum("bhc,kh->cbk", shaped, first)
    partial_value = complex_times(partial_value, twist)
    result = complex_einsum("jb,cbk->cjk", second, partial_value)
    return (result[0].reshape(width, length), result[1].reshape(width, length))


def exchange_pair(pair):
    return tuple(
        lax.all_to_all(
            part.astype(BF16), ("ty", "tx"), split_axis=1, concat_axis=1, tiled=True
        ).astype(F32)
        for part in pair
    )


def plain_gradient(tile, gains, observed, vis_weight):
    devices = lax.axis_size("ty") * lax.axis_size("tx")
    slab = lax.all_to_all(tile.astype(BF16), "tx", split_axis=0, concat_axis=1, tiled=True)
    moved = exchange_pair(along_last(slab.astype(F32), None, devices, -1.0))
    spectrum = across_groups(moved, devices, -1.0)
    spectrum = (spectrum[0] * (1.0 / N), spectrum[1] * (1.0 / N))
    model = complex_times((gains[0], gains[1]), spectrum)
    misfit = (vis_weight * (model[0] - observed[0]), vis_weight * (model[1] - observed[1]))
    back = complex_times((gains[0], -gains[1]), misfit)
    returned = exchange_pair(along_last(back[0], back[1], devices, 1.0))
    slab_grad = across_groups(returned, devices, 1.0)[0] * (1.0 / N)
    return lax.all_to_all(slab_grad.astype(BF16), "tx", split_axis=1, concat_axis=0, tiled=True)


def embed_complex(angle, row_axis, col_axis):
    cos, sin = np.cos(angle), np.sin(angle)
    top = np.stack([cos, sin], axis=col_axis)
    bottom = np.stack([-sin, cos], axis=col_axis)
    return np.stack([top, bottom], axis=row_axis)


def wheel(length, product):
    return 2.0 * math.pi / length * (product % length)


@functools.lru_cache(maxsize=None)
def row_constants():
    k = np.arange(TOK)
    angle = wheel(TOK, k[:, None] * k[None, :])
    first = np.concatenate([np.cos(angle), -np.sin(angle)], axis=1)
    b = np.repeat(np.arange(PATCH), PATCH)
    angle = wheel(N, b[:, None] * k[None, :])
    twist = np.stack([np.cos(angle), -np.sin(angle)])
    p = np.arange(PATCH)
    small = embed_complex(wheel(PATCH, p[:, None] * p[None, :]), 1, 1)
    second = np.einsum("kpqb,xy->kpxqby", small, np.eye(PATCH)).reshape(2 * PIXELS, 2 * PIXELS)
    return (
        first.astype(ml_dtypes.bfloat16),
        twist.astype(np.float32),
        second.astype(ml_dtypes.bfloat16),
        np.ascontiguousarray(second.T).astype(ml_dtypes.bfloat16),
    )


@functools.lru_cache(maxsize=None)
def column_constants(devices, rows):
    s = np.arange(devices)
    small = embed_complex(wheel(devices, s[:, None] * s[None, :]), 1, 2)
    wide = devices * 2 * PATCH
    outer = np.einsum("qpsr,xy->qpxsry", small, np.eye(PATCH)).reshape(wide, wide)
    kr = s[:, None] + devices * np.arange(rows)[None, :]
    angle = wheel(N, kr[:, :, None] * np.arange(rows)[None, None, :])
    inner = embed_complex(angle, 1, 2).reshape(devices, 2 * rows, 2 * rows) / N
    return tuple(
        np.ascontiguousarray(value).astype(ml_dtypes.bfloat16)
        for value in (outer, outer.T, inner, inner.transpose(0, 2, 1))
    )


def row_forward(x_ref, first_ref, twist_ref, second_ref, out_ref):
    count = x_ref.shape[1]

    def step(i, carry):
        band = x_ref[:, i].reshape(TOK, PIXELS)
        mixed = mm(band, first_ref[...], TN)
        real, imag = mixed[:, :TOK], mixed[:, TOK:]
        tr, ti = twist_ref[0], twist_ref[1]
        turned = jnp.concatenate(
            [(real * tr - imag * ti).astype(BF16), (real * ti + imag * tr).astype(BF16)], axis=0
        )
        result = mm(second_ref[...], turned).astype(BF16).reshape(PATCH, 2, PATCH, TOK)
        half = TOK // 2
        rows = pl.ds(pl.multiple_of(i * PATCH, PATCH), PATCH)
        out_ref[:, 0, :, rows, :] = result[..., :half]
        out_ref[:, 1, :, rows, :] = result[..., half:]
        return carry

    lax.fori_loop(0, count, step, 0)


def row_inverse(v_ref, first_ref, twist_ref, second_ref, out_ref):
    parts, count, cols, _ = out_ref.shape

    def step(i, carry):
        rows = pl.ds(pl.multiple_of(i * PATCH, PATCH), PATCH)
        wide = jnp.concatenate(
            [
                v_ref[:, 0, :, rows, :].reshape(2 * PIXELS, TOK // 2),
                v_ref[:, 1, :, rows, :].reshape(2 * PIXELS, TOK // 2),
            ],
            axis=1,
        )
        mixed = mm(second_ref[...], wide)
        real, imag = mixed[:PIXELS], mixed[PIXELS:]
        tr, ti = twist_ref[0], twist_ref[1]
        turned = jnp.concatenate(
            [(real * tr + imag * ti).astype(BF16), (imag * tr - real * ti).astype(BF16)], axis=1
        )
        result = mm(first_ref[...], turned, NT).astype(BF16)
        out_ref[:, i] = result.reshape(parts, cols, PIXELS)
        return carry

    lax.fori_loop(0, count, step, 0)


def row_places(devices, rows, lanes, chunks):
    across = devices // lanes
    tile = N // across
    places = []
    for group in range(rows // PATCH):
        place = []
        for high in range(devices):
            ty, rest = divmod(high * rows + group * PATCH, tile)
            chunk, rest = divmod(rest, tile // chunks)
            tx, rest = divmod(rest, tile // chunks // lanes)
            place.append((chunk, ty * lanes + tx, rest))
        places.append(place)
    return places


def column_both(places, chunks, phased, *refs):
    x_refs, refs = refs[:chunks], refs[chunks:]
    if phased:
        phase_ref, refs = refs[0], refs[1:]
    outer_ref, inner_hbm, scale_hbm, data_hbm, inner_t_hbm, outer_t_hbm = refs[:6]
    out_refs, refs = refs[6 : 6 + chunks], refs[6 + chunks :]
    mid_ref, inner_ref, scale_ref, data_ref, inner_t_ref, outer_t_ref, sems = refs
    devices, _, rows, width = mid_ref.shape
    copies = [
        pltpu.make_async_copy(source, target, sems.at[n])
        for n, (source, target) in enumerate(
            (
                (inner_hbm, inner_ref),
                (scale_hbm, scale_ref),
                (data_hbm, data_ref),
                (inner_t_hbm, inner_t_ref),
                (outer_t_hbm, outer_t_ref),
            )
        )
    ]
    for copy in copies:
        copy.start()
    span = 2 * PATCH

    for pair in range(len(places) // 2):
        groups = (2 * pair, 2 * pair + 1)
        both = jnp.concatenate(
            [
                jnp.concatenate(
                    [
                        x_refs[m][source, :, row : row + PATCH, :].reshape(span, width)
                        for m, source, row in places[group]
                    ],
                    axis=0,
                )
                for group in groups
            ],
            axis=1,
        )
        result = mm(outer_ref[...], both).astype(BF16)
        for n, group in enumerate(groups):
            mid_ref[:, :, group * PATCH : (group + 1) * PATCH, :] = result[
                :, n * width : (n + 1) * width
            ].reshape(devices, 2, PATCH, width)

    for copy in copies[:4]:
        copy.wait()

    def step(q, carry):
        spectrum = mm(inner_ref[q], mid_ref[q].reshape(2 * rows, width))
        real, imag = spectrum[:rows], spectrum[rows:]
        if phased:
            pr, pi = phase_ref[q, 0], phase_ref[q, 1]
            real = real.reshape(rows // 8, 8, width)
            imag = imag.reshape(rows // 8, 8, width)
            real, imag = real * pr - imag * pi, real * pi + imag * pr
            real, imag = real.reshape(rows, width), imag.reshape(rows, width)
        scale = scale_ref[q].astype(F32)
        real = real * scale - data_ref[0, q].astype(F32)
        imag = imag * scale - data_ref[1, q].astype(F32)
        back = jnp.concatenate([real.astype(BF16), imag.astype(BF16)], axis=0)
        mid_ref[q] = mm(inner_t_ref[q], back).astype(BF16).reshape(2, rows, width)
        return carry

    lax.fori_loop(0, devices, step, 0, unroll=8)
    copies[4].wait()

    for pair in range(len(places) // 2):
        groups = (2 * pair, 2 * pair + 1)
        both = jnp.concatenate(
            [
                mid_ref[:, :, group * PATCH : (group + 1) * PATCH, :].reshape(
                    devices * span, width
                )
                for group in groups
            ],
            axis=1,
        )
        result = mm(outer_t_ref[...], both).astype(BF16)
        for n, group in enumerate(groups):
            for high, (m, source, row) in enumerate(places[group]):
                out_refs[m][source, :, row : row + PATCH, :] = result[
                    high * span : (high + 1) * span, n * width : (n + 1) * width
                ].reshape(2, PATCH, width)


def spectrum_inputs(gains, observed, vis_weight, devices):
    width = vis_weight.shape[0]

    def turned(value):
        shaped = value.astype(BF16).reshape(width, N // devices, devices)
        return shaped.transpose(2, 1, 0)

    gr, gi = gains[0], gains[1]
    scale = turned(vis_weight * (gr * gr + gi * gi))
    data = jnp.stack(
        [
            turned(vis_weight * (gr * observed[0] + gi * observed[1])),
            turned(vis_weight * (gr * observed[1] - gi * observed[0])),
        ]
    )
    return scale, data


def row_matrix(shift):
    first = row_constants()[0]
    if shift is None:
        return jnp.asarray(first)
    twice = jnp.asarray(np.concatenate([first, first[: 2 * WIN]], axis=0))
    return lax.dynamic_slice(twice, (shift, jnp.zeros((), jnp.int32)), first.shape)


def phase_table(shift, devices, width):
    kr = counting(devices)[:, None] + devices * counting(8)[None, :]
    angle = 2.0 * math.pi / TOK * (kr * shift % TOK).astype(F32)
    table = jnp.stack([jnp.cos(angle), -jnp.sin(angle)], axis=1)
    return jnp.broadcast_to(table[..., None], (devices, 2, 8, width))


def patch_gradient(chunks, scale, data, shift):
    lanes = lax.axis_size("tx")
    devices = lax.axis_size("ty") * lanes
    rows, cols, _ = chunks[0].shape
    count = len(chunks)
    own = rows // lanes
    slab = N // devices
    first, twist, second, second_t = (jnp.asarray(value) for value in row_constants())
    outer, outer_t, inner, inner_t = (
        jnp.asarray(value) for value in column_constants(devices, slab)
    )
    start = row_matrix(None if shift is None else shift[1])
    part = (devices, 2, own * PATCH, slab)
    split = (PATCH, devices // PATCH) + part[1:]
    moved = []
    for chunk in chunks:
        gathered = lax.all_to_all(
            chunk.reshape(lanes, own, cols, PIXELS), "tx", split_axis=0, concat_axis=0, tiled=True
        )
        sent = pl.pallas_call(
            row_forward,
            out_shape=jax.ShapeDtypeStruct(split, BF16),
            compiler_params=PARAMS,
        )(gathered, start, twist, second)
        moved.append(
            lax.all_to_all(
                sent.reshape(part), ("ty", "tx"), split_axis=0, concat_axis=0, tiled=True
            )
        )
    operands = list(moved)
    if shift is not None:
        operands.append(phase_table(shift[0], devices, slab))
    held = len(operands) + 1
    away = (inner, scale, data, inner_t, outer_t)
    waves = pl.pallas_call(
        functools.partial(
            column_both, row_places(devices, slab, lanes, count), count, shift is not None
        ),
        in_specs=[pl.BlockSpec(memory_space=pltpu.VMEM)] * held
        + [pl.BlockSpec(memory_space=pl.ANY)] * len(away),
        out_shape=[jax.ShapeDtypeStruct(part, BF16)] * count,
        scratch_shapes=[pltpu.VMEM((devices, 2, slab, slab), BF16)]
        + [pltpu.VMEM(value.shape, BF16) for value in away]
        + [pltpu.SemaphoreType.DMA((len(away),))],
        compiler_params=PARAMS,
    )(*operands, outer, *away)
    grads = []
    for wave in waves:
        returned = lax.all_to_all(wave, ("ty", "tx"), split_axis=0, concat_axis=0, tiled=True)
        slabs = pl.pallas_call(
            row_inverse,
            out_shape=jax.ShapeDtypeStruct((lanes, own, cols, PIXELS), BF16),
            compiler_params=PARAMS,
        )(returned.reshape(split), first, twist, second_t)
        grad = lax.all_to_all(slabs, "tx", split_axis=0, concat_axis=0, tiled=True)
        grads.append(grad.reshape(rows, cols, PIXELS))
    return grads


def layer_norm(values, gain):
    centre = jnp.mean(values, axis=-1, keepdims=True)
    shifted = values - centre
    spread = jnp.mean(shifted * shifted, axis=-1, keepdims=True)
    return (shifted * lax.rsqrt(spread + EPSILON) * gain).astype(BF16)


def to_windows(band):
    rows, cols, feats = band.shape
    pieces = [
        band[:, w * WIN : (w + 1) * WIN, :].reshape(SPAN, feats) for w in range(cols // WIN)
    ]
    return jnp.concatenate(pieces, axis=0)


def from_windows(tokens, cols):
    feats = tokens.shape[-1]
    pieces = [
        tokens[w * SPAN : (w + 1) * SPAN].reshape(WIN, WIN, feats) for w in range(cols // WIN)
    ]
    return jnp.concatenate(pieces, axis=1)


def swin_band(
    flow, bias_ref, qkv_ref, proj_ref, up_ref, down_ref, gain_ref, mixed_ref, score_ref, prob_ref
):
    count = flow.shape[0] // SPAN
    pairs = HEADS // 2
    depth = D // HEADS
    wide = 2 * depth
    normed = layer_norm(flow, gain_ref[0:1, :])
    scale = 1.0 / math.sqrt(depth)
    mixed_ref[:, :D] = (mm(normed, qkv_ref[:, :D]) * scale).astype(BF16)
    mixed_ref[:, D : 2 * D] = mm(normed, qkv_ref[:, D : 2 * D]).astype(BF16)
    mixed_ref[:, 2 * D :] = mm(normed, qkv_ref[:, 2 * D :]).astype(BF16)
    lower = lax.broadcasted_iota(jnp.int32, (SPAN, wide), 1) < depth
    for w in range(count):
        rows = slice(w * SPAN, (w + 1) * SPAN)
        for p in range(pairs):
            query = mixed_ref[rows, p * wide : (p + 1) * wide]
            key = mixed_ref[rows, D + p * wide : D + (p + 1) * wide]
            zero = jnp.zeros_like(query)
            split = jnp.concatenate(
                [jnp.where(lower, query, zero), jnp.where(lower, zero, query)], axis=0
            )
            score_ref[w, :, p * wide : (p + 1) * wide] = mm(key, split, NT)
    for w in range(count):
        bias = bias_ref[w]
        for p in range(pairs):
            lanes = slice(p * wide, (p + 1) * wide)
            scores = score_ref[w, :, lanes] + bias
            weights = jnp.exp(scores - jnp.max(scores, axis=0, keepdims=True))
            share = 1.0 / jnp.sum(weights, axis=0, keepdims=True)
            prob_ref[w, :, lanes] = (weights * share).astype(BF16)
    for w in range(count):
        rows = slice(w * SPAN, (w + 1) * SPAN)
        for p in range(pairs):
            lanes = slice(p * wide, (p + 1) * wide)
            value = mixed_ref[rows, 2 * D + p * wide : 2 * D + (p + 1) * wide]
            mixture = mm(prob_ref[w, :, lanes], value, TN)
            mixed_ref[rows, lanes] = jnp.where(lower, mixture[:SPAN], mixture[SPAN:]).astype(BF16)
    flow = flow + mm(mixed_ref[:, :D], proj_ref[...])
    normed = layer_norm(flow, gain_ref[1:2, :])
    chunks = up_ref.shape[1] // D
    total = jnp.zeros_like(flow)
    ahead = mm(normed, up_ref[:, :D])
    for c in range(chunks):
        value = ahead
        if c + 1 < chunks:
            ahead = mm(normed, up_ref[:, (c + 1) * D : (c + 2) * D])
        inside = value * (GELU_IN + GELU_CUBE * (value * value))
        active = (value + value * jnp.tanh(inside)).astype(BF16)
        total = total + mm(active, down_ref[c * D : (c + 1) * D, :])
    return flow + 0.5 * total


def first_kernel(zeta, sigma, *refs):
    state_ref, grad_ref = refs[:2]
    refs = refs[2:]
    if sigma is not None:
        noise_ref, refs = refs[0], refs[1:]
    bias_ref, embed_ref, qkv_ref, proj_ref, up_ref, down_ref, gain_ref = refs[:7]
    base_ref, out_ref, *scratch = refs[7:]
    half = state_ref[...] - zeta * grad_ref[...].astype(F32)
    tokens = mm(to_windows(half).astype(BF16), embed_ref[...]).astype(BF16).astype(F32)
    if sigma is None:
        base_ref[...] = half
    else:
        base = half + sigma * noise_ref[...]
        base_ref[...] = base
        out_ref[:, :, D:] = base.astype(BF16)
    flow = swin_band(tokens, bias_ref, qkv_ref, proj_ref, up_ref, down_ref, gain_ref, *scratch)
    out_ref[:, :, :D] = from_windows(flow, half.shape[1]).astype(BF16)


def second_kernel(sigma, *refs):
    shift_ref, grid_ref, bias_ref, qkv_ref, proj_ref, up_ref, down_ref, gain_ref = refs[:8]
    unembed_ref, out_ref, *scratch = refs[8:]
    if sigma is not None:
        state_ref, scratch = scratch[0], scratch[1:]
    cols = out_ref.shape[1]
    top = pl.program_id(0) * WIN + shift_ref[0]
    wide = grid_ref[pl.ds(top, WIN)]
    place = lax.broadcasted_iota(jnp.int32, (cols, wide.shape[1]), 1)
    target = lax.broadcasted_iota(jnp.int32, (cols, wide.shape[1]), 0) + shift_ref[1]
    pick = jnp.where(place == target, 1.0, 0.0).astype(BF16)
    band = jnp.stack([mm(pick, wide[n]) for n in range(WIN)])
    tokens = to_windows(band[:, :, :D])
    flow = swin_band(tokens, bias_ref, qkv_ref, proj_ref, up_ref, down_ref, gain_ref, *scratch)
    estimate = from_windows(mm(flow.astype(BF16), unembed_ref[...]), cols)
    out_ref[...] = estimate.astype(BF16)
    if sigma is not None:
        state_ref[...] = (band[:, :, D:] - sigma * estimate).astype(BF16)


def whole(array):
    zeros = (0,) * array.ndim
    return pl.BlockSpec(array.shape, lambda *_: zeros)


def band_of(step, cols):
    return pl.BlockSpec((step, cols, PIXELS), lambda n: (n, 0, 0))


def member(array, j):
    place = (j,) + (0,) * (array.ndim - 1)
    return pl.BlockSpec((None,) + array.shape[1:], lambda *_: place)


def band_spec(cols, feats):
    return pl.BlockSpec((WIN, cols, feats), lambda n, *_: (n, 0, 0))


def bias_spec(cols, skip):
    return pl.BlockSpec((cols // WIN, SPAN, 2 * SPAN), lambda n, *_: (n + skip, 0, 0))


def band_scratch(cols):
    count = cols // WIN
    return [
        pltpu.VMEM((WIN * cols, 3 * D), BF16),
        pltpu.VMEM((count, SPAN, HEADS * SPAN), F32),
        pltpu.VMEM((count, SPAN, HEADS * SPAN), BF16),
    ]


def first_block(m, zeta, sigma, state, grad, noise, bias, w_embed, weights):
    rows, cols, _ = state.shape
    fields = [state, grad] + ([] if sigma is None else [noise])
    feats = D if sigma is None else D + PIXELS
    return pl.pallas_call(
        functools.partial(first_kernel, zeta, sigma),
        grid=(rows // WIN,),
        in_specs=[band_spec(cols, PIXELS)] * len(fields)
        + [bias_spec(cols, m * rows // WIN), whole(w_embed)]
        + [member(value, 0) for value in weights],
        out_specs=[band_spec(cols, PIXELS), band_spec(cols, feats)],
        out_shape=[
            jax.ShapeDtypeStruct((rows, cols, PIXELS), F32),
            jax.ShapeDtypeStruct((rows, cols, feats), BF16),
        ],
        scratch_shapes=band_scratch(cols),
        compiler_params=PARAMS,
    )(*fields, bias, w_embed, *weights)


def second_block(m, sigma, shift, grid, bias, w_unembed, weights):
    rows, cols = grid.shape[0] - WIN, grid.shape[1] - WIN
    outs = 1 if sigma is None else 2
    return pl.pallas_call(
        functools.partial(second_kernel, sigma),
        grid_spec=pltpu.PrefetchScalarGridSpec(
            num_scalar_prefetch=1,
            grid=(rows // WIN,),
            in_specs=[whole(grid), bias_spec(cols, m * rows // WIN)]
            + [member(value, 1) for value in weights]
            + [whole(w_unembed)],
            out_specs=[band_spec(cols, PIXELS)] * outs,
            scratch_shapes=band_scratch(cols),
        ),
        out_shape=[jax.ShapeDtypeStruct((rows, cols, PIXELS), BF16)] * outs,
        compiler_params=PARAMS,
    )(shift, grid, bias, *weights, w_unembed)


def from_behind(shard, axis, by):
    size = lax.axis_size(axis)
    return lax.ppermute(shard, axis, [(i, (i + by) % size) for i in range(size)])


def with_next(chunks):
    wide = [
        jnp.concatenate([chunk, from_behind(chunk[:, :WIN], "tx", -1)], axis=1) for chunk in chunks
    ]
    heads = [chunk[:WIN] for chunk in wide[1:]] + [from_behind(wide[0][:WIN], "ty", -1)]
    return [jnp.concatenate(pair, axis=0) for pair in zip(wide, heads)]


def with_previous(chunks):
    wide = [
        jnp.concatenate([from_behind(chunk[:, -WIN:], "tx", 1), chunk], axis=1) for chunk in chunks
    ]
    tails = [from_behind(wide[-1][-WIN:], "ty", 1)] + [chunk[-WIN:] for chunk in wide[:-1]]
    return [jnp.concatenate(pair, axis=0) for pair in zip(tails, wide)]


def windows_of(grid):
    rows, cols = grid.shape
    shaped = grid.reshape(rows // WIN, WIN, cols // WIN, WIN).transpose(0, 2, 1, 3)
    return shaped.reshape(rows // WIN * (cols // WIN), SPAN)


def bias_of(labels, keep):
    allowed = jnp.ones((1, SPAN, SPAN), bool)
    if labels is not None:
        label = windows_of(labels)
        allowed = label[:, :, None] == label[:, None, :]
    if keep is not None:
        kept = windows_of(keep)[:, :, None] == 1
        allowed = allowed & (kept | jnp.eye(SPAN, dtype=bool)[None])
    bias = jnp.where(allowed, 0.0, -1e30).astype(F32)
    return jnp.concatenate([bias, bias], axis=2)


def region(index, shift):
    return jnp.where(index < TOK - WIN, 0, jnp.where(index < TOK - shift, 1, 2)).astype(jnp.int32)


@functools.lru_cache(maxsize=None)
def lane_order(cols):
    parts = LANES // cols
    groups = PATCH // parts
    lane = np.arange(PATCH * cols)
    g, h, k = lane // LANES, lane % LANES // cols, lane % cols
    source = PATCH * k + h * groups + g
    matrix = np.zeros((PATCH * cols, PATCH * cols), np.float32)
    matrix[source, lane] = 1.0
    return matrix.astype(ml_dtypes.bfloat16), np.ascontiguousarray(matrix.T).astype(
        ml_dtypes.bfloat16
    )


def move_lanes(values, matrix):
    high = values.astype(BF16)
    low = (values - high.astype(F32)).astype(BF16)
    return mm(high, matrix) + mm(low, matrix)


def to_patches_kernel(tile_ref, order_ref, *out_refs):
    count, cols, _ = out_refs[0].shape
    parts = LANES // cols
    groups = PATCH // parts
    ordered = move_lanes(tile_ref[...], order_ref[...])
    for i in range(count):
        band = ordered[i * PATCH : (i + 1) * PATCH]
        stacked = jnp.concatenate(
            [band[:, g * LANES : (g + 1) * LANES] for g in range(groups)], axis=0
        )
        turned = stacked.T
        patch = jnp.concatenate([turned[h * cols : (h + 1) * cols] for h in range(parts)], axis=1)
        for out_ref in out_refs:
            out_ref[i] = patch.astype(out_ref.dtype)


def to_tile_kernel(scale, patch_ref, noise_ref, order_ref, out_ref):
    count, cols, _ = patch_ref.shape
    parts = LANES // cols
    groups = PATCH // parts
    width = groups * PATCH
    bands = []
    for i in range(count):
        patch = patch_ref[i]
        stacked = jnp.concatenate(
            [patch[:, h * width : (h + 1) * width] for h in range(parts)], axis=0
        )
        turned = stacked.T
        bands.append(
            jnp.concatenate([turned[g * PATCH : (g + 1) * PATCH] for g in range(groups)], axis=1)
        )
    moved = move_lanes(jnp.concatenate(bands, axis=0), order_ref[...])
    out_ref[...] = moved + scale * noise_ref[...]


def patches_of(tiles, j, chunks, narrow=False):
    rows, cols = tiles.shape[1] // PATCH // chunks, tiles.shape[2] // PATCH
    order = jnp.asarray(lane_order(cols)[0])
    step = rows // 2
    kinds = [F32, BF16] if narrow else [F32]
    return [
        pl.pallas_call(
            to_patches_kernel,
            grid=(rows // step,),
            in_specs=[
                pl.BlockSpec(
                    (None, step * PATCH, cols * PATCH),
                    functools.partial(lambda skip, n: (j, skip + n, 0), m * (rows // step)),
                ),
                whole(order),
            ],
            out_specs=[band_of(step, cols)] * len(kinds),
            out_shape=[jax.ShapeDtypeStruct((rows, cols, PIXELS), kind) for kind in kinds],
            compiler_params=PARAMS,
        )(tiles, order)
        for m in range(chunks)
    ]


def tile_of(patches, scale, noise, j):
    rows, cols, _ = patches.shape
    order = jnp.asarray(lane_order(cols)[1])
    step = rows // 4
    return pl.pallas_call(
        functools.partial(to_tile_kernel, scale),
        grid=(rows // step,),
        in_specs=[
            band_of(step, cols),
            pl.BlockSpec((None, step * PATCH, cols * PATCH), lambda n: (j, n, 0)),
            whole(order),
        ],
        out_specs=pl.BlockSpec((step * PATCH, cols * PATCH), lambda n: (n, 0)),
        out_shape=jax.ShapeDtypeStruct((rows * PATCH, cols * PATCH), F32),
        compiler_params=PARAMS,
    )(patches, noise, order)


def per_device(
    image, noise, offsets, key_mask, gains, observed, vis_weight,
    w_embed, w_qkv, w_proj, w_up, w_down, w_unembed, norm_gains,
):
    rows = image.shape[0] // PATCH
    cols = image.shape[1] // PATCH
    devices = lax.axis_size("ty") * lax.axis_size("tx")
    fast = N // devices == TOK // 2
    row_index = lax.axis_index("ty") * rows + counting(rows)
    col_index = lax.axis_index("tx") * cols + counting(cols)
    weights = (w_qkv, w_proj, w_up, w_down, norm_gains)
    w_embed = w_embed.reshape(PATCH, PATCH, D).transpose(1, 0, 2).reshape(PIXELS, D)
    w_unembed = w_unembed.reshape(D, PATCH, PATCH).transpose(0, 2, 1).reshape(D, PIXELS)
    chunks = CHUNKS
    begin = patches_of(image[None], 0, chunks, narrow=True)
    state = [pair[0] for pair in begin]
    moving = [pair[1] for pair in begin]
    shift = None
    if fast:
        scale, data = spectrum_inputs(gains, observed, vis_weight, devices)
    first_bias = bias_of(None, key_mask)
    for step in range(STEPS):
        if fast:
            grad = patch_gradient(moving, scale, data, shift)
        else:
            tile = tile_of(jnp.concatenate(state), 0.0, noise, 0)
            grad = plain_gradient(tile, gains, observed, vis_weight).astype(F32)
            grad = [part[0].astype(BF16) for part in patches_of(grad[None], 0, chunks)]
        last = step + 1 == STEPS
        extra = [[None]] * chunks if last else patches_of(noise, step, chunks)
        sigma = None if last else SIGMAS[step + 1]
        blocks = [
            first_block(
                m, STEP_SIZES[step], sigma, state[m], grad[m], extra[m][0], first_bias, w_embed,
                weights,
            )
            for m in range(chunks)
        ]
        shift = offsets[step]
        labels = 3 * region(row_index, shift[0])[:, None] + region(col_index, shift[1])[None, :]
        second_bias = bias_of(labels, None)
        grids = with_next([block[1] for block in blocks])
        rolled = [
            second_block(
                m, None if last else SIGMAS[step], shift, grids[m], second_bias, w_unembed, weights
            )
            for m in range(chunks)
        ]
        moving = [part[-1] for part in rolled]
        corner = (WIN - shift[0], WIN - shift[1], jnp.zeros((), jnp.int32))
        state = [
            block[0] - SIGMAS[step] * lax.dynamic_slice(part, corner, block[0].shape).astype(F32)
            for block, part in zip(blocks, with_previous([part[0] for part in rolled]))
        ]
    return tile_of(jnp.concatenate(state), SIGMAS[STEPS], noise, STEPS - 1)


def solution(mesh):
    in_specs = (
        P("ty", "tx"),
        P(None, "ty", "tx"),
        P(),
        P("ty", "tx"),
        P(None, ("ty", "tx"), None),
        P(None, ("ty", "tx"), None),
        P(("ty", "tx"), None),
        P(),
        P(),
        P(),
        P(),
        P(),
        P(),
        P(),
    )
    out_specs = P("ty", "tx")
    return jax.shard_map(
        per_device, mesh=mesh, in_specs=in_specs, out_specs=out_specs, check_vma=False
    )
```

```python
import functools
import math

import jax
import jax.numpy as jnp
import ml_dtypes
import numpy as np
from jax import lax
from jax.experimental import pallas as pl
from jax.experimental.pallas import tpu as pltpu
from jax.sharding import PartitionSpec as P

N = 4096
PATCH = 16
PIXELS = PATCH * PATCH
WIN = 8
D = 512
HEADS = 8
STEPS = 2
SPAN = WIN * WIN
LANES = 128
TOK = N // PATCH

SIGMAS = (0.8, 0.5, 0.3)
STEP_SIZES = (0.9, 0.7)
EPSILON = 1e-05
HIGHEST = lax.Precision.HIGHEST
BF16 = jnp.bfloat16
F32 = jnp.float32
GELU_IN = math.sqrt(2.0 / math.pi)
GELU_CUBE = 0.044715 * GELU_IN
VMEM_LIMIT = 56 * 1024 * 1024
PARAMS = pltpu.CompilerParams(vmem_limit_bytes=VMEM_LIMIT)
TN = (((0,), (0,)), ((), ()))
NT = (((1,), (1,)), ((), ()))
NN = (((1,), (0,)), ((), ()))


def mm(left, right, dims=NN):
    return lax.dot_general(left, right, dims, preferred_element_type=F32)


def counting(length):
    return jnp.arange(length, dtype=jnp.int32)


def roots(length, outer, inner, sign):
    product = outer[:, None] * inner[None, :] % length
    angle = 2.0 * math.pi / length * product.astype(F32)
    return (jnp.cos(angle), sign * jnp.sin(angle))


def complex_einsum(form, left, right):
    real = jnp.einsum(form, left[0], right[0], precision=HIGHEST) - jnp.einsum(
        form, left[1], right[1], precision=HIGHEST
    )
    imag = jnp.einsum(form, left[0], right[1], precision=HIGHEST) + jnp.einsum(
        form, left[1], right[0], precision=HIGHEST
    )
    return (real, imag)


def complex_times(left, right):
    return (left[0] * right[0] - left[1] * right[1], left[0] * right[1] + left[1] * right[0])


def along_last(real_part, imag_part, groups, sign):
    rows, length = real_part.shape
    inner = length // groups
    first = roots(groups, counting(groups), counting(groups), sign)
    twist = roots(length, counting(inner), counting(groups), sign)
    second = roots(inner, counting(inner), counting(inner), sign)
    shaped = real_part.reshape(rows, groups, inner)
    if imag_part is None:
        partial_value = (
            jnp.einsum("mab,ka->mbk", shaped, first[0], precision=HIGHEST),
            jnp.einsum("mab,ka->mbk", shaped, first[1], precision=HIGHEST),
        )
    else:
        partial_value = complex_einsum(
            "mab,ka->mbk", (shaped, imag_part.reshape(rows, groups, inner)), first
        )
    partial_value = complex_times(partial_value, twist)
    result = complex_einsum("jb,mbk->mjk", second, partial_value)
    return (result[0].reshape(rows, length), result[1].reshape(rows, length))


def across_groups(pair, groups, sign):
    inner, cols = pair[0].shape
    width = cols // groups
    length = groups * inner
    first = roots(groups, counting(groups), counting(groups), sign)
    twist = roots(length, counting(inner), counting(groups), sign)
    second = roots(inner, counting(inner), counting(inner), sign)
    shaped = (pair[0].reshape(inner, groups, width), pair[1].reshape(inner, groups, width))
    partial_value = complex_einsum("bhc,kh->cbk", shaped, first)
    partial_value = complex_times(partial_value, twist)
    result = complex_einsum("jb,cbk->cjk", second, partial_value)
    return (result[0].reshape(width, length), result[1].reshape(width, length))


def exchange_pair(pair):
    return tuple(
        lax.all_to_all(
            part.astype(BF16), ("ty", "tx"), split_axis=1, concat_axis=1, tiled=True
        ).astype(F32)
        for part in pair
    )


def plain_gradient(tile, gains, observed, vis_weight):
    devices = lax.axis_size("ty") * lax.axis_size("tx")
    slab = lax.all_to_all(tile.astype(BF16), "tx", split_axis=0, concat_axis=1, tiled=True)
    moved = exchange_pair(along_last(slab.astype(F32), None, devices, -1.0))
    spectrum = across_groups(moved, devices, -1.0)
    spectrum = (spectrum[0] * (1.0 / N), spectrum[1] * (1.0 / N))
    model = complex_times((gains[0], gains[1]), spectrum)
    misfit = (vis_weight * (model[0] - observed[0]), vis_weight * (model[1] - observed[1]))
    back = complex_times((gains[0], -gains[1]), misfit)
    returned = exchange_pair(along_last(back[0], back[1], devices, 1.0))
    slab_grad = across_groups(returned, devices, 1.0)[0] * (1.0 / N)
    return lax.all_to_all(slab_grad.astype(BF16), "tx", split_axis=1, concat_axis=0, tiled=True)


def embed_complex(angle, row_axis, col_axis):
    cos, sin = np.cos(angle), np.sin(angle)
    top = np.stack([cos, sin], axis=col_axis)
    bottom = np.stack([-sin, cos], axis=col_axis)
    return np.stack([top, bottom], axis=row_axis)


def wheel(length, product):
    return 2.0 * math.pi / length * (product % length)


@functools.lru_cache(maxsize=None)
def row_constants():
    k = np.arange(TOK)
    angle = wheel(TOK, k[:, None] * k[None, :])
    first = np.concatenate([np.cos(angle), -np.sin(angle)], axis=1)
    b = np.repeat(np.arange(PATCH), PATCH)
    angle = wheel(N, b[:, None] * k[None, :])
    twist = np.stack([np.cos(angle), -np.sin(angle)])
    p = np.arange(PATCH)
    small = embed_complex(wheel(PATCH, p[:, None] * p[None, :]), 1, 1)
    second = np.einsum("kpqb,xy->kpxqby", small, np.eye(PATCH)).reshape(2 * PIXELS, 2 * PIXELS)
    return (
        first.astype(ml_dtypes.bfloat16),
        twist.astype(np.float32),
        second.astype(ml_dtypes.bfloat16),
        np.ascontiguousarray(second.T).astype(ml_dtypes.bfloat16),
    )


@functools.lru_cache(maxsize=None)
def half_constants():
    _, twist, second, _ = row_constants()
    half, quarter = TOK // 2, TOK // 4
    low = np.concatenate([1 + np.arange(quarter), 1 + half + np.arange(quarter)])
    digits = np.concatenate([low, low - 1])
    k = np.arange(TOK)
    angle = wheel(TOK, k[:, None] * digits[None, :])
    first = np.concatenate([np.cos(angle), -np.sin(angle)], axis=1)
    zero_line = np.concatenate([np.tile(np.eye(PATCH), PATCH), np.zeros((PATCH, PIXELS))], axis=1)
    upper = np.concatenate([second[PIXELS:].astype(np.float32), zero_line])
    lower = second[:PIXELS].astype(np.float32)
    return (first.astype(ml_dtypes.bfloat16), np.ascontiguousarray(twist[:, :, digits])) + tuple(
        np.ascontiguousarray(value).astype(ml_dtypes.bfloat16)
        for value in (lower, upper, lower.T, upper.T)
    )


@functools.lru_cache(maxsize=None)
def column_constants(devices, rows):
    s = np.arange(devices)
    small = embed_complex(wheel(devices, s[:, None] * s[None, :]), 1, 2)
    wide = devices * 2 * PATCH
    outer = np.einsum("qpsr,xy->qpxsry", small, np.eye(PATCH)).reshape(wide, wide)
    kr = s[:, None] + devices * np.arange(rows)[None, :]
    angle = wheel(N, kr[:, :, None] * np.arange(rows)[None, None, :])
    inner = embed_complex(angle, 1, 2).reshape(devices, 2 * rows, 2 * rows) / N
    return tuple(
        np.ascontiguousarray(value).astype(ml_dtypes.bfloat16)
        for value in (outer, outer.T, inner, inner.transpose(0, 2, 1))
    )


def row_forward(x_ref, first_ref, twist_ref, second_ref, out_ref):
    count = x_ref.shape[1]

    def step(i, carry):
        band = x_ref[:, i].reshape(TOK, PIXELS)
        mixed = mm(band, first_ref[...], TN)
        real, imag = mixed[:, :TOK], mixed[:, TOK:]
        tr, ti = twist_ref[0], twist_ref[1]
        turned = jnp.concatenate(
            [(real * tr - imag * ti).astype(BF16), (real * ti + imag * tr).astype(BF16)], axis=0
        )
        result = mm(second_ref[...], turned).astype(BF16).reshape(PATCH, 2, PATCH, TOK)
        half = TOK // 2
        rows = pl.ds(pl.multiple_of(i * PATCH, PATCH), PATCH)
        out_ref[:, 0, :, rows, :] = result[..., :half]
        out_ref[:, 1, :, rows, :] = result[..., half:]
        return carry

    lax.fori_loop(0, count, step, 0)


def row_inverse(v_ref, first_ref, twist_ref, second_ref, out_ref):
    parts, count, cols, _ = out_ref.shape

    def step(i, carry):
        rows = pl.ds(pl.multiple_of(i * PATCH, PATCH), PATCH)
        wide = jnp.concatenate(
            [
                v_ref[:, 0, :, rows, :].reshape(2 * PIXELS, TOK // 2),
                v_ref[:, 1, :, rows, :].reshape(2 * PIXELS, TOK // 2),
            ],
            axis=1,
        )
        mixed = mm(second_ref[...], wide)
        real, imag = mixed[:PIXELS], mixed[PIXELS:]
        tr, ti = twist_ref[0], twist_ref[1]
        turned = jnp.concatenate(
            [(real * tr + imag * ti).astype(BF16), (imag * tr - real * ti).astype(BF16)], axis=1
        )
        result = mm(first_ref[...], turned, NT).astype(BF16)
        out_ref[:, i] = result.reshape(parts, cols, PIXELS)
        return carry

    lax.fori_loop(0, count, step, 0)


def lane_index(shape):
    return lax.broadcasted_iota(jnp.int32, shape, len(shape) - 1)


def swap_halves(values):
    return pltpu.roll(values, values.shape[-1] // 2, len(values.shape) - 1)


def row_forward_half(x_ref, first_ref, twist_ref, lower_ref, upper_ref, out_ref):
    count = x_ref.shape[1]
    half = TOK // 2

    def packed(real, imag, rows, high):
        left = lane_index(real.shape) < half // 2
        out_ref[high, 0, rows, :] = jnp.where(left, real, swap_halves(imag)).astype(BF16)
        out_ref[high, 1, rows, :] = jnp.where(left, swap_halves(real), imag).astype(BF16)

    def step(i, carry):
        band = x_ref[:, i].reshape(TOK, PIXELS)
        mixed = mm(band, first_ref[...], TN)
        real, imag = mixed[:, :TOK], mixed[:, TOK:]
        tr, ti = twist_ref[0], twist_ref[1]
        turned = jnp.concatenate(
            [(real * tr - imag * ti).astype(BF16), (real * ti + imag * tr).astype(BF16)], axis=0
        )
        rows = pl.ds(pl.multiple_of(i * PATCH, PATCH), PATCH)
        lower = mm(lower_ref[...], turned[:, :half]).reshape(PATCH // 2, 2, PATCH, half)
        packed(lower[:, 0], lower[:, 1], rows, slice(0, PATCH // 2))
        upper = mm(upper_ref[...], turned[:, half:])
        line = upper[PIXELS:]
        upper = upper[:PIXELS].reshape(PATCH // 2, 2, PATCH, half)
        imag = upper[:, 1]
        head = jnp.where(lane_index(line.shape) == 0, line, imag[0])
        imag = jnp.concatenate([head[None], imag[1:]], axis=0)
        packed(upper[:, 0], imag, rows, slice(PATCH // 2, PATCH))
        return carry

    lax.fori_loop(0, count, step, 0)


def row_inverse_half(v_ref, first_ref, twist_ref, lower_ref, upper_ref, out_ref):
    parts, count, cols, _ = out_ref.shape
    half = TOK // 2

    def unpacked(rows, high):
        even = v_ref[high, 0, rows, :].astype(F32)
        odd = v_ref[high, 1, rows, :].astype(F32)
        left = lane_index(even.shape) < half // 2
        return jnp.where(left, even, swap_halves(odd)), jnp.where(left, swap_halves(even), odd)

    def step(i, carry):
        rows = pl.ds(pl.multiple_of(i * PATCH, PATCH), PATCH)
        real, imag = unpacked(rows, slice(0, PATCH // 2))
        lower = jnp.stack([real, imag], axis=1).reshape(PIXELS, half)
        real, imag = unpacked(rows, slice(PATCH // 2, PATCH))
        head = imag[0]
        at_zero = lane_index(head.shape) == 0
        nothing = jnp.zeros_like(head)
        imag = jnp.concatenate([jnp.where(at_zero, nothing, head)[None], imag[1:]], axis=0)
        upper = jnp.stack([real, imag], axis=1).reshape(PIXELS, half)
        upper = jnp.concatenate([upper, jnp.where(at_zero, head, nothing)], axis=0)
        mixed = jnp.concatenate(
            [mm(lower_ref[...], lower.astype(BF16)), mm(upper_ref[...], upper.astype(BF16))], axis=1
        )
        real, imag = mixed[:PIXELS], mixed[PIXELS:]
        tr, ti = twist_ref[0], twist_ref[1]
        turned = jnp.concatenate(
            [(real * tr + imag * ti).astype(BF16), (imag * tr - real * ti).astype(BF16)], axis=1
        )
        result = mm(first_ref[...], turned, NT).astype(BF16)
        out_ref[:, i] = result.reshape(parts, cols, PIXELS)
        return carry

    lax.fori_loop(0, count, step, 0)


def column_kernel(halved, *refs):
    if halved:
        flag_ref, phase_ref, refs = refs[0], refs[1], refs[2:]
    x_ref, outer_ref, *refs = refs
    count = 4 if halved else 5
    sources, out_ref = refs[:count], refs[count]
    mid_ref, *targets, sems = refs[count + 1 :]
    copies = [
        pltpu.make_async_copy(source, target, sems.at[n])
        for n, (source, target) in enumerate(zip(sources, targets))
    ]
    for copy in copies:
        copy.start()
    inner_ref, scale_ref, inner_t_ref, outer_t_ref = targets[:4]
    devices, _, rows, width = mid_ref.shape
    wide = devices * 2 * PATCH
    if halved:
        lane = lane_index((devices, PATCH, width))
        centre = flag_ref[0] == 1
        half = width // 2
        hidden = (lane == half) | (centre & (lane == 0))
        real_lane = (lane < half) | (centre & (lane == half))

    def load(group):
        place = slice(group * PATCH, (group + 1) * PATCH)
        if not halved:
            return x_ref[:, :, place, :].reshape(wide, width)
        piece = x_ref[:, place, :]
        other = swap_halves(piece.astype(F32))
        other = jnp.where(hidden, jnp.zeros_like(other), other).astype(BF16)
        return jnp.stack([piece, other], axis=1).reshape(wide, width)

    def store(group, value):
        place = slice(group * PATCH, (group + 1) * PATCH)
        value = value.reshape(devices, 2, PATCH, width)
        if halved:
            value = jnp.where(real_lane, value[:, 0], swap_halves(value[:, 1])).astype(BF16)
            out_ref[:, place, :] = value
        else:
            out_ref[:, :, place, :] = value.astype(BF16)

    for pair in range(0, rows // PATCH, 2):
        result = mm(outer_ref[...], jnp.concatenate([load(pair), load(pair + 1)], axis=1))
        result = result.astype(BF16)
        for n in range(2):
            place = slice((pair + n) * PATCH, (pair + n + 1) * PATCH)
            mid_ref[:, :, place, :] = result[:, n * width : (n + 1) * width].reshape(
                devices, 2, PATCH, width
            )

    for n, copy in enumerate(copies):
        if n != 3:
            copy.wait()

    def step(q, carry):
        spectrum = mm(inner_ref[q], mid_ref[q].reshape(2 * rows, width))
        real, imag = spectrum[:rows], spectrum[rows:]
        scale = scale_ref[q].astype(F32)
        if halved:
            pr, pi = phase_ref[q, 0], phase_ref[q, 1]
            real = real.reshape(rows // 8, 8, width)
            imag = imag.reshape(rows // 8, 8, width)
            real, imag = real * pr - imag * pi, real * pi + imag * pr
            real, imag = real.reshape(rows, width) * scale, imag.reshape(rows, width) * scale
        else:
            data_ref = targets[4]
            real = real * scale - data_ref[0, q].astype(F32)
            imag = imag * scale - data_ref[1, q].astype(F32)
        back = jnp.concatenate([real.astype(BF16), imag.astype(BF16)], axis=0)
        mid_ref[q] = mm(inner_t_ref[q], back).astype(BF16).reshape(2, rows, width)
        return carry

    lax.fori_loop(0, devices, step, 0, unroll=8)
    copies[3].wait()

    for pair in range(0, rows // PATCH, 2):
        both = jnp.concatenate(
            [
                mid_ref[:, :, n * PATCH : (n + 1) * PATCH, :].reshape(wide, width)
                for n in (pair, pair + 1)
            ],
            axis=1,
        )
        result = mm(outer_t_ref[...], both)
        store(pair, result[:, :width])
        store(pair + 1, result[:, width:])


def turned(value, devices):
    lines = value.shape[0]
    return value.astype(BF16).reshape(lines, N // devices, devices).transpose(2, 1, 0)


def spectrum_inputs(gains, observed, vis_weight, devices):
    gr, gi = gains[0], gains[1]
    weight = vis_weight * (gr * gr + gi * gi)
    data = jnp.stack(
        [
            turned(vis_weight * (gr * observed[0] + gi * observed[1]), devices),
            turned(vis_weight * (gr * observed[1] - gi * observed[0]), devices),
        ]
    )
    return turned(weight, devices), data, mirrored_weight(weight.astype(BF16), devices)


def mirrored_weight(weight, devices):
    slab = weight.shape[0]
    half, middle = slab // 2, devices // 2
    me = lax.axis_index(("ty", "tx"))
    facing = [(e, devices - 1 - e) for e in range(devices)]
    partner = [(e, devices - e) for e in range(1, devices) if e != middle]
    partner = partner + [(0, middle), (middle, 0)]
    upper = lax.ppermute(weight[half:], ("ty", "tx"), facing)[::-1]
    line = lax.ppermute(weight[:1], ("ty", "tx"), partner)
    other = jnp.where(me < middle, upper, jnp.concatenate([line, upper[:-1]], axis=0))
    first_row = lax.broadcasted_iota(jnp.int32, other.shape, 0) == 0
    other = jnp.where((me == middle) & first_row, 0, other)
    back = jnp.concatenate([other, jnp.where(me == middle, line, 0)], axis=0)
    back = jnp.roll(back[:, ::-1], 1, axis=1).astype(F32)
    own = jnp.where(me < middle, weight[1 : half + 1], weight[:half]).astype(F32)
    total = jnp.concatenate([own + back[:half], back[half:]], axis=0)
    return turned(jnp.pad(total, ((0, slab - half - 1), (0, 0))), devices)


def row_matrix(shift):
    first = half_constants()[0]
    twice = jnp.asarray(np.concatenate([first, first[: 2 * WIN]], axis=0))
    return lax.dynamic_slice(twice, (shift, jnp.zeros((), jnp.int32)), first.shape)


def phase_table(shift, devices, width):
    kr = counting(devices)[:, None] + devices * counting(8)[None, :]
    angle = 2.0 * math.pi / TOK * (kr * shift % TOK).astype(F32)
    table = jnp.stack([jnp.cos(angle), -jnp.sin(angle)], axis=1)
    return jnp.broadcast_to(table[..., None], (devices, 2, 8, width))


def patch_gradient(state, scale, data, shift):
    lanes = lax.axis_size("tx")
    devices = lax.axis_size("ty") * lanes
    rows, cols, _ = state.shape
    own = rows // lanes
    slab = N // devices
    halved = data is None
    outer, outer_t, inner, inner_t = (
        jnp.asarray(value) for value in column_constants(devices, slab)
    )
    if halved:
        first, twist, low, high, low_t, high_t = (jnp.asarray(value) for value in half_constants())
        part = (devices, slab, slab)
        onward = (row_forward_half, (row_matrix(shift[1]), twist, low, high))
        backward = (row_inverse_half, (first, twist, low_t, high_t))
        middle = lax.axis_index(("ty", "tx")) == devices // 2
        extra = (middle.astype(jnp.int32).reshape(1), phase_table(shift[0], devices, slab))
        away = (inner, scale, inner_t, outer_t)
    else:
        first, twist, second, second_t = (jnp.asarray(value) for value in row_constants())
        part = (devices, 2, slab, slab)
        onward = (row_forward, (first, twist, second))
        backward = (row_inverse, (first, twist, second_t))
        extra = ()
        away = (inner, scale, inner_t, outer_t, data)
    split = (PATCH, devices // PATCH) + part[1:]
    gathered = lax.all_to_all(
        state.reshape(lanes, own, cols, PIXELS), "tx", split_axis=0, concat_axis=0, tiled=True
    )
    sent = pl.pallas_call(
        onward[0], out_shape=jax.ShapeDtypeStruct(split, BF16), compiler_params=PARAMS
    )(gathered, *onward[1])
    moved = lax.all_to_all(
        sent.reshape(part), ("ty", "tx"), split_axis=0, concat_axis=0, tiled=True
    )
    spaces = [pltpu.SMEM, pltpu.VMEM][: len(extra)] + [pltpu.VMEM] * 2 + [pl.ANY] * len(away)
    wave = pl.pallas_call(
        functools.partial(column_kernel, halved),
        in_specs=[pl.BlockSpec(memory_space=space) for space in spaces],
        out_shape=jax.ShapeDtypeStruct(part, BF16),
        scratch_shapes=[pltpu.VMEM((devices, 2, slab, slab), BF16)]
        + [pltpu.VMEM(value.shape, BF16) for value in away]
        + [pltpu.SemaphoreType.DMA((len(away),))],
        compiler_params=PARAMS,
    )(*extra, moved, outer, *away)
    returned = lax.all_to_all(wave, ("ty", "tx"), split_axis=0, concat_axis=0, tiled=True)
    slabs = pl.pallas_call(
        backward[0],
        out_shape=jax.ShapeDtypeStruct((lanes, own, cols, PIXELS), BF16),
        compiler_params=PARAMS,
    )(returned.reshape(split), *backward[1])
    grad = lax.all_to_all(slabs, "tx", split_axis=0, concat_axis=0, tiled=True)
    return grad.reshape(rows, cols, PIXELS)


def layer_norm(values, gain):
    centre = jnp.mean(values, axis=-1, keepdims=True)
    shifted = values - centre
    spread = jnp.mean(shifted * shifted, axis=-1, keepdims=True)
    return (shifted * lax.rsqrt(spread + EPSILON) * gain).astype(BF16)


def to_windows(band):
    rows, cols, feats = band.shape
    pieces = [
        band[:, w * WIN : (w + 1) * WIN, :].reshape(SPAN, feats) for w in range(cols // WIN)
    ]
    return jnp.concatenate(pieces, axis=0)


def from_windows(tokens, cols):
    feats = tokens.shape[-1]
    pieces = [
        tokens[w * SPAN : (w + 1) * SPAN].reshape(WIN, WIN, feats) for w in range(cols // WIN)
    ]
    return jnp.concatenate(pieces, axis=1)


def swin_band(
    flow, bias_ref, qkv_ref, proj_ref, up_ref, down_ref, gain_ref, mixed_ref, score_ref, prob_ref
):
    count = flow.shape[0] // SPAN
    pairs = HEADS // 2
    depth = D // HEADS
    wide = 2 * depth
    normed = layer_norm(flow, gain_ref[0:1, :])
    scale = 1.0 / math.sqrt(depth)
    mixed_ref[:, :D] = (mm(normed, qkv_ref[:, :D]) * scale).astype(BF16)
    mixed_ref[:, D : 2 * D] = mm(normed, qkv_ref[:, D : 2 * D]).astype(BF16)
    mixed_ref[:, 2 * D :] = mm(normed, qkv_ref[:, 2 * D :]).astype(BF16)
    lower = lax.broadcasted_iota(jnp.int32, (SPAN, wide), 1) < depth
    for w in range(count):
        rows = slice(w * SPAN, (w + 1) * SPAN)
        for p in range(pairs):
            query = mixed_ref[rows, p * wide : (p + 1) * wide]
            key = mixed_ref[rows, D + p * wide : D + (p + 1) * wide]
            zero = jnp.zeros_like(query)
            split = jnp.concatenate(
                [jnp.where(lower, query, zero), jnp.where(lower, zero, query)], axis=0
            )
            score_ref[w, :, p * wide : (p + 1) * wide] = mm(key, split, NT)
    for w in range(count):
        bias = bias_ref[w]
        for p in range(pairs):
            lanes = slice(p * wide, (p + 1) * wide)
            scores = score_ref[w, :, lanes] + bias
            weights = jnp.exp(scores - jnp.max(scores, axis=0, keepdims=True))
            share = 1.0 / jnp.sum(weights, axis=0, keepdims=True)
            prob_ref[w, :, lanes] = (weights * share).astype(BF16)
    for w in range(count):
        rows = slice(w * SPAN, (w + 1) * SPAN)
        for p in range(pairs):
            lanes = slice(p * wide, (p + 1) * wide)
            value = mixed_ref[rows, 2 * D + p * wide : 2 * D + (p + 1) * wide]
            mixture = mm(prob_ref[w, :, lanes], value, TN)
            mixed_ref[rows, lanes] = jnp.where(lower, mixture[:SPAN], mixture[SPAN:]).astype(BF16)
    flow = flow + mm(mixed_ref[:, :D], proj_ref[...])
    normed = layer_norm(flow, gain_ref[1:2, :])
    chunks = up_ref.shape[1] // D
    total = jnp.zeros_like(flow)
    ahead = mm(normed, up_ref[:, :D])
    for c in range(chunks):
        value = ahead
        if c + 1 < chunks:
            ahead = mm(normed, up_ref[:, (c + 1) * D : (c + 2) * D])
        inside = value * (GELU_IN + GELU_CUBE * (value * value))
        active = (value + value * jnp.tanh(inside)).astype(BF16)
        total = total + mm(active, down_ref[c * D : (c + 1) * D, :])
    return flow + 0.5 * total


def first_kernel(zeta, sigma, count, *refs):
    state_ref, grad_refs, refs = refs[0], refs[1 : 1 + count], refs[1 + count :]
    if sigma is not None:
        noise_ref, refs = refs[0], refs[1:]
    bias_ref, embed_ref, qkv_ref, proj_ref, up_ref, down_ref, gain_ref = refs[:7]
    base_ref, out_ref, *scratch = refs[7:]
    step = zeta * sum(grad_ref[...].astype(F32) for grad_ref in grad_refs)
    half = state_ref[...] - step
    tokens = mm(to_windows(half).astype(BF16), embed_ref[...]).astype(BF16).astype(F32)
    if sigma is None:
        base_ref[...] = half
    else:
        noise = sigma * noise_ref[...]
        base_ref[...] = half + noise
        out_ref[:, :, D:] = (noise - step).astype(BF16)
    flow = swin_band(tokens, bias_ref, qkv_ref, proj_ref, up_ref, down_ref, gain_ref, *scratch)
    out_ref[:, :, :D] = from_windows(flow, half.shape[1]).astype(BF16)


def second_kernel(sigma, *refs):
    shift_ref, grid_ref, bias_ref, qkv_ref, proj_ref, up_ref, down_ref, gain_ref = refs[:8]
    unembed_ref, out_ref, *scratch = refs[8:]
    if sigma is not None:
        state_ref, scratch = scratch[0], scratch[1:]
    cols = out_ref.shape[1]
    top = pl.program_id(0) * WIN + shift_ref[0]
    wide = grid_ref[pl.ds(top, WIN)]
    place = lax.broadcasted_iota(jnp.int32, (cols, wide.shape[1]), 1)
    target = lax.broadcasted_iota(jnp.int32, (cols, wide.shape[1]), 0) + shift_ref[1]
    pick = jnp.where(place == target, 1.0, 0.0).astype(BF16)
    band = jnp.stack([mm(pick, wide[n]) for n in range(WIN)])
    tokens = to_windows(band[:, :, :D])
    flow = swin_band(tokens, bias_ref, qkv_ref, proj_ref, up_ref, down_ref, gain_ref, *scratch)
    estimate = from_windows(mm(flow.astype(BF16), unembed_ref[...]), cols)
    out_ref[...] = estimate.astype(BF16)
    if sigma is not None:
        state_ref[...] = (band[:, :, D:] - sigma * estimate).astype(BF16)


def whole(array):
    zeros = (0,) * array.ndim
    return pl.BlockSpec(array.shape, lambda *_: zeros)


def band_of(step, cols):
    return pl.BlockSpec((step, cols, PIXELS), lambda n: (n, 0, 0))


def member(array, j):
    place = (j,) + (0,) * (array.ndim - 1)
    return pl.BlockSpec((None,) + array.shape[1:], lambda *_: place)


def band_spec(cols, feats):
    return pl.BlockSpec((WIN, cols, feats), lambda n, *_: (n, 0, 0))


def bias_spec(cols):
    return pl.BlockSpec((cols // WIN, SPAN, 2 * SPAN), lambda n, *_: (n, 0, 0))


def band_scratch(cols):
    count = cols // WIN
    return [
        pltpu.VMEM((WIN * cols, 3 * D), BF16),
        pltpu.VMEM((count, SPAN, HEADS * SPAN), F32),
        pltpu.VMEM((count, SPAN, HEADS * SPAN), BF16),
    ]


def first_block(zeta, sigma, state, grads, noise, bias, w_embed, weights):
    rows, cols, _ = state.shape
    fields = [state, *grads] + ([] if sigma is None else [noise])
    feats = D if sigma is None else D + PIXELS
    return pl.pallas_call(
        functools.partial(first_kernel, zeta, sigma, len(grads)),
        grid=(rows // WIN,),
        in_specs=[band_spec(cols, PIXELS)] * len(fields)
        + [bias_spec(cols), whole(w_embed)]
        + [member(value, 0) for value in weights],
        out_specs=[band_spec(cols, PIXELS), band_spec(cols, feats)],
        out_shape=[
            jax.ShapeDtypeStruct((rows, cols, PIXELS), F32),
            jax.ShapeDtypeStruct((rows, cols, feats), BF16),
        ],
        scratch_shapes=band_scratch(cols),
        compiler_params=PARAMS,
    )(*fields, bias, w_embed, *weights)


def second_block(sigma, shift, grid, bias, w_unembed, weights):
    rows, cols = grid.shape[0] - WIN, grid.shape[1] - WIN
    outs = 1 if sigma is None else 2
    return pl.pallas_call(
        functools.partial(second_kernel, sigma),
        grid_spec=pltpu.PrefetchScalarGridSpec(
            num_scalar_prefetch=1,
            grid=(rows // WIN,),
            in_specs=[whole(grid), bias_spec(cols)]
            + [member(value, 1) for value in weights]
            + [whole(w_unembed)],
            out_specs=[band_spec(cols, PIXELS)] * outs,
            scratch_shapes=band_scratch(cols),
        ),
        out_shape=[jax.ShapeDtypeStruct((rows, cols, PIXELS), BF16)] * outs,
        compiler_params=PARAMS,
    )(shift, grid, bias, *weights, w_unembed)


def from_behind(shard, axis, by):
    size = lax.axis_size(axis)
    return lax.ppermute(shard, axis, [(i, (i + by) % size) for i in range(size)])


def with_next(grid):
    wide = jnp.concatenate([grid, from_behind(grid[:, :WIN], "tx", -1)], axis=1)
    return jnp.concatenate([wide, from_behind(wide[:WIN], "ty", -1)], axis=0)


def with_previous(grid):
    wide = jnp.concatenate([from_behind(grid[:, -WIN:], "tx", 1), grid], axis=1)
    return jnp.concatenate([from_behind(wide[-WIN:], "ty", 1), wide], axis=0)


def windows_of(grid):
    rows, cols = grid.shape
    shaped = grid.reshape(rows // WIN, WIN, cols // WIN, WIN).transpose(0, 2, 1, 3)
    return shaped.reshape(rows // WIN * (cols // WIN), SPAN)


def bias_of(labels, keep):
    allowed = jnp.ones((1, SPAN, SPAN), bool)
    if labels is not None:
        label = windows_of(labels)
        allowed = label[:, :, None] == label[:, None, :]
    if keep is not None:
        kept = windows_of(keep)[:, :, None] == 1
        allowed = allowed & (kept | jnp.eye(SPAN, dtype=bool)[None])
    bias = jnp.where(allowed, 0.0, -1e30).astype(F32)
    return jnp.concatenate([bias, bias], axis=2)


def region(index, shift):
    return jnp.where(index < TOK - WIN, 0, jnp.where(index < TOK - shift, 1, 2)).astype(jnp.int32)


@functools.lru_cache(maxsize=None)
def lane_order(cols):
    parts = LANES // cols
    groups = PATCH // parts
    lane = np.arange(PATCH * cols)
    g, h, k = lane // LANES, lane % LANES // cols, lane % cols
    source = PATCH * k + h * groups + g
    matrix = np.zeros((PATCH * cols, PATCH * cols), np.float32)
    matrix[source, lane] = 1.0
    return matrix.astype(ml_dtypes.bfloat16), np.ascontiguousarray(matrix.T).astype(
        ml_dtypes.bfloat16
    )


def move_lanes(values, matrix):
    high = values.astype(BF16)
    low = (values - high.astype(F32)).astype(BF16)
    return mm(high, matrix) + mm(low, matrix)


def to_patches_kernel(tile_ref, order_ref, *out_refs):
    count, cols, _ = out_refs[0].shape
    parts = LANES // cols
    groups = PATCH // parts
    ordered = move_lanes(tile_ref[...], order_ref[...])
    for i in range(count):
        band = ordered[i * PATCH : (i + 1) * PATCH]
        stacked = jnp.concatenate(
            [band[:, g * LANES : (g + 1) * LANES] for g in range(groups)], axis=0
        )
        turned = stacked.T
        patch = jnp.concatenate([turned[h * cols : (h + 1) * cols] for h in range(parts)], axis=1)
        for out_ref in out_refs:
            out_ref[i] = patch.astype(out_ref.dtype)


def to_tile_kernel(scale, patch_ref, noise_ref, order_ref, out_ref):
    count, cols, _ = patch_ref.shape
    parts = LANES // cols
    groups = PATCH // parts
    width = groups * PATCH
    bands = []
    for i in range(count):
        patch = patch_ref[i]
        stacked = jnp.concatenate(
            [patch[:, h * width : (h + 1) * width] for h in range(parts)], axis=0
        )
        turned = stacked.T
        bands.append(
            jnp.concatenate([turned[g * PATCH : (g + 1) * PATCH] for g in range(groups)], axis=1)
        )
    moved = move_lanes(jnp.concatenate(bands, axis=0), order_ref[...])
    out_ref[...] = moved + scale * noise_ref[...]


def patches_of(tiles, j, kinds=(F32,)):
    rows, cols = tiles.shape[1] // PATCH, tiles.shape[2] // PATCH
    order = jnp.asarray(lane_order(cols)[0])
    step = rows // 4
    return pl.pallas_call(
        to_patches_kernel,
        grid=(rows // step,),
        in_specs=[
            pl.BlockSpec((None, step * PATCH, cols * PATCH), lambda n: (j, n, 0)),
            whole(order),
        ],
        out_specs=[band_of(step, cols)] * len(kinds),
        out_shape=[jax.ShapeDtypeStruct((rows, cols, PIXELS), kind) for kind in kinds],
        compiler_params=PARAMS,
    )(tiles, order)


def tile_of(patches, scale, noise, j):
    rows, cols, _ = patches.shape
    order = jnp.asarray(lane_order(cols)[1])
    step = rows // 4
    return pl.pallas_call(
        functools.partial(to_tile_kernel, scale),
        grid=(rows // step,),
        in_specs=[
            band_of(step, cols),
            pl.BlockSpec((None, step * PATCH, cols * PATCH), lambda n: (j, n, 0)),
            whole(order),
        ],
        out_specs=pl.BlockSpec((step * PATCH, cols * PATCH), lambda n: (n, 0)),
        out_shape=jax.ShapeDtypeStruct((rows * PATCH, cols * PATCH), F32),
        compiler_params=PARAMS,
    )(patches, noise, order)


def per_device(
    image, noise, offsets, key_mask, gains, observed, vis_weight,
    w_embed, w_qkv, w_proj, w_up, w_down, w_unembed, norm_gains,
):
    rows = image.shape[0] // PATCH
    cols = image.shape[1] // PATCH
    devices = lax.axis_size("ty") * lax.axis_size("tx")
    fast = N // devices == TOK // 2
    row_index = lax.axis_index("ty") * rows + counting(rows)
    col_index = lax.axis_index("tx") * cols + counting(cols)
    weights = (w_qkv, w_proj, w_up, w_down, norm_gains)
    w_embed = w_embed.reshape(PATCH, PATCH, D).transpose(1, 0, 2).reshape(PIXELS, D)
    w_unembed = w_unembed.reshape(D, PATCH, PATCH).transpose(0, 2, 1).reshape(D, PIXELS)
    state, moving = patches_of(image[None], 0, (F32, BF16))
    shift = None
    grads = []
    if fast:
        scale, data, mirrored = spectrum_inputs(gains, observed, vis_weight, devices)
    first_bias = bias_of(None, key_mask)
    for step in range(STEPS):
        if not fast:
            grad = plain_gradient(tile_of(state, 0.0, noise, 0), gains, observed, vis_weight)
            grads = patches_of(grad.astype(F32)[None], 0, (BF16,))
        elif step == 0:
            grads = [patch_gradient(moving, scale, data, None)]
        else:
            grads = grads + [patch_gradient(moving, mirrored, None, shift)]
        last = step + 1 == STEPS
        sigma = None if last else SIGMAS[step + 1]
        extra = None if last else patches_of(noise, step)[0]
        base, first = first_block(
            STEP_SIZES[step], sigma, state, grads, extra, first_bias, w_embed, weights
        )
        shift = offsets[step]
        labels = 3 * region(row_index, shift[0])[:, None] + region(col_index, shift[1])[None, :]
        rolled, *moving = second_block(
            None if last else SIGMAS[step], shift, with_next(first), bias_of(labels, None),
            w_unembed, weights,
        )
        moving = None if last else moving[0]
        corner = (WIN - shift[0], WIN - shift[1], jnp.zeros((), jnp.int32))
        estimate = lax.dynamic_slice(with_previous(rolled), corner, base.shape)
        state = base - SIGMAS[step] * estimate.astype(F32)
    return tile_of(state, SIGMAS[STEPS], noise, STEPS - 1)


def solution(mesh):
    in_specs = (
        P("ty", "tx"),
        P(None, "ty", "tx"),
        P(),
        P("ty", "tx"),
        P(None, ("ty", "tx"), None),
        P(None, ("ty", "tx"), None),
        P(("ty", "tx"), None),
        P(),
        P(),
        P(),
        P(),
        P(),
        P(),
        P(),
    )
    out_specs = P("ty", "tx")
    return jax.shard_map(
        per_device, mesh=mesh, in_specs=in_specs, out_specs=out_specs, check_vma=False
    )
```

```python
import functools
import math

import jax
import jax.numpy as jnp
import ml_dtypes
import numpy as np
from jax import lax
from jax.experimental import pallas as pl
from jax.experimental.pallas import tpu as pltpu
from jax.sharding import PartitionSpec as P

N = 4096
PATCH = 16
PIXELS = PATCH * PATCH
WIN = 8
D = 512
HEADS = 8
STEPS = 2
SPAN = WIN * WIN
LANES = 128
TOK = N // PATCH

SIGMAS = (0.8, 0.5, 0.3)
STEP_SIZES = (0.9, 0.7)
EPSILON = 1e-05
HIGHEST = lax.Precision.HIGHEST
BF16 = jnp.bfloat16
F32 = jnp.float32
GELU_IN = math.sqrt(2.0 / math.pi)
GELU_CUBE = 0.044715 * GELU_IN
VMEM_LIMIT = 56 * 1024 * 1024
PARAMS = pltpu.CompilerParams(vmem_limit_bytes=VMEM_LIMIT)
TN = (((0,), (0,)), ((), ()))
NT = (((1,), (1,)), ((), ()))
NN = (((1,), (0,)), ((), ()))


def mm(left, right, dims=NN):
    return lax.dot_general(left, right, dims, preferred_element_type=F32)


def counting(length):
    return jnp.arange(length, dtype=jnp.int32)


def roots(length, outer, inner, sign):
    product = outer[:, None] * inner[None, :] % length
    angle = 2.0 * math.pi / length * product.astype(F32)
    return (jnp.cos(angle), sign * jnp.sin(angle))


def complex_einsum(form, left, right):
    real = jnp.einsum(form, left[0], right[0], precision=HIGHEST) - jnp.einsum(
        form, left[1], right[1], precision=HIGHEST
    )
    imag = jnp.einsum(form, left[0], right[1], precision=HIGHEST) + jnp.einsum(
        form, left[1], right[0], precision=HIGHEST
    )
    return (real, imag)


def complex_times(left, right):
    return (left[0] * right[0] - left[1] * right[1], left[0] * right[1] + left[1] * right[0])


def along_last(real_part, imag_part, groups, sign):
    rows, length = real_part.shape
    inner = length // groups
    first = roots(groups, counting(groups), counting(groups), sign)
    twist = roots(length, counting(inner), counting(groups), sign)
    second = roots(inner, counting(inner), counting(inner), sign)
    shaped = real_part.reshape(rows, groups, inner)
    if imag_part is None:
        partial_value = (
            jnp.einsum("mab,ka->mbk", shaped, first[0], precision=HIGHEST),
            jnp.einsum("mab,ka->mbk", shaped, first[1], precision=HIGHEST),
        )
    else:
        partial_value = complex_einsum(
            "mab,ka->mbk", (shaped, imag_part.reshape(rows, groups, inner)), first
        )
    partial_value = complex_times(partial_value, twist)
    result = complex_einsum("jb,mbk->mjk", second, partial_value)
    return (result[0].reshape(rows, length), result[1].reshape(rows, length))


def across_groups(pair, groups, sign):
    inner, cols = pair[0].shape
    width = cols // groups
    length = groups * inner
    first = roots(groups, counting(groups), counting(groups), sign)
    twist = roots(length, counting(inner), counting(groups), sign)
    second = roots(inner, counting(inner), counting(inner), sign)
    shaped = (pair[0].reshape(inner, groups, width), pair[1].reshape(inner, groups, width))
    partial_value = complex_einsum("bhc,kh->cbk", shaped, first)
    partial_value = complex_times(partial_value, twist)
    result = complex_einsum("jb,cbk->cjk", second, partial_value)
    return (result[0].reshape(width, length), result[1].reshape(width, length))


def exchange_pair(pair):
    return tuple(
        lax.all_to_all(
            part.astype(BF16), ("ty", "tx"), split_axis=1, concat_axis=1, tiled=True
        ).astype(F32)
        for part in pair
    )


def plain_gradient(tile, gains, observed, vis_weight):
    devices = lax.axis_size("ty") * lax.axis_size("tx")
    slab = lax.all_to_all(tile.astype(BF16), "tx", split_axis=0, concat_axis=1, tiled=True)
    moved = exchange_pair(along_last(slab.astype(F32), None, devices, -1.0))
    spectrum = across_groups(moved, devices, -1.0)
    spectrum = (spectrum[0] * (1.0 / N), spectrum[1] * (1.0 / N))
    model = complex_times((gains[0], gains[1]), spectrum)
    misfit = (vis_weight * (model[0] - observed[0]), vis_weight * (model[1] - observed[1]))
    back = complex_times((gains[0], -gains[1]), misfit)
    returned = exchange_pair(along_last(back[0], back[1], devices, 1.0))
    slab_grad = across_groups(returned, devices, 1.0)[0] * (1.0 / N)
    return lax.all_to_all(slab_grad.astype(BF16), "tx", split_axis=1, concat_axis=0, tiled=True)


def embed_complex(angle, row_axis, col_axis):
    cos, sin = np.cos(angle), np.sin(angle)
    top = np.stack([cos, sin], axis=col_axis)
    bottom = np.stack([-sin, cos], axis=col_axis)
    return np.stack([top, bottom], axis=row_axis)


def wheel(length, product):
    return 2.0 * math.pi / length * (product % length)


@functools.lru_cache(maxsize=None)
def row_constants():
    k = np.arange(TOK)
    angle = wheel(TOK, k[:, None] * k[None, :])
    first = np.concatenate([np.cos(angle), -np.sin(angle)], axis=1)
    b = np.repeat(np.arange(PATCH), PATCH)
    angle = wheel(N, b[:, None] * k[None, :])
    twist = np.stack([np.cos(angle), -np.sin(angle)])
    p = np.arange(PATCH)
    small = embed_complex(wheel(PATCH, p[:, None] * p[None, :]), 1, 1)
    second = np.einsum("kpqb,xy->kpxqby", small, np.eye(PATCH)).reshape(2 * PIXELS, 2 * PIXELS)
    return (
        first.astype(ml_dtypes.bfloat16),
        twist.astype(np.float32),
        second.astype(ml_dtypes.bfloat16),
        np.ascontiguousarray(second.T).astype(ml_dtypes.bfloat16),
    )


@functools.lru_cache(maxsize=None)
def half_constants():
    _, twist, second, _ = row_constants()
    half, quarter = TOK // 2, TOK // 4
    low = np.concatenate([1 + np.arange(quarter), 1 + half + np.arange(quarter)])
    digits = np.concatenate([low, low - 1])
    k = np.arange(TOK)
    angle = wheel(TOK, k[:, None] * digits[None, :])
    first = np.concatenate([np.cos(angle), -np.sin(angle)], axis=1)
    zero_line = np.concatenate([np.tile(np.eye(PATCH), PATCH), np.zeros((PATCH, PIXELS))], axis=1)
    upper = np.concatenate([second[PIXELS:].astype(np.float32), zero_line])
    lower = second[:PIXELS].astype(np.float32)
    return (first.astype(ml_dtypes.bfloat16), np.ascontiguousarray(twist[:, :, digits])) + tuple(
        np.ascontiguousarray(value).astype(ml_dtypes.bfloat16)
        for value in (lower, upper, lower.T, upper.T)
    )


@functools.lru_cache(maxsize=None)
def column_constants(devices, rows):
    s = np.arange(devices)
    small = embed_complex(wheel(devices, s[:, None] * s[None, :]), 1, 2)
    wide = devices * 2 * PATCH
    outer = np.einsum("qpsr,xy->qpxsry", small, np.eye(PATCH)).reshape(wide, wide)
    kr = s[:, None] + devices * np.arange(rows)[None, :]
    angle = wheel(N, kr[:, :, None] * np.arange(rows)[None, None, :])
    inner = embed_complex(angle, 1, 2).reshape(devices, 2 * rows, 2 * rows) / N
    return tuple(
        np.ascontiguousarray(value).astype(ml_dtypes.bfloat16)
        for value in (outer, outer.T, inner, inner.transpose(0, 2, 1))
    )


def row_forward(x_ref, first_ref, twist_ref, second_ref, out_ref):
    count = x_ref.shape[1]

    def step(i, carry):
        band = x_ref[:, i].reshape(TOK, PIXELS)
        mixed = mm(band, first_ref[...], TN)
        real, imag = mixed[:, :TOK], mixed[:, TOK:]
        tr, ti = twist_ref[0], twist_ref[1]
        turned = jnp.concatenate(
            [(real * tr - imag * ti).astype(BF16), (real * ti + imag * tr).astype(BF16)], axis=0
        )
        result = mm(second_ref[...], turned).astype(BF16).reshape(PATCH, 2, PATCH, TOK)
        half = TOK // 2
        rows = pl.ds(pl.multiple_of(i * PATCH, PATCH), PATCH)
        out_ref[:, 0, :, rows, :] = result[..., :half]
        out_ref[:, 1, :, rows, :] = result[..., half:]
        return carry

    lax.fori_loop(0, count, step, 0, unroll=4)


def row_inverse(v_ref, first_ref, twist_ref, second_ref, out_ref):
    parts, count, cols, _ = out_ref.shape

    def step(i, carry):
        rows = pl.ds(pl.multiple_of(i * PATCH, PATCH), PATCH)
        wide = jnp.concatenate(
            [
                v_ref[:, 0, :, rows, :].reshape(2 * PIXELS, TOK // 2),
                v_ref[:, 1, :, rows, :].reshape(2 * PIXELS, TOK // 2),
            ],
            axis=1,
        )
        mixed = mm(second_ref[...], wide)
        real, imag = mixed[:PIXELS], mixed[PIXELS:]
        tr, ti = twist_ref[0], twist_ref[1]
        turned = jnp.concatenate(
            [(real * tr + imag * ti).astype(BF16), (imag * tr - real * ti).astype(BF16)], axis=1
        )
        result = mm(first_ref[...], turned, NT).astype(BF16)
        out_ref[:, i] = result.reshape(parts, cols, PIXELS)
        return carry

    lax.fori_loop(0, count, step, 0, unroll=4)


def lane_index(shape):
    return lax.broadcasted_iota(jnp.int32, shape, len(shape) - 1)


def swap_halves(values):
    return pltpu.roll(values, values.shape[-1] // 2, len(values.shape) - 1)


def row_forward_half(x_ref, first_ref, twist_ref, lower_ref, upper_ref, out_ref):
    count = x_ref.shape[1]
    half = TOK // 2

    def packed(real, imag, rows, high):
        left = lane_index(real.shape) < half // 2
        out_ref[high, 0, rows, :] = jnp.where(left, real, swap_halves(imag)).astype(BF16)
        out_ref[high, 1, rows, :] = jnp.where(left, swap_halves(real), imag).astype(BF16)

    def step(i, carry):
        band = x_ref[:, i].reshape(TOK, PIXELS)
        mixed = mm(band, first_ref[...], TN)
        real, imag = mixed[:, :TOK], mixed[:, TOK:]
        tr, ti = twist_ref[0], twist_ref[1]
        turned = jnp.concatenate(
            [(real * tr - imag * ti).astype(BF16), (real * ti + imag * tr).astype(BF16)], axis=0
        )
        rows = pl.ds(pl.multiple_of(i * PATCH, PATCH), PATCH)
        lower = mm(lower_ref[...], turned[:, :half]).reshape(PATCH // 2, 2, PATCH, half)
        packed(lower[:, 0], lower[:, 1], rows, slice(0, PATCH // 2))
        upper = mm(upper_ref[...], turned[:, half:])
        line = upper[PIXELS:]
        upper = upper[:PIXELS].reshape(PATCH // 2, 2, PATCH, half)
        imag = upper[:, 1]
        head = jnp.where(lane_index(line.shape) == 0, line, imag[0])
        imag = jnp.concatenate([head[None], imag[1:]], axis=0)
        packed(upper[:, 0], imag, rows, slice(PATCH // 2, PATCH))
        return carry

    lax.fori_loop(0, count, step, 0, unroll=4)


def row_inverse_half(v_ref, first_ref, twist_ref, lower_ref, upper_ref, out_ref):
    parts, count, cols, _ = out_ref.shape
    half = TOK // 2

    def unpacked(rows, high):
        even = v_ref[high, 0, rows, :].astype(F32)
        odd = v_ref[high, 1, rows, :].astype(F32)
        left = lane_index(even.shape) < half // 2
        return jnp.where(left, even, swap_halves(odd)), jnp.where(left, swap_halves(even), odd)

    def step(i, carry):
        rows = pl.ds(pl.multiple_of(i * PATCH, PATCH), PATCH)
        real, imag = unpacked(rows, slice(0, PATCH // 2))
        lower = jnp.stack([real, imag], axis=1).reshape(PIXELS, half)
        real, imag = unpacked(rows, slice(PATCH // 2, PATCH))
        head = imag[0]
        at_zero = lane_index(head.shape) == 0
        nothing = jnp.zeros_like(head)
        imag = jnp.concatenate([jnp.where(at_zero, nothing, head)[None], imag[1:]], axis=0)
        upper = jnp.stack([real, imag], axis=1).reshape(PIXELS, half)
        upper = jnp.concatenate([upper, jnp.where(at_zero, head, nothing)], axis=0)
        mixed = jnp.concatenate(
            [mm(lower_ref[...], lower.astype(BF16)), mm(upper_ref[...], upper.astype(BF16))], axis=1
        )
        real, imag = mixed[:PIXELS], mixed[PIXELS:]
        tr, ti = twist_ref[0], twist_ref[1]
        turned = jnp.concatenate(
            [(real * tr + imag * ti).astype(BF16), (imag * tr - real * ti).astype(BF16)], axis=1
        )
        result = mm(first_ref[...], turned, NT).astype(BF16)
        out_ref[:, i] = result.reshape(parts, cols, PIXELS)
        return carry

    lax.fori_loop(0, count, step, 0, unroll=4)


def column_kernel(halved, *refs):
    if halved:
        flag_ref, phase_ref, refs = refs[0], refs[1], refs[2:]
    x_ref, outer_ref, *refs = refs
    count = 4 if halved else 5
    sources, out_ref = refs[:count], refs[count]
    mid_ref, *targets, sems = refs[count + 1 :]
    copies = [
        pltpu.make_async_copy(source, target, sems.at[n])
        for n, (source, target) in enumerate(zip(sources, targets))
    ]
    for copy in copies:
        copy.start()
    inner_ref, scale_ref, inner_t_ref, outer_t_ref = targets[:4]
    devices, _, rows, width = mid_ref.shape
    wide = devices * 2 * PATCH
    if halved:
        lane = lane_index((devices, PATCH, width))
        centre = flag_ref[0] == 1
        half = width // 2
        hidden = (lane == half) | (centre & (lane == 0))
        real_lane = (lane < half) | (centre & (lane == half))

    def load(group):
        place = slice(group * PATCH, (group + 1) * PATCH)
        if not halved:
            return x_ref[:, :, place, :].reshape(wide, width)
        piece = x_ref[:, place, :]
        other = swap_halves(piece.astype(F32))
        other = jnp.where(hidden, jnp.zeros_like(other), other).astype(BF16)
        return jnp.stack([piece, other], axis=1).reshape(wide, width)

    def store(group, value):
        place = slice(group * PATCH, (group + 1) * PATCH)
        value = value.reshape(devices, 2, PATCH, width)
        if halved:
            value = jnp.where(real_lane, value[:, 0], swap_halves(value[:, 1])).astype(BF16)
            out_ref[:, place, :] = value
        else:
            out_ref[:, :, place, :] = value.astype(BF16)

    for pair in range(0, rows // PATCH, 2):
        result = mm(outer_ref[...], jnp.concatenate([load(pair), load(pair + 1)], axis=1))
        result = result.astype(BF16)
        for n in range(2):
            place = slice((pair + n) * PATCH, (pair + n + 1) * PATCH)
            mid_ref[:, :, place, :] = result[:, n * width : (n + 1) * width].reshape(
                devices, 2, PATCH, width
            )

    for n, copy in enumerate(copies):
        if n != 3:
            copy.wait()

    def step(q, carry):
        spectrum = mm(inner_ref[q], mid_ref[q].reshape(2 * rows, width))
        real, imag = spectrum[:rows], spectrum[rows:]
        scale = scale_ref[q].astype(F32)
        if halved:
            pr, pi = phase_ref[q, 0], phase_ref[q, 1]
            real = real.reshape(rows // 8, 8, width)
            imag = imag.reshape(rows // 8, 8, width)
            real, imag = real * pr - imag * pi, real * pi + imag * pr
            real, imag = real.reshape(rows, width) * scale, imag.reshape(rows, width) * scale
        else:
            data_ref = targets[4]
            real = real * scale - data_ref[0, q].astype(F32)
            imag = imag * scale - data_ref[1, q].astype(F32)
        back = jnp.concatenate([real.astype(BF16), imag.astype(BF16)], axis=0)
        mid_ref[q] = mm(inner_t_ref[q], back).astype(BF16).reshape(2, rows, width)
        return carry

    lax.fori_loop(0, devices, step, 0, unroll=8)
    copies[3].wait()

    for pair in range(0, rows // PATCH, 2):
        both = jnp.concatenate(
            [
                mid_ref[:, :, n * PATCH : (n + 1) * PATCH, :].reshape(wide, width)
                for n in (pair, pair + 1)
            ],
            axis=1,
        )
        result = mm(outer_t_ref[...], both)
        store(pair, result[:, :width])
        store(pair + 1, result[:, width:])


def turned(value, devices):
    lines = value.shape[0]
    return value.astype(BF16).reshape(lines, N // devices, devices).transpose(2, 1, 0)


def spectrum_inputs(gains, observed, vis_weight, devices):
    gr, gi = gains[0], gains[1]
    weight = (vis_weight * (gr * gr + gi * gi)).astype(BF16)
    data = jnp.stack(
        [
            turned(vis_weight * (gr * observed[0] + gi * observed[1]), devices),
            turned(vis_weight * (gr * observed[1] - gi * observed[0]), devices),
        ]
    )
    return weight, turned(weight, devices), data


def mirror_kernel(scale_ref, got_ref, pick_ref, flip_ref, out_ref):
    devices = out_ref.shape[0]
    for q in range(devices):
        facing = mm(flip_ref[min(q, 1)], got_ref[(devices - q) % devices]).astype(BF16)
        total = mm(scale_ref[q], pick_ref[0]) + mm(facing, pick_ref[1])
        out_ref[q] = total.astype(BF16)


def mirrored_exchange(weight):
    devices = N // weight.shape[0]
    half, middle = weight.shape[0] // 2, devices // 2
    facing = [(e, devices - 1 - e) for e in range(devices)]
    partner = [(e, devices - e) for e in range(1, devices) if e != middle]
    partner = partner + [(0, middle), (middle, 0)]
    upper = lax.ppermute(weight[half:], ("ty", "tx"), facing)
    line = lax.ppermute(weight[:1], ("ty", "tx"), partner)
    return upper, line


def mirrored_weight(scale, upper, line):
    devices, slab, _ = scale.shape
    half, middle = slab // 2, devices // 2
    me = lax.axis_index(("ty", "tx"))
    got = jnp.concatenate([upper, jnp.broadcast_to(line, (half, N))], axis=0)
    source = lax.broadcasted_iota(jnp.int32, (slab, slab), 0)
    slot = lax.broadcasted_iota(jnp.int32, (slab, slab), 1)
    low = (me < middle).astype(jnp.int32)
    own = (slot < half) & (source == slot + low)
    other = (slot < half) & (source == half - low - slot)
    other = other & ((me != middle) | (slot > 0))
    other = other | ((me == middle) & (slot == half) & (source == half))
    picks = jnp.stack([own, other]).astype(BF16)
    q2 = np.arange(slab)
    flips = np.stack([q2[:, None] == (slab - q2) % slab, q2[:, None] == slab - 1 - q2])
    return pl.pallas_call(
        mirror_kernel,
        out_shape=jax.ShapeDtypeStruct(scale.shape, BF16),
        compiler_params=PARAMS,
    )(scale, turned(got, devices), picks, jnp.asarray(flips.astype(ml_dtypes.bfloat16)))


def row_matrix(shift):
    first = half_constants()[0]
    twice = jnp.asarray(np.concatenate([first, first[: 2 * WIN]], axis=0))
    return lax.dynamic_slice(twice, (shift, jnp.zeros((), jnp.int32)), first.shape)


def phase_table(shift, devices, width):
    kr = counting(devices)[:, None] + devices * counting(8)[None, :]
    angle = 2.0 * math.pi / TOK * (kr * shift % TOK).astype(F32)
    table = jnp.stack([jnp.cos(angle), -jnp.sin(angle)], axis=1)
    return jnp.broadcast_to(table[..., None], (devices, 2, 8, width))


def patch_gradient(state, scale, data, shift, mirror, beside):
    lanes = lax.axis_size("tx")
    devices = lax.axis_size("ty") * lanes
    rows, cols, _ = state.shape
    own = rows // lanes
    slab = N // devices
    halved = data is None
    outer, outer_t, inner, inner_t = (
        jnp.asarray(value) for value in column_constants(devices, slab)
    )
    if halved:
        first, twist, low, high, low_t, high_t = (jnp.asarray(value) for value in half_constants())
        part = (devices, slab, slab)
        onward = (row_forward_half, (row_matrix(shift[1]), twist, low, high))
        backward = (row_inverse_half, (first, twist, low_t, high_t))
        middle = lax.axis_index(("ty", "tx")) == devices // 2
    else:
        first, twist, second, second_t = (jnp.asarray(value) for value in row_constants())
        part = (devices, 2, slab, slab)
        onward = (row_forward, (first, twist, second))
        backward = (row_inverse, (first, twist, second_t))
        extra = ()
        away = (inner, scale, inner_t, outer_t, data)
    split = (PATCH, devices // PATCH) + part[1:]
    gathered = lax.all_to_all(
        state.reshape(lanes, own, cols, PIXELS), "tx", split_axis=0, concat_axis=0, tiled=True
    )
    sent = pl.pallas_call(
        onward[0], out_shape=jax.ShapeDtypeStruct(split, BF16), compiler_params=PARAMS
    )(gathered, *onward[1])
    if halved:
        sent, mirror, shift = lax.optimization_barrier((sent, mirror, shift))
        extra = (middle.astype(jnp.int32).reshape(1), phase_table(shift[0], devices, slab))
        away = (inner, mirrored_weight(scale, *mirror), inner_t, outer_t)
    moved = lax.all_to_all(
        sent.reshape(part), ("ty", "tx"), split_axis=0, concat_axis=0, tiled=True
    )
    spaces = [pltpu.SMEM, pltpu.VMEM][: len(extra)] + [pltpu.VMEM] * 2 + [pl.ANY] * len(away)
    wave = pl.pallas_call(
        functools.partial(column_kernel, halved),
        in_specs=[pl.BlockSpec(memory_space=space) for space in spaces],
        out_shape=jax.ShapeDtypeStruct(part, BF16),
        scratch_shapes=[pltpu.VMEM((devices, 2, slab, slab), BF16)]
        + [pltpu.VMEM(value.shape, BF16) for value in away]
        + [pltpu.SemaphoreType.DMA((len(away),))],
        compiler_params=PARAMS,
    )(*extra, moved, outer, *away)
    returned = lax.all_to_all(wave, ("ty", "tx"), split_axis=0, concat_axis=0, tiled=True)
    returned, beside = lax.optimization_barrier((returned, beside))
    slabs = pl.pallas_call(
        backward[0],
        out_shape=jax.ShapeDtypeStruct((lanes, own, cols, PIXELS), BF16),
        compiler_params=PARAMS,
    )(returned.reshape(split), *backward[1])
    grad = lax.all_to_all(slabs, "tx", split_axis=0, concat_axis=0, tiled=True)
    return grad.reshape(rows, cols, PIXELS), beside


def layer_norm(values, gain):
    centre = jnp.mean(values, axis=-1, keepdims=True)
    shifted = values - centre
    spread = jnp.mean(shifted * shifted, axis=-1, keepdims=True)
    return (shifted * lax.rsqrt(spread + EPSILON) * gain).astype(BF16)


def to_windows(band):
    rows, cols, feats = band.shape
    pieces = [
        band[:, w * WIN : (w + 1) * WIN, :].reshape(SPAN, feats) for w in range(cols // WIN)
    ]
    return jnp.concatenate(pieces, axis=0)


def from_windows(tokens, cols):
    feats = tokens.shape[-1]
    pieces = [
        tokens[w * SPAN : (w + 1) * SPAN].reshape(WIN, WIN, feats) for w in range(cols // WIN)
    ]
    return jnp.concatenate(pieces, axis=1)


def swin_band(
    flow, bias_ref, qkv_ref, proj_ref, up_ref, down_ref, gain_ref, mixed_ref, score_ref, prob_ref
):
    count = flow.shape[0] // SPAN
    pairs = HEADS // 2
    depth = D // HEADS
    wide = 2 * depth
    normed = layer_norm(flow, gain_ref[0:1, :])
    scale = 1.0 / math.sqrt(depth)
    mixed_ref[:, :D] = (mm(normed, qkv_ref[:, :D]) * scale).astype(BF16)
    mixed_ref[:, D : 2 * D] = mm(normed, qkv_ref[:, D : 2 * D]).astype(BF16)
    mixed_ref[:, 2 * D :] = mm(normed, qkv_ref[:, 2 * D :]).astype(BF16)
    lower = lax.broadcasted_iota(jnp.int32, (SPAN, wide), 1) < depth
    for w in range(count):
        rows = slice(w * SPAN, (w + 1) * SPAN)
        for p in range(pairs):
            query = mixed_ref[rows, p * wide : (p + 1) * wide]
            key = mixed_ref[rows, D + p * wide : D + (p + 1) * wide]
            zero = jnp.zeros_like(query)
            split = jnp.concatenate(
                [jnp.where(lower, query, zero), jnp.where(lower, zero, query)], axis=0
            )
            score_ref[w, :, p * wide : (p + 1) * wide] = mm(key, split, NT)
    for w in range(count):
        bias = bias_ref[w]
        for p in range(pairs):
            lanes = slice(p * wide, (p + 1) * wide)
            scores = score_ref[w, :, lanes] + bias
            weights = jnp.exp(scores - jnp.max(scores, axis=0, keepdims=True))
            share = 1.0 / jnp.sum(weights, axis=0, keepdims=True)
            prob_ref[w, :, lanes] = (weights * share).astype(BF16)
    for w in range(count):
        rows = slice(w * SPAN, (w + 1) * SPAN)
        for p in range(pairs):
            lanes = slice(p * wide, (p + 1) * wide)
            value = mixed_ref[rows, 2 * D + p * wide : 2 * D + (p + 1) * wide]
            mixture = mm(prob_ref[w, :, lanes], value, TN)
            mixed_ref[rows, lanes] = jnp.where(lower, mixture[:SPAN], mixture[SPAN:]).astype(BF16)
    flow = flow + mm(mixed_ref[:, :D], proj_ref[...])
    normed = layer_norm(flow, gain_ref[1:2, :])
    chunks = up_ref.shape[1] // D
    total = jnp.zeros_like(flow)
    ahead = mm(normed, up_ref[:, :D])
    for c in range(chunks):
        value = ahead
        if c + 1 < chunks:
            ahead = mm(normed, up_ref[:, (c + 1) * D : (c + 2) * D])
        inside = value * (GELU_IN + GELU_CUBE * (value * value))
        active = (value + value * jnp.tanh(inside)).astype(BF16)
        total = total + mm(active, down_ref[c * D : (c + 1) * D, :])
    return flow + 0.5 * total


def first_kernel(zeta, sigma, count, *refs):
    state_ref, grad_refs, refs = refs[0], refs[1 : 1 + count], refs[1 + count :]
    if sigma is not None:
        noise_ref, refs = refs[0], refs[1:]
    bias_ref, embed_ref, qkv_ref, proj_ref, up_ref, down_ref, gain_ref = refs[:7]
    base_ref, out_ref, *scratch = refs[7:]
    step = zeta * sum(grad_ref[...].astype(F32) for grad_ref in grad_refs)
    half = state_ref[...] - step
    tokens = mm(to_windows(half).astype(BF16), embed_ref[...]).astype(BF16).astype(F32)
    if sigma is None:
        base_ref[...] = half
    else:
        noise = sigma * noise_ref[...]
        base_ref[...] = half + noise
        out_ref[:, :, D:] = (noise - step).astype(BF16)
    flow = swin_band(tokens, bias_ref, qkv_ref, proj_ref, up_ref, down_ref, gain_ref, *scratch)
    out_ref[:, :, :D] = from_windows(flow, half.shape[1]).astype(BF16)


def second_kernel(sigma, *refs):
    shift_ref, grid_ref, bias_ref, qkv_ref, proj_ref, up_ref, down_ref, gain_ref = refs[:8]
    unembed_ref, out_ref, *scratch = refs[8:]
    if sigma is not None:
        state_ref, scratch = scratch[0], scratch[1:]
    cols = out_ref.shape[1]
    top = pl.program_id(0) * WIN + shift_ref[0]
    wide = grid_ref[pl.ds(top, WIN)]
    place = lax.broadcasted_iota(jnp.int32, (cols, wide.shape[1]), 1)
    target = lax.broadcasted_iota(jnp.int32, (cols, wide.shape[1]), 0) + shift_ref[1]
    pick = jnp.where(place == target, 1.0, 0.0).astype(BF16)
    band = jnp.stack([mm(pick, wide[n]) for n in range(WIN)])
    tokens = to_windows(band[:, :, :D])
    flow = swin_band(tokens, bias_ref, qkv_ref, proj_ref, up_ref, down_ref, gain_ref, *scratch)
    estimate = from_windows(mm(flow.astype(BF16), unembed_ref[...]), cols)
    out_ref[...] = estimate.astype(BF16)
    if sigma is not None:
        state_ref[...] = (band[:, :, D:] - sigma * estimate).astype(BF16)


def whole(array):
    zeros = (0,) * array.ndim
    return pl.BlockSpec(array.shape, lambda *_: zeros)


def band_of(step, cols):
    return pl.BlockSpec((step, cols, PIXELS), lambda n: (n, 0, 0))


def member(array, j):
    place = (j,) + (0,) * (array.ndim - 1)
    return pl.BlockSpec((None,) + array.shape[1:], lambda *_: place)


def band_spec(cols, feats):
    return pl.BlockSpec((WIN, cols, feats), lambda n, *_: (n, 0, 0))


def bias_spec(cols):
    return pl.BlockSpec((cols // WIN, SPAN, 2 * SPAN), lambda n, *_: (n, 0, 0))


def band_scratch(cols):
    count = cols // WIN
    return [
        pltpu.VMEM((WIN * cols, 3 * D), BF16),
        pltpu.VMEM((count, SPAN, HEADS * SPAN), F32),
        pltpu.VMEM((count, SPAN, HEADS * SPAN), BF16),
    ]


def first_block(zeta, sigma, state, grads, noise, bias, w_embed, weights):
    rows, cols, _ = state.shape
    fields = [state, *grads] + ([] if sigma is None else [noise])
    feats = D if sigma is None else D + PIXELS
    return pl.pallas_call(
        functools.partial(first_kernel, zeta, sigma, len(grads)),
        grid=(rows // WIN,),
        in_specs=[band_spec(cols, PIXELS)] * len(fields)
        + [bias_spec(cols), whole(w_embed)]
        + [member(value, 0) for value in weights],
        out_specs=[band_spec(cols, PIXELS), band_spec(cols, feats)],
        out_shape=[
            jax.ShapeDtypeStruct((rows, cols, PIXELS), F32),
            jax.ShapeDtypeStruct((rows, cols, feats), BF16),
        ],
        scratch_shapes=band_scratch(cols),
        compiler_params=PARAMS,
    )(*fields, bias, w_embed, *weights)


def second_block(sigma, shift, grid, bias, w_unembed, weights):
    rows, cols = grid.shape[0] - WIN, grid.shape[1] - WIN
    outs = 1 if sigma is None else 2
    return pl.pallas_call(
        functools.partial(second_kernel, sigma),
        grid_spec=pltpu.PrefetchScalarGridSpec(
            num_scalar_prefetch=1,
            grid=(rows // WIN,),
            in_specs=[whole(grid), bias_spec(cols)]
            + [member(value, 1) for value in weights]
            + [whole(w_unembed)],
            out_specs=[band_spec(cols, PIXELS)] * outs,
            scratch_shapes=band_scratch(cols),
        ),
        out_shape=[jax.ShapeDtypeStruct((rows, cols, PIXELS), BF16)] * outs,
        compiler_params=PARAMS,
    )(shift, grid, bias, *weights, w_unembed)


def from_behind(shard, axis, by):
    size = lax.axis_size(axis)
    return lax.ppermute(shard, axis, [(i, (i + by) % size) for i in range(size)])


def with_next(grid):
    wide = jnp.concatenate([grid, from_behind(grid[:, :WIN], "tx", -1)], axis=1)
    return jnp.concatenate([wide, from_behind(wide[:WIN], "ty", -1)], axis=0)


def with_previous(grid):
    wide = jnp.concatenate([from_behind(grid[:, -WIN:], "tx", 1), grid], axis=1)
    return jnp.concatenate([from_behind(wide[-WIN:], "ty", 1), wide], axis=0)


def windows_of(grid):
    rows, cols = grid.shape
    shaped = grid.reshape(rows // WIN, WIN, cols // WIN, WIN).transpose(0, 2, 1, 3)
    return shaped.reshape(rows // WIN * (cols // WIN), SPAN)


def bias_of(labels, keep):
    allowed = jnp.ones((1, SPAN, SPAN), bool)
    if labels is not None:
        label = windows_of(labels)
        allowed = label[:, :, None] == label[:, None, :]
    if keep is not None:
        kept = windows_of(keep)[:, :, None] == 1
        allowed = allowed & (kept | jnp.eye(SPAN, dtype=bool)[None])
    bias = jnp.where(allowed, 0.0, -1e30).astype(F32)
    return jnp.concatenate([bias, bias], axis=2)


def region(index, shift):
    return jnp.where(index < TOK - WIN, 0, jnp.where(index < TOK - shift, 1, 2)).astype(jnp.int32)


@functools.lru_cache(maxsize=None)
def lane_order(cols):
    parts = LANES // cols
    groups = PATCH // parts
    lane = np.arange(PATCH * cols)
    g, h, k = lane // LANES, lane % LANES // cols, lane % cols
    source = PATCH * k + h * groups + g
    matrix = np.zeros((PATCH * cols, PATCH * cols), np.float32)
    matrix[source, lane] = 1.0
    return matrix.astype(ml_dtypes.bfloat16), np.ascontiguousarray(matrix.T).astype(
        ml_dtypes.bfloat16
    )


def move_lanes(values, matrix):
    high = values.astype(BF16)
    low = (values - high.astype(F32)).astype(BF16)
    return mm(high, matrix) + mm(low, matrix)


def to_patches_kernel(tile_ref, order_ref, out_ref):
    count, cols, _ = out_ref.shape
    parts = LANES // cols
    groups = PATCH // parts
    if out_ref.dtype == BF16:
        ordered = mm(tile_ref[...].astype(BF16), order_ref[...])
    else:
        ordered = move_lanes(tile_ref[...], order_ref[...])
    for i in range(count):
        band = ordered[i * PATCH : (i + 1) * PATCH]
        stacked = jnp.concatenate(
            [band[:, g * LANES : (g + 1) * LANES] for g in range(groups)], axis=0
        )
        turned = stacked.T
        patch = jnp.concatenate([turned[h * cols : (h + 1) * cols] for h in range(parts)], axis=1)
        out_ref[i] = patch.astype(out_ref.dtype)


def to_tile_kernel(scale, patch_ref, noise_ref, order_ref, out_ref):
    count, cols, _ = patch_ref.shape
    parts = LANES // cols
    groups = PATCH // parts
    width = groups * PATCH
    bands = []
    for i in range(count):
        patch = patch_ref[i]
        stacked = jnp.concatenate(
            [patch[:, h * width : (h + 1) * width] for h in range(parts)], axis=0
        )
        turned = stacked.T
        bands.append(
            jnp.concatenate([turned[g * PATCH : (g + 1) * PATCH] for g in range(groups)], axis=1)
        )
    moved = move_lanes(jnp.concatenate(bands, axis=0), order_ref[...])
    out_ref[...] = moved + scale * noise_ref[...]


def patches_of(tiles, j, kind=F32):
    rows, cols = tiles.shape[1] // PATCH, tiles.shape[2] // PATCH
    order = jnp.asarray(lane_order(cols)[0])
    step = rows // 4
    return pl.pallas_call(
        to_patches_kernel,
        grid=(rows // step,),
        in_specs=[
            pl.BlockSpec((None, step * PATCH, cols * PATCH), lambda n: (j, n, 0)),
            whole(order),
        ],
        out_specs=band_of(step, cols),
        out_shape=jax.ShapeDtypeStruct((rows, cols, PIXELS), kind),
        compiler_params=PARAMS,
    )(tiles, order)


def tile_of(patches, scale, noise, j):
    rows, cols, _ = patches.shape
    order = jnp.asarray(lane_order(cols)[1])
    step = rows // 4
    return pl.pallas_call(
        functools.partial(to_tile_kernel, scale),
        grid=(rows // step,),
        in_specs=[
            band_of(step, cols),
            pl.BlockSpec((None, step * PATCH, cols * PATCH), lambda n: (j, n, 0)),
            whole(order),
        ],
        out_specs=pl.BlockSpec((step * PATCH, cols * PATCH), lambda n: (n, 0)),
        out_shape=jax.ShapeDtypeStruct((rows * PATCH, cols * PATCH), F32),
        compiler_params=PARAMS,
    )(patches, noise, order)


def per_device(
    image, noise, offsets, key_mask, gains, observed, vis_weight,
    w_embed, w_qkv, w_proj, w_up, w_down, w_unembed, norm_gains,
):
    rows = image.shape[0] // PATCH
    cols = image.shape[1] // PATCH
    devices = lax.axis_size("ty") * lax.axis_size("tx")
    fast = N // devices == TOK // 2
    row_index = lax.axis_index("ty") * rows + counting(rows)
    col_index = lax.axis_index("tx") * cols + counting(cols)
    weights = (w_qkv, w_proj, w_up, w_down, norm_gains)
    w_embed = w_embed.reshape(PATCH, PATCH, D).transpose(1, 0, 2).reshape(PIXELS, D)
    w_unembed = w_unembed.reshape(D, PATCH, PATCH).transpose(0, 2, 1).reshape(D, PIXELS)
    state = patches_of(image[None], 0)
    extras = [patches_of(noise, step) for step in range(STEPS - 1)] + [None]
    first_bias = bias_of(None, key_mask)
    biases = []
    for step in range(STEPS):
        labels = (
            3 * region(row_index, offsets[step, 0])[:, None]
            + region(col_index, offsets[step, 1])[None, :]
        )
        biases.append(bias_of(labels, None))
    beside = (state, extras, first_bias, biases, w_embed, w_unembed)
    shift = moving = mirror = None
    grads = []
    if fast:
        weight, scale, data = spectrum_inputs(gains, observed, vis_weight, devices)
        grad, beside = patch_gradient(
            patches_of(image[None], 0, BF16), scale, data, None, None, beside
        )
        grads = [grad]
        state, extras, first_bias, biases, w_embed, w_unembed = beside
    for step in range(STEPS):
        if not fast:
            grad = plain_gradient(tile_of(state, 0.0, noise, 0), gains, observed, vis_weight)
            grads = [patches_of(grad.astype(F32)[None], 0, BF16)]
        elif step > 0:
            grads = grads + [patch_gradient(moving, scale, None, shift, mirror, ())[0]]
        last = step + 1 == STEPS
        sigma = None if last else SIGMAS[step + 1]
        base, first = first_block(
            STEP_SIZES[step], sigma, state, grads, extras[step], first_bias, w_embed, weights
        )
        shift = offsets[step]
        grid = with_next(first)
        if fast and step == 0:
            grid, weight = lax.optimization_barrier((grid, weight))
            mirror = mirrored_exchange(weight)
        rolled, *moving = second_block(
            None if last else SIGMAS[step], shift, grid, biases[step], w_unembed, weights
        )
        moving = None if last else moving[0]
        corner = (WIN - shift[0], WIN - shift[1], jnp.zeros((), jnp.int32))
        estimate = lax.dynamic_slice(with_previous(rolled), corner, base.shape)
        state = base - SIGMAS[step] * estimate.astype(F32)
    return tile_of(state, SIGMAS[STEPS], noise, STEPS - 1)


def solution(mesh):
    in_specs = (
        P("ty", "tx"),
        P(None, "ty", "tx"),
        P(),
        P("ty", "tx"),
        P(None, ("ty", "tx"), None),
        P(None, ("ty", "tx"), None),
        P(("ty", "tx"), None),
        P(),
        P(),
        P(),
        P(),
        P(),
        P(),
        P(),
    )
    out_specs = P("ty", "tx")
    return jax.shard_map(
        per_device, mesh=mesh, in_specs=in_specs, out_specs=out_specs, check_vma=False
    )
```

```python
import functools
import math

import jax
import jax.numpy as jnp
import ml_dtypes
import numpy as np
from jax import lax
from jax.experimental import pallas as pl
from jax.experimental.pallas import tpu as pltpu
from jax.sharding import PartitionSpec as P

N = 4096
PATCH = 16
PIXELS = PATCH * PATCH
WIN = 8
D = 512
HEADS = 8
STEPS = 2
SPAN = WIN * WIN
LANES = 128
TOK = N // PATCH

SIGMAS = (0.8, 0.5, 0.3)
STEP_SIZES = (0.9, 0.7)
EPSILON = 1e-05
HIGHEST = lax.Precision.HIGHEST
BF16 = jnp.bfloat16
F32 = jnp.float32
GELU_IN = math.sqrt(2.0 / math.pi)
GELU_CUBE = 0.044715 * GELU_IN
VMEM_LIMIT = 56 * 1024 * 1024
PARAMS = pltpu.CompilerParams(vmem_limit_bytes=VMEM_LIMIT)
TN = (((0,), (0,)), ((), ()))
NT = (((1,), (1,)), ((), ()))
NN = (((1,), (0,)), ((), ()))


def mm(left, right, dims=NN):
    return lax.dot_general(left, right, dims, preferred_element_type=F32)


def counting(length):
    return jnp.arange(length, dtype=jnp.int32)


def roots(length, outer, inner, sign):
    product = outer[:, None] * inner[None, :] % length
    angle = 2.0 * math.pi / length * product.astype(F32)
    return (jnp.cos(angle), sign * jnp.sin(angle))


def complex_einsum(form, left, right):
    real = jnp.einsum(form, left[0], right[0], precision=HIGHEST) - jnp.einsum(
        form, left[1], right[1], precision=HIGHEST
    )
    imag = jnp.einsum(form, left[0], right[1], precision=HIGHEST) + jnp.einsum(
        form, left[1], right[0], precision=HIGHEST
    )
    return (real, imag)


def complex_times(left, right):
    return (left[0] * right[0] - left[1] * right[1], left[0] * right[1] + left[1] * right[0])


def along_last(real_part, imag_part, groups, sign):
    rows, length = real_part.shape
    inner = length // groups
    first = roots(groups, counting(groups), counting(groups), sign)
    twist = roots(length, counting(inner), counting(groups), sign)
    second = roots(inner, counting(inner), counting(inner), sign)
    shaped = real_part.reshape(rows, groups, inner)
    if imag_part is None:
        partial_value = (
            jnp.einsum("mab,ka->mbk", shaped, first[0], precision=HIGHEST),
            jnp.einsum("mab,ka->mbk", shaped, first[1], precision=HIGHEST),
        )
    else:
        partial_value = complex_einsum(
            "mab,ka->mbk", (shaped, imag_part.reshape(rows, groups, inner)), first
        )
    partial_value = complex_times(partial_value, twist)
    result = complex_einsum("jb,mbk->mjk", second, partial_value)
    return (result[0].reshape(rows, length), result[1].reshape(rows, length))


def across_groups(pair, groups, sign):
    inner, cols = pair[0].shape
    width = cols // groups
    length = groups * inner
    first = roots(groups, counting(groups), counting(groups), sign)
    twist = roots(length, counting(inner), counting(groups), sign)
    second = roots(inner, counting(inner), counting(inner), sign)
    shaped = (pair[0].reshape(inner, groups, width), pair[1].reshape(inner, groups, width))
    partial_value = complex_einsum("bhc,kh->cbk", shaped, first)
    partial_value = complex_times(partial_value, twist)
    result = complex_einsum("jb,cbk->cjk", second, partial_value)
    return (result[0].reshape(width, length), result[1].reshape(width, length))


def exchange_pair(pair):
    return tuple(
        lax.all_to_all(
            part.astype(BF16), ("ty", "tx"), split_axis=1, concat_axis=1, tiled=True
        ).astype(F32)
        for part in pair
    )


def plain_gradient(tile, gains, observed, vis_weight):
    devices = lax.axis_size("ty") * lax.axis_size("tx")
    slab = lax.all_to_all(tile.astype(BF16), "tx", split_axis=0, concat_axis=1, tiled=True)
    moved = exchange_pair(along_last(slab.astype(F32), None, devices, -1.0))
    spectrum = across_groups(moved, devices, -1.0)
    spectrum = (spectrum[0] * (1.0 / N), spectrum[1] * (1.0 / N))
    model = complex_times((gains[0], gains[1]), spectrum)
    misfit = (vis_weight * (model[0] - observed[0]), vis_weight * (model[1] - observed[1]))
    back = complex_times((gains[0], -gains[1]), misfit)
    returned = exchange_pair(along_last(back[0], back[1], devices, 1.0))
    slab_grad = across_groups(returned, devices, 1.0)[0] * (1.0 / N)
    return lax.all_to_all(slab_grad.astype(BF16), "tx", split_axis=1, concat_axis=0, tiled=True)


def embed_complex(angle, row_axis, col_axis):
    cos, sin = np.cos(angle), np.sin(angle)
    top = np.stack([cos, sin], axis=col_axis)
    bottom = np.stack([-sin, cos], axis=col_axis)
    return np.stack([top, bottom], axis=row_axis)


def wheel(length, product):
    return 2.0 * math.pi / length * (product % length)


@functools.lru_cache(maxsize=None)
def row_constants():
    k = np.arange(TOK)
    angle = wheel(TOK, k[:, None] * k[None, :])
    first = np.concatenate([np.cos(angle), -np.sin(angle)], axis=1)
    b = np.repeat(np.arange(PATCH), PATCH)
    angle = wheel(N, b[:, None] * k[None, :])
    twist = np.stack([np.cos(angle), -np.sin(angle)])
    p = np.arange(PATCH)
    small = embed_complex(wheel(PATCH, p[:, None] * p[None, :]), 1, 1)
    second = np.einsum("kpqb,xy->kpxqby", small, np.eye(PATCH)).reshape(2 * PIXELS, 2 * PIXELS)
    return (
        first.astype(ml_dtypes.bfloat16),
        twist.astype(np.float32),
        second.astype(ml_dtypes.bfloat16),
        np.ascontiguousarray(second.T).astype(ml_dtypes.bfloat16),
    )


@functools.lru_cache(maxsize=None)
def half_constants():
    _, twist, second, _ = row_constants()
    half, quarter = TOK // 2, TOK // 4
    low = np.concatenate([1 + np.arange(quarter), 1 + half + np.arange(quarter)])
    digits = np.concatenate([low, low - 1])
    k = np.arange(TOK)
    angle = wheel(TOK, k[:, None] * digits[None, :])
    first = np.concatenate([np.cos(angle), -np.sin(angle)], axis=1)
    zero_line = np.concatenate([np.tile(np.eye(PATCH), PATCH), np.zeros((PATCH, PIXELS))], axis=1)
    upper = np.concatenate([second[PIXELS:].astype(np.float32), zero_line])
    lower = second[:PIXELS].astype(np.float32)
    return (first.astype(ml_dtypes.bfloat16), np.ascontiguousarray(twist[:, :, digits])) + tuple(
        np.ascontiguousarray(value).astype(ml_dtypes.bfloat16)
        for value in (lower, upper, lower.T, upper.T)
    )


@functools.lru_cache(maxsize=None)
def column_constants(devices, rows):
    s = np.arange(devices)
    small = embed_complex(wheel(devices, s[:, None] * s[None, :]), 1, 2)
    wide = devices * 2 * PATCH
    outer = np.einsum("qpsr,xy->qpxsry", small, np.eye(PATCH)).reshape(wide, wide)
    kr = s[:, None] + devices * np.arange(rows)[None, :]
    angle = wheel(N, kr[:, :, None] * np.arange(rows)[None, None, :])
    inner = embed_complex(angle, 1, 2).reshape(devices, 2 * rows, 2 * rows) / N
    return tuple(
        np.ascontiguousarray(value).astype(ml_dtypes.bfloat16)
        for value in (outer, outer.T, inner, inner.transpose(0, 2, 1))
    )


def row_forward(x_ref, first_ref, twist_ref, second_ref, out_ref):
    count = x_ref.shape[1]

    def step(i, carry):
        band = x_ref[:, i].reshape(TOK, PIXELS)
        mixed = mm(band, first_ref[...], TN)
        real, imag = mixed[:, :TOK], mixed[:, TOK:]
        tr, ti = twist_ref[0], twist_ref[1]
        turned = jnp.concatenate(
            [(real * tr - imag * ti).astype(BF16), (real * ti + imag * tr).astype(BF16)], axis=0
        )
        result = mm(second_ref[...], turned).astype(BF16).reshape(PATCH, 2, PATCH, TOK)
        half = TOK // 2
        rows = pl.ds(pl.multiple_of(i * PATCH, PATCH), PATCH)
        out_ref[:, 0, :, rows, :] = result[..., :half]
        out_ref[:, 1, :, rows, :] = result[..., half:]
        return carry

    lax.fori_loop(0, count, step, 0, unroll=4)


def row_inverse(v_ref, first_ref, twist_ref, second_ref, out_ref):
    parts, count, cols, _ = out_ref.shape

    def step(i, carry):
        rows = pl.ds(pl.multiple_of(i * PATCH, PATCH), PATCH)
        wide = jnp.concatenate(
            [
                v_ref[:, 0, :, rows, :].reshape(2 * PIXELS, TOK // 2),
                v_ref[:, 1, :, rows, :].reshape(2 * PIXELS, TOK // 2),
            ],
            axis=1,
        )
        mixed = mm(second_ref[...], wide)
        real, imag = mixed[:PIXELS], mixed[PIXELS:]
        tr, ti = twist_ref[0], twist_ref[1]
        turned = jnp.concatenate(
            [(real * tr + imag * ti).astype(BF16), (imag * tr - real * ti).astype(BF16)], axis=1
        )
        result = mm(first_ref[...], turned, NT).astype(BF16)
        out_ref[:, i] = result.reshape(parts, cols, PIXELS)
        return carry

    lax.fori_loop(0, count, step, 0, unroll=4)


def lane_index(shape):
    return lax.broadcasted_iota(jnp.int32, shape, len(shape) - 1)


def swap_halves(values):
    return pltpu.roll(values, values.shape[-1] // 2, len(values.shape) - 1)


def row_forward_half(x_ref, first_ref, twist_ref, lower_ref, upper_ref, out_ref):
    count = x_ref.shape[1]
    half = TOK // 2

    def packed(real, imag, rows, high):
        left = lane_index(real.shape) < half // 2
        out_ref[high, 0, rows, :] = jnp.where(left, real, swap_halves(imag)).astype(BF16)
        out_ref[high, 1, rows, :] = jnp.where(left, swap_halves(real), imag).astype(BF16)

    def step(i, carry):
        band = x_ref[:, i].reshape(TOK, PIXELS)
        mixed = mm(band, first_ref[...], TN)
        real, imag = mixed[:, :TOK], mixed[:, TOK:]
        tr, ti = twist_ref[0], twist_ref[1]
        turned = jnp.concatenate(
            [(real * tr - imag * ti).astype(BF16), (real * ti + imag * tr).astype(BF16)], axis=0
        )
        rows = pl.ds(pl.multiple_of(i * PATCH, PATCH), PATCH)
        lower = mm(lower_ref[...], turned[:, :half]).reshape(PATCH // 2, 2, PATCH, half)
        packed(lower[:, 0], lower[:, 1], rows, slice(0, PATCH // 2))
        upper = mm(upper_ref[...], turned[:, half:])
        line = upper[PIXELS:]
        upper = upper[:PIXELS].reshape(PATCH // 2, 2, PATCH, half)
        imag = upper[:, 1]
        head = jnp.where(lane_index(line.shape) == 0, line, imag[0])
        imag = jnp.concatenate([head[None], imag[1:]], axis=0)
        packed(upper[:, 0], imag, rows, slice(PATCH // 2, PATCH))
        return carry

    lax.fori_loop(0, count, step, 0, unroll=4)


def row_inverse_half(v_ref, first_ref, twist_ref, lower_ref, upper_ref, out_ref):
    parts, count, cols, _ = out_ref.shape
    half = TOK // 2

    def unpacked(rows, high):
        even = v_ref[high, 0, rows, :].astype(F32)
        odd = v_ref[high, 1, rows, :].astype(F32)
        left = lane_index(even.shape) < half // 2
        return jnp.where(left, even, swap_halves(odd)), jnp.where(left, swap_halves(even), odd)

    def step(i, carry):
        rows = pl.ds(pl.multiple_of(i * PATCH, PATCH), PATCH)
        real, imag = unpacked(rows, slice(0, PATCH // 2))
        lower = jnp.stack([real, imag], axis=1).reshape(PIXELS, half)
        real, imag = unpacked(rows, slice(PATCH // 2, PATCH))
        head = imag[0]
        at_zero = lane_index(head.shape) == 0
        nothing = jnp.zeros_like(head)
        imag = jnp.concatenate([jnp.where(at_zero, nothing, head)[None], imag[1:]], axis=0)
        upper = jnp.stack([real, imag], axis=1).reshape(PIXELS, half)
        upper = jnp.concatenate([upper, jnp.where(at_zero, head, nothing)], axis=0)
        mixed = jnp.concatenate(
            [mm(lower_ref[...], lower.astype(BF16)), mm(upper_ref[...], upper.astype(BF16))], axis=1
        )
        real, imag = mixed[:PIXELS], mixed[PIXELS:]
        tr, ti = twist_ref[0], twist_ref[1]
        turned = jnp.concatenate(
            [(real * tr + imag * ti).astype(BF16), (imag * tr - real * ti).astype(BF16)], axis=1
        )
        result = mm(first_ref[...], turned, NT).astype(BF16)
        out_ref[:, i] = result.reshape(parts, cols, PIXELS)
        return carry

    lax.fori_loop(0, count, step, 0, unroll=4)


def column_kernel(halved, *refs):
    if halved:
        flag_ref, phase_ref, refs = refs[0], refs[1], refs[2:]
    x_ref, outer_ref, *refs = refs
    count = 4 if halved else 5
    sources, out_ref = refs[:count], refs[count]
    mid_ref, *targets, sems = refs[count + 1 :]
    copies = [
        pltpu.make_async_copy(source, target, sems.at[n])
        for n, (source, target) in enumerate(zip(sources, targets))
    ]
    for copy in copies:
        copy.start()
    inner_ref, scale_ref, inner_t_ref, outer_t_ref = targets[:4]
    devices, _, rows, width = mid_ref.shape
    wide = devices * 2 * PATCH
    if halved:
        lane = lane_index((devices, PATCH, width))
        centre = flag_ref[0] == 1
        half = width // 2
        hidden = (lane == half) | (centre & (lane == 0))
        real_lane = (lane < half) | (centre & (lane == half))

    def load(group):
        place = slice(group * PATCH, (group + 1) * PATCH)
        if not halved:
            return x_ref[:, :, place, :].reshape(wide, width)
        piece = x_ref[:, place, :]
        other = swap_halves(piece.astype(F32))
        other = jnp.where(hidden, jnp.zeros_like(other), other).astype(BF16)
        return jnp.stack([piece, other], axis=1).reshape(wide, width)

    def store(group, value):
        place = slice(group * PATCH, (group + 1) * PATCH)
        value = value.reshape(devices, 2, PATCH, width)
        if halved:
            value = jnp.where(real_lane, value[:, 0], swap_halves(value[:, 1])).astype(BF16)
            out_ref[:, place, :] = value
        else:
            out_ref[:, :, place, :] = value.astype(BF16)

    for pair in range(0, rows // PATCH, 2):
        result = mm(outer_ref[...], jnp.concatenate([load(pair), load(pair + 1)], axis=1))
        result = result.astype(BF16)
        for n in range(2):
            place = slice((pair + n) * PATCH, (pair + n + 1) * PATCH)
            mid_ref[:, :, place, :] = result[:, n * width : (n + 1) * width].reshape(
                devices, 2, PATCH, width
            )

    for n, copy in enumerate(copies):
        if n != 3:
            copy.wait()

    def step(q, carry):
        spectrum = mm(inner_ref[q], mid_ref[q].reshape(2 * rows, width))
        real, imag = spectrum[:rows], spectrum[rows:]
        scale = scale_ref[q].astype(F32)
        if halved:
            pr, pi = phase_ref[q, 0], phase_ref[q, 1]
            real = real.reshape(rows // 8, 8, width)
            imag = imag.reshape(rows // 8, 8, width)
            real, imag = real * pr - imag * pi, real * pi + imag * pr
            real, imag = real.reshape(rows, width) * scale, imag.reshape(rows, width) * scale
        else:
            data_ref = targets[4]
            real = real * scale - data_ref[0, q].astype(F32)
            imag = imag * scale - data_ref[1, q].astype(F32)
        back = jnp.concatenate([real.astype(BF16), imag.astype(BF16)], axis=0)
        mid_ref[q] = mm(inner_t_ref[q], back).astype(BF16).reshape(2, rows, width)
        return carry

    lax.fori_loop(0, devices, step, 0, unroll=8)
    copies[3].wait()

    for pair in range(0, rows // PATCH, 2):
        both = jnp.concatenate(
            [
                mid_ref[:, :, n * PATCH : (n + 1) * PATCH, :].reshape(wide, width)
                for n in (pair, pair + 1)
            ],
            axis=1,
        )
        result = mm(outer_t_ref[...], both)
        store(pair, result[:, :width])
        store(pair + 1, result[:, width:])


def turned(value, devices):
    lines = value.shape[0]
    return value.astype(BF16).reshape(lines, N // devices, devices).transpose(2, 1, 0)


def spectrum_inputs(gains, observed, vis_weight, devices):
    gr, gi = gains[0], gains[1]
    weight = (vis_weight * (gr * gr + gi * gi)).astype(BF16)
    data = jnp.stack(
        [
            turned(vis_weight * (gr * observed[0] + gi * observed[1]), devices),
            turned(vis_weight * (gr * observed[1] - gi * observed[0]), devices),
        ]
    )
    return weight, turned(weight, devices), data


def mirror_kernel(scale_ref, got_ref, pick_ref, flip_ref, out_ref):
    devices = out_ref.shape[0]
    for q in range(devices):
        facing = mm(flip_ref[min(q, 1)], got_ref[(devices - q) % devices]).astype(BF16)
        total = mm(scale_ref[q], pick_ref[0]) + mm(facing, pick_ref[1])
        out_ref[q] = total.astype(BF16)


def mirrored_exchange(weight):
    devices = N // weight.shape[0]
    half, middle = weight.shape[0] // 2, devices // 2
    facing = [(e, devices - 1 - e) for e in range(devices)]
    partner = [(e, devices - e) for e in range(1, devices) if e != middle]
    partner = partner + [(0, middle), (middle, 0)]
    upper = lax.ppermute(weight[half:], ("ty", "tx"), facing)
    line = lax.ppermute(weight[:1], ("ty", "tx"), partner)
    return upper, line


def mirrored_weight(scale, upper, line):
    devices, slab, _ = scale.shape
    half, middle = slab // 2, devices // 2
    me = lax.axis_index(("ty", "tx"))
    got = jnp.concatenate([upper, jnp.broadcast_to(line, (half, N))], axis=0)
    source = lax.broadcasted_iota(jnp.int32, (slab, slab), 0)
    slot = lax.broadcasted_iota(jnp.int32, (slab, slab), 1)
    low = (me < middle).astype(jnp.int32)
    own = (slot < half) & (source == slot + low)
    other = (slot < half) & (source == half - low - slot)
    other = other & ((me != middle) | (slot > 0))
    other = other | ((me == middle) & (slot == half) & (source == half))
    picks = jnp.stack([own, other]).astype(BF16)
    q2 = np.arange(slab)
    flips = np.stack([q2[:, None] == (slab - q2) % slab, q2[:, None] == slab - 1 - q2])
    return pl.pallas_call(
        mirror_kernel,
        out_shape=jax.ShapeDtypeStruct(scale.shape, BF16),
        compiler_params=PARAMS,
    )(scale, turned(got, devices), picks, jnp.asarray(flips.astype(ml_dtypes.bfloat16)))


def row_matrix(shift):
    first = half_constants()[0]
    twice = jnp.asarray(np.concatenate([first, first[: 2 * WIN]], axis=0))
    return lax.dynamic_slice(twice, (shift, jnp.zeros((), jnp.int32)), first.shape)


def phase_table(shift, devices, width):
    kr = counting(devices)[:, None] + devices * counting(8)[None, :]
    angle = 2.0 * math.pi / TOK * (kr * shift % TOK).astype(F32)
    table = jnp.stack([jnp.cos(angle), -jnp.sin(angle)], axis=1)
    return jnp.broadcast_to(table[..., None], (devices, 2, 8, width))


def patch_gradient(state, scale, data, shift, mirror, beside):
    lanes = lax.axis_size("tx")
    devices = lax.axis_size("ty") * lanes
    rows, cols, _ = state.shape
    own = rows // lanes
    slab = N // devices
    halved = data is None
    outer, outer_t, inner, inner_t = (
        jnp.asarray(value) for value in column_constants(devices, slab)
    )
    if halved:
        first, twist, low, high, low_t, high_t = (jnp.asarray(value) for value in half_constants())
        part = (devices, slab, slab)
        onward = (row_forward_half, (row_matrix(shift[1]), twist, low, high))
        backward = (row_inverse_half, (first, twist, low_t, high_t))
        middle = lax.axis_index(("ty", "tx")) == devices // 2
    else:
        first, twist, second, second_t = (jnp.asarray(value) for value in row_constants())
        part = (devices, 2, slab, slab)
        onward = (row_forward, (first, twist, second))
        backward = (row_inverse, (first, twist, second_t))
        extra = ()
        away = (inner, scale, inner_t, outer_t, data)
    split = (PATCH, devices // PATCH) + part[1:]
    gathered = lax.all_to_all(
        state.reshape(lanes, own, cols, PIXELS), "tx", split_axis=0, concat_axis=0, tiled=True
    )
    sent = pl.pallas_call(
        onward[0], out_shape=jax.ShapeDtypeStruct(split, BF16), compiler_params=PARAMS
    )(gathered, *onward[1])
    if halved:
        sent, mirror, shift = lax.optimization_barrier((sent, mirror, shift))
        extra = (middle.astype(jnp.int32).reshape(1), phase_table(shift[0], devices, slab))
        away = (inner, mirrored_weight(scale, *mirror), inner_t, outer_t)
    moved = lax.all_to_all(
        sent.reshape(part), ("ty", "tx"), split_axis=0, concat_axis=0, tiled=True
    )
    spaces = [pltpu.SMEM, pltpu.VMEM][: len(extra)] + [pltpu.VMEM] * 2 + [pl.ANY] * len(away)
    wave = pl.pallas_call(
        functools.partial(column_kernel, halved),
        in_specs=[pl.BlockSpec(memory_space=space) for space in spaces],
        out_shape=jax.ShapeDtypeStruct(part, BF16),
        scratch_shapes=[pltpu.VMEM((devices, 2, slab, slab), BF16)]
        + [pltpu.VMEM(value.shape, BF16) for value in away]
        + [pltpu.SemaphoreType.DMA((len(away),))],
        compiler_params=PARAMS,
    )(*extra, moved, outer, *away)
    returned = lax.all_to_all(wave, ("ty", "tx"), split_axis=0, concat_axis=0, tiled=True)
    returned, beside = lax.optimization_barrier((returned, beside))
    slabs = pl.pallas_call(
        backward[0],
        out_shape=jax.ShapeDtypeStruct((lanes, own, cols, PIXELS), BF16),
        compiler_params=PARAMS,
    )(returned.reshape(split), *backward[1])
    grad = lax.all_to_all(slabs, "tx", split_axis=0, concat_axis=0, tiled=True)
    return grad.reshape(rows, cols, PIXELS), beside


def layer_norm(values, gain):
    centre = jnp.mean(values, axis=-1, keepdims=True)
    shifted = values - centre
    spread = jnp.mean(shifted * shifted, axis=-1, keepdims=True)
    return (shifted * lax.rsqrt(spread + EPSILON) * gain).astype(BF16)


def to_windows(band):
    rows, cols, feats = band.shape
    pieces = [
        band[:, w * WIN : (w + 1) * WIN, :].reshape(SPAN, feats) for w in range(cols // WIN)
    ]
    return jnp.concatenate(pieces, axis=0)


def from_windows(tokens, cols):
    feats = tokens.shape[-1]
    pieces = [
        tokens[w * SPAN : (w + 1) * SPAN].reshape(WIN, WIN, feats) for w in range(cols // WIN)
    ]
    return jnp.concatenate(pieces, axis=1)


def swin_band(
    flow, bias_ref, qkv_ref, proj_ref, up_ref, down_ref, gain_ref, mixed_ref, score_ref, prob_ref
):
    count = flow.shape[0] // SPAN
    pairs = HEADS // 2
    depth = D // HEADS
    wide = 2 * depth
    normed = layer_norm(flow, gain_ref[0:1, :])
    scale = 1.0 / math.sqrt(depth)
    mixed_ref[:, :D] = (mm(normed, qkv_ref[:, :D]) * scale).astype(BF16)
    mixed_ref[:, D : 2 * D] = mm(normed, qkv_ref[:, D : 2 * D]).astype(BF16)
    mixed_ref[:, 2 * D :] = mm(normed, qkv_ref[:, 2 * D :]).astype(BF16)
    lower = lax.broadcasted_iota(jnp.int32, (SPAN, wide), 1) < depth
    for w in range(count):
        rows = slice(w * SPAN, (w + 1) * SPAN)
        for p in range(pairs):
            query = mixed_ref[rows, p * wide : (p + 1) * wide]
            key = mixed_ref[rows, D + p * wide : D + (p + 1) * wide]
            zero = jnp.zeros_like(query)
            split = jnp.concatenate(
                [jnp.where(lower, query, zero), jnp.where(lower, zero, query)], axis=0
            )
            score_ref[w, :, p * wide : (p + 1) * wide] = mm(key, split, NT)
    for w in range(count):
        bias = bias_ref[w]
        for p in range(pairs):
            lanes = slice(p * wide, (p + 1) * wide)
            scores = score_ref[w, :, lanes] + bias
            weights = jnp.exp(scores - jnp.max(scores, axis=0, keepdims=True))
            share = 1.0 / jnp.sum(weights, axis=0, keepdims=True)
            prob_ref[w, :, lanes] = (weights * share).astype(BF16)
    for w in range(count):
        rows = slice(w * SPAN, (w + 1) * SPAN)
        for p in range(pairs):
            lanes = slice(p * wide, (p + 1) * wide)
            value = mixed_ref[rows, 2 * D + p * wide : 2 * D + (p + 1) * wide]
            mixture = mm(prob_ref[w, :, lanes], value, TN)
            mixed_ref[rows, lanes] = jnp.where(lower, mixture[:SPAN], mixture[SPAN:]).astype(BF16)
    flow = flow + mm(mixed_ref[:, :D], proj_ref[...])
    normed = layer_norm(flow, gain_ref[1:2, :])
    chunks = up_ref.shape[1] // D
    total = jnp.zeros_like(flow)
    ahead = mm(normed, up_ref[:, :D])
    for c in range(chunks):
        value = ahead
        if c + 1 < chunks:
            ahead = mm(normed, up_ref[:, (c + 1) * D : (c + 2) * D])
        inside = value * (GELU_IN + GELU_CUBE * (value * value))
        active = (value + value * jnp.tanh(inside)).astype(BF16)
        total = total + mm(active, down_ref[c * D : (c + 1) * D, :])
    return flow + 0.5 * total


def rolled_band(sign, shift_ref, refs, rows):
    main_ref, side_ref, edge_ref, corner_ref = refs
    cols = main_ref.shape[1]
    top = pl.program_id(0) * WIN + sign * shift_ref[0]
    behind = -rows if sign > 0 else WIN
    beside = -cols if sign > 0 else WIN

    def pick(width, offset):
        source = lax.broadcasted_iota(jnp.int32, (cols, width), 1)
        wanted = lax.broadcasted_iota(jnp.int32, (cols, width), 0) + sign * shift_ref[1] + offset
        return jnp.where(source == wanted, 1.0, 0.0).astype(BF16)

    pick_main, pick_side = pick(cols, 0), pick(WIN, beside)
    band = []
    for j in range(WIN):
        row = top + j
        inside = (row >= 0) & (row < rows)
        here, there = jnp.clip(row, 0, rows - 1), jnp.clip(row + behind, 0, WIN - 1)
        main = jnp.where(inside, main_ref[here], edge_ref[there])
        side = jnp.where(inside, side_ref[here], corner_ref[there])
        band.append(mm(pick_main, main) + mm(pick_side, side))
    return jnp.stack(band)


def first_kernel(zeta, sigma, count, rows, before, *refs):
    shift_ref, state_ref, *refs = refs
    state = state_ref[...]
    if before is not None:
        state = state - before * rolled_band(-1, shift_ref, refs[:4], rows)
        refs = refs[4:]
    grad_refs, refs = refs[:count], refs[count:]
    if sigma is not None:
        noise_ref, *refs = refs
    bias_ref, embed_ref, qkv_ref, proj_ref, up_ref, down_ref, gain_ref = refs[:7]
    base_ref, out_ref, side_ref, edge_ref, corner_ref, *scratch = refs[7:]
    step = zeta * sum(grad_ref[...].astype(F32) for grad_ref in grad_refs)
    half = state - step
    tokens = mm(to_windows(half).astype(BF16), embed_ref[...]).astype(BF16).astype(F32)
    flow = swin_band(tokens, bias_ref, qkv_ref, proj_ref, up_ref, down_ref, gain_ref, *scratch)
    result = from_windows(flow, half.shape[1]).astype(BF16)
    out_ref[:, :, :D] = result
    side_ref[:, :, :D] = result[:, :WIN]
    if sigma is None:
        base_ref[...] = half
    else:
        noise = sigma * noise_ref[...]
        base_ref[...] = half + noise
        change = (noise - step).astype(BF16)
        out_ref[:, :, D:] = change
        side_ref[:, :, D:] = change[:, :WIN]

    @pl.when(pl.program_id(0) == 0)
    def _():
        edge_ref[...] = out_ref[...]
        corner_ref[...] = side_ref[...]


def second_kernel(sigma, rows, *refs):
    shift_ref, *refs = refs
    tile_refs, refs = refs[:4], refs[4:]
    bias_ref, qkv_ref, proj_ref, up_ref, down_ref, gain_ref, unembed_ref = refs[:7]
    out_ref, side_ref, edge_ref, corner_ref, *scratch = refs[7:]
    if sigma is not None:
        state_ref, *scratch = scratch
    cols = out_ref.shape[1]
    band = rolled_band(1, shift_ref, tile_refs, rows)
    tokens = to_windows(band[:, :, :D])
    flow = swin_band(tokens, bias_ref, qkv_ref, proj_ref, up_ref, down_ref, gain_ref, *scratch)
    estimate = from_windows(mm(flow.astype(BF16), unembed_ref[...]), cols)
    narrow = estimate.astype(BF16)
    out_ref[...] = narrow
    edge_ref[...] = narrow
    side_ref[...] = narrow[:, cols - WIN :]
    corner_ref[...] = narrow[:, cols - WIN :]
    if sigma is not None:
        state_ref[...] = (band[:, :, D:] - sigma * estimate).astype(BF16)


def whole(array):
    zeros = (0,) * array.ndim
    return pl.BlockSpec(array.shape, lambda *_: zeros)


def band_of(step, cols):
    return pl.BlockSpec((step, cols, PIXELS), lambda n, *_: (n, 0, 0))


def member(array, j):
    place = (j,) + (0,) * (array.ndim - 1)
    return pl.BlockSpec((None,) + array.shape[1:], lambda *_: place)


def band_spec(cols, feats):
    return pl.BlockSpec((WIN, cols, feats), lambda n, *_: (n, 0, 0))


def bias_spec(cols):
    return pl.BlockSpec((cols // WIN, SPAN, 2 * SPAN), lambda n, *_: (n, 0, 0))


def band_scratch(cols):
    count = cols // WIN
    return [
        pltpu.VMEM((WIN * cols, 3 * D), BF16),
        pltpu.VMEM((count, SPAN, HEADS * SPAN), F32),
        pltpu.VMEM((count, SPAN, HEADS * SPAN), BF16),
    ]


def strip_outs(rows, cols, feats):
    specs = [band_spec(cols, feats), band_spec(WIN, feats)]
    specs += [
        pl.BlockSpec((WIN, width, feats), lambda *_: (0, 0, 0)) for width in (cols, WIN)
    ]
    shapes = [(rows, cols), (rows, WIN), (WIN, cols), (WIN, WIN)]
    return specs, [jax.ShapeDtypeStruct(shape + (feats,), BF16) for shape in shapes]


def first_block(zeta, sigma, state, before, shift, back, grads, noise, bias, w_embed, weights):
    rows, cols, _ = state.shape
    fields = [*grads] + ([] if sigma is None else [noise])
    feats = D if sigma is None else D + PIXELS
    specs, shapes = strip_outs(rows, cols, feats)
    return pl.pallas_call(
        functools.partial(first_kernel, zeta, sigma, len(grads), rows, before),
        grid_spec=pltpu.PrefetchScalarGridSpec(
            num_scalar_prefetch=1,
            grid=(rows // WIN,),
            in_specs=[band_spec(cols, PIXELS)]
            + [whole(value) for value in back]
            + [band_spec(cols, PIXELS)] * len(fields)
            + [bias_spec(cols), whole(w_embed)]
            + [member(value, 0) for value in weights],
            out_specs=[band_spec(cols, PIXELS)] + specs,
            scratch_shapes=band_scratch(cols),
        ),
        out_shape=[jax.ShapeDtypeStruct((rows, cols, PIXELS), F32)] + shapes,
        compiler_params=PARAMS,
    )(shift, state, *back, *fields, bias, w_embed, *weights)


def second_block(sigma, shift, tile, bias, w_unembed, weights):
    rows, cols, _ = tile[0].shape
    specs, shapes = strip_outs(rows, cols, PIXELS)
    if sigma is not None:
        specs, shapes = specs + specs[:1], shapes + shapes[:1]
    return pl.pallas_call(
        functools.partial(second_kernel, sigma, rows),
        grid_spec=pltpu.PrefetchScalarGridSpec(
            num_scalar_prefetch=1,
            grid=(rows // WIN,),
            in_specs=[whole(value) for value in tile]
            + [bias_spec(cols)]
            + [member(value, 1) for value in weights]
            + [whole(w_unembed)],
            out_specs=specs,
            scratch_shapes=band_scratch(cols),
        ),
        out_shape=shapes,
        compiler_params=PARAMS,
    )(shift, *tile, bias, *weights, w_unembed)


def from_neighbours(tile, by):
    main, side, edge, corner = tile
    ty, tx = lax.axis_size("ty"), lax.axis_size("tx")
    across = [
        (i * tx + k, (i + by) % ty * tx + (k + by) % tx) for i in range(ty) for k in range(tx)
    ]
    return (
        main,
        lax.ppermute(side, "tx", [(k, (k + by) % tx) for k in range(tx)]),
        lax.ppermute(edge, "ty", [(i, (i + by) % ty) for i in range(ty)]),
        lax.ppermute(corner, ("ty", "tx"), across),
    )


def windows_of(grid):
    rows, cols = grid.shape
    shaped = grid.reshape(rows // WIN, WIN, cols // WIN, WIN).transpose(0, 2, 1, 3)
    return shaped.reshape(rows // WIN * (cols // WIN), SPAN)


def bias_of(labels, keep):
    allowed = jnp.ones((1, SPAN, SPAN), bool)
    if labels is not None:
        label = windows_of(labels)
        allowed = label[:, :, None] == label[:, None, :]
    if keep is not None:
        kept = windows_of(keep)[:, :, None] == 1
        allowed = allowed & (kept | jnp.eye(SPAN, dtype=bool)[None])
    bias = jnp.where(allowed, 0.0, -1e30).astype(F32)
    return jnp.concatenate([bias, bias], axis=2)


def region(index, shift):
    return jnp.where(index < TOK - WIN, 0, jnp.where(index < TOK - shift, 1, 2)).astype(jnp.int32)


@functools.lru_cache(maxsize=None)
def lane_order(cols):
    parts = LANES // cols
    groups = PATCH // parts
    lane = np.arange(PATCH * cols)
    g, h, k = lane // LANES, lane % LANES // cols, lane % cols
    source = PATCH * k + h * groups + g
    matrix = np.zeros((PATCH * cols, PATCH * cols), np.float32)
    matrix[source, lane] = 1.0
    return matrix.astype(ml_dtypes.bfloat16), np.ascontiguousarray(matrix.T).astype(
        ml_dtypes.bfloat16
    )


def move_lanes(values, matrix):
    high = values.astype(BF16)
    low = (values - high.astype(F32)).astype(BF16)
    return mm(high, matrix) + mm(low, matrix)


def to_patches_kernel(tile_ref, order_ref, out_ref):
    count, cols, _ = out_ref.shape
    parts = LANES // cols
    groups = PATCH // parts
    if out_ref.dtype == BF16:
        ordered = mm(tile_ref[...].astype(BF16), order_ref[...])
    else:
        ordered = move_lanes(tile_ref[...], order_ref[...])
    for i in range(count):
        band = ordered[i * PATCH : (i + 1) * PATCH]
        stacked = jnp.concatenate(
            [band[:, g * LANES : (g + 1) * LANES] for g in range(groups)], axis=0
        )
        turned = stacked.T
        patch = jnp.concatenate([turned[h * cols : (h + 1) * cols] for h in range(parts)], axis=1)
        out_ref[i] = patch.astype(out_ref.dtype)


def to_tile_kernel(sigma, scale, rows, *refs):
    shift_ref, base_ref, *refs = refs
    noise_ref, order_ref, out_ref = refs[4:]
    count, cols, _ = base_ref.shape
    parts = LANES // cols
    groups = PATCH // parts
    width = groups * PATCH
    state = base_ref[...] - sigma * rolled_band(-1, shift_ref, refs[:4], rows)
    bands = []
    for i in range(count):
        stacked = jnp.concatenate(
            [state[i, :, h * width : (h + 1) * width] for h in range(parts)], axis=0
        )
        turned = stacked.T
        bands.append(
            jnp.concatenate([turned[g * PATCH : (g + 1) * PATCH] for g in range(groups)], axis=1)
        )
    moved = move_lanes(jnp.concatenate(bands, axis=0), order_ref[...])
    out_ref[...] = moved + scale * noise_ref[...]


def patches_of(tiles, j, kind=F32):
    rows, cols = tiles.shape[1] // PATCH, tiles.shape[2] // PATCH
    order = jnp.asarray(lane_order(cols)[0])
    step = rows // 4
    return pl.pallas_call(
        to_patches_kernel,
        grid=(rows // step,),
        in_specs=[
            pl.BlockSpec((None, step * PATCH, cols * PATCH), lambda n: (j, n, 0)),
            whole(order),
        ],
        out_specs=band_of(step, cols),
        out_shape=jax.ShapeDtypeStruct((rows, cols, PIXELS), kind),
        compiler_params=PARAMS,
    )(tiles, order)


def tile_of(base, sigma, shift, back, scale, noise, j):
    rows, cols, _ = base.shape
    order = jnp.asarray(lane_order(cols)[1])
    return pl.pallas_call(
        functools.partial(to_tile_kernel, sigma, scale, rows),
        grid_spec=pltpu.PrefetchScalarGridSpec(
            num_scalar_prefetch=1,
            grid=(rows // WIN,),
            in_specs=[band_spec(cols, PIXELS)]
            + [whole(value) for value in back]
            + [
                pl.BlockSpec((None, WIN * PATCH, cols * PATCH), lambda n, *_: (j, n, 0)),
                whole(order),
            ],
            out_specs=pl.BlockSpec((WIN * PATCH, cols * PATCH), lambda n, *_: (n, 0)),
        ),
        out_shape=jax.ShapeDtypeStruct((rows * PATCH, cols * PATCH), F32),
        compiler_params=PARAMS,
    )(shift, base, *back, noise, order)


def per_device(
    image, noise, offsets, key_mask, gains, observed, vis_weight,
    w_embed, w_qkv, w_proj, w_up, w_down, w_unembed, norm_gains,
):
    rows = image.shape[0] // PATCH
    cols = image.shape[1] // PATCH
    devices = lax.axis_size("ty") * lax.axis_size("tx")
    fast = N // devices == TOK // 2
    row_index = lax.axis_index("ty") * rows + counting(rows)
    col_index = lax.axis_index("tx") * cols + counting(cols)
    weights = (w_qkv, w_proj, w_up, w_down, norm_gains)
    w_embed = w_embed.reshape(PATCH, PATCH, D).transpose(1, 0, 2).reshape(PIXELS, D)
    w_unembed = w_unembed.reshape(D, PATCH, PATCH).transpose(0, 2, 1).reshape(D, PIXELS)
    state = patches_of(image[None], 0)
    extras = [patches_of(noise, step) for step in range(STEPS - 1)] + [None]
    first_bias = bias_of(None, key_mask)
    biases = []
    for step in range(STEPS):
        labels = (
            3 * region(row_index, offsets[step, 0])[:, None]
            + region(col_index, offsets[step, 1])[None, :]
        )
        biases.append(bias_of(labels, None))
    beside = (state, extras, first_bias, biases, w_embed, w_unembed)
    shift, before, back, moving, mirror = offsets[0], None, (), None, None
    grads = []
    if fast:
        weight, scale, data = spectrum_inputs(gains, observed, vis_weight, devices)
        grad, beside = patch_gradient(
            patches_of(image[None], 0, BF16), scale, data, None, None, beside
        )
        grads = [grad]
        state, extras, first_bias, biases, w_embed, w_unembed = beside
    for step in range(STEPS):
        if not fast:
            tile = image if step == 0 else tile_of(state, before, shift, back, 0.0, noise, 0)
            grad = plain_gradient(tile, gains, observed, vis_weight)
            grads = [patches_of(grad.astype(F32)[None], 0, BF16)]
        elif step > 0:
            grads = grads + [patch_gradient(moving, scale, None, shift, mirror, ())[0]]
        last = step + 1 == STEPS
        sigma = None if last else SIGMAS[step + 1]
        state, *first = first_block(
            STEP_SIZES[step], sigma, state, before, shift, back, grads, extras[step], first_bias,
            w_embed, weights,
        )
        shift, before = offsets[step], SIGMAS[step]
        first = from_neighbours(first, -1)
        if fast and step == 0:
            first, weight = lax.optimization_barrier((first, weight))
            mirror = mirrored_exchange(weight)
        rolled = second_block(
            None if last else before, shift, first, biases[step], w_unembed, weights
        )
        if not last:
            *rolled, moving = rolled
        if fast and step == 0:
            moving, mirror = lax.optimization_barrier((moving, mirror))
        back = from_neighbours(rolled, 1)
    return tile_of(state, before, shift, back, SIGMAS[STEPS], noise, STEPS - 1)


def solution(mesh):
    in_specs = (
        P("ty", "tx"),
        P(None, "ty", "tx"),
        P(),
        P("ty", "tx"),
        P(None, ("ty", "tx"), None),
        P(None, ("ty", "tx"), None),
        P(("ty", "tx"), None),
        P(),
        P(),
        P(),
        P(),
        P(),
        P(),
        P(),
    )
    out_specs = P("ty", "tx")
    return jax.shard_map(
        per_device, mesh=mesh, in_specs=in_specs, out_specs=out_specs, check_vma=False
    )
```

```python
import functools
import math

import jax
import jax.numpy as jnp
import ml_dtypes
import numpy as np
from jax import lax
from jax.experimental import pallas as pl
from jax.experimental.pallas import tpu as pltpu
from jax.sharding import PartitionSpec as P

N = 4096
PATCH = 16
PIXELS = PATCH * PATCH
WIN = 8
D = 512
HEADS = 8
STEPS = 2
SPAN = WIN * WIN
LANES = 128
TOK = N // PATCH

SIGMAS = (0.8, 0.5, 0.3)
STEP_SIZES = (0.9, 0.7)
EPSILON = 1e-05
HIGHEST = lax.Precision.HIGHEST
BF16 = jnp.bfloat16
F32 = jnp.float32
GELU_IN = math.sqrt(2.0 / math.pi)
GELU_CUBE = 0.044715 * GELU_IN
VMEM_LIMIT = 56 * 1024 * 1024
PARAMS = pltpu.CompilerParams(vmem_limit_bytes=VMEM_LIMIT)
TN = (((0,), (0,)), ((), ()))
NT = (((1,), (1,)), ((), ()))
NN = (((1,), (0,)), ((), ()))


def mm(left, right, dims=NN):
    return lax.dot_general(left, right, dims, preferred_element_type=F32)


def counting(length):
    return jnp.arange(length, dtype=jnp.int32)


def roots(length, outer, inner, sign):
    product = outer[:, None] * inner[None, :] % length
    angle = 2.0 * math.pi / length * product.astype(F32)
    return (jnp.cos(angle), sign * jnp.sin(angle))


def complex_einsum(form, left, right):
    real = jnp.einsum(form, left[0], right[0], precision=HIGHEST) - jnp.einsum(
        form, left[1], right[1], precision=HIGHEST
    )
    imag = jnp.einsum(form, left[0], right[1], precision=HIGHEST) + jnp.einsum(
        form, left[1], right[0], precision=HIGHEST
    )
    return (real, imag)


def complex_times(left, right):
    return (left[0] * right[0] - left[1] * right[1], left[0] * right[1] + left[1] * right[0])


def along_last(real_part, imag_part, groups, sign):
    rows, length = real_part.shape
    inner = length // groups
    first = roots(groups, counting(groups), counting(groups), sign)
    twist = roots(length, counting(inner), counting(groups), sign)
    second = roots(inner, counting(inner), counting(inner), sign)
    shaped = real_part.reshape(rows, groups, inner)
    if imag_part is None:
        partial_value = (
            jnp.einsum("mab,ka->mbk", shaped, first[0], precision=HIGHEST),
            jnp.einsum("mab,ka->mbk", shaped, first[1], precision=HIGHEST),
        )
    else:
        partial_value = complex_einsum(
            "mab,ka->mbk", (shaped, imag_part.reshape(rows, groups, inner)), first
        )
    partial_value = complex_times(partial_value, twist)
    result = complex_einsum("jb,mbk->mjk", second, partial_value)
    return (result[0].reshape(rows, length), result[1].reshape(rows, length))


def across_groups(pair, groups, sign):
    inner, cols = pair[0].shape
    width = cols // groups
    length = groups * inner
    first = roots(groups, counting(groups), counting(groups), sign)
    twist = roots(length, counting(inner), counting(groups), sign)
    second = roots(inner, counting(inner), counting(inner), sign)
    shaped = (pair[0].reshape(inner, groups, width), pair[1].reshape(inner, groups, width))
    partial_value = complex_einsum("bhc,kh->cbk", shaped, first)
    partial_value = complex_times(partial_value, twist)
    result = complex_einsum("jb,cbk->cjk", second, partial_value)
    return (result[0].reshape(width, length), result[1].reshape(width, length))


def exchange_pair(pair):
    return tuple(
        lax.all_to_all(
            part.astype(BF16), ("ty", "tx"), split_axis=1, concat_axis=1, tiled=True
        ).astype(F32)
        for part in pair
    )


def plain_gradient(tile, gains, observed, vis_weight):
    devices = lax.axis_size("ty") * lax.axis_size("tx")
    slab = lax.all_to_all(tile.astype(BF16), "tx", split_axis=0, concat_axis=1, tiled=True)
    moved = exchange_pair(along_last(slab.astype(F32), None, devices, -1.0))
    spectrum = across_groups(moved, devices, -1.0)
    spectrum = (spectrum[0] * (1.0 / N), spectrum[1] * (1.0 / N))
    model = complex_times((gains[0], gains[1]), spectrum)
    misfit = (vis_weight * (model[0] - observed[0]), vis_weight * (model[1] - observed[1]))
    back = complex_times((gains[0], -gains[1]), misfit)
    returned = exchange_pair(along_last(back[0], back[1], devices, 1.0))
    slab_grad = across_groups(returned, devices, 1.0)[0] * (1.0 / N)
    return lax.all_to_all(slab_grad.astype(BF16), "tx", split_axis=1, concat_axis=0, tiled=True)


def embed_complex(angle, row_axis, col_axis):
    cos, sin = np.cos(angle), np.sin(angle)
    top = np.stack([cos, sin], axis=col_axis)
    bottom = np.stack([-sin, cos], axis=col_axis)
    return np.stack([top, bottom], axis=row_axis)


def wheel(length, product):
    return 2.0 * math.pi / length * (product % length)


@functools.lru_cache(maxsize=None)
def row_constants():
    k = np.arange(TOK)
    angle = wheel(TOK, k[:, None] * k[None, :])
    first = np.concatenate([np.cos(angle), -np.sin(angle)], axis=1)
    b = np.repeat(np.arange(PATCH), PATCH)
    angle = wheel(N, b[:, None] * k[None, :])
    twist = np.stack([np.cos(angle), -np.sin(angle)])
    p = np.arange(PATCH)
    small = embed_complex(wheel(PATCH, p[:, None] * p[None, :]), 1, 1)
    second = np.einsum("kpqb,xy->kpxqby", small, np.eye(PATCH)).reshape(2 * PIXELS, 2 * PIXELS)
    return (
        first.astype(ml_dtypes.bfloat16),
        twist.astype(np.float32),
        second.astype(ml_dtypes.bfloat16),
        np.ascontiguousarray(second.T).astype(ml_dtypes.bfloat16),
    )


@functools.lru_cache(maxsize=None)
def half_constants():
    _, twist, second, _ = row_constants()
    half, quarter = TOK // 2, TOK // 4
    low = np.concatenate([1 + np.arange(quarter), 1 + half + np.arange(quarter)])
    digits = np.concatenate([low, low - 1])
    k = np.arange(TOK)
    angle = wheel(TOK, k[:, None] * digits[None, :])
    first = np.concatenate([np.cos(angle), -np.sin(angle)], axis=1)
    zero_line = np.concatenate([np.tile(np.eye(PATCH), PATCH), np.zeros((PATCH, PIXELS))], axis=1)
    upper = np.concatenate([second[PIXELS:].astype(np.float32), zero_line])
    lower = second[:PIXELS].astype(np.float32)
    return (first.astype(ml_dtypes.bfloat16), np.ascontiguousarray(twist[:, :, digits])) + tuple(
        np.ascontiguousarray(value).astype(ml_dtypes.bfloat16)
        for value in (lower, upper, lower.T, upper.T)
    )


@functools.lru_cache(maxsize=None)
def column_constants(devices, rows):
    s = np.arange(devices)
    small = embed_complex(wheel(devices, s[:, None] * s[None, :]), 1, 2)
    wide = devices * 2 * PATCH
    outer = np.einsum("qpsr,xy->qpxsry", small, np.eye(PATCH)).reshape(wide, wide)
    kr = s[:, None] + devices * np.arange(rows)[None, :]
    angle = wheel(N, kr[:, :, None] * np.arange(rows)[None, None, :])
    inner = embed_complex(angle, 1, 2).reshape(devices, 2 * rows, 2 * rows) / N
    return tuple(
        np.ascontiguousarray(value).astype(ml_dtypes.bfloat16)
        for value in (outer, outer.T, inner, inner.transpose(0, 2, 1))
    )


def row_forward(x_ref, first_ref, twist_ref, second_ref, out_ref):
    count = x_ref.shape[1]

    def step(i, carry):
        band = x_ref[:, i].reshape(TOK, PIXELS)
        mixed = mm(band, first_ref[...], TN)
        real, imag = mixed[:, :TOK], mixed[:, TOK:]
        tr, ti = twist_ref[0], twist_ref[1]
        turned = jnp.concatenate(
            [(real * tr - imag * ti).astype(BF16), (real * ti + imag * tr).astype(BF16)], axis=0
        )
        result = mm(second_ref[...], turned).astype(BF16).reshape(PATCH, 2, PATCH, TOK)
        half = TOK // 2
        rows = pl.ds(pl.multiple_of(i * PATCH, PATCH), PATCH)
        out_ref[:, 0, :, rows, :] = result[..., :half]
        out_ref[:, 1, :, rows, :] = result[..., half:]
        return carry

    lax.fori_loop(0, count, step, 0, unroll=4)


def row_inverse(v_ref, first_ref, twist_ref, second_ref, out_ref):
    parts, count, cols, _ = out_ref.shape

    def step(i, carry):
        rows = pl.ds(pl.multiple_of(i * PATCH, PATCH), PATCH)
        wide = jnp.concatenate(
            [
                v_ref[:, 0, :, rows, :].reshape(2 * PIXELS, TOK // 2),
                v_ref[:, 1, :, rows, :].reshape(2 * PIXELS, TOK // 2),
            ],
            axis=1,
        )
        mixed = mm(second_ref[...], wide)
        real, imag = mixed[:PIXELS], mixed[PIXELS:]
        tr, ti = twist_ref[0], twist_ref[1]
        turned = jnp.concatenate(
            [(real * tr + imag * ti).astype(BF16), (imag * tr - real * ti).astype(BF16)], axis=1
        )
        result = mm(first_ref[...], turned, NT).astype(BF16)
        out_ref[:, i] = result.reshape(parts, cols, PIXELS)
        return carry

    lax.fori_loop(0, count, step, 0, unroll=4)


def lane_index(shape):
    return lax.broadcasted_iota(jnp.int32, shape, len(shape) - 1)


def swap_halves(values):
    return pltpu.roll(values, values.shape[-1] // 2, len(values.shape) - 1)


def row_forward_half(x_ref, first_ref, twist_ref, lower_ref, upper_ref, out_ref):
    count = x_ref.shape[1]
    half = TOK // 2

    def packed(real, imag, rows, high):
        left = lane_index(real.shape) < half // 2
        out_ref[high, 0, rows, :] = jnp.where(left, real, swap_halves(imag)).astype(BF16)
        out_ref[high, 1, rows, :] = jnp.where(left, swap_halves(real), imag).astype(BF16)

    def step(i, carry):
        band = x_ref[:, i].reshape(TOK, PIXELS)
        mixed = mm(band, first_ref[...], TN)
        real, imag = mixed[:, :TOK], mixed[:, TOK:]
        tr, ti = twist_ref[0], twist_ref[1]
        turned = jnp.concatenate(
            [(real * tr - imag * ti).astype(BF16), (real * ti + imag * tr).astype(BF16)], axis=0
        )
        rows = pl.ds(pl.multiple_of(i * PATCH, PATCH), PATCH)
        lower = mm(lower_ref[...], turned[:, :half]).reshape(PATCH // 2, 2, PATCH, half)
        packed(lower[:, 0], lower[:, 1], rows, slice(0, PATCH // 2))
        upper = mm(upper_ref[...], turned[:, half:])
        line = upper[PIXELS:]
        upper = upper[:PIXELS].reshape(PATCH // 2, 2, PATCH, half)
        imag = upper[:, 1]
        head = jnp.where(lane_index(line.shape) == 0, line, imag[0])
        imag = jnp.concatenate([head[None], imag[1:]], axis=0)
        packed(upper[:, 0], imag, rows, slice(PATCH // 2, PATCH))
        return carry

    lax.fori_loop(0, count, step, 0, unroll=4)


def row_inverse_half(v_ref, first_ref, twist_ref, lower_ref, upper_ref, out_ref):
    parts, count, cols, _ = out_ref.shape
    half = TOK // 2

    def unpacked(rows, high):
        even = v_ref[high, 0, rows, :].astype(F32)
        odd = v_ref[high, 1, rows, :].astype(F32)
        left = lane_index(even.shape) < half // 2
        return jnp.where(left, even, swap_halves(odd)), jnp.where(left, swap_halves(even), odd)

    def step(i, carry):
        rows = pl.ds(pl.multiple_of(i * PATCH, PATCH), PATCH)
        real, imag = unpacked(rows, slice(0, PATCH // 2))
        lower = jnp.stack([real, imag], axis=1).reshape(PIXELS, half)
        real, imag = unpacked(rows, slice(PATCH // 2, PATCH))
        head = imag[0]
        at_zero = lane_index(head.shape) == 0
        nothing = jnp.zeros_like(head)
        imag = jnp.concatenate([jnp.where(at_zero, nothing, head)[None], imag[1:]], axis=0)
        upper = jnp.stack([real, imag], axis=1).reshape(PIXELS, half)
        upper = jnp.concatenate([upper, jnp.where(at_zero, head, nothing)], axis=0)
        mixed = jnp.concatenate(
            [mm(lower_ref[...], lower.astype(BF16)), mm(upper_ref[...], upper.astype(BF16))], axis=1
        )
        real, imag = mixed[:PIXELS], mixed[PIXELS:]
        tr, ti = twist_ref[0], twist_ref[1]
        turned = jnp.concatenate(
            [(real * tr + imag * ti).astype(BF16), (imag * tr - real * ti).astype(BF16)], axis=1
        )
        result = mm(first_ref[...], turned, NT).astype(BF16)
        out_ref[:, i] = result.reshape(parts, cols, PIXELS)
        return carry

    lax.fori_loop(0, count, step, 0, unroll=4)


def column_kernel(halved, *refs):
    if halved:
        flag_ref, phase_ref, refs = refs[0], refs[1], refs[2:]
    x_ref, outer_ref, *refs = refs
    count = 4 if halved else 5
    sources, out_ref = refs[:count], refs[count]
    mid_ref, *targets, sems = refs[count + 1 :]
    copies = [
        pltpu.make_async_copy(source, target, sems.at[n])
        for n, (source, target) in enumerate(zip(sources, targets))
    ]
    for copy in copies:
        copy.start()
    inner_ref, scale_ref, inner_t_ref, outer_t_ref = targets[:4]
    devices, _, rows, width = mid_ref.shape
    wide = devices * 2 * PATCH
    if halved:
        lane = lane_index((devices, PATCH, width))
        centre = flag_ref[0] == 1
        half = width // 2
        hidden = (lane == half) | (centre & (lane == 0))
        real_lane = (lane < half) | (centre & (lane == half))

    def load(group):
        place = slice(group * PATCH, (group + 1) * PATCH)
        if not halved:
            return x_ref[:, :, place, :].reshape(wide, width)
        piece = x_ref[:, place, :]
        other = swap_halves(piece.astype(F32))
        other = jnp.where(hidden, jnp.zeros_like(other), other).astype(BF16)
        return jnp.stack([piece, other], axis=1).reshape(wide, width)

    def store(group, value):
        place = slice(group * PATCH, (group + 1) * PATCH)
        value = value.reshape(devices, 2, PATCH, width)
        if halved:
            value = jnp.where(real_lane, value[:, 0], swap_halves(value[:, 1])).astype(BF16)
            out_ref[:, place, :] = value
        else:
            out_ref[:, :, place, :] = value.astype(BF16)

    for pair in range(0, rows // PATCH, 2):
        result = mm(outer_ref[...], jnp.concatenate([load(pair), load(pair + 1)], axis=1))
        result = result.astype(BF16)
        for n in range(2):
            place = slice((pair + n) * PATCH, (pair + n + 1) * PATCH)
            mid_ref[:, :, place, :] = result[:, n * width : (n + 1) * width].reshape(
                devices, 2, PATCH, width
            )

    for n, copy in enumerate(copies):
        if n != 3:
            copy.wait()

    def step(q, carry):
        spectrum = mm(inner_ref[q], mid_ref[q].reshape(2 * rows, width))
        real, imag = spectrum[:rows], spectrum[rows:]
        scale = scale_ref[q].astype(F32)
        if halved:
            pr, pi = phase_ref[q, 0], phase_ref[q, 1]
            real = real.reshape(rows // 8, 8, width)
            imag = imag.reshape(rows // 8, 8, width)
            real, imag = real * pr - imag * pi, real * pi + imag * pr
            real, imag = real.reshape(rows, width) * scale, imag.reshape(rows, width) * scale
        else:
            data_ref = targets[4]
            real = real * scale - data_ref[0, q].astype(F32)
            imag = imag * scale - data_ref[1, q].astype(F32)
        back = jnp.concatenate([real.astype(BF16), imag.astype(BF16)], axis=0)
        mid_ref[q] = mm(inner_t_ref[q], back).astype(BF16).reshape(2, rows, width)
        return carry

    lax.fori_loop(0, devices, step, 0, unroll=8)
    copies[3].wait()

    for pair in range(0, rows // PATCH, 2):
        both = jnp.concatenate(
            [
                mid_ref[:, :, n * PATCH : (n + 1) * PATCH, :].reshape(wide, width)
                for n in (pair, pair + 1)
            ],
            axis=1,
        )
        result = mm(outer_t_ref[...], both)
        store(pair, result[:, :width])
        store(pair + 1, result[:, width:])


def turned(value, devices):
    lines = value.shape[0]
    return value.astype(BF16).reshape(lines, N // devices, devices).transpose(2, 1, 0)


def spectrum_inputs(gains, observed, vis_weight, devices):
    gr, gi = gains[0], gains[1]
    weight = (vis_weight * (gr * gr + gi * gi)).astype(BF16)
    data = jnp.stack(
        [
            turned(vis_weight * (gr * observed[0] + gi * observed[1]), devices),
            turned(vis_weight * (gr * observed[1] - gi * observed[0]), devices),
        ]
    )
    return weight, turned(weight, devices), data


def mirror_kernel(scale_ref, got_ref, pick_ref, flip_ref, out_ref):
    devices = out_ref.shape[0]
    for q in range(devices):
        facing = mm(flip_ref[min(q, 1)], got_ref[(devices - q) % devices]).astype(BF16)
        total = mm(scale_ref[q], pick_ref[0]) + mm(facing, pick_ref[1])
        out_ref[q] = total.astype(BF16)


def mirrored_exchange(weight):
    devices = N // weight.shape[0]
    half, middle = weight.shape[0] // 2, devices // 2
    facing = [(e, devices - 1 - e) for e in range(devices)]
    partner = [(e, devices - e) for e in range(1, devices) if e != middle]
    partner = partner + [(0, middle), (middle, 0)]
    upper = lax.ppermute(weight[half:], ("ty", "tx"), facing)
    line = lax.ppermute(weight[:1], ("ty", "tx"), partner)
    return upper, line


def mirrored_weight(scale, upper, line):
    devices, slab, _ = scale.shape
    half, middle = slab // 2, devices // 2
    me = lax.axis_index(("ty", "tx"))
    got = jnp.concatenate([upper, jnp.broadcast_to(line, (half, N))], axis=0)
    source = lax.broadcasted_iota(jnp.int32, (slab, slab), 0)
    slot = lax.broadcasted_iota(jnp.int32, (slab, slab), 1)
    low = (me < middle).astype(jnp.int32)
    own = (slot < half) & (source == slot + low)
    other = (slot < half) & (source == half - low - slot)
    other = other & ((me != middle) | (slot > 0))
    other = other | ((me == middle) & (slot == half) & (source == half))
    picks = jnp.stack([own, other]).astype(BF16)
    q2 = np.arange(slab)
    flips = np.stack([q2[:, None] == (slab - q2) % slab, q2[:, None] == slab - 1 - q2])
    return pl.pallas_call(
        mirror_kernel,
        out_shape=jax.ShapeDtypeStruct(scale.shape, BF16),
        compiler_params=PARAMS,
    )(scale, turned(got, devices), picks, jnp.asarray(flips.astype(ml_dtypes.bfloat16)))


def row_matrix(shift):
    first = half_constants()[0]
    twice = jnp.asarray(np.concatenate([first, first[: 2 * WIN]], axis=0))
    return lax.dynamic_slice(twice, (shift, jnp.zeros((), jnp.int32)), first.shape)


def phase_table(shift, devices, width):
    kr = counting(devices)[:, None] + devices * counting(8)[None, :]
    angle = 2.0 * math.pi / TOK * (kr * shift % TOK).astype(F32)
    table = jnp.stack([jnp.cos(angle), -jnp.sin(angle)], axis=1)
    return jnp.broadcast_to(table[..., None], (devices, 2, 8, width))


def patch_gradient(state, scale, data, shift, mirror, beside):
    lanes = lax.axis_size("tx")
    devices = lax.axis_size("ty") * lanes
    rows, cols, _ = state.shape
    own = rows // lanes
    slab = N // devices
    halved = data is None
    outer, outer_t, inner, inner_t = (
        jnp.asarray(value) for value in column_constants(devices, slab)
    )
    if halved:
        first, twist, low, high, low_t, high_t = (jnp.asarray(value) for value in half_constants())
        part = (devices, slab, slab)
        onward = (row_forward_half, (row_matrix(shift[1]), twist, low, high))
        backward = (row_inverse_half, (first, twist, low_t, high_t))
        middle = lax.axis_index(("ty", "tx")) == devices // 2
    else:
        first, twist, second, second_t = (jnp.asarray(value) for value in row_constants())
        part = (devices, 2, slab, slab)
        onward = (row_forward, (first, twist, second))
        backward = (row_inverse, (first, twist, second_t))
        extra = ()
        away = (inner, scale, inner_t, outer_t, data)
    split = (PATCH, devices // PATCH) + part[1:]
    gathered = lax.all_to_all(
        state.reshape(lanes, own, cols, PIXELS), "tx", split_axis=0, concat_axis=0, tiled=True
    )
    sent = pl.pallas_call(
        onward[0], out_shape=jax.ShapeDtypeStruct(split, BF16), compiler_params=PARAMS
    )(gathered, *onward[1])
    if halved:
        sent, mirror, shift = lax.optimization_barrier((sent, mirror, shift))
        extra = (middle.astype(jnp.int32).reshape(1), phase_table(shift[0], devices, slab))
        away = (inner, mirrored_weight(scale, *mirror), inner_t, outer_t)
    moved = lax.all_to_all(
        sent.reshape(part), ("ty", "tx"), split_axis=0, concat_axis=0, tiled=True
    )
    if halved:
        moved, beside = lax.optimization_barrier((moved, beside))
    spaces = [pltpu.SMEM, pltpu.VMEM][: len(extra)] + [pltpu.VMEM] * 2 + [pl.ANY] * len(away)
    wave = pl.pallas_call(
        functools.partial(column_kernel, halved),
        in_specs=[pl.BlockSpec(memory_space=space) for space in spaces],
        out_shape=jax.ShapeDtypeStruct(part, BF16),
        scratch_shapes=[pltpu.VMEM((devices, 2, slab, slab), BF16)]
        + [pltpu.VMEM(value.shape, BF16) for value in away]
        + [pltpu.SemaphoreType.DMA((len(away),))],
        compiler_params=PARAMS,
    )(*extra, moved, outer, *away)
    returned = lax.all_to_all(wave, ("ty", "tx"), split_axis=0, concat_axis=0, tiled=True)
    if not halved:
        returned, beside = lax.optimization_barrier((returned, beside))
    slabs = pl.pallas_call(
        backward[0],
        out_shape=jax.ShapeDtypeStruct((lanes, own, cols, PIXELS), BF16),
        compiler_params=PARAMS,
    )(returned.reshape(split), *backward[1])
    grad = lax.all_to_all(slabs, "tx", split_axis=0, concat_axis=0, tiled=True)
    return grad.reshape(rows, cols, PIXELS), beside


def layer_norm(values, gain):
    centre = jnp.mean(values, axis=-1, keepdims=True)
    shifted = values - centre
    spread = jnp.mean(shifted * shifted, axis=-1, keepdims=True)
    return (shifted * lax.rsqrt(spread + EPSILON) * gain).astype(BF16)


def to_windows(band):
    rows, cols, feats = band.shape
    pieces = [
        band[:, w * WIN : (w + 1) * WIN, :].reshape(SPAN, feats) for w in range(cols // WIN)
    ]
    return jnp.concatenate(pieces, axis=0)


def from_windows(tokens, cols):
    feats = tokens.shape[-1]
    pieces = [
        tokens[w * SPAN : (w + 1) * SPAN].reshape(WIN, WIN, feats) for w in range(cols // WIN)
    ]
    return jnp.concatenate(pieces, axis=1)


def gelu_twice(value):
    value = value.astype(BF16)
    inside = value * (BF16(GELU_IN) + BF16(GELU_CUBE) * (value * value))
    return value + value * jnp.tanh(inside)


def load_weights(j, sources, targets, sems):
    copies = [
        pltpu.make_async_copy(source.at[j], target, sems.at[n])
        for n, (source, target) in enumerate(zip(sources, targets))
    ]

    @pl.when(pl.program_id(0) == 0)
    def _():
        for copy in copies:
            copy.start()

    def wait(which):
        @pl.when(pl.program_id(0) == 0)
        def _():
            for n in which:
                copies[n].wait()

    return wait


def swin_band(flow, wait, bias_ref, gain_ref, weight_refs, scratch):
    qkv_ref, proj_ref, up_ref, down_ref = weight_refs
    mixed_ref, score_ref, prob_ref, *active_ref = scratch
    count = flow.shape[0] // SPAN
    pairs = HEADS // 2
    depth = D // HEADS
    wide = 2 * depth
    normed = layer_norm(flow, gain_ref[0:1, :])
    scale = 1.0 / math.sqrt(depth)
    wait((0,))
    mixed_ref[:, :D] = (mm(normed, qkv_ref[:, :D]) * scale).astype(BF16)
    mixed_ref[:, D : 2 * D] = mm(normed, qkv_ref[:, D : 2 * D]).astype(BF16)
    mixed_ref[:, 2 * D :] = mm(normed, qkv_ref[:, 2 * D :]).astype(BF16)
    lower = lax.broadcasted_iota(jnp.int32, (SPAN, wide), 1) < depth

    def scores_of(w):
        rows = slice(w * SPAN, (w + 1) * SPAN)
        for p in range(pairs):
            query = mixed_ref[rows, p * wide : (p + 1) * wide]
            key = mixed_ref[rows, D + p * wide : D + (p + 1) * wide]
            zero = jnp.zeros_like(query)
            split = jnp.concatenate(
                [jnp.where(lower, query, zero), jnp.where(lower, zero, query)], axis=0
            )
            score_ref[w, :, p * wide : (p + 1) * wide] = mm(key, split, NT)

    def probs_of(w):
        bias = bias_ref[w]
        for p in range(pairs):
            lanes = slice(p * wide, (p + 1) * wide)
            scores = score_ref[w, :, lanes] + bias
            weights = jnp.exp(scores - jnp.max(scores, axis=0, keepdims=True))
            share = 1.0 / jnp.sum(weights, axis=0, keepdims=True)
            prob_ref[w, :, lanes] = (weights * share).astype(BF16)

    def mixture_of(w):
        rows = slice(w * SPAN, (w + 1) * SPAN)
        for p in range(pairs):
            lanes = slice(p * wide, (p + 1) * wide)
            value = mixed_ref[rows, 2 * D + p * wide : 2 * D + (p + 1) * wide]
            mixture = mm(prob_ref[w, :, lanes], value, TN)
            mixed_ref[rows, lanes] = jnp.where(lower, mixture[:SPAN], mixture[SPAN:]).astype(BF16)

    for turn in range(count + 2):
        if turn < count:
            scores_of(turn)
        if 0 <= turn - 1 < count:
            probs_of(turn - 1)
        if 0 <= turn - 2:
            mixture_of(turn - 2)
    wait((1, 2, 3))
    flow = flow + mm(mixed_ref[:, :D], proj_ref[...])
    normed = layer_norm(flow, gain_ref[1:2, :])
    chunks = up_ref.shape[1] // D
    if active_ref:
        for c in range(chunks):
            part = slice(c * D, (c + 1) * D)
            active_ref[0][:, part] = gelu_twice(mm(normed, up_ref[:, part]))
        return flow + 0.5 * mm(active_ref[0][...], down_ref[...])
    total = jnp.zeros_like(flow)
    ahead = mm(normed, up_ref[:, :D])
    for c in range(chunks):
        value = ahead
        if c + 1 < chunks:
            ahead = mm(normed, up_ref[:, (c + 1) * D : (c + 2) * D])
        total = total + mm(gelu_twice(value), down_ref[c * D : (c + 1) * D, :])
    return flow + 0.5 * total


def rolled_band(sign, shift_ref, refs, rows):
    main_ref, side_ref, edge_ref, corner_ref = refs
    cols = main_ref.shape[1]
    top = pl.program_id(0) * WIN + sign * shift_ref[0]
    behind = -rows if sign > 0 else WIN
    beside = -cols if sign > 0 else WIN

    def pick(width, offset):
        source = lax.broadcasted_iota(jnp.int32, (cols, width), 1)
        wanted = lax.broadcasted_iota(jnp.int32, (cols, width), 0) + sign * shift_ref[1] + offset
        return jnp.where(source == wanted, 1.0, 0.0).astype(BF16)

    pick_main, pick_side = pick(cols, 0), pick(WIN, beside)
    band = []
    for j in range(WIN):
        row = top + j
        inside = (row >= 0) & (row < rows)
        here, there = jnp.clip(row, 0, rows - 1), jnp.clip(row + behind, 0, WIN - 1)
        main = jnp.where(inside, main_ref[here], edge_ref[there])
        side = jnp.where(inside, side_ref[here], corner_ref[there])
        band.append(mm(pick_main, main) + mm(pick_side, side))
    return jnp.stack(band)


def first_kernel(zeta, sigma, count, rows, before, *refs):
    shift_ref, state_ref, *refs = refs
    if before is not None:
        back_refs, refs = refs[:4], refs[4:]
    grad_refs, refs = refs[:count], refs[count:]
    if sigma is not None:
        noise_ref, *refs = refs
    bias_ref, embed_ref, gain_ref, *sources = refs[:7]
    base_ref, out_ref, side_ref, edge_ref, corner_ref, *scratch = refs[7:]
    targets, sems, scratch = scratch[:4], scratch[4], scratch[5:]
    wait = load_weights(0, sources, targets, sems)
    state = state_ref[...]
    if before is not None:
        state = state - before * rolled_band(-1, shift_ref, back_refs, rows)
    step = zeta * sum(grad_ref[...].astype(F32) for grad_ref in grad_refs)
    half = state - step
    tokens = mm(to_windows(half).astype(BF16), embed_ref[...]).astype(BF16).astype(F32)
    flow = swin_band(tokens, wait, bias_ref, gain_ref, targets, scratch)
    result = from_windows(flow, half.shape[1]).astype(BF16)
    out_ref[:, :, :D] = result
    side_ref[:, :, :D] = result[:, :WIN]
    if sigma is None:
        base_ref[...] = half
    else:
        noise = sigma * noise_ref[...]
        base_ref[...] = half + noise
        change = (noise - step).astype(BF16)
        out_ref[:, :, D:] = change
        side_ref[:, :, D:] = change[:, :WIN]

    @pl.when(pl.program_id(0) == 0)
    def _():
        edge_ref[...] = out_ref[...]
        corner_ref[...] = side_ref[...]


def second_kernel(sigma, rows, *refs):
    shift_ref, *refs = refs
    tile_refs, refs = refs[:4], refs[4:]
    bias_ref, unembed_ref, gain_ref, *sources = refs[:7]
    out_ref, side_ref, edge_ref, corner_ref, *scratch = refs[7:]
    if sigma is not None:
        state_ref, *scratch = scratch
    targets, sems, scratch = scratch[:4], scratch[4], scratch[5:]
    wait = load_weights(1, sources, targets, sems)
    cols = out_ref.shape[1]
    band = rolled_band(1, shift_ref, tile_refs, rows)
    tokens = to_windows(band[:, :, :D])
    flow = swin_band(tokens, wait, bias_ref, gain_ref, targets, scratch)
    estimate = from_windows(mm(flow.astype(BF16), unembed_ref[...]), cols)
    narrow = estimate.astype(BF16)
    out_ref[...] = narrow
    edge_ref[...] = narrow
    side_ref[...] = narrow[:, cols - WIN :]
    corner_ref[...] = narrow[:, cols - WIN :]
    if sigma is not None:
        state_ref[...] = (band[:, :, D:] - sigma * estimate).astype(BF16)


def whole(array):
    zeros = (0,) * array.ndim
    return pl.BlockSpec(array.shape, lambda *_: zeros)


def band_of(step, cols):
    return pl.BlockSpec((step, cols, PIXELS), lambda n, *_: (n, 0, 0))


def member(array, j):
    place = (j,) + (0,) * (array.ndim - 1)
    return pl.BlockSpec((None,) + array.shape[1:], lambda *_: place)


def band_spec(cols, feats):
    return pl.BlockSpec((WIN, cols, feats), lambda n, *_: (n, 0, 0))


def bias_spec(cols):
    return pl.BlockSpec((cols // WIN, SPAN, 2 * SPAN), lambda n, *_: (n, 0, 0))


def band_scratch(cols, weights):
    count = cols // WIN
    return [pltpu.VMEM(value.shape[1:], BF16) for value in weights] + [
        pltpu.SemaphoreType.DMA((len(weights),)),
        pltpu.VMEM((WIN * cols, 3 * D), BF16),
        pltpu.VMEM((count, SPAN, HEADS * SPAN), F32),
        pltpu.VMEM((count, SPAN, HEADS * SPAN), BF16),
    ]


def strip_outs(rows, cols, feats):
    specs = [band_spec(cols, feats), band_spec(WIN, feats)]
    specs += [
        pl.BlockSpec((WIN, width, feats), lambda *_: (0, 0, 0)) for width in (cols, WIN)
    ]
    shapes = [(rows, cols), (rows, WIN), (WIN, cols), (WIN, WIN)]
    return specs, [jax.ShapeDtypeStruct(shape + (feats,), BF16) for shape in shapes]


def first_block(zeta, sigma, state, before, shift, back, grads, noise, bias, w_embed, weights):
    *weights, gains = weights
    rows, cols, _ = state.shape
    fields = [*grads] + ([] if sigma is None else [noise])
    feats = D if sigma is None else D + PIXELS
    specs, shapes = strip_outs(rows, cols, feats)
    return pl.pallas_call(
        functools.partial(first_kernel, zeta, sigma, len(grads), rows, before),
        grid_spec=pltpu.PrefetchScalarGridSpec(
            num_scalar_prefetch=1,
            grid=(rows // WIN,),
            in_specs=[band_spec(cols, PIXELS)]
            + [whole(value) for value in back]
            + [band_spec(cols, PIXELS)] * len(fields)
            + [bias_spec(cols), whole(w_embed), member(gains, 0)]
            + [pl.BlockSpec(memory_space=pl.ANY)] * len(weights),
            out_specs=[band_spec(cols, PIXELS)] + specs,
            scratch_shapes=band_scratch(cols, weights),
        ),
        out_shape=[jax.ShapeDtypeStruct((rows, cols, PIXELS), F32)] + shapes,
        compiler_params=PARAMS,
    )(shift, state, *back, *fields, bias, w_embed, gains, *weights)


def second_block(sigma, shift, tile, bias, w_unembed, weights):
    *weights, gains = weights
    rows, cols, _ = tile[0].shape
    specs, shapes = strip_outs(rows, cols, PIXELS)
    if sigma is not None:
        specs, shapes = specs + specs[:1], shapes + shapes[:1]
    return pl.pallas_call(
        functools.partial(second_kernel, sigma, rows),
        grid_spec=pltpu.PrefetchScalarGridSpec(
            num_scalar_prefetch=1,
            grid=(rows // WIN,),
            in_specs=[whole(value) for value in tile]
            + [bias_spec(cols), whole(w_unembed), member(gains, 1)]
            + [pl.BlockSpec(memory_space=pl.ANY)] * len(weights),
            out_specs=specs,
            scratch_shapes=band_scratch(cols, weights)
            + [pltpu.VMEM((WIN * cols, weights[2].shape[2]), BF16)],
        ),
        out_shape=shapes,
        compiler_params=PARAMS,
    )(shift, *tile, bias, w_unembed, gains, *weights)


def from_neighbours(tile, by):
    main, side, edge, corner = tile
    ty, tx = lax.axis_size("ty"), lax.axis_size("tx")
    across = [
        (i * tx + k, (i + by) % ty * tx + (k + by) % tx) for i in range(ty) for k in range(tx)
    ]
    return (
        main,
        lax.ppermute(side, "tx", [(k, (k + by) % tx) for k in range(tx)]),
        lax.ppermute(edge, "ty", [(i, (i + by) % ty) for i in range(ty)]),
        lax.ppermute(corner, ("ty", "tx"), across),
    )


def windows_of(grid):
    rows, cols = grid.shape
    shaped = grid.reshape(rows // WIN, WIN, cols // WIN, WIN).transpose(0, 2, 1, 3)
    return shaped.reshape(rows // WIN * (cols // WIN), SPAN)


def bias_of(labels, keep):
    allowed = jnp.ones((1, SPAN, SPAN), bool)
    if labels is not None:
        label = windows_of(labels)
        allowed = label[:, :, None] == label[:, None, :]
    if keep is not None:
        kept = windows_of(keep)[:, :, None] == 1
        allowed = allowed & (kept | jnp.eye(SPAN, dtype=bool)[None])
    bias = jnp.where(allowed, 0.0, -1e30).astype(F32)
    return jnp.concatenate([bias, bias], axis=2)


def region(index, shift):
    return jnp.where(index < TOK - WIN, 0, jnp.where(index < TOK - shift, 1, 2)).astype(jnp.int32)


@functools.lru_cache(maxsize=None)
def lane_order(cols):
    parts = LANES // cols
    groups = PATCH // parts
    lane = np.arange(PATCH * cols)
    g, h, k = lane // LANES, lane % LANES // cols, lane % cols
    source = PATCH * k + h * groups + g
    matrix = np.zeros((PATCH * cols, PATCH * cols), np.float32)
    matrix[source, lane] = 1.0
    return matrix.astype(ml_dtypes.bfloat16), np.ascontiguousarray(matrix.T).astype(
        ml_dtypes.bfloat16
    )


def move_lanes(values, matrix):
    high = values.astype(BF16)
    low = (values - high.astype(F32)).astype(BF16)
    return mm(high, matrix) + mm(low, matrix)


def to_patches_kernel(tile_ref, order_ref, out_ref):
    count, cols, _ = out_ref.shape
    parts = LANES // cols
    groups = PATCH // parts
    if out_ref.dtype == BF16:
        ordered = mm(tile_ref[...].astype(BF16), order_ref[...])
    else:
        ordered = move_lanes(tile_ref[...], order_ref[...])
    for i in range(count):
        band = ordered[i * PATCH : (i + 1) * PATCH]
        stacked = jnp.concatenate(
            [band[:, g * LANES : (g + 1) * LANES] for g in range(groups)], axis=0
        )
        turned = stacked.T
        patch = jnp.concatenate([turned[h * cols : (h + 1) * cols] for h in range(parts)], axis=1)
        out_ref[i] = patch.astype(out_ref.dtype)


def to_tile_kernel(sigma, scale, rows, *refs):
    shift_ref, base_ref, *refs = refs
    noise_ref, order_ref, out_ref = refs[4:]
    count, cols, _ = base_ref.shape
    parts = LANES // cols
    groups = PATCH // parts
    width = groups * PATCH
    state = base_ref[...] - sigma * rolled_band(-1, shift_ref, refs[:4], rows)
    bands = []
    for i in range(count):
        stacked = jnp.concatenate(
            [state[i, :, h * width : (h + 1) * width] for h in range(parts)], axis=0
        )
        turned = stacked.T
        bands.append(
            jnp.concatenate([turned[g * PATCH : (g + 1) * PATCH] for g in range(groups)], axis=1)
        )
    moved = move_lanes(jnp.concatenate(bands, axis=0), order_ref[...])
    out_ref[...] = moved + scale * noise_ref[...]


def patches_of(tiles, j, kind=F32):
    rows, cols = tiles.shape[1] // PATCH, tiles.shape[2] // PATCH
    order = jnp.asarray(lane_order(cols)[0])
    step = rows // 4
    return pl.pallas_call(
        to_patches_kernel,
        grid=(rows // step,),
        in_specs=[
            pl.BlockSpec((None, step * PATCH, cols * PATCH), lambda n: (j, n, 0)),
            whole(order),
        ],
        out_specs=band_of(step, cols),
        out_shape=jax.ShapeDtypeStruct((rows, cols, PIXELS), kind),
        compiler_params=PARAMS,
    )(tiles, order)


def tile_of(base, sigma, shift, back, scale, noise, j):
    rows, cols, _ = base.shape
    order = jnp.asarray(lane_order(cols)[1])
    return pl.pallas_call(
        functools.partial(to_tile_kernel, sigma, scale, rows),
        grid_spec=pltpu.PrefetchScalarGridSpec(
            num_scalar_prefetch=1,
            grid=(rows // WIN,),
            in_specs=[band_spec(cols, PIXELS)]
            + [whole(value) for value in back]
            + [
                pl.BlockSpec((None, WIN * PATCH, cols * PATCH), lambda n, *_: (j, n, 0)),
                whole(order),
            ],
            out_specs=pl.BlockSpec((WIN * PATCH, cols * PATCH), lambda n, *_: (n, 0)),
        ),
        out_shape=jax.ShapeDtypeStruct((rows * PATCH, cols * PATCH), F32),
        compiler_params=PARAMS,
    )(shift, base, *back, noise, order)


def per_device(
    image, noise, offsets, key_mask, gains, observed, vis_weight,
    w_embed, w_qkv, w_proj, w_up, w_down, w_unembed, norm_gains,
):
    rows = image.shape[0] // PATCH
    cols = image.shape[1] // PATCH
    devices = lax.axis_size("ty") * lax.axis_size("tx")
    fast = N // devices == TOK // 2
    row_index = lax.axis_index("ty") * rows + counting(rows)
    col_index = lax.axis_index("tx") * cols + counting(cols)
    weights = (w_qkv, w_proj, w_up, w_down, norm_gains)
    w_embed = w_embed.reshape(PATCH, PATCH, D).transpose(1, 0, 2).reshape(PIXELS, D)
    w_unembed = w_unembed.reshape(D, PATCH, PATCH).transpose(0, 2, 1).reshape(D, PIXELS)
    state = patches_of(image[None], 0)
    extras = [patches_of(noise, step) for step in range(STEPS - 1)] + [None]
    first_bias = bias_of(None, key_mask)
    biases = []
    for step in range(STEPS):
        labels = (
            3 * region(row_index, offsets[step, 0])[:, None]
            + region(col_index, offsets[step, 1])[None, :]
        )
        biases.append(bias_of(labels, None))
    beside = (state, extras, first_bias, biases, w_embed, w_unembed)
    shift, before, back, moving, mirror = offsets[0], None, (), None, None
    grads = []
    if fast:
        weight, scale, data = spectrum_inputs(gains, observed, vis_weight, devices)
        grad, beside = patch_gradient(
            patches_of(image[None], 0, BF16), scale, data, None, None, beside
        )
        grads = [grad]
        state, extras, first_bias, biases, w_embed, w_unembed = beside
    for step in range(STEPS):
        if not fast:
            tile = image if step == 0 else tile_of(state, before, shift, back, 0.0, noise, 0)
            grad = plain_gradient(tile, gains, observed, vis_weight)
            grads = [patches_of(grad.astype(F32)[None], 0, BF16)]
        elif step > 0:
            grad, back = patch_gradient(moving, scale, None, shift, mirror, back)
            grads = grads + [grad]
        last = step + 1 == STEPS
        sigma = None if last else SIGMAS[step + 1]
        state, *first = first_block(
            STEP_SIZES[step], sigma, state, before, shift, back, grads, extras[step], first_bias,
            w_embed, weights,
        )
        shift, before = offsets[step], SIGMAS[step]
        first = from_neighbours(first, -1)
        if fast and step == 0:
            first, weight = lax.optimization_barrier((first, weight))
            mirror = mirrored_exchange(weight)
        rolled = second_block(
            None if last else before, shift, first, biases[step], w_unembed, weights
        )
        if not last:
            *rolled, moving = rolled
        if fast and step == 0:
            moving, mirror = lax.optimization_barrier((moving, mirror))
        back = from_neighbours(rolled, 1)
    return tile_of(state, before, shift, back, SIGMAS[STEPS], noise, STEPS - 1)


def solution(mesh):
    in_specs = (
        P("ty", "tx"),
        P(None, "ty", "tx"),
        P(),
        P("ty", "tx"),
        P(None, ("ty", "tx"), None),
        P(None, ("ty", "tx"), None),
        P(("ty", "tx"), None),
        P(),
        P(),
        P(),
        P(),
        P(),
        P(),
        P(),
    )
    out_specs = P("ty", "tx")
    return jax.shard_map(
        per_device, mesh=mesh, in_specs=in_specs, out_specs=out_specs, check_vma=False
    )
```

```python
import functools
import math

import jax
import jax.numpy as jnp
import ml_dtypes
import numpy as np
from jax import lax
from jax.experimental import pallas as pl
from jax.experimental.pallas import tpu as pltpu
from jax.sharding import PartitionSpec as P

N = 4096
PATCH = 16
PIXELS = PATCH * PATCH
WIN = 8
D = 512
HEADS = 8
STEPS = 2
SPAN = WIN * WIN
LANES = 128
TOK = N // PATCH

SIGMAS = (0.8, 0.5, 0.3)
STEP_SIZES = (0.9, 0.7)
EPSILON = 1e-05
HIGHEST = lax.Precision.HIGHEST
BF16 = jnp.bfloat16
F32 = jnp.float32
GELU_IN = math.sqrt(2.0 / math.pi)
GELU_CUBE = 0.044715 * GELU_IN
VMEM_LIMIT = 56 * 1024 * 1024
PARAMS = pltpu.CompilerParams(vmem_limit_bytes=VMEM_LIMIT)
TN = (((0,), (0,)), ((), ()))
NT = (((1,), (1,)), ((), ()))
NN = (((1,), (0,)), ((), ()))


def mm(left, right, dims=NN):
    return lax.dot_general(left, right, dims, preferred_element_type=F32)


def counting(length):
    return jnp.arange(length, dtype=jnp.int32)


def roots(length, outer, inner, sign):
    product = outer[:, None] * inner[None, :] % length
    angle = 2.0 * math.pi / length * product.astype(F32)
    return (jnp.cos(angle), sign * jnp.sin(angle))


def complex_einsum(form, left, right):
    real = jnp.einsum(form, left[0], right[0], precision=HIGHEST) - jnp.einsum(
        form, left[1], right[1], precision=HIGHEST
    )
    imag = jnp.einsum(form, left[0], right[1], precision=HIGHEST) + jnp.einsum(
        form, left[1], right[0], precision=HIGHEST
    )
    return (real, imag)


def complex_times(left, right):
    return (left[0] * right[0] - left[1] * right[1], left[0] * right[1] + left[1] * right[0])


def along_last(real_part, imag_part, groups, sign):
    rows, length = real_part.shape
    inner = length // groups
    first = roots(groups, counting(groups), counting(groups), sign)
    twist = roots(length, counting(inner), counting(groups), sign)
    second = roots(inner, counting(inner), counting(inner), sign)
    shaped = real_part.reshape(rows, groups, inner)
    if imag_part is None:
        partial_value = (
            jnp.einsum("mab,ka->mbk", shaped, first[0], precision=HIGHEST),
            jnp.einsum("mab,ka->mbk", shaped, first[1], precision=HIGHEST),
        )
    else:
        partial_value = complex_einsum(
            "mab,ka->mbk", (shaped, imag_part.reshape(rows, groups, inner)), first
        )
    partial_value = complex_times(partial_value, twist)
    result = complex_einsum("jb,mbk->mjk", second, partial_value)
    return (result[0].reshape(rows, length), result[1].reshape(rows, length))


def across_groups(pair, groups, sign):
    inner, cols = pair[0].shape
    width = cols // groups
    length = groups * inner
    first = roots(groups, counting(groups), counting(groups), sign)
    twist = roots(length, counting(inner), counting(groups), sign)
    second = roots(inner, counting(inner), counting(inner), sign)
    shaped = (pair[0].reshape(inner, groups, width), pair[1].reshape(inner, groups, width))
    partial_value = complex_einsum("bhc,kh->cbk", shaped, first)
    partial_value = complex_times(partial_value, twist)
    result = complex_einsum("jb,cbk->cjk", second, partial_value)
    return (result[0].reshape(width, length), result[1].reshape(width, length))


def exchange_pair(pair):
    return tuple(
        lax.all_to_all(
            part.astype(BF16), ("ty", "tx"), split_axis=1, concat_axis=1, tiled=True
        ).astype(F32)
        for part in pair
    )


def plain_gradient(tile, gains, observed, vis_weight):
    devices = lax.axis_size("ty") * lax.axis_size("tx")
    slab = lax.all_to_all(tile.astype(BF16), "tx", split_axis=0, concat_axis=1, tiled=True)
    moved = exchange_pair(along_last(slab.astype(F32), None, devices, -1.0))
    spectrum = across_groups(moved, devices, -1.0)
    spectrum = (spectrum[0] * (1.0 / N), spectrum[1] * (1.0 / N))
    model = complex_times((gains[0], gains[1]), spectrum)
    misfit = (vis_weight * (model[0] - observed[0]), vis_weight * (model[1] - observed[1]))
    back = complex_times((gains[0], -gains[1]), misfit)
    returned = exchange_pair(along_last(back[0], back[1], devices, 1.0))
    slab_grad = across_groups(returned, devices, 1.0)[0] * (1.0 / N)
    return lax.all_to_all(slab_grad.astype(BF16), "tx", split_axis=1, concat_axis=0, tiled=True)


def embed_complex(angle, row_axis, col_axis):
    cos, sin = np.cos(angle), np.sin(angle)
    top = np.stack([cos, sin], axis=col_axis)
    bottom = np.stack([-sin, cos], axis=col_axis)
    return np.stack([top, bottom], axis=row_axis)


def wheel(length, product):
    return 2.0 * math.pi / length * (product % length)


@functools.lru_cache(maxsize=None)
def row_constants():
    k = np.arange(TOK)
    angle = wheel(TOK, k[:, None] * k[None, :])
    first = np.concatenate([np.cos(angle), -np.sin(angle)], axis=1)
    b = np.repeat(np.arange(PATCH), PATCH)
    angle = wheel(N, b[:, None] * k[None, :])
    twist = np.stack([np.cos(angle), -np.sin(angle)])
    p = np.arange(PATCH)
    small = embed_complex(wheel(PATCH, p[:, None] * p[None, :]), 1, 1)
    second = np.einsum("kpqb,xy->kpxqby", small, np.eye(PATCH)).reshape(2 * PIXELS, 2 * PIXELS)
    return (
        first.astype(ml_dtypes.bfloat16),
        twist.astype(np.float32),
        second.astype(ml_dtypes.bfloat16),
        np.ascontiguousarray(second.T).astype(ml_dtypes.bfloat16),
    )


@functools.lru_cache(maxsize=None)
def half_constants():
    _, twist, second, _ = row_constants()
    half, quarter = TOK // 2, TOK // 4
    low = np.concatenate([1 + np.arange(quarter), 1 + half + np.arange(quarter)])
    digits = np.concatenate([low, low - 1])
    k = np.arange(TOK)
    angle = wheel(TOK, k[:, None] * digits[None, :])
    first = np.concatenate([np.cos(angle), -np.sin(angle)], axis=1)
    zero_line = np.concatenate([np.tile(np.eye(PATCH), PATCH), np.zeros((PATCH, PIXELS))], axis=1)
    upper = np.concatenate([second[PIXELS:].astype(np.float32), zero_line])
    lower = second[:PIXELS].astype(np.float32)
    return (first.astype(ml_dtypes.bfloat16), np.ascontiguousarray(twist[:, :, digits])) + tuple(
        np.ascontiguousarray(value).astype(ml_dtypes.bfloat16)
        for value in (lower, upper, lower.T, upper.T)
    )


@functools.lru_cache(maxsize=None)
def column_constants(devices, rows):
    s = np.arange(devices)
    small = embed_complex(wheel(devices, s[:, None] * s[None, :]), 1, 2)
    wide = devices * 2 * PATCH
    outer = np.einsum("qpsr,xy->qpxsry", small, np.eye(PATCH)).reshape(wide, wide)
    kr = s[:, None] + devices * np.arange(rows)[None, :]
    angle = wheel(N, kr[:, :, None] * np.arange(rows)[None, None, :])
    inner = embed_complex(angle, 1, 2).reshape(devices, 2 * rows, 2 * rows) / N
    return tuple(
        np.ascontiguousarray(value).astype(ml_dtypes.bfloat16)
        for value in (outer, outer.T, inner, inner.transpose(0, 2, 1))
    )


def row_forward(*refs):
    *x_refs, first_ref, twist_ref, second_ref, out_ref = refs
    count = x_refs[0].shape[0]

    def step(i, carry):
        band = jnp.concatenate([x_ref[i] for x_ref in x_refs], axis=0)
        mixed = mm(band, first_ref[...], TN)
        real, imag = mixed[:, :TOK], mixed[:, TOK:]
        tr, ti = twist_ref[0], twist_ref[1]
        turned = jnp.concatenate(
            [(real * tr - imag * ti).astype(BF16), (real * ti + imag * tr).astype(BF16)], axis=0
        )
        result = mm(second_ref[...], turned).astype(BF16).reshape(PATCH, 2, PATCH, TOK)
        half = TOK // 2
        rows = pl.ds(pl.multiple_of(i * PATCH, PATCH), PATCH)
        out_ref[:, 0, :, rows, :] = result[..., :half]
        out_ref[:, 1, :, rows, :] = result[..., half:]
        return carry

    lax.fori_loop(0, count, step, 0, unroll=4)


def row_inverse(v_ref, first_ref, twist_ref, second_ref, *out_refs):
    count, cols, _ = out_refs[0].shape

    def step(i, carry):
        rows = pl.ds(pl.multiple_of(i * PATCH, PATCH), PATCH)
        wide = jnp.concatenate(
            [
                v_ref[:, 0, :, rows, :].reshape(2 * PIXELS, TOK // 2),
                v_ref[:, 1, :, rows, :].reshape(2 * PIXELS, TOK // 2),
            ],
            axis=1,
        )
        mixed = mm(second_ref[...], wide)
        real, imag = mixed[:PIXELS], mixed[PIXELS:]
        tr, ti = twist_ref[0], twist_ref[1]
        turned = jnp.concatenate(
            [(real * tr + imag * ti).astype(BF16), (imag * tr - real * ti).astype(BF16)], axis=1
        )
        result = mm(first_ref[...], turned, NT).astype(BF16)
        for m, out_ref in enumerate(out_refs):
            out_ref[i] = result[m * cols : (m + 1) * cols]
        return carry

    lax.fori_loop(0, count, step, 0, unroll=4)


def lane_index(shape):
    return lax.broadcasted_iota(jnp.int32, shape, len(shape) - 1)


def swap_halves(values):
    return pltpu.roll(values, values.shape[-1] // 2, len(values.shape) - 1)


def row_forward_half(*refs):
    *x_refs, first_ref, twist_ref, lower_ref, upper_ref, out_ref = refs
    count = x_refs[0].shape[0]
    half = TOK // 2

    def packed(real, imag, rows, high):
        left = lane_index(real.shape) < half // 2
        out_ref[high, 0, rows, :] = jnp.where(left, real, swap_halves(imag)).astype(BF16)
        out_ref[high, 1, rows, :] = jnp.where(left, swap_halves(real), imag).astype(BF16)

    def step(i, carry):
        band = jnp.concatenate([x_ref[i] for x_ref in x_refs], axis=0)
        mixed = mm(band, first_ref[...], TN)
        real, imag = mixed[:, :TOK], mixed[:, TOK:]
        tr, ti = twist_ref[0], twist_ref[1]
        turned = jnp.concatenate(
            [(real * tr - imag * ti).astype(BF16), (real * ti + imag * tr).astype(BF16)], axis=0
        )
        rows = pl.ds(pl.multiple_of(i * PATCH, PATCH), PATCH)
        lower = mm(lower_ref[...], turned[:, :half]).reshape(PATCH // 2, 2, PATCH, half)
        packed(lower[:, 0], lower[:, 1], rows, slice(0, PATCH // 2))
        upper = mm(upper_ref[...], turned[:, half:])
        line = upper[PIXELS:]
        upper = upper[:PIXELS].reshape(PATCH // 2, 2, PATCH, half)
        imag = upper[:, 1]
        head = jnp.where(lane_index(line.shape) == 0, line, imag[0])
        imag = jnp.concatenate([head[None], imag[1:]], axis=0)
        packed(upper[:, 0], imag, rows, slice(PATCH // 2, PATCH))
        return carry

    lax.fori_loop(0, count, step, 0, unroll=4)


def row_inverse_half(v_ref, first_ref, twist_ref, lower_ref, upper_ref, *out_refs):
    count, cols, _ = out_refs[0].shape
    half = TOK // 2

    def unpacked(rows, high):
        even = v_ref[high, 0, rows, :].astype(F32)
        odd = v_ref[high, 1, rows, :].astype(F32)
        left = lane_index(even.shape) < half // 2
        return jnp.where(left, even, swap_halves(odd)), jnp.where(left, swap_halves(even), odd)

    def step(i, carry):
        rows = pl.ds(pl.multiple_of(i * PATCH, PATCH), PATCH)
        real, imag = unpacked(rows, slice(0, PATCH // 2))
        lower = jnp.stack([real, imag], axis=1).reshape(PIXELS, half)
        real, imag = unpacked(rows, slice(PATCH // 2, PATCH))
        head = imag[0]
        at_zero = lane_index(head.shape) == 0
        nothing = jnp.zeros_like(head)
        imag = jnp.concatenate([jnp.where(at_zero, nothing, head)[None], imag[1:]], axis=0)
        upper = jnp.stack([real, imag], axis=1).reshape(PIXELS, half)
        upper = jnp.concatenate([upper, jnp.where(at_zero, head, nothing)], axis=0)
        mixed = jnp.concatenate(
            [mm(lower_ref[...], lower.astype(BF16)), mm(upper_ref[...], upper.astype(BF16))], axis=1
        )
        real, imag = mixed[:PIXELS], mixed[PIXELS:]
        tr, ti = twist_ref[0], twist_ref[1]
        turned = jnp.concatenate(
            [(real * tr + imag * ti).astype(BF16), (imag * tr - real * ti).astype(BF16)], axis=1
        )
        result = mm(first_ref[...], turned, NT).astype(BF16)
        for m, out_ref in enumerate(out_refs):
            out_ref[i] = result[m * cols : (m + 1) * cols]
        return carry

    lax.fori_loop(0, count, step, 0, unroll=4)


def column_kernel(halved, *refs):
    if halved:
        flag_ref, phase_ref, refs = refs[0], refs[1], refs[2:]
    x_ref, outer_ref, *refs = refs
    count = 4 if halved else 5
    sources, out_ref = refs[:count], refs[count]
    mid_ref, *targets, sems = refs[count + 1 :]
    copies = [
        pltpu.make_async_copy(source, target, sems.at[n])
        for n, (source, target) in enumerate(zip(sources, targets))
    ]
    for copy in copies:
        copy.start()
    inner_ref, scale_ref, inner_t_ref, outer_t_ref = targets[:4]
    devices, _, rows, width = mid_ref.shape
    wide = devices * 2 * PATCH
    if halved:
        lane = lane_index((devices, PATCH, width))
        centre = flag_ref[0] == 1
        half = width // 2
        hidden = (lane == half) | (centre & (lane == 0))
        real_lane = (lane < half) | (centre & (lane == half))

    def load(group):
        place = slice(group * PATCH, (group + 1) * PATCH)
        if not halved:
            return x_ref[:, :, place, :].reshape(wide, width)
        piece = x_ref[:, place, :]
        other = swap_halves(piece.astype(F32))
        other = jnp.where(hidden, jnp.zeros_like(other), other).astype(BF16)
        return jnp.stack([piece, other], axis=1).reshape(wide, width)

    def store(group, value):
        place = slice(group * PATCH, (group + 1) * PATCH)
        value = value.reshape(devices, 2, PATCH, width)
        if halved:
            value = jnp.where(real_lane, value[:, 0], swap_halves(value[:, 1])).astype(BF16)
            out_ref[:, place, :] = value
        else:
            out_ref[:, :, place, :] = value.astype(BF16)

    for pair in range(0, rows // PATCH, 2):
        result = mm(outer_ref[...], jnp.concatenate([load(pair), load(pair + 1)], axis=1))
        result = result.astype(BF16)
        for n in range(2):
            place = slice((pair + n) * PATCH, (pair + n + 1) * PATCH)
            mid_ref[:, :, place, :] = result[:, n * width : (n + 1) * width].reshape(
                devices, 2, PATCH, width
            )

    for n, copy in enumerate(copies):
        if n != 3:
            copy.wait()

    def step(q, carry):
        spectrum = mm(inner_ref[q], mid_ref[q].reshape(2 * rows, width))
        real, imag = spectrum[:rows], spectrum[rows:]
        scale = scale_ref[q].astype(F32)
        if halved:
            pr, pi = phase_ref[q, 0], phase_ref[q, 1]
            real = real.reshape(rows // 8, 8, width)
            imag = imag.reshape(rows // 8, 8, width)
            real, imag = real * pr - imag * pi, real * pi + imag * pr
            real, imag = real.reshape(rows, width) * scale, imag.reshape(rows, width) * scale
        else:
            data_ref = targets[4]
            real = real * scale - data_ref[0, q].astype(F32)
            imag = imag * scale - data_ref[1, q].astype(F32)
        back = jnp.concatenate([real.astype(BF16), imag.astype(BF16)], axis=0)
        mid_ref[q] = mm(inner_t_ref[q], back).astype(BF16).reshape(2, rows, width)
        return carry

    lax.fori_loop(0, devices, step, 0, unroll=8)
    copies[3].wait()

    for pair in range(0, rows // PATCH, 2):
        both = jnp.concatenate(
            [
                mid_ref[:, :, n * PATCH : (n + 1) * PATCH, :].reshape(wide, width)
                for n in (pair, pair + 1)
            ],
            axis=1,
        )
        result = mm(outer_t_ref[...], both)
        store(pair, result[:, :width])
        store(pair + 1, result[:, width:])


def turned(value, devices):
    lines = value.shape[0]
    return value.astype(BF16).reshape(lines, N // devices, devices).transpose(2, 1, 0)


def spectrum_inputs(gains, observed, vis_weight, devices):
    gr, gi = gains[0], gains[1]
    weight = (vis_weight * (gr * gr + gi * gi)).astype(BF16)
    data = jnp.stack(
        [
            turned(vis_weight * (gr * observed[0] + gi * observed[1]), devices),
            turned(vis_weight * (gr * observed[1] - gi * observed[0]), devices),
        ]
    )
    return weight, turned(weight, devices), data


def mirror_kernel(scale_ref, got_ref, pick_ref, flip_ref, out_ref):
    devices = out_ref.shape[0]
    for q in range(devices):
        facing = mm(flip_ref[min(q, 1)], got_ref[(devices - q) % devices]).astype(BF16)
        total = mm(scale_ref[q], pick_ref[0]) + mm(facing, pick_ref[1])
        out_ref[q] = total.astype(BF16)


def mirrored_exchange(upper, line, devices):
    middle = devices // 2
    facing = [(e, devices - 1 - e) for e in range(devices)]
    partner = [(e, devices - e) for e in range(1, devices) if e != middle]
    partner = partner + [(0, middle), (middle, 0)]
    upper = lax.ppermute(upper, ("ty", "tx"), facing)
    line = lax.ppermute(line, ("ty", "tx"), partner)
    return upper, line


def mirrored_weight(scale, upper, line):
    devices, slab, _ = scale.shape
    half, middle = slab // 2, devices // 2
    me = lax.axis_index(("ty", "tx"))
    got = jnp.concatenate([upper, jnp.broadcast_to(line, (half, N))], axis=0)
    source = lax.broadcasted_iota(jnp.int32, (slab, slab), 0)
    slot = lax.broadcasted_iota(jnp.int32, (slab, slab), 1)
    low = (me < middle).astype(jnp.int32)
    own = (slot < half) & (source == slot + low)
    other = (slot < half) & (source == half - low - slot)
    other = other & ((me != middle) | (slot > 0))
    other = other | ((me == middle) & (slot == half) & (source == half))
    picks = jnp.stack([own, other]).astype(BF16)
    q2 = np.arange(slab)
    flips = np.stack([q2[:, None] == (slab - q2) % slab, q2[:, None] == slab - 1 - q2])
    return pl.pallas_call(
        mirror_kernel,
        out_shape=jax.ShapeDtypeStruct(scale.shape, BF16),
        compiler_params=PARAMS,
    )(scale, turned(got, devices), picks, jnp.asarray(flips.astype(ml_dtypes.bfloat16)))


def row_matrix(first, cols, lanes, shift):
    twice = jnp.asarray(np.concatenate([first, first[: 2 * WIN]], axis=0))
    me = lax.axis_index("tx")
    zero = jnp.zeros((), jnp.int32)
    starts = [(me ^ m) * cols + (0 if shift is None else shift) for m in range(lanes)]
    rows = [lax.dynamic_slice(twice, (start, zero), (cols, first.shape[1])) for start in starts]
    return jnp.concatenate(rows, axis=0)


def swap_pieces(pieces):
    lanes = len(pieces)
    return [pieces[0]] + [
        lax.ppermute(pieces[m], "tx", [(k, k ^ m) for k in range(lanes)]) for m in range(1, lanes)
    ]


def phase_table(shift, devices, width):
    kr = counting(devices)[:, None] + devices * counting(8)[None, :]
    angle = 2.0 * math.pi / TOK * (kr * shift % TOK).astype(F32)
    table = jnp.stack([jnp.cos(angle), -jnp.sin(angle)], axis=1)
    return jnp.broadcast_to(table[..., None], (devices, 2, 8, width))


def patch_gradient(pieces, scale, data, shift, mirror, beside):
    lanes = lax.axis_size("tx")
    devices = lax.axis_size("ty") * lanes
    own, cols, _ = pieces[0].shape
    slab = N // devices
    halved = data is None
    outer, outer_t, inner, inner_t = (
        jnp.asarray(value) for value in column_constants(devices, slab)
    )
    if halved:
        first = half_constants()[0]
        twist, low, high, low_t, high_t = (jnp.asarray(value) for value in half_constants()[1:])
        part = (devices, slab, slab)
        onward = (row_forward_half, (row_matrix(first, cols, lanes, shift[1]), twist, low, high))
        backward = (row_inverse_half, (row_matrix(first, cols, lanes, None), twist, low_t, high_t))
        middle = lax.axis_index(("ty", "tx")) == devices // 2
    else:
        first = row_matrix(row_constants()[0], cols, lanes, None)
        twist, second, second_t = (jnp.asarray(value) for value in row_constants()[1:])
        part = (devices, 2, slab, slab)
        onward = (row_forward, (first, twist, second))
        backward = (row_inverse, (first, twist, second_t))
        extra = ()
        away = (inner, scale, inner_t, outer_t, data)
    split = (PATCH, devices // PATCH) + part[1:]
    sent = pl.pallas_call(
        onward[0], out_shape=jax.ShapeDtypeStruct(split, BF16), compiler_params=PARAMS
    )(*swap_pieces(pieces), *onward[1])
    if halved:
        sent, mirror, shift = lax.optimization_barrier((sent, mirror, shift))
        extra = (middle.astype(jnp.int32).reshape(1), phase_table(shift[0], devices, slab))
        away = (inner, mirrored_weight(scale, *mirror), inner_t, outer_t)
    moved = lax.all_to_all(
        sent.reshape(part), ("ty", "tx"), split_axis=0, concat_axis=0, tiled=True
    )
    if halved:
        moved, beside = lax.optimization_barrier((moved, beside))
    spaces = [pltpu.SMEM, pltpu.VMEM][: len(extra)] + [pltpu.VMEM] * 2 + [pl.ANY] * len(away)
    wave = pl.pallas_call(
        functools.partial(column_kernel, halved),
        in_specs=[pl.BlockSpec(memory_space=space) for space in spaces],
        out_shape=jax.ShapeDtypeStruct(part, BF16),
        scratch_shapes=[pltpu.VMEM((devices, 2, slab, slab), BF16)]
        + [pltpu.VMEM(value.shape, BF16) for value in away]
        + [pltpu.SemaphoreType.DMA((len(away),))],
        compiler_params=PARAMS,
    )(*extra, moved, outer, *away)
    returned = lax.all_to_all(wave, ("ty", "tx"), split_axis=0, concat_axis=0, tiled=True)
    if not halved:
        returned, beside = lax.optimization_barrier((returned, beside))
    slabs = pl.pallas_call(
        backward[0],
        out_shape=[jax.ShapeDtypeStruct((own, cols, PIXELS), BF16)] * lanes,
        compiler_params=PARAMS,
    )(returned.reshape(split), *backward[1])
    return swap_pieces(slabs), beside


def layer_norm(values, gain):
    centre = jnp.mean(values, axis=-1, keepdims=True)
    shifted = values - centre
    spread = jnp.mean(shifted * shifted, axis=-1, keepdims=True)
    return (shifted * lax.rsqrt(spread + EPSILON) * gain).astype(BF16)


def to_windows(band):
    rows, cols, feats = band.shape
    pieces = [
        band[n : n + WIN, k : k + WIN, :].reshape(SPAN, feats)
        for n in range(0, rows, WIN)
        for k in range(0, cols, WIN)
    ]
    return jnp.concatenate(pieces, axis=0)


def from_windows(tokens, cols):
    feats = tokens.shape[-1]
    size = SPAN * cols // WIN
    bands = []
    for top in range(0, tokens.shape[0], size):
        pieces = [
            tokens[n : n + SPAN].reshape(WIN, WIN, feats) for n in range(top, top + size, SPAN)
        ]
        bands.append(jnp.concatenate(pieces, axis=1))
    return jnp.concatenate(bands, axis=0)


def gelu_twice(value):
    value = value.astype(BF16)
    inside = value * (BF16(GELU_IN) + BF16(GELU_CUBE) * (value * value))
    return value + value * jnp.tanh(inside)


def load_weights(j, sources, targets, sems):
    copies = [
        pltpu.make_async_copy(source.at[j], target, sems.at[n])
        for n, (source, target) in enumerate(zip(sources, targets))
    ]

    @pl.when(pl.program_id(0) == 0)
    def _():
        for copy in copies:
            copy.start()

    def wait(which):
        @pl.when(pl.program_id(0) == 0)
        def _():
            for n in which:
                copies[n].wait()

    return wait


def swin_band(flow, wait, bias_ref, gain_ref, weight_refs, scratch):
    qkv_ref, proj_ref, up_ref, down_ref = weight_refs
    mixed_ref, score_ref, prob_ref, *active_ref = scratch
    count = flow.shape[0] // SPAN
    pairs = HEADS // 2
    depth = D // HEADS
    wide = 2 * depth
    normed = layer_norm(flow, gain_ref[0:1, :])
    scale = 1.0 / math.sqrt(depth)
    wait((0,))
    mixed_ref[:, :D] = (mm(normed, qkv_ref[:, :D]) * scale).astype(BF16)
    mixed_ref[:, D : 2 * D] = mm(normed, qkv_ref[:, D : 2 * D]).astype(BF16)
    mixed_ref[:, 2 * D :] = mm(normed, qkv_ref[:, 2 * D :]).astype(BF16)
    lower = lax.broadcasted_iota(jnp.int32, (SPAN, wide), 1) < depth

    def scores_of(w):
        rows = slice(w * SPAN, (w + 1) * SPAN)
        for p in range(pairs):
            query = mixed_ref[rows, p * wide : (p + 1) * wide]
            key = mixed_ref[rows, D + p * wide : D + (p + 1) * wide]
            zero = jnp.zeros_like(query)
            split = jnp.concatenate(
                [jnp.where(lower, query, zero), jnp.where(lower, zero, query)], axis=0
            )
            score_ref[w, :, p * wide : (p + 1) * wide] = mm(key, split, NT)

    def probs_of(w):
        bias = bias_ref[w]
        for p in range(pairs):
            lanes = slice(p * wide, (p + 1) * wide)
            scores = score_ref[w, :, lanes] + bias
            weights = jnp.exp(scores - jnp.max(scores, axis=0, keepdims=True))
            share = 1.0 / jnp.sum(weights, axis=0, keepdims=True)
            prob_ref[w, :, lanes] = (weights * share).astype(BF16)

    def mixture_of(w):
        rows = slice(w * SPAN, (w + 1) * SPAN)
        for p in range(pairs):
            lanes = slice(p * wide, (p + 1) * wide)
            value = mixed_ref[rows, 2 * D + p * wide : 2 * D + (p + 1) * wide]
            mixture = mm(prob_ref[w, :, lanes], value, TN)
            mixed_ref[rows, lanes] = jnp.where(lower, mixture[:SPAN], mixture[SPAN:]).astype(BF16)

    for turn in range(count + 2):
        if turn < count:
            scores_of(turn)
        if 0 <= turn - 1 < count:
            probs_of(turn - 1)
        if 0 <= turn - 2:
            mixture_of(turn - 2)
    wait((1, 2, 3))
    flow = flow + mm(mixed_ref[:, :D], proj_ref[...])
    normed = layer_norm(flow, gain_ref[1:2, :])
    chunks = up_ref.shape[1] // D
    if active_ref:
        for c in range(chunks):
            part = slice(c * D, (c + 1) * D)
            active_ref[0][:, part] = gelu_twice(mm(normed, up_ref[:, part]))
        return flow + 0.5 * mm(active_ref[0][...], down_ref[...])
    total = jnp.zeros_like(flow)
    ahead = mm(normed, up_ref[:, :D])
    for c in range(chunks):
        value = ahead
        if c + 1 < chunks:
            ahead = mm(normed, up_ref[:, (c + 1) * D : (c + 2) * D])
        total = total + mm(gelu_twice(value), down_ref[c * D : (c + 1) * D, :])
    return flow + 0.5 * total


def rolled_band(sign, shift_ref, refs, rows, count=WIN):
    main_ref, side_ref, edge_ref, corner_ref = refs
    cols = main_ref.shape[1]
    top = pl.program_id(0) * count + sign * shift_ref[0]
    behind = -rows if sign > 0 else WIN
    beside = -cols if sign > 0 else WIN

    def pick(width, offset):
        source = lax.broadcasted_iota(jnp.int32, (cols, width), 1)
        wanted = lax.broadcasted_iota(jnp.int32, (cols, width), 0) + sign * shift_ref[1] + offset
        return jnp.where(source == wanted, 1.0, 0.0).astype(BF16)

    pick_main, pick_side = pick(cols, 0), pick(WIN, beside)
    band = []
    for j in range(count):
        row = top + j
        inside = (row >= 0) & (row < rows)
        here, there = jnp.clip(row, 0, rows - 1), jnp.clip(row + behind, 0, WIN - 1)
        main = jnp.where(inside, main_ref[here], edge_ref[there])
        side = jnp.where(inside, side_ref[here], corner_ref[there])
        band.append(mm(pick_main, main) + mm(pick_side, side))
    return jnp.stack(band)


def first_kernel(zeta, sigma, count, parts, rows, before, *refs):
    shift_ref, state_ref, *refs = refs
    if before is not None:
        back_refs, refs = refs[:4], refs[4:]
    grad_refs, refs = refs[: count * parts], refs[count * parts :]
    if sigma is not None:
        noise_ref, *refs = refs
    bias_ref, embed_ref, gain_ref, *sources = refs[:7]
    base_ref, out_ref, side_ref, edge_ref, corner_ref, *scratch = refs[7:]
    targets, sems, scratch = scratch[:4], scratch[4], scratch[5:]
    wait = load_weights(0, sources, targets, sems)
    state = state_ref[...]
    if before is not None:
        state = state - before * rolled_band(-1, shift_ref, back_refs, rows)
    turn = pl.program_id(0) ^ shift_ref[2]
    grad = 0.0
    if parts == 1:
        grad = grad_refs[0][...].astype(F32)
        count = 0
    for n in range(0, count * parts, parts):
        piece = grad_refs[n][...]
        for m in range(1, parts):
            piece = jnp.where(turn == m, grad_refs[n + m][...], piece)
        grad = grad + piece.astype(F32)
    step = zeta * grad
    half = state - step
    tokens = mm(to_windows(half).astype(BF16), embed_ref[...]).astype(BF16).astype(F32)
    flow = swin_band(tokens, wait, bias_ref, gain_ref, targets, scratch)
    result = from_windows(flow, half.shape[1]).astype(BF16)
    out_ref[:, :, :D] = result
    side_ref[:, :, :D] = result[:, :WIN]
    if sigma is None:
        base_ref[...] = half
    else:
        noise = sigma * noise_ref[...]
        base_ref[...] = half + noise
        change = (noise - step).astype(BF16)
        out_ref[:, :, D:] = change
        side_ref[:, :, D:] = change[:, :WIN]

    @pl.when(pl.program_id(0) == 0)
    def _():
        edge_ref[...] = out_ref[...]
        corner_ref[...] = side_ref[...]


def write_pieces(turn, refs, value):
    for m, ref in enumerate(refs):

        def write(ref=ref):
            ref[...] = value

        pl.when(turn == m)(write)


def second_kernel(sigma, rows, parts, *refs):
    shift_ref, *refs = refs
    tile_refs, refs = refs[:4], refs[4:]
    bias_ref, unembed_ref, gain_ref, *sources = refs[:7]
    out_ref, side_ref, edge_ref, corner_ref, *scratch = refs[7:]
    state_refs, scratch = scratch[:parts], scratch[parts:]
    targets, sems, scratch = scratch[:4], scratch[4], scratch[5:]
    wait = load_weights(1, sources, targets, sems)
    height, cols, _ = out_ref.shape
    band = rolled_band(1, shift_ref, tile_refs, rows, height)
    tokens = to_windows(band[:, :, :D])
    flow = swin_band(tokens, wait, bias_ref, gain_ref, targets, scratch)
    estimate = from_windows(mm(flow.astype(BF16), unembed_ref[...]), cols)
    narrow = estimate.astype(BF16)
    out_ref[...] = narrow
    side_ref[...] = narrow[:, cols - WIN :]
    edge_ref[...] = narrow[height - WIN :]
    corner_ref[...] = narrow[height - WIN :, cols - WIN :]
    if parts > 0:
        change = (band[:, :, D:] - sigma * estimate).astype(BF16)
        for n in range(height // WIN):
            turn = (pl.program_id(0) * (height // WIN) + n) ^ shift_ref[2]
            write_pieces(turn, state_refs, change[n * WIN : (n + 1) * WIN])


def whole(array):
    zeros = (0,) * array.ndim
    return pl.BlockSpec(array.shape, lambda *_: zeros)


def member(array, j):
    place = (j,) + (0,) * (array.ndim - 1)
    return pl.BlockSpec((None,) + array.shape[1:], lambda *_: place)


def band_spec(cols, feats, height=WIN):
    return pl.BlockSpec((height, cols, feats), lambda n, *_: (n, 0, 0))


def bias_spec(cols, height=WIN):
    count = height * cols // SPAN
    return pl.BlockSpec((count, SPAN, 2 * SPAN), lambda n, *_: (n, 0, 0))


def band_scratch(cols, weights, height=WIN):
    count = height * cols // SPAN
    return [pltpu.VMEM(value.shape[1:], BF16) for value in weights] + [
        pltpu.SemaphoreType.DMA((len(weights),)),
        pltpu.VMEM((height * cols, 3 * D), BF16),
        pltpu.VMEM((count, SPAN, HEADS * SPAN), F32),
        pltpu.VMEM((count, SPAN, HEADS * SPAN), BF16),
    ]


def strip_outs(rows, cols, feats, height=WIN):
    specs = [band_spec(cols, feats, height), band_spec(WIN, feats, height)]
    specs += [
        pl.BlockSpec((WIN, width, feats), lambda *_: (0, 0, 0)) for width in (cols, WIN)
    ]
    shapes = [(rows, cols), (rows, WIN), (WIN, cols), (WIN, WIN)]
    return specs, [jax.ShapeDtypeStruct(shape + (feats,), BF16) for shape in shapes]


def first_block(zeta, sigma, state, before, shift, back, grads, noise, bias, w_embed, weights):
    *weights, gains = weights
    rows, cols, _ = state.shape
    parts = len(grads[0])
    pieces = [piece for grad in grads for piece in grad]
    fields = [] if sigma is None else [noise]
    feats = D if sigma is None else D + PIXELS
    specs, shapes = strip_outs(rows, cols, feats)
    return pl.pallas_call(
        functools.partial(first_kernel, zeta, sigma, len(grads), parts, rows, before),
        grid_spec=pltpu.PrefetchScalarGridSpec(
            num_scalar_prefetch=1,
            grid=(rows // WIN,),
            in_specs=[band_spec(cols, PIXELS)]
            + [whole(value) for value in back]
            + [band_spec(cols, PIXELS) if parts == 1 else whole(value) for value in pieces]
            + [band_spec(cols, PIXELS)] * len(fields)
            + [bias_spec(cols), whole(w_embed), member(gains, 0)]
            + [pl.BlockSpec(memory_space=pl.ANY)] * len(weights),
            out_specs=[band_spec(cols, PIXELS)] + specs,
            scratch_shapes=band_scratch(cols, weights),
        ),
        out_shape=[jax.ShapeDtypeStruct((rows, cols, PIXELS), F32)] + shapes,
        compiler_params=PARAMS,
    )(shift, state, *back, *pieces, *fields, bias, w_embed, gains, *weights)


def second_block(sigma, shift, tile, bias, w_unembed, weights, parts):
    *weights, gains = weights
    rows, cols, _ = tile[0].shape
    height = 2 * WIN
    specs, shapes = strip_outs(rows, cols, PIXELS, height)
    specs += [pl.BlockSpec((WIN, cols, PIXELS), lambda *_: (0, 0, 0))] * parts
    shapes += [jax.ShapeDtypeStruct((WIN, cols, PIXELS), BF16)] * parts
    return pl.pallas_call(
        functools.partial(second_kernel, sigma, rows, parts),
        grid_spec=pltpu.PrefetchScalarGridSpec(
            num_scalar_prefetch=1,
            grid=(rows // height,),
            in_specs=[whole(value) for value in tile]
            + [bias_spec(cols, height), whole(w_unembed), member(gains, 1)]
            + [pl.BlockSpec(memory_space=pl.ANY)] * len(weights),
            out_specs=specs,
            scratch_shapes=band_scratch(cols, weights, height)
            + [pltpu.VMEM((height * cols, weights[2].shape[2]), BF16)],
        ),
        out_shape=shapes,
        compiler_params=PARAMS,
    )(shift, *tile, bias, w_unembed, gains, *weights)


def from_neighbours(tile, by):
    main, side, edge, corner = tile
    ty, tx = lax.axis_size("ty"), lax.axis_size("tx")
    across = [
        (i * tx + k, (i + by) % ty * tx + (k + by) % tx) for i in range(ty) for k in range(tx)
    ]
    return (
        main,
        lax.ppermute(side, "tx", [(k, (k + by) % tx) for k in range(tx)]),
        lax.ppermute(edge, "ty", [(i, (i + by) % ty) for i in range(ty)]),
        lax.ppermute(corner, ("ty", "tx"), across),
    )


def windows_of(grid):
    rows, cols = grid.shape
    shaped = grid.reshape(rows // WIN, WIN, cols // WIN, WIN).transpose(0, 2, 1, 3)
    return shaped.reshape(rows // WIN * (cols // WIN), SPAN)


def bias_of(labels, keep):
    allowed = jnp.ones((1, SPAN, SPAN), bool)
    if labels is not None:
        label = windows_of(labels)
        allowed = label[:, :, None] == label[:, None, :]
    if keep is not None:
        kept = windows_of(keep)[:, :, None] == 1
        allowed = allowed & (kept | jnp.eye(SPAN, dtype=bool)[None])
    bias = jnp.where(allowed, 0.0, -1e30).astype(F32)
    return jnp.concatenate([bias, bias], axis=2)


def region(index, shift):
    return jnp.where(index < TOK - WIN, 0, jnp.where(index < TOK - shift, 1, 2)).astype(jnp.int32)


@functools.lru_cache(maxsize=None)
def lane_order(cols):
    parts = LANES // cols
    groups = PATCH // parts
    lane = np.arange(PATCH * cols)
    g, h, k = lane // LANES, lane % LANES // cols, lane % cols
    source = PATCH * k + h * groups + g
    matrix = np.zeros((PATCH * cols, PATCH * cols), np.float32)
    matrix[source, lane] = 1.0
    return matrix.astype(ml_dtypes.bfloat16), np.ascontiguousarray(matrix.T).astype(
        ml_dtypes.bfloat16
    )


def move_lanes(values, matrix):
    high = values.astype(BF16)
    low = (values - high.astype(F32)).astype(BF16)
    return mm(high, matrix) + mm(low, matrix)


def to_patches_kernel(narrow, place_ref, tile_ref, order_ref, *out_refs):
    count, cols, _ = out_refs[0].shape
    parts = LANES // cols
    groups = PATCH // parts
    if narrow:
        ordered = mm(tile_ref[...].astype(BF16), order_ref[...])
    else:
        ordered = move_lanes(tile_ref[...], order_ref[...])
    patches = []
    for i in range(count):
        band = ordered[i * PATCH : (i + 1) * PATCH]
        stacked = jnp.concatenate(
            [band[:, g * LANES : (g + 1) * LANES] for g in range(groups)], axis=0
        )
        turned = stacked.T
        patches.append(
            jnp.concatenate([turned[h * cols : (h + 1) * cols] for h in range(parts)], axis=1)
        )
    result = jnp.stack(patches).astype(out_refs[0].dtype)
    if len(out_refs) == 1:
        out_refs[0][...] = result
    else:
        write_pieces(pl.program_id(0) ^ place_ref[2], out_refs, result)


def to_tile_kernel(sigma, scale, rows, *refs):
    shift_ref, base_ref, *refs = refs
    noise_ref, order_ref, out_ref = refs[4:]
    count, cols, _ = base_ref.shape
    parts = LANES // cols
    groups = PATCH // parts
    width = groups * PATCH
    state = base_ref[...] - sigma * rolled_band(-1, shift_ref, refs[:4], rows)
    bands = []
    for i in range(count):
        stacked = jnp.concatenate(
            [state[i, :, h * width : (h + 1) * width] for h in range(parts)], axis=0
        )
        turned = stacked.T
        bands.append(
            jnp.concatenate([turned[g * PATCH : (g + 1) * PATCH] for g in range(groups)], axis=1)
        )
    moved = move_lanes(jnp.concatenate(bands, axis=0), order_ref[...])
    out_ref[...] = moved + scale * noise_ref[...]


def patches_of(tiles, j, place, kind=F32, parts=1):
    rows, cols = tiles.shape[1] // PATCH, tiles.shape[2] // PATCH
    order = jnp.asarray(lane_order(cols)[0])
    spec, shape = band_spec(cols, PIXELS), (rows, cols, PIXELS)
    if parts > 1:
        spec = pl.BlockSpec((WIN, cols, PIXELS), lambda *_: (0, 0, 0))
        shape = (WIN, cols, PIXELS)
    return pl.pallas_call(
        functools.partial(to_patches_kernel, kind == BF16),
        grid_spec=pltpu.PrefetchScalarGridSpec(
            num_scalar_prefetch=1,
            grid=(rows // WIN,),
            in_specs=[
                pl.BlockSpec((None, WIN * PATCH, cols * PATCH), lambda n, *_: (j, n, 0)),
                whole(order),
            ],
            out_specs=[spec] * parts,
        ),
        out_shape=[jax.ShapeDtypeStruct(shape, kind)] * parts,
        compiler_params=PARAMS,
    )(place, tiles, order)


def tile_of(base, sigma, shift, back, scale, noise, j):
    rows, cols, _ = base.shape
    order = jnp.asarray(lane_order(cols)[1])
    return pl.pallas_call(
        functools.partial(to_tile_kernel, sigma, scale, rows),
        grid_spec=pltpu.PrefetchScalarGridSpec(
            num_scalar_prefetch=1,
            grid=(rows // WIN,),
            in_specs=[band_spec(cols, PIXELS)]
            + [whole(value) for value in back]
            + [
                pl.BlockSpec((None, WIN * PATCH, cols * PATCH), lambda n, *_: (j, n, 0)),
                whole(order),
            ],
            out_specs=pl.BlockSpec((WIN * PATCH, cols * PATCH), lambda n, *_: (n, 0)),
        ),
        out_shape=jax.ShapeDtypeStruct((rows * PATCH, cols * PATCH), F32),
        compiler_params=PARAMS,
    )(shift, base, *back, noise, order)


def per_device(
    image, noise, offsets, key_mask, gains, observed, vis_weight,
    w_embed, w_qkv, w_proj, w_up, w_down, w_unembed, norm_gains,
):
    rows = image.shape[0] // PATCH
    cols = image.shape[1] // PATCH
    devices = lax.axis_size("ty") * lax.axis_size("tx")
    lanes = lax.axis_size("tx")
    fast = N // devices == TOK // 2 and rows == lanes * WIN and lanes & (lanes - 1) == 0
    places = [
        jnp.concatenate([offsets[step], lax.axis_index("tx")[None]]).astype(jnp.int32)
        for step in range(STEPS)
    ]
    row_index = lax.axis_index("ty") * rows + counting(rows)
    col_index = lax.axis_index("tx") * cols + counting(cols)
    weights = (w_qkv, w_proj, w_up, w_down, norm_gains)
    w_embed = w_embed.reshape(PATCH, PATCH, D).transpose(1, 0, 2).reshape(PIXELS, D)
    w_unembed = w_unembed.reshape(D, PATCH, PATCH).transpose(0, 2, 1).reshape(D, PIXELS)
    state = patches_of(image[None], 0, places[0])[0]
    extras = [patches_of(noise, step, places[0])[0] for step in range(STEPS - 1)] + [None]
    first_bias = bias_of(None, key_mask)
    biases = []
    for step in range(STEPS):
        labels = (
            3 * region(row_index, offsets[step, 0])[:, None]
            + region(col_index, offsets[step, 1])[None, :]
        )
        biases.append(bias_of(labels, None))
    beside = (state, extras, first_bias, biases, w_embed, w_unembed)
    shift, before, back, moving, mirror = places[0], None, (), None, None
    grads = []
    if fast:
        weight, scale, data = spectrum_inputs(gains, observed, vis_weight, devices)
        half = weight.shape[0] // 2
        lines = (weight[half:], weight[:1])
        grad, (beside, lines) = patch_gradient(
            patches_of(image[None], 0, places[0], BF16, lanes), scale, data, None, None,
            (beside, lines),
        )
        grad, lines = lax.optimization_barrier((grad, lines))
        mirror = mirrored_exchange(*lines, devices)
        grads = [grad]
        state, extras, first_bias, biases, w_embed, w_unembed = beside
    for step in range(STEPS):
        if not fast:
            tile = image if step == 0 else tile_of(state, before, shift, back, 0.0, noise, 0)
            grad = plain_gradient(tile, gains, observed, vis_weight)
            grad = patches_of(grad.astype(F32)[None], 0, places[0], BF16)[0]
            grads = [[grad]]
        elif step > 0:
            grad, back = patch_gradient(moving, scale, None, shift, mirror, back)
            grads = grads + [grad]
        last = step + 1 == STEPS
        sigma = None if last else SIGMAS[step + 1]
        state, *first = first_block(
            STEP_SIZES[step], sigma, state, before, shift, back, grads, extras[step], first_bias,
            w_embed, weights,
        )
        shift, before = places[step], SIGMAS[step]
        if fast and step == 0:
            first, mirror = lax.optimization_barrier((first, mirror))
        rolled = second_block(
            before, shift, from_neighbours(first, -1), biases[step], w_unembed, weights,
            lanes if fast and not last else 0,
        )
        rolled, moving = rolled[:4], rolled[4:]
        back = from_neighbours(rolled, 1)
    return tile_of(state, before, shift, back, SIGMAS[STEPS], noise, STEPS - 1)


def solution(mesh):
    in_specs = (
        P("ty", "tx"),
        P(None, "ty", "tx"),
        P(),
        P("ty", "tx"),
        P(None, ("ty", "tx"), None),
        P(None, ("ty", "tx"), None),
        P(("ty", "tx"), None),
        P(),
        P(),
        P(),
        P(),
        P(),
        P(),
        P(),
    )
    out_specs = P("ty", "tx")
    return jax.shard_map(
        per_device, mesh=mesh, in_specs=in_specs, out_specs=out_specs, check_vma=False
    )
```

```python
import functools
import math

import jax
import jax.numpy as jnp
import ml_dtypes
import numpy as np
from jax import lax
from jax.experimental import pallas as pl
from jax.experimental.pallas import tpu as pltpu
from jax.sharding import PartitionSpec as P

N = 4096
PATCH = 16
PIXELS = PATCH * PATCH
WIN = 8
D = 512
HEADS = 8
STEPS = 2
SPAN = WIN * WIN
LANES = 128
GROUP = 8
TOK = N // PATCH

SIGMAS = (0.8, 0.5, 0.3)
STEP_SIZES = (0.9, 0.7)
EPSILON = 1e-05
HIGHEST = lax.Precision.HIGHEST
BF16 = jnp.bfloat16
F32 = jnp.float32
GELU_IN = math.sqrt(2.0 / math.pi)
GELU_CUBE = 0.044715 * GELU_IN
VMEM_LIMIT = 56 * 1024 * 1024
PARAMS = pltpu.CompilerParams(vmem_limit_bytes=VMEM_LIMIT)
TN = (((0,), (0,)), ((), ()))
NT = (((1,), (1,)), ((), ()))
NN = (((1,), (0,)), ((), ()))


def mm(left, right, dims=NN):
    return lax.dot_general(left, right, dims, preferred_element_type=F32)


def counting(length):
    return jnp.arange(length, dtype=jnp.int32)


def roots(length, outer, inner, sign):
    product = outer[:, None] * inner[None, :] % length
    angle = 2.0 * math.pi / length * product.astype(F32)
    return (jnp.cos(angle), sign * jnp.sin(angle))


def complex_einsum(form, left, right):
    real = jnp.einsum(form, left[0], right[0], precision=HIGHEST) - jnp.einsum(
        form, left[1], right[1], precision=HIGHEST
    )
    imag = jnp.einsum(form, left[0], right[1], precision=HIGHEST) + jnp.einsum(
        form, left[1], right[0], precision=HIGHEST
    )
    return (real, imag)


def complex_times(left, right):
    return (left[0] * right[0] - left[1] * right[1], left[0] * right[1] + left[1] * right[0])


def along_last(real_part, imag_part, groups, sign):
    rows, length = real_part.shape
    inner = length // groups
    first = roots(groups, counting(groups), counting(groups), sign)
    twist = roots(length, counting(inner), counting(groups), sign)
    second = roots(inner, counting(inner), counting(inner), sign)
    shaped = real_part.reshape(rows, groups, inner)
    if imag_part is None:
        partial_value = (
            jnp.einsum("mab,ka->mbk", shaped, first[0], precision=HIGHEST),
            jnp.einsum("mab,ka->mbk", shaped, first[1], precision=HIGHEST),
        )
    else:
        partial_value = complex_einsum(
            "mab,ka->mbk", (shaped, imag_part.reshape(rows, groups, inner)), first
        )
    partial_value = complex_times(partial_value, twist)
    result = complex_einsum("jb,mbk->mjk", second, partial_value)
    return (result[0].reshape(rows, length), result[1].reshape(rows, length))


def across_groups(pair, groups, sign):
    inner, cols = pair[0].shape
    width = cols // groups
    length = groups * inner
    first = roots(groups, counting(groups), counting(groups), sign)
    twist = roots(length, counting(inner), counting(groups), sign)
    second = roots(inner, counting(inner), counting(inner), sign)
    shaped = (pair[0].reshape(inner, groups, width), pair[1].reshape(inner, groups, width))
    partial_value = complex_einsum("bhc,kh->cbk", shaped, first)
    partial_value = complex_times(partial_value, twist)
    result = complex_einsum("jb,cbk->cjk", second, partial_value)
    return (result[0].reshape(width, length), result[1].reshape(width, length))


def exchange_pair(pair):
    return tuple(
        lax.all_to_all(
            part.astype(BF16), ("ty", "tx"), split_axis=1, concat_axis=1, tiled=True
        ).astype(F32)
        for part in pair
    )


def plain_gradient(tile, gains, observed, vis_weight):
    devices = lax.axis_size("ty") * lax.axis_size("tx")
    slab = lax.all_to_all(tile.astype(BF16), "tx", split_axis=0, concat_axis=1, tiled=True)
    moved = exchange_pair(along_last(slab.astype(F32), None, devices, -1.0))
    spectrum = across_groups(moved, devices, -1.0)
    spectrum = (spectrum[0] * (1.0 / N), spectrum[1] * (1.0 / N))
    model = complex_times((gains[0], gains[1]), spectrum)
    misfit = (vis_weight * (model[0] - observed[0]), vis_weight * (model[1] - observed[1]))
    back = complex_times((gains[0], -gains[1]), misfit)
    returned = exchange_pair(along_last(back[0], back[1], devices, 1.0))
    slab_grad = across_groups(returned, devices, 1.0)[0] * (1.0 / N)
    return lax.all_to_all(slab_grad.astype(BF16), "tx", split_axis=1, concat_axis=0, tiled=True)


def embed_complex(angle, row_axis, col_axis):
    cos, sin = np.cos(angle), np.sin(angle)
    top = np.stack([cos, sin], axis=col_axis)
    bottom = np.stack([-sin, cos], axis=col_axis)
    return np.stack([top, bottom], axis=row_axis)


def wheel(length, product):
    return 2.0 * math.pi / length * (product % length)


@functools.lru_cache(maxsize=None)
def row_constants():
    k = np.arange(TOK)
    angle = wheel(TOK, k[:, None] * k[None, :])
    first = np.concatenate([np.cos(angle), -np.sin(angle)], axis=1)
    b = np.repeat(np.arange(PATCH), PATCH)
    angle = wheel(N, b[:, None] * k[None, :])
    twist = np.stack([np.cos(angle), -np.sin(angle)])
    p = np.arange(PATCH)
    small = embed_complex(wheel(PATCH, p[:, None] * p[None, :]), 1, 1)
    second = np.einsum("kpqb,xy->kpxqby", small, np.eye(PATCH)).reshape(2 * PIXELS, 2 * PIXELS)
    return (
        first.astype(ml_dtypes.bfloat16),
        twist.astype(np.float32),
        second.astype(ml_dtypes.bfloat16),
        np.ascontiguousarray(second.T).astype(ml_dtypes.bfloat16),
    )


@functools.lru_cache(maxsize=None)
def half_constants():
    _, twist, second, _ = row_constants()
    half, quarter = TOK // 2, TOK // 4
    low = np.concatenate([1 + np.arange(quarter), 1 + half + np.arange(quarter)])
    digits = np.concatenate([low, low - 1])
    k = np.arange(TOK)
    angle = wheel(TOK, k[:, None] * digits[None, :])
    first = np.concatenate([np.cos(angle), -np.sin(angle)], axis=1)
    zero_line = np.concatenate([np.tile(np.eye(PATCH), PATCH), np.zeros((PATCH, PIXELS))], axis=1)
    upper = np.concatenate([second[PIXELS:].astype(np.float32), zero_line])
    lower = second[:PIXELS].astype(np.float32)
    return (first.astype(ml_dtypes.bfloat16), np.ascontiguousarray(twist[:, :, digits])) + tuple(
        np.ascontiguousarray(value).astype(ml_dtypes.bfloat16)
        for value in (lower, upper, lower.T, upper.T)
    )


@functools.lru_cache(maxsize=None)
def column_constants(devices, rows):
    s = np.arange(devices)
    small = embed_complex(wheel(devices, s[:, None] * s[None, :]), 1, 2)
    wide = devices * 2 * GROUP
    outer = np.einsum("qpsr,xy->qpxsry", small, np.eye(GROUP)).reshape(wide, wide)
    kr = s[:, None] + devices * np.arange(rows)[None, :]
    angle = wheel(N, kr[:, :, None] * np.arange(rows)[None, None, :])
    inner = embed_complex(angle, 1, 2).reshape(devices, 2 * rows, 2 * rows) / N
    return tuple(
        np.ascontiguousarray(value).astype(ml_dtypes.bfloat16)
        for value in (outer, outer.T, inner, inner.transpose(0, 2, 1))
    )


def row_forward(*refs):
    *x_refs, first_ref, twist_ref, second_ref, out_ref = refs
    count = x_refs[0].shape[0]

    def step(i, carry):
        band = jnp.concatenate([x_ref[i] for x_ref in x_refs], axis=0)
        mixed = mm(band, first_ref[...], TN)
        real, imag = mixed[:, :TOK], mixed[:, TOK:]
        tr, ti = twist_ref[0], twist_ref[1]
        turned = jnp.concatenate(
            [(real * tr - imag * ti).astype(BF16), (real * ti + imag * tr).astype(BF16)], axis=0
        )
        result = mm(second_ref[...], turned).astype(BF16).reshape(PATCH, 2, PATCH, TOK)
        half = TOK // 2
        rows = pl.ds(pl.multiple_of(i * PATCH, PATCH), PATCH)
        out_ref[:, 0, :, rows, :] = result[..., :half]
        out_ref[:, 1, :, rows, :] = result[..., half:]
        return carry

    lax.fori_loop(0, count, step, 0, unroll=4)


def row_inverse(v_ref, first_ref, twist_ref, second_ref, *out_refs):
    count, cols, _ = out_refs[0].shape

    def step(i, carry):
        rows = pl.ds(pl.multiple_of(i * PATCH, PATCH), PATCH)
        wide = jnp.concatenate(
            [
                v_ref[:, 0, :, rows, :].reshape(2 * PIXELS, TOK // 2),
                v_ref[:, 1, :, rows, :].reshape(2 * PIXELS, TOK // 2),
            ],
            axis=1,
        )
        mixed = mm(second_ref[...], wide)
        real, imag = mixed[:PIXELS], mixed[PIXELS:]
        tr, ti = twist_ref[0], twist_ref[1]
        turned = jnp.concatenate(
            [(real * tr + imag * ti).astype(BF16), (imag * tr - real * ti).astype(BF16)], axis=1
        )
        result = mm(first_ref[...], turned, NT).astype(BF16)
        for m, out_ref in enumerate(out_refs):
            out_ref[i] = result[m * cols : (m + 1) * cols]
        return carry

    lax.fori_loop(0, count, step, 0, unroll=4)


def lane_index(shape):
    return lax.broadcasted_iota(jnp.int32, shape, len(shape) - 1)


def swap_halves(values):
    return pltpu.roll(values, values.shape[-1] // 2, len(values.shape) - 1)


def row_forward_half(*refs):
    *x_refs, first_ref, twist_ref, lower_ref, upper_ref, out_ref = refs
    count = x_refs[0].shape[0]
    half = TOK // 2

    def packed(real, imag, rows, high):
        left = lane_index(real.shape) < half // 2
        out_ref[high, 0, rows, :] = jnp.where(left, real, swap_halves(imag)).astype(BF16)
        out_ref[high, 1, rows, :] = jnp.where(left, swap_halves(real), imag).astype(BF16)

    def step(i, carry):
        band = jnp.concatenate([x_ref[i] for x_ref in x_refs], axis=0)
        mixed = mm(band, first_ref[...], TN)
        real, imag = mixed[:, :TOK], mixed[:, TOK:]
        tr, ti = twist_ref[0], twist_ref[1]
        turned = jnp.concatenate(
            [(real * tr - imag * ti).astype(BF16), (real * ti + imag * tr).astype(BF16)], axis=0
        )
        rows = pl.ds(pl.multiple_of(i * PATCH, PATCH), PATCH)
        lower = mm(lower_ref[...], turned[:, :half]).reshape(PATCH // 2, 2, PATCH, half)
        packed(lower[:, 0], lower[:, 1], rows, slice(0, PATCH // 2))
        upper = mm(upper_ref[...], turned[:, half:])
        line = upper[PIXELS:]
        upper = upper[:PIXELS].reshape(PATCH // 2, 2, PATCH, half)
        imag = upper[:, 1]
        head = jnp.where(lane_index(line.shape) == 0, line, imag[0])
        imag = jnp.concatenate([head[None], imag[1:]], axis=0)
        packed(upper[:, 0], imag, rows, slice(PATCH // 2, PATCH))
        return carry

    lax.fori_loop(0, count, step, 0, unroll=4)


def row_inverse_half(v_ref, first_ref, twist_ref, lower_ref, upper_ref, *out_refs):
    count, cols, _ = out_refs[0].shape
    half = TOK // 2

    def unpacked(rows, high):
        even = v_ref[high, 0, rows, :].astype(F32)
        odd = v_ref[high, 1, rows, :].astype(F32)
        left = lane_index(even.shape) < half // 2
        return jnp.where(left, even, swap_halves(odd)), jnp.where(left, swap_halves(even), odd)

    def step(i, carry):
        rows = pl.ds(pl.multiple_of(i * PATCH, PATCH), PATCH)
        real, imag = unpacked(rows, slice(0, PATCH // 2))
        lower = jnp.stack([real, imag], axis=1).reshape(PIXELS, half)
        real, imag = unpacked(rows, slice(PATCH // 2, PATCH))
        head = imag[0]
        at_zero = lane_index(head.shape) == 0
        nothing = jnp.zeros_like(head)
        imag = jnp.concatenate([jnp.where(at_zero, nothing, head)[None], imag[1:]], axis=0)
        upper = jnp.stack([real, imag], axis=1).reshape(PIXELS, half)
        upper = jnp.concatenate([upper, jnp.where(at_zero, head, nothing)], axis=0)
        mixed = jnp.concatenate(
            [mm(lower_ref[...], lower.astype(BF16)), mm(upper_ref[...], upper.astype(BF16))], axis=1
        )
        real, imag = mixed[:PIXELS], mixed[PIXELS:]
        tr, ti = twist_ref[0], twist_ref[1]
        turned = jnp.concatenate(
            [(real * tr + imag * ti).astype(BF16), (imag * tr - real * ti).astype(BF16)], axis=1
        )
        result = mm(first_ref[...], turned, NT).astype(BF16)
        for m, out_ref in enumerate(out_refs):
            out_ref[i] = result[m * cols : (m + 1) * cols]
        return carry

    lax.fori_loop(0, count, step, 0, unroll=4)


def column_kernel(halved, *refs):
    if halved:
        flag_ref, phase_ref, refs = refs[0], refs[1], refs[2:]
    x_ref, outer_ref, *refs = refs
    count = 4 if halved else 5
    sources, out_ref = refs[:count], refs[count]
    mid_ref, *targets, sems = refs[count + 1 :]
    copies = [
        pltpu.make_async_copy(source, target, sems.at[n])
        for n, (source, target) in enumerate(zip(sources, targets))
    ]
    for copy in copies:
        copy.start()
    inner_ref, scale_ref, inner_t_ref, outer_t_ref = targets[:4]
    devices, _, rows, width = mid_ref.shape
    wide = devices * 2 * GROUP
    if halved:
        lane = lane_index((devices, PATCH, width))
        centre = flag_ref[0] == 1
        half = width // 2
        hidden = (lane == half) | (centre & (lane == 0))
        real_lane = (lane < half) | (centre & (lane == half))

    def load(place):
        if not halved:
            return x_ref[:, :, place, :].astype(F32)
        piece = x_ref[:, place, :].astype(F32)
        other = swap_halves(piece)
        return jnp.stack([piece, jnp.where(hidden, jnp.zeros_like(other), other)], axis=1)

    def store(place, value):
        if halved:
            value = jnp.where(real_lane, value[:, 0], swap_halves(value[:, 1])).astype(BF16)
            out_ref[:, place, :] = value
        else:
            out_ref[:, :, place, :] = value.astype(BF16)

    def outer(matrix_ref, value):
        groups = [
            value[:, :, n : n + GROUP, :].reshape(wide, width) for n in range(0, PATCH, GROUP)
        ]
        result = mm(matrix_ref[...], jnp.concatenate(groups, axis=1).astype(BF16))
        parts = [
            result[:, n : n + width].reshape(devices, 2, GROUP, width)
            for n in range(0, result.shape[1], width)
        ]
        return jnp.concatenate(parts, axis=2)

    for top in range(0, rows, PATCH):
        place = slice(top, top + PATCH)
        mid_ref[:, :, place, :] = outer(outer_ref, load(place)).astype(BF16)

    for n, copy in enumerate(copies):
        if n != 3:
            copy.wait()

    def step(q, carry):
        spectrum = mm(inner_ref[q], mid_ref[q].reshape(2 * rows, width))
        real, imag = spectrum[:rows], spectrum[rows:]
        scale = scale_ref[q].astype(F32)
        if halved:
            pr, pi = phase_ref[q, 0], phase_ref[q, 1]
            real = real.reshape(rows // 8, 8, width)
            imag = imag.reshape(rows // 8, 8, width)
            real, imag = real * pr - imag * pi, real * pi + imag * pr
            real, imag = real.reshape(rows, width) * scale, imag.reshape(rows, width) * scale
        else:
            data_ref = targets[4]
            real = real * scale - data_ref[0, q].astype(F32)
            imag = imag * scale - data_ref[1, q].astype(F32)
        back = jnp.concatenate([real.astype(BF16), imag.astype(BF16)], axis=0)
        mid_ref[q] = mm(inner_t_ref[q], back).astype(BF16).reshape(2, rows, width)
        return carry

    lax.fori_loop(0, devices, step, 0, unroll=8)
    copies[3].wait()

    for top in range(0, rows, PATCH):
        place = slice(top, top + PATCH)
        store(place, outer(outer_t_ref, mid_ref[:, :, place, :].astype(F32)))


def turned(value, devices):
    lines = value.shape[0]
    return value.astype(BF16).reshape(lines, N // devices, devices).transpose(2, 1, 0)


def spectrum_inputs(gains, observed, vis_weight, devices):
    gr, gi = gains[0], gains[1]
    weight = (vis_weight * (gr * gr + gi * gi)).astype(BF16)
    data = jnp.stack(
        [
            turned(vis_weight * (gr * observed[0] + gi * observed[1]), devices),
            turned(vis_weight * (gr * observed[1] - gi * observed[0]), devices),
        ]
    )
    return weight, turned(weight, devices), data


def mirror_kernel(scale_ref, got_ref, pick_ref, flip_ref, out_ref):
    devices = out_ref.shape[0]
    for q in range(devices):
        facing = mm(flip_ref[min(q, 1)], got_ref[(devices - q) % devices]).astype(BF16)
        total = mm(scale_ref[q], pick_ref[0]) + mm(facing, pick_ref[1])
        out_ref[q] = total.astype(BF16)


def mirrored_exchange(upper, line, devices):
    middle = devices // 2
    facing = [(e, devices - 1 - e) for e in range(devices)]
    partner = [(e, devices - e) for e in range(1, devices) if e != middle]
    partner = partner + [(0, middle), (middle, 0)]
    upper = lax.ppermute(upper, ("ty", "tx"), facing)
    line = lax.ppermute(line, ("ty", "tx"), partner)
    return upper, line


def mirrored_weight(scale, upper, line):
    devices, slab, _ = scale.shape
    half, middle = slab // 2, devices // 2
    me = lax.axis_index(("ty", "tx"))
    got = jnp.concatenate([upper, jnp.broadcast_to(line, (half, N))], axis=0)
    source = lax.broadcasted_iota(jnp.int32, (slab, slab), 0)
    slot = lax.broadcasted_iota(jnp.int32, (slab, slab), 1)
    low = (me < middle).astype(jnp.int32)
    own = (slot < half) & (source == slot + low)
    other = (slot < half) & (source == half - low - slot)
    other = other & ((me != middle) | (slot > 0))
    other = other | ((me == middle) & (slot == half) & (source == half))
    picks = jnp.stack([own, other]).astype(BF16)
    q2 = np.arange(slab)
    flips = np.stack([q2[:, None] == (slab - q2) % slab, q2[:, None] == slab - 1 - q2])
    return pl.pallas_call(
        mirror_kernel,
        out_shape=jax.ShapeDtypeStruct(scale.shape, BF16),
        compiler_params=PARAMS,
    )(scale, turned(got, devices), picks, jnp.asarray(flips.astype(ml_dtypes.bfloat16)))


def row_matrix(first, cols, lanes, shift):
    twice = jnp.asarray(np.concatenate([first, first[: 2 * WIN]], axis=0))
    me = lax.axis_index("tx")
    zero = jnp.zeros((), jnp.int32)
    starts = [(me ^ m) * cols + (0 if shift is None else shift) for m in range(lanes)]
    rows = [lax.dynamic_slice(twice, (start, zero), (cols, first.shape[1])) for start in starts]
    return jnp.concatenate(rows, axis=0)


def swap_pieces(pieces):
    lanes = len(pieces)
    return [pieces[0]] + [
        lax.ppermute(pieces[m], "tx", [(k, k ^ m) for k in range(lanes)]) for m in range(1, lanes)
    ]


def phase_table(shift, devices, width):
    kr = counting(devices)[:, None] + devices * counting(8)[None, :]
    angle = 2.0 * math.pi / TOK * (kr * shift % TOK).astype(F32)
    table = jnp.stack([jnp.cos(angle), -jnp.sin(angle)], axis=1)
    return jnp.broadcast_to(table[..., None], (devices, 2, 8, width))


def patch_gradient(pieces, scale, data, shift, mirror, beside):
    lanes = lax.axis_size("tx")
    devices = lax.axis_size("ty") * lanes
    own, cols, _ = pieces[0].shape
    slab = N // devices
    halved = data is None
    outer, outer_t, inner, inner_t = (
        jnp.asarray(value) for value in column_constants(devices, slab)
    )
    if halved:
        first = half_constants()[0]
        twist, low, high, low_t, high_t = (jnp.asarray(value) for value in half_constants()[1:])
        part = (devices, slab, slab)
        onward = (row_forward_half, (row_matrix(first, cols, lanes, shift[1]), twist, low, high))
        backward = (row_inverse_half, (row_matrix(first, cols, lanes, None), twist, low_t, high_t))
        middle = lax.axis_index(("ty", "tx")) == devices // 2
    else:
        first = row_matrix(row_constants()[0], cols, lanes, None)
        twist, second, second_t = (jnp.asarray(value) for value in row_constants()[1:])
        part = (devices, 2, slab, slab)
        onward = (row_forward, (first, twist, second))
        backward = (row_inverse, (first, twist, second_t))
        extra = ()
        away = (inner, scale, inner_t, outer_t, data)
    split = (PATCH, devices // PATCH) + part[1:]
    sent = pl.pallas_call(
        onward[0], out_shape=jax.ShapeDtypeStruct(split, BF16), compiler_params=PARAMS
    )(*swap_pieces(pieces), *onward[1])
    if halved:
        sent, mirror, shift = lax.optimization_barrier((sent, mirror, shift))
        extra = (middle.astype(jnp.int32).reshape(1), phase_table(shift[0], devices, slab))
        away = (inner, mirrored_weight(scale, *mirror), inner_t, outer_t)
    moved = lax.all_to_all(
        sent.reshape(part), ("ty", "tx"), split_axis=0, concat_axis=0, tiled=True
    )
    if halved:
        moved, beside = lax.optimization_barrier((moved, beside))
        beside = from_neighbours(beside, 1)
    spaces = [pltpu.SMEM, pltpu.VMEM][: len(extra)] + [pltpu.VMEM] * 2 + [pl.ANY] * len(away)
    wave = pl.pallas_call(
        functools.partial(column_kernel, halved),
        in_specs=[pl.BlockSpec(memory_space=space) for space in spaces],
        out_shape=jax.ShapeDtypeStruct(part, BF16),
        scratch_shapes=[pltpu.VMEM((devices, 2, slab, slab), BF16)]
        + [pltpu.VMEM(value.shape, BF16) for value in away]
        + [pltpu.SemaphoreType.DMA((len(away),))],
        compiler_params=PARAMS,
    )(*extra, moved, outer, *away)
    if halved:
        wave, beside = lax.optimization_barrier((wave, beside))
    returned = lax.all_to_all(wave, ("ty", "tx"), split_axis=0, concat_axis=0, tiled=True)
    if not halved:
        returned, beside = lax.optimization_barrier((returned, beside))
    slabs = pl.pallas_call(
        backward[0],
        out_shape=[jax.ShapeDtypeStruct((own, cols, PIXELS), BF16)] * lanes,
        compiler_params=PARAMS,
    )(returned.reshape(split), *backward[1])
    return swap_pieces(slabs), beside


def layer_norm(values, gain):
    centre = jnp.mean(values, axis=-1, keepdims=True)
    shifted = values - centre
    spread = jnp.mean(shifted * shifted, axis=-1, keepdims=True)
    return (shifted * lax.rsqrt(spread + EPSILON) * gain).astype(BF16)


def to_windows(band):
    rows, cols, feats = band.shape
    pieces = [
        band[n : n + WIN, k : k + WIN, :].reshape(SPAN, feats)
        for n in range(0, rows, WIN)
        for k in range(0, cols, WIN)
    ]
    return jnp.concatenate(pieces, axis=0)


def from_windows(tokens, cols):
    feats = tokens.shape[-1]
    size = SPAN * cols // WIN
    bands = []
    for top in range(0, tokens.shape[0], size):
        pieces = [
            tokens[n : n + SPAN].reshape(WIN, WIN, feats) for n in range(top, top + size, SPAN)
        ]
        bands.append(jnp.concatenate(pieces, axis=1))
    return jnp.concatenate(bands, axis=0)


def gelu_twice(value):
    value = value.astype(BF16)
    inside = value * (BF16(GELU_IN) + BF16(GELU_CUBE) * (value * value))
    return value + value * jnp.tanh(inside)


def load_weights(j, sources, targets, sems):
    copies = [
        pltpu.make_async_copy(source.at[j], target, sems.at[n])
        for n, (source, target) in enumerate(zip(sources, targets))
    ]

    @pl.when(pl.program_id(0) == 0)
    def _():
        for copy in copies:
            copy.start()

    def wait(which):
        @pl.when(pl.program_id(0) == 0)
        def _():
            for n in which:
                copies[n].wait()

    return wait


def swin_band(flow, wait, bias_ref, gain_ref, weight_refs, scratch):
    qkv_ref, proj_ref, up_ref, down_ref = weight_refs
    mixed_ref, score_ref, prob_ref, active_ref = scratch
    count = flow.shape[0] // SPAN
    pairs = HEADS // 2
    depth = D // HEADS
    wide = 2 * depth
    normed = layer_norm(flow, gain_ref[0:1, :])
    scale = 1.0 / math.sqrt(depth)
    wait((0,))
    mixed_ref[:, :D] = (mm(normed, qkv_ref[:, :D]) * scale).astype(BF16)
    mixed_ref[:, D : 2 * D] = mm(normed, qkv_ref[:, D : 2 * D]).astype(BF16)
    mixed_ref[:, 2 * D :] = mm(normed, qkv_ref[:, 2 * D :]).astype(BF16)
    lower = lax.broadcasted_iota(jnp.int32, (SPAN, wide), 1) < depth

    def scores_of(w):
        rows = slice(w * SPAN, (w + 1) * SPAN)
        for p in range(pairs):
            query = mixed_ref[rows, p * wide : (p + 1) * wide]
            key = mixed_ref[rows, D + p * wide : D + (p + 1) * wide]
            zero = jnp.zeros_like(query)
            split = jnp.concatenate(
                [jnp.where(lower, query, zero), jnp.where(lower, zero, query)], axis=0
            )
            score_ref[w, :, p * wide : (p + 1) * wide] = mm(key, split, NT)

    def probs_of(w):
        bias = bias_ref[w]
        for p in range(pairs):
            lanes = slice(p * wide, (p + 1) * wide)
            scores = score_ref[w, :, lanes] + bias
            weights = jnp.exp(scores - jnp.max(scores, axis=0, keepdims=True))
            share = 1.0 / jnp.sum(weights, axis=0, keepdims=True)
            prob_ref[w, :, lanes] = (weights * share).astype(BF16)

    def mixture_of(w):
        rows = slice(w * SPAN, (w + 1) * SPAN)
        for p in range(pairs):
            lanes = slice(p * wide, (p + 1) * wide)
            value = mixed_ref[rows, 2 * D + p * wide : 2 * D + (p + 1) * wide]
            mixture = mm(prob_ref[w, :, lanes], value, TN)
            mixed_ref[rows, lanes] = jnp.where(lower, mixture[:SPAN], mixture[SPAN:]).astype(BF16)

    for turn in range(count + 2):
        if turn < count:
            scores_of(turn)
        if 0 <= turn - 1 < count:
            probs_of(turn - 1)
        if 0 <= turn - 2:
            mixture_of(turn - 2)
    wait((1, 2, 3))
    flow = flow + mm(mixed_ref[:, :D], proj_ref[...])
    normed = layer_norm(flow, gain_ref[1:2, :])
    chunks = up_ref.shape[1] // D
    for c in range(chunks):
        part = slice(c * D, (c + 1) * D)
        active_ref[:, part] = gelu_twice(mm(normed, up_ref[:, part]))
    return flow + 0.5 * mm(active_ref[...], down_ref[...])


def rolled_band(sign, shift_ref, refs, rows, count=WIN):
    main_ref, side_ref, edge_ref, corner_ref = refs
    cols = main_ref.shape[1]
    top = pl.program_id(0) * count + sign * shift_ref[0]
    behind = -rows if sign > 0 else WIN
    beside = -cols if sign > 0 else WIN

    def pick(width, offset):
        source = lax.broadcasted_iota(jnp.int32, (cols, width), 1)
        wanted = lax.broadcasted_iota(jnp.int32, (cols, width), 0) + sign * shift_ref[1] + offset
        return jnp.where(source == wanted, 1.0, 0.0).astype(BF16)

    pick_main, pick_side = pick(cols, 0), pick(WIN, beside)
    band = []
    for j in range(count):
        row = top + j
        inside = (row >= 0) & (row < rows)
        here, there = jnp.clip(row, 0, rows - 1), jnp.clip(row + behind, 0, WIN - 1)
        main = jnp.where(inside, main_ref[here], edge_ref[there])
        side = jnp.where(inside, side_ref[here], corner_ref[there])
        band.append(mm(pick_main, main) + mm(pick_side, side))
    return jnp.stack(band)


def first_kernel(zeta, sigma, count, parts, rows, before, *refs):
    shift_ref, state_ref, *refs = refs
    if before is not None:
        back_refs, refs = refs[:4], refs[4:]
    grad_refs, refs = refs[: count * parts], refs[count * parts :]
    if sigma is not None:
        noise_ref, *refs = refs
    bias_ref, embed_ref, gain_ref, *sources = refs[:7]
    base_ref, out_ref, side_ref, edge_ref, corner_ref, *scratch = refs[7:]
    targets, sems, scratch = scratch[:4], scratch[4], scratch[5:]
    wait = load_weights(0, sources, targets, sems)
    state = state_ref[...]
    if before is not None:
        state = state - before * rolled_band(-1, shift_ref, back_refs, rows, state.shape[0])
    height = state.shape[0]
    if parts == 1:
        grad = grad_refs[0][...].astype(F32)
    else:
        bands = []
        for k in range(height // WIN):
            turn = (pl.program_id(0) * (height // WIN) + k) ^ shift_ref[2]
            band = 0.0
            for n in range(0, count * parts, parts):
                piece = grad_refs[n][...]
                for m in range(1, parts):
                    piece = jnp.where(turn == m, grad_refs[n + m][...], piece)
                band = band + piece.astype(F32)
            bands.append(band)
        grad = jnp.concatenate(bands, axis=0)
    step = zeta * grad
    half = state - step
    tokens = mm(to_windows(half).astype(BF16), embed_ref[...]).astype(BF16).astype(F32)
    flow = swin_band(tokens, wait, bias_ref, gain_ref, targets, scratch)
    result = from_windows(flow, half.shape[1]).astype(BF16)
    out_ref[:, :, :D] = result
    side_ref[:, :, :D] = result[:, :WIN]
    if sigma is None:
        base_ref[...] = half
    else:
        noise = sigma * noise_ref[...]
        base_ref[...] = half + noise
        change = (noise - step).astype(BF16)
        out_ref[:, :, D:] = change
        side_ref[:, :, D:] = change[:, :WIN]

    @pl.when(pl.program_id(0) == 0)
    def _():
        edge_ref[...] = out_ref[:WIN]
        corner_ref[...] = side_ref[:WIN]


def write_pieces(turn, refs, value):
    for m, ref in enumerate(refs):

        def write(ref=ref):
            ref[...] = value

        pl.when(turn == m)(write)


def second_kernel(sigma, rows, parts, *refs):
    shift_ref, *refs = refs
    tile_refs, refs = refs[:4], refs[4:]
    bias_ref, unembed_ref, gain_ref, *sources = refs[:7]
    out_ref, side_ref, edge_ref, corner_ref, *scratch = refs[7:]
    state_refs, scratch = scratch[:parts], scratch[parts:]
    targets, sems, scratch = scratch[:4], scratch[4], scratch[5:]
    wait = load_weights(1, sources, targets, sems)
    height, cols, _ = out_ref.shape
    band = rolled_band(1, shift_ref, tile_refs, rows, height)
    tokens = to_windows(band[:, :, :D])
    flow = swin_band(tokens, wait, bias_ref, gain_ref, targets, scratch)
    estimate = from_windows(mm(flow.astype(BF16), unembed_ref[...]), cols)
    narrow = estimate.astype(BF16)
    out_ref[...] = narrow
    side_ref[...] = narrow[:, cols - WIN :]
    edge_ref[...] = narrow[height - WIN :]
    corner_ref[...] = narrow[height - WIN :, cols - WIN :]
    if parts > 0:
        change = (band[:, :, D:] - sigma * estimate).astype(BF16)
        for n in range(height // WIN):
            turn = (pl.program_id(0) * (height // WIN) + n) ^ shift_ref[2]
            write_pieces(turn, state_refs, change[n * WIN : (n + 1) * WIN])


def whole(array):
    zeros = (0,) * array.ndim
    return pl.BlockSpec(array.shape, lambda *_: zeros)


def member(array, j):
    place = (j,) + (0,) * (array.ndim - 1)
    return pl.BlockSpec((None,) + array.shape[1:], lambda *_: place)


def band_spec(cols, feats, height=WIN):
    return pl.BlockSpec((height, cols, feats), lambda n, *_: (n, 0, 0))


def bias_spec(cols, height=WIN):
    count = height * cols // SPAN
    return pl.BlockSpec((count, SPAN, 2 * SPAN), lambda n, *_: (n, 0, 0))


def band_scratch(cols, weights, height=WIN):
    count = height * cols // SPAN
    return [pltpu.VMEM(value.shape[1:], BF16) for value in weights] + [
        pltpu.SemaphoreType.DMA((len(weights),)),
        pltpu.VMEM((height * cols, 3 * D), BF16),
        pltpu.VMEM((count, SPAN, HEADS * SPAN), F32),
        pltpu.VMEM((count, SPAN, HEADS * SPAN), BF16),
    ]


def strip_outs(rows, cols, feats, height=WIN):
    specs = [band_spec(cols, feats, height), band_spec(WIN, feats, height)]
    specs += [
        pl.BlockSpec((WIN, width, feats), lambda *_: (0, 0, 0)) for width in (cols, WIN)
    ]
    shapes = [(rows, cols), (rows, WIN), (WIN, cols), (WIN, WIN)]
    return specs, [jax.ShapeDtypeStruct(shape + (feats,), BF16) for shape in shapes]


def first_block(zeta, sigma, state, before, shift, back, grads, noise, bias, w_embed, weights):
    *weights, gains = weights
    rows, cols, _ = state.shape
    parts = len(grads[0])
    pieces = [piece for grad in grads for piece in grad]
    fields = [] if sigma is None else [noise]
    feats = D if sigma is None else D + PIXELS
    height = 2 * WIN
    specs, shapes = strip_outs(rows, cols, feats, height)
    band = band_spec(cols, PIXELS, height)
    return pl.pallas_call(
        functools.partial(first_kernel, zeta, sigma, len(grads), parts, rows, before),
        grid_spec=pltpu.PrefetchScalarGridSpec(
            num_scalar_prefetch=1,
            grid=(rows // height,),
            in_specs=[band]
            + [whole(value) for value in back]
            + [band if parts == 1 else whole(value) for value in pieces]
            + [band] * len(fields)
            + [bias_spec(cols, height), whole(w_embed), member(gains, 0)]
            + [pl.BlockSpec(memory_space=pl.ANY)] * len(weights),
            out_specs=[band] + specs,
            scratch_shapes=band_scratch(cols, weights, height)
            + [pltpu.VMEM((height * cols, weights[2].shape[2]), BF16)],
        ),
        out_shape=[jax.ShapeDtypeStruct((rows, cols, PIXELS), F32)] + shapes,
        compiler_params=PARAMS,
    )(shift, state, *back, *pieces, *fields, bias, w_embed, gains, *weights)


def second_block(sigma, shift, tile, bias, w_unembed, weights, parts):
    *weights, gains = weights
    rows, cols, _ = tile[0].shape
    height = 2 * WIN
    specs, shapes = strip_outs(rows, cols, PIXELS, height)
    specs += [pl.BlockSpec((WIN, cols, PIXELS), lambda *_: (0, 0, 0))] * parts
    shapes += [jax.ShapeDtypeStruct((WIN, cols, PIXELS), BF16)] * parts
    return pl.pallas_call(
        functools.partial(second_kernel, sigma, rows, parts),
        grid_spec=pltpu.PrefetchScalarGridSpec(
            num_scalar_prefetch=1,
            grid=(rows // height,),
            in_specs=[whole(value) for value in tile]
            + [bias_spec(cols, height), whole(w_unembed), member(gains, 1)]
            + [pl.BlockSpec(memory_space=pl.ANY)] * len(weights),
            out_specs=specs,
            scratch_shapes=band_scratch(cols, weights, height)
            + [pltpu.VMEM((height * cols, weights[2].shape[2]), BF16)],
        ),
        out_shape=shapes,
        compiler_params=PARAMS,
    )(shift, *tile, bias, w_unembed, gains, *weights)


def from_neighbours(tile, by):
    main, side, edge, corner = tile
    ty, tx = lax.axis_size("ty"), lax.axis_size("tx")
    across = [
        (i * tx + k, (i + by) % ty * tx + (k + by) % tx) for i in range(ty) for k in range(tx)
    ]
    return (
        main,
        lax.ppermute(side, "tx", [(k, (k + by) % tx) for k in range(tx)]),
        lax.ppermute(edge, "ty", [(i, (i + by) % ty) for i in range(ty)]),
        lax.ppermute(corner, ("ty", "tx"), across),
    )


def windows_of(grid):
    rows, cols = grid.shape
    shaped = grid.reshape(rows // WIN, WIN, cols // WIN, WIN).transpose(0, 2, 1, 3)
    return shaped.reshape(rows // WIN * (cols // WIN), SPAN)


def bias_of(labels, keep):
    allowed = jnp.ones((1, SPAN, SPAN), bool)
    if labels is not None:
        label = windows_of(labels)
        allowed = label[:, :, None] == label[:, None, :]
    if keep is not None:
        kept = windows_of(keep)[:, :, None] == 1
        allowed = allowed & (kept | jnp.eye(SPAN, dtype=bool)[None])
    bias = jnp.where(allowed, 0.0, -1e30).astype(F32)
    return jnp.concatenate([bias, bias], axis=2)


def region(index, shift):
    return jnp.where(index < TOK - WIN, 0, jnp.where(index < TOK - shift, 1, 2)).astype(jnp.int32)


@functools.lru_cache(maxsize=None)
def lane_order(cols):
    parts = LANES // cols
    groups = PATCH // parts
    lane = np.arange(PATCH * cols)
    g, h, k = lane // LANES, lane % LANES // cols, lane % cols
    source = PATCH * k + h * groups + g
    matrix = np.zeros((PATCH * cols, PATCH * cols), np.float32)
    matrix[source, lane] = 1.0
    return matrix.astype(ml_dtypes.bfloat16), np.ascontiguousarray(matrix.T).astype(
        ml_dtypes.bfloat16
    )


def move_lanes(values, matrix):
    high = values.astype(BF16)
    low = (values - high.astype(F32)).astype(BF16)
    return mm(high, matrix) + mm(low, matrix)


def to_patches_kernel(narrow, place_ref, tile_ref, order_ref, *out_refs):
    count, cols, _ = out_refs[0].shape
    parts = LANES // cols
    groups = PATCH // parts
    if narrow:
        ordered = mm(tile_ref[...].astype(BF16), order_ref[...])
    else:
        ordered = move_lanes(tile_ref[...], order_ref[...])
    patches = []
    for i in range(count):
        band = ordered[i * PATCH : (i + 1) * PATCH]
        stacked = jnp.concatenate(
            [band[:, g * LANES : (g + 1) * LANES] for g in range(groups)], axis=0
        )
        turned = stacked.T
        patches.append(
            jnp.concatenate([turned[h * cols : (h + 1) * cols] for h in range(parts)], axis=1)
        )
    result = jnp.stack(patches).astype(out_refs[0].dtype)
    if len(out_refs) == 1:
        out_refs[0][...] = result
    else:
        write_pieces(pl.program_id(0) ^ place_ref[0], out_refs, result)


def to_tile_kernel(sigma, scale, rows, *refs):
    shift_ref, base_ref, *refs = refs
    noise_ref, order_ref, out_ref = refs[4:]
    count, cols, _ = base_ref.shape
    parts = LANES // cols
    groups = PATCH // parts
    width = groups * PATCH
    state = base_ref[...] - sigma * rolled_band(-1, shift_ref, refs[:4], rows)
    bands = []
    for i in range(count):
        stacked = jnp.concatenate(
            [state[i, :, h * width : (h + 1) * width] for h in range(parts)], axis=0
        )
        turned = stacked.T
        bands.append(
            jnp.concatenate([turned[g * PATCH : (g + 1) * PATCH] for g in range(groups)], axis=1)
        )
    moved = move_lanes(jnp.concatenate(bands, axis=0), order_ref[...])
    out_ref[...] = moved + scale * noise_ref[...]


def patches_of(tiles, j, place, kind=F32, parts=1):
    rows, cols = tiles.shape[1] // PATCH, tiles.shape[2] // PATCH
    order = jnp.asarray(lane_order(cols)[0])
    spec, shape = band_spec(cols, PIXELS), (rows, cols, PIXELS)
    if parts > 1:
        spec = pl.BlockSpec((WIN, cols, PIXELS), lambda *_: (0, 0, 0))
        shape = (WIN, cols, PIXELS)
    return pl.pallas_call(
        functools.partial(to_patches_kernel, kind == BF16),
        grid_spec=pltpu.PrefetchScalarGridSpec(
            num_scalar_prefetch=1,
            grid=(rows // WIN,),
            in_specs=[
                pl.BlockSpec((None, WIN * PATCH, cols * PATCH), lambda n, *_: (j, n, 0)),
                whole(order),
            ],
            out_specs=[spec] * parts,
        ),
        out_shape=[jax.ShapeDtypeStruct(shape, kind)] * parts,
        compiler_params=PARAMS,
    )(place, tiles, order)


def tile_of(base, sigma, shift, back, scale, noise, j):
    rows, cols, _ = base.shape
    order = jnp.asarray(lane_order(cols)[1])
    return pl.pallas_call(
        functools.partial(to_tile_kernel, sigma, scale, rows),
        grid_spec=pltpu.PrefetchScalarGridSpec(
            num_scalar_prefetch=1,
            grid=(rows // WIN,),
            in_specs=[band_spec(cols, PIXELS)]
            + [whole(value) for value in back]
            + [
                pl.BlockSpec((None, WIN * PATCH, cols * PATCH), lambda n, *_: (j, n, 0)),
                whole(order),
            ],
            out_specs=pl.BlockSpec((WIN * PATCH, cols * PATCH), lambda n, *_: (n, 0)),
        ),
        out_shape=jax.ShapeDtypeStruct((rows * PATCH, cols * PATCH), F32),
        compiler_params=PARAMS,
    )(shift, base, *back, noise, order)


def per_device(
    image, noise, offsets, key_mask, gains, observed, vis_weight,
    w_embed, w_qkv, w_proj, w_up, w_down, w_unembed, norm_gains,
):
    rows = image.shape[0] // PATCH
    cols = image.shape[1] // PATCH
    devices = lax.axis_size("ty") * lax.axis_size("tx")
    lanes = lax.axis_size("tx")
    fast = N // devices == TOK // 2 and rows == lanes * WIN and lanes & (lanes - 1) == 0
    column = lax.axis_index("tx").astype(jnp.int32)[None]
    places = [jnp.concatenate([offsets[step], column]) for step in range(STEPS)]
    row_index = lax.axis_index("ty") * rows + counting(rows)
    col_index = lax.axis_index("tx") * cols + counting(cols)
    weights = (w_qkv, w_proj, w_up, w_down, norm_gains)
    w_embed = w_embed.reshape(PATCH, PATCH, D).transpose(1, 0, 2).reshape(PIXELS, D)
    w_unembed = w_unembed.reshape(D, PATCH, PATCH).transpose(0, 2, 1).reshape(D, PIXELS)
    state = patches_of(image[None], 0, column)[0]
    extras = [patches_of(noise, step, column)[0] for step in range(STEPS - 1)] + [None]
    first_bias = bias_of(None, key_mask)
    biases = []
    for step in range(STEPS):
        labels = (
            3 * region(row_index, offsets[step, 0])[:, None]
            + region(col_index, offsets[step, 1])[None, :]
        )
        biases.append(bias_of(labels, None))
    beside = (state, extras, first_bias, biases, w_embed, w_unembed)
    shift, before, back, moving, mirror = places[0], None, (), None, None
    grads = []
    if fast:
        weight, scale, data = spectrum_inputs(gains, observed, vis_weight, devices)
        half = weight.shape[0] // 2
        lines = (weight[half:], weight[:1])
        grad, (beside, lines) = patch_gradient(
            patches_of(image[None], 0, column, BF16, lanes), scale, data, None, None,
            (beside, lines),
        )
        grad, lines = lax.optimization_barrier((grad, lines))
        mirror = mirrored_exchange(*lines, devices)
        grads = [grad]
        state, extras, first_bias, biases, w_embed, w_unembed = beside
    for step in range(STEPS):
        if not fast:
            tile = image if step == 0 else tile_of(state, before, shift, back, 0.0, noise, 0)
            grad = plain_gradient(tile, gains, observed, vis_weight)
            grad = patches_of(grad.astype(F32)[None], 0, column, BF16)[0]
            grads = [[grad]]
        elif step > 0:
            grad, back = patch_gradient(moving, scale, None, shift, mirror, back)
            grads = grads + [grad]
        last = step + 1 == STEPS
        sigma = None if last else SIGMAS[step + 1]
        state, *first = first_block(
            STEP_SIZES[step], sigma, state, before, shift, back, grads, extras[step], first_bias,
            w_embed, weights,
        )
        shift, before = places[step], SIGMAS[step]
        if fast and step == 0:
            first, mirror = lax.optimization_barrier((first, mirror))
        rolled = second_block(
            before, shift, from_neighbours(first, -1), biases[step], w_unembed, weights,
            lanes if fast and not last else 0,
        )
        back, moving = rolled[:4], rolled[4:]
        if last or not fast:
            back = from_neighbours(back, 1)
    return tile_of(state, before, shift, back, SIGMAS[STEPS], noise, STEPS - 1)


def solution(mesh):
    in_specs = (
        P("ty", "tx"),
        P(None, "ty", "tx"),
        P(),
        P("ty", "tx"),
        P(None, ("ty", "tx"), None),
        P(None, ("ty", "tx"), None),
        P(("ty", "tx"), None),
        P(),
        P(),
        P(),
        P(),
        P(),
        P(),
        P(),
    )
    out_specs = P("ty", "tx")
    return jax.shard_map(
        per_device, mesh=mesh, in_specs=in_specs, out_specs=out_specs, check_vma=False
    )
```

```python
import functools
import math

import jax
import jax.numpy as jnp
import ml_dtypes
import numpy as np
from jax import lax
from jax.experimental import pallas as pl
from jax.experimental.pallas import tpu as pltpu
from jax.sharding import PartitionSpec as P

N = 4096
PATCH = 16
PIXELS = PATCH * PATCH
WIN = 8
D = 512
HEADS = 8
STEPS = 2
SPAN = WIN * WIN
LANES = 128
GROUP = 8
HEIGHT = 2 * WIN
TOK = N // PATCH

SIGMAS = (0.8, 0.5, 0.3)
STEP_SIZES = (0.9, 0.7)
EPSILON = 1e-05
HIGHEST = lax.Precision.HIGHEST
BF16 = jnp.bfloat16
F32 = jnp.float32
GELU_IN = math.sqrt(2.0 / math.pi)
GELU_CUBE = 0.044715 * GELU_IN
VMEM_LIMIT = 56 * 1024 * 1024
PARAMS = pltpu.CompilerParams(vmem_limit_bytes=VMEM_LIMIT)
TN = (((0,), (0,)), ((), ()))
NT = (((1,), (1,)), ((), ()))
NN = (((1,), (0,)), ((), ()))


def mm(left, right, dims=NN):
    return lax.dot_general(left, right, dims, preferred_element_type=F32)


def counting(length):
    return jnp.arange(length, dtype=jnp.int32)


def roots(length, outer, inner, sign):
    product = outer[:, None] * inner[None, :] % length
    angle = 2.0 * math.pi / length * product.astype(F32)
    return (jnp.cos(angle), sign * jnp.sin(angle))


def complex_einsum(form, left, right):
    real = jnp.einsum(form, left[0], right[0], precision=HIGHEST) - jnp.einsum(
        form, left[1], right[1], precision=HIGHEST
    )
    imag = jnp.einsum(form, left[0], right[1], precision=HIGHEST) + jnp.einsum(
        form, left[1], right[0], precision=HIGHEST
    )
    return (real, imag)


def complex_times(left, right):
    return (left[0] * right[0] - left[1] * right[1], left[0] * right[1] + left[1] * right[0])


def along_last(real_part, imag_part, groups, sign):
    rows, length = real_part.shape
    inner = length // groups
    first = roots(groups, counting(groups), counting(groups), sign)
    twist = roots(length, counting(inner), counting(groups), sign)
    second = roots(inner, counting(inner), counting(inner), sign)
    shaped = real_part.reshape(rows, groups, inner)
    if imag_part is None:
        partial_value = (
            jnp.einsum("mab,ka->mbk", shaped, first[0], precision=HIGHEST),
            jnp.einsum("mab,ka->mbk", shaped, first[1], precision=HIGHEST),
        )
    else:
        partial_value = complex_einsum(
            "mab,ka->mbk", (shaped, imag_part.reshape(rows, groups, inner)), first
        )
    partial_value = complex_times(partial_value, twist)
    result = complex_einsum("jb,mbk->mjk", second, partial_value)
    return (result[0].reshape(rows, length), result[1].reshape(rows, length))


def across_groups(pair, groups, sign):
    inner, cols = pair[0].shape
    width = cols // groups
    length = groups * inner
    first = roots(groups, counting(groups), counting(groups), sign)
    twist = roots(length, counting(inner), counting(groups), sign)
    second = roots(inner, counting(inner), counting(inner), sign)
    shaped = (pair[0].reshape(inner, groups, width), pair[1].reshape(inner, groups, width))
    partial_value = complex_einsum("bhc,kh->cbk", shaped, first)
    partial_value = complex_times(partial_value, twist)
    result = complex_einsum("jb,cbk->cjk", second, partial_value)
    return (result[0].reshape(width, length), result[1].reshape(width, length))


def exchange_pair(pair):
    return tuple(
        lax.all_to_all(
            part.astype(BF16), ("ty", "tx"), split_axis=1, concat_axis=1, tiled=True
        ).astype(F32)
        for part in pair
    )


def plain_gradient(tile, gains, observed, vis_weight):
    devices = lax.axis_size("ty") * lax.axis_size("tx")
    slab = lax.all_to_all(tile.astype(BF16), "tx", split_axis=0, concat_axis=1, tiled=True)
    moved = exchange_pair(along_last(slab.astype(F32), None, devices, -1.0))
    spectrum = across_groups(moved, devices, -1.0)
    spectrum = (spectrum[0] * (1.0 / N), spectrum[1] * (1.0 / N))
    model = complex_times((gains[0], gains[1]), spectrum)
    misfit = (vis_weight * (model[0] - observed[0]), vis_weight * (model[1] - observed[1]))
    back = complex_times((gains[0], -gains[1]), misfit)
    returned = exchange_pair(along_last(back[0], back[1], devices, 1.0))
    slab_grad = across_groups(returned, devices, 1.0)[0] * (1.0 / N)
    return lax.all_to_all(slab_grad.astype(BF16), "tx", split_axis=1, concat_axis=0, tiled=True)


def embed_complex(angle, row_axis, col_axis):
    cos, sin = np.cos(angle), np.sin(angle)
    top = np.stack([cos, sin], axis=col_axis)
    bottom = np.stack([-sin, cos], axis=col_axis)
    return np.stack([top, bottom], axis=row_axis)


def wheel(length, product):
    return 2.0 * math.pi / length * (product % length)


@functools.lru_cache(maxsize=None)
def row_constants():
    k = np.arange(TOK)
    angle = wheel(TOK, k[:, None] * k[None, :])
    first = np.concatenate([np.cos(angle), -np.sin(angle)], axis=1)
    b = np.repeat(np.arange(PATCH), PATCH)
    angle = wheel(N, b[:, None] * k[None, :])
    twist = np.stack([np.cos(angle), -np.sin(angle)])
    p = np.arange(PATCH)
    small = embed_complex(wheel(PATCH, p[:, None] * p[None, :]), 1, 1)
    second = np.einsum("kpqb,xy->kpxqby", small, np.eye(PATCH)).reshape(2 * PIXELS, 2 * PIXELS)
    return (
        first.astype(ml_dtypes.bfloat16),
        twist.astype(np.float32),
        second.astype(ml_dtypes.bfloat16),
        np.ascontiguousarray(second.T).astype(ml_dtypes.bfloat16),
    )


@functools.lru_cache(maxsize=None)
def half_constants():
    _, twist, second, _ = row_constants()
    half, quarter = TOK // 2, TOK // 4
    low = np.concatenate([1 + np.arange(quarter), 1 + half + np.arange(quarter)])
    digits = np.concatenate([low, low - 1])
    k = np.arange(TOK)
    angle = wheel(TOK, k[:, None] * digits[None, :])
    first = np.concatenate([np.cos(angle), -np.sin(angle)], axis=1)
    zero_line = np.concatenate([np.tile(np.eye(PATCH), PATCH), np.zeros((PATCH, PIXELS))], axis=1)
    upper = np.concatenate([second[PIXELS:].astype(np.float32), zero_line])
    lower = second[:PIXELS].astype(np.float32)
    return (first.astype(ml_dtypes.bfloat16), np.ascontiguousarray(twist[:, :, digits])) + tuple(
        np.ascontiguousarray(value).astype(ml_dtypes.bfloat16)
        for value in (lower, upper, lower.T, upper.T)
    )


@functools.lru_cache(maxsize=None)
def column_constants(devices, rows):
    s = np.arange(devices)
    small = embed_complex(wheel(devices, s[:, None] * s[None, :]), 1, 2)
    wide = devices * 2 * GROUP
    outer = np.einsum("qpsr,xy->qpxsry", small, np.eye(GROUP)).reshape(wide, wide)
    kr = s[:, None] + devices * np.arange(rows)[None, :]
    angle = wheel(N, kr[:, :, None] * np.arange(rows)[None, None, :])
    inner = embed_complex(angle, 1, 2).reshape(devices, 2 * rows, 2 * rows) / N
    return tuple(
        np.ascontiguousarray(value).astype(ml_dtypes.bfloat16)
        for value in (outer, outer.T, inner, inner.transpose(0, 2, 1))
    )


def row_forward(*refs):
    *x_refs, first_ref, twist_ref, second_ref, out_ref = refs
    count = x_refs[0].shape[0]

    def step(i, carry):
        band = jnp.concatenate([x_ref[i] for x_ref in x_refs], axis=0)
        mixed = mm(band, first_ref[...], TN)
        real, imag = mixed[:, :TOK], mixed[:, TOK:]
        tr, ti = twist_ref[0], twist_ref[1]
        turned = jnp.concatenate(
            [(real * tr - imag * ti).astype(BF16), (real * ti + imag * tr).astype(BF16)], axis=0
        )
        result = mm(second_ref[...], turned).astype(BF16).reshape(PATCH, 2, PATCH, TOK)
        half = TOK // 2
        rows = pl.ds(pl.multiple_of(i * PATCH, PATCH), PATCH)
        out_ref[:, 0, :, rows, :] = result[..., :half]
        out_ref[:, 1, :, rows, :] = result[..., half:]
        return carry

    lax.fori_loop(0, count, step, 0, unroll=4)


def row_inverse(v_ref, first_ref, twist_ref, second_ref, *out_refs):
    count, cols, _ = out_refs[0].shape

    def step(i, carry):
        rows = pl.ds(pl.multiple_of(i * PATCH, PATCH), PATCH)
        wide = jnp.concatenate(
            [
                v_ref[:, 0, :, rows, :].reshape(2 * PIXELS, TOK // 2),
                v_ref[:, 1, :, rows, :].reshape(2 * PIXELS, TOK // 2),
            ],
            axis=1,
        )
        mixed = mm(second_ref[...], wide)
        real, imag = mixed[:PIXELS], mixed[PIXELS:]
        tr, ti = twist_ref[0], twist_ref[1]
        turned = jnp.concatenate(
            [(real * tr + imag * ti).astype(BF16), (imag * tr - real * ti).astype(BF16)], axis=1
        )
        result = mm(first_ref[...], turned, NT).astype(BF16)
        for m, out_ref in enumerate(out_refs):
            out_ref[i] = result[m * cols : (m + 1) * cols]
        return carry

    lax.fori_loop(0, count, step, 0, unroll=4)


def lane_index(shape):
    return lax.broadcasted_iota(jnp.int32, shape, len(shape) - 1)


def swap_halves(values):
    return pltpu.roll(values, values.shape[-1] // 2, len(values.shape) - 1)


def row_forward_half(*refs):
    *x_refs, first_ref, twist_ref, lower_ref, upper_ref, out_ref = refs
    count = x_refs[0].shape[0]
    half = TOK // 2

    def packed(real, imag, rows, high):
        left = lane_index(real.shape) < half // 2
        out_ref[high, 0, rows, :] = jnp.where(left, real, swap_halves(imag)).astype(BF16)
        out_ref[high, 1, rows, :] = jnp.where(left, swap_halves(real), imag).astype(BF16)

    def step(i, carry):
        band = jnp.concatenate([x_ref[i] for x_ref in x_refs], axis=0)
        mixed = mm(band, first_ref[...], TN)
        real, imag = mixed[:, :TOK], mixed[:, TOK:]
        tr, ti = twist_ref[0], twist_ref[1]
        turned = jnp.concatenate(
            [(real * tr - imag * ti).astype(BF16), (real * ti + imag * tr).astype(BF16)], axis=0
        )
        rows = pl.ds(pl.multiple_of(i * PATCH, PATCH), PATCH)
        lower = mm(lower_ref[...], turned[:, :half]).reshape(PATCH // 2, 2, PATCH, half)
        packed(lower[:, 0], lower[:, 1], rows, slice(0, PATCH // 2))
        upper = mm(upper_ref[...], turned[:, half:])
        line = upper[PIXELS:]
        upper = upper[:PIXELS].reshape(PATCH // 2, 2, PATCH, half)
        imag = upper[:, 1]
        head = jnp.where(lane_index(line.shape) == 0, line, imag[0])
        imag = jnp.concatenate([head[None], imag[1:]], axis=0)
        packed(upper[:, 0], imag, rows, slice(PATCH // 2, PATCH))
        return carry

    lax.fori_loop(0, count, step, 0, unroll=4)


def row_inverse_half(v_ref, first_ref, twist_ref, lower_ref, upper_ref, *out_refs):
    count, cols, _ = out_refs[0].shape
    half = TOK // 2

    def unpacked(rows, high):
        even = v_ref[high, 0, rows, :].astype(F32)
        odd = v_ref[high, 1, rows, :].astype(F32)
        left = lane_index(even.shape) < half // 2
        return jnp.where(left, even, swap_halves(odd)), jnp.where(left, swap_halves(even), odd)

    def step(i, carry):
        rows = pl.ds(pl.multiple_of(i * PATCH, PATCH), PATCH)
        real, imag = unpacked(rows, slice(0, PATCH // 2))
        lower = jnp.stack([real, imag], axis=1).reshape(PIXELS, half)
        real, imag = unpacked(rows, slice(PATCH // 2, PATCH))
        head = imag[0]
        at_zero = lane_index(head.shape) == 0
        nothing = jnp.zeros_like(head)
        imag = jnp.concatenate([jnp.where(at_zero, nothing, head)[None], imag[1:]], axis=0)
        upper = jnp.stack([real, imag], axis=1).reshape(PIXELS, half)
        upper = jnp.concatenate([upper, jnp.where(at_zero, head, nothing)], axis=0)
        mixed = jnp.concatenate(
            [mm(lower_ref[...], lower.astype(BF16)), mm(upper_ref[...], upper.astype(BF16))], axis=1
        )
        real, imag = mixed[:PIXELS], mixed[PIXELS:]
        tr, ti = twist_ref[0], twist_ref[1]
        turned = jnp.concatenate(
            [(real * tr + imag * ti).astype(BF16), (imag * tr - real * ti).astype(BF16)], axis=1
        )
        result = mm(first_ref[...], turned, NT).astype(BF16)
        for m, out_ref in enumerate(out_refs):
            out_ref[i] = result[m * cols : (m + 1) * cols]
        return carry

    lax.fori_loop(0, count, step, 0, unroll=4)


def column_kernel(halved, *refs):
    if halved:
        flag_ref, phase_ref, refs = refs[0], refs[1], refs[2:]
    x_ref, outer_ref, *refs = refs
    count = 4 if halved else 5
    sources, out_ref = refs[:count], refs[count]
    mid_ref, *targets, sems = refs[count + 1 :]
    copies = [
        pltpu.make_async_copy(source, target, sems.at[n])
        for n, (source, target) in enumerate(zip(sources, targets))
    ]
    for copy in copies:
        copy.start()
    inner_ref, scale_ref, inner_t_ref, outer_t_ref = targets[:4]
    devices, _, rows, width = mid_ref.shape
    wide = devices * 2 * GROUP
    if halved:
        lane = lane_index((devices, PATCH, width))
        centre = flag_ref[0] == 1
        half = width // 2
        hidden = (lane == half) | (centre & (lane == 0))
        real_lane = (lane < half) | (centre & (lane == half))

    def load(place):
        if not halved:
            return x_ref[:, :, place, :].astype(F32)
        piece = x_ref[:, place, :].astype(F32)
        other = swap_halves(piece)
        return jnp.stack([piece, jnp.where(hidden, jnp.zeros_like(other), other)], axis=1)

    def store(place, value):
        if halved:
            value = jnp.where(real_lane, value[:, 0], swap_halves(value[:, 1])).astype(BF16)
            out_ref[:, place, :] = value
        else:
            out_ref[:, :, place, :] = value.astype(BF16)

    def outer(matrix_ref, value):
        groups = [
            value[:, :, n : n + GROUP, :].reshape(wide, width) for n in range(0, PATCH, GROUP)
        ]
        result = mm(matrix_ref[...], jnp.concatenate(groups, axis=1).astype(BF16))
        parts = [
            result[:, n : n + width].reshape(devices, 2, GROUP, width)
            for n in range(0, result.shape[1], width)
        ]
        return jnp.concatenate(parts, axis=2)

    for top in range(0, rows, PATCH):
        place = slice(top, top + PATCH)
        mid_ref[:, :, place, :] = outer(outer_ref, load(place)).astype(BF16)

    for n, copy in enumerate(copies):
        if n != 3:
            copy.wait()

    def step(q, carry):
        spectrum = mm(inner_ref[q], mid_ref[q].reshape(2 * rows, width))
        real, imag = spectrum[:rows], spectrum[rows:]
        scale = scale_ref[q].astype(F32)
        if halved:
            pr, pi = phase_ref[q, 0], phase_ref[q, 1]
            real = real.reshape(rows // 8, 8, width)
            imag = imag.reshape(rows // 8, 8, width)
            real, imag = real * pr - imag * pi, real * pi + imag * pr
            real, imag = real.reshape(rows, width) * scale, imag.reshape(rows, width) * scale
        else:
            data_ref = targets[4]
            real = real * scale - data_ref[0, q].astype(F32)
            imag = imag * scale - data_ref[1, q].astype(F32)
        back = jnp.concatenate([real.astype(BF16), imag.astype(BF16)], axis=0)
        mid_ref[q] = mm(inner_t_ref[q], back).astype(BF16).reshape(2, rows, width)
        return carry

    lax.fori_loop(0, devices, step, 0, unroll=8)
    copies[3].wait()

    for top in range(0, rows, PATCH):
        place = slice(top, top + PATCH)
        store(place, outer(outer_t_ref, mid_ref[:, :, place, :].astype(F32)))


def turned(value, devices):
    lines = value.shape[0]
    return value.astype(BF16).reshape(lines, N // devices, devices).transpose(2, 1, 0)


def spectrum_inputs(gains, observed, vis_weight, devices):
    gr, gi = gains[0], gains[1]
    weight = (vis_weight * (gr * gr + gi * gi)).astype(BF16)
    data = jnp.stack(
        [
            turned(vis_weight * (gr * observed[0] + gi * observed[1]), devices),
            turned(vis_weight * (gr * observed[1] - gi * observed[0]), devices),
        ]
    )
    return weight, turned(weight, devices), data


def mirror_kernel(scale_ref, got_ref, pick_ref, flip_ref, out_ref):
    devices = out_ref.shape[0]
    for q in range(devices):
        facing = mm(flip_ref[min(q, 1)], got_ref[(devices - q) % devices]).astype(BF16)
        total = mm(scale_ref[q], pick_ref[0]) + mm(facing, pick_ref[1])
        out_ref[q] = total.astype(BF16)


def mirrored_exchange(upper, line, devices):
    middle = devices // 2
    facing = [(e, devices - 1 - e) for e in range(devices)]
    partner = [(e, devices - e) for e in range(1, devices) if e != middle]
    partner = partner + [(0, middle), (middle, 0)]
    upper = lax.ppermute(upper, ("ty", "tx"), facing)
    line = lax.ppermute(line, ("ty", "tx"), partner)
    return upper, line


def mirrored_weight(scale, upper, line):
    devices, slab, _ = scale.shape
    half, middle = slab // 2, devices // 2
    me = lax.axis_index(("ty", "tx"))
    got = jnp.concatenate([upper, jnp.broadcast_to(line, (half, N))], axis=0)
    source = lax.broadcasted_iota(jnp.int32, (slab, slab), 0)
    slot = lax.broadcasted_iota(jnp.int32, (slab, slab), 1)
    low = (me < middle).astype(jnp.int32)
    own = (slot < half) & (source == slot + low)
    other = (slot < half) & (source == half - low - slot)
    other = other & ((me != middle) | (slot > 0))
    other = other | ((me == middle) & (slot == half) & (source == half))
    picks = jnp.stack([own, other]).astype(BF16)
    q2 = np.arange(slab)
    flips = np.stack([q2[:, None] == (slab - q2) % slab, q2[:, None] == slab - 1 - q2])
    return pl.pallas_call(
        mirror_kernel,
        out_shape=jax.ShapeDtypeStruct(scale.shape, BF16),
        compiler_params=PARAMS,
    )(scale, turned(got, devices), picks, jnp.asarray(flips.astype(ml_dtypes.bfloat16)))


def row_matrix(first, cols, lanes, shift):
    twice = jnp.asarray(np.concatenate([first, first[: 2 * WIN]], axis=0))
    me = lax.axis_index("tx")
    zero = jnp.zeros((), jnp.int32)
    starts = [(me ^ m) * cols + (0 if shift is None else shift) for m in range(lanes)]
    rows = [lax.dynamic_slice(twice, (start, zero), (cols, first.shape[1])) for start in starts]
    return jnp.concatenate(rows, axis=0)


def swap_pieces(pieces):
    lanes = len(pieces)
    return [pieces[0]] + [
        lax.ppermute(pieces[m], "tx", [(k, k ^ m) for k in range(lanes)]) for m in range(1, lanes)
    ]


def phase_table(shift, devices, width):
    kr = counting(devices)[:, None] + devices * counting(8)[None, :]
    angle = 2.0 * math.pi / TOK * (kr * shift % TOK).astype(F32)
    table = jnp.stack([jnp.cos(angle), -jnp.sin(angle)], axis=1)
    return jnp.broadcast_to(table[..., None], (devices, 2, 8, width))


def patch_gradient(pieces, scale, data, shift, mirror, beside):
    lanes = lax.axis_size("tx")
    devices = lax.axis_size("ty") * lanes
    own, cols, _ = pieces[0].shape
    slab = N // devices
    halved = data is None
    outer, outer_t, inner, inner_t = (
        jnp.asarray(value) for value in column_constants(devices, slab)
    )
    if halved:
        first = half_constants()[0]
        twist, low, high, low_t, high_t = (jnp.asarray(value) for value in half_constants()[1:])
        part = (devices, slab, slab)
        onward = (row_forward_half, (row_matrix(first, cols, lanes, shift[1]), twist, low, high))
        backward = (row_inverse_half, (row_matrix(first, cols, lanes, None), twist, low_t, high_t))
        middle = lax.axis_index(("ty", "tx")) == devices // 2
    else:
        first = row_matrix(row_constants()[0], cols, lanes, None)
        twist, second, second_t = (jnp.asarray(value) for value in row_constants()[1:])
        part = (devices, 2, slab, slab)
        onward = (row_forward, (first, twist, second))
        backward = (row_inverse, (first, twist, second_t))
        extra = ()
        away = (inner, scale, inner_t, outer_t, data)
    split = (PATCH, devices // PATCH) + part[1:]
    sent = pl.pallas_call(
        onward[0], out_shape=jax.ShapeDtypeStruct(split, BF16), compiler_params=PARAMS
    )(*swap_pieces(pieces), *onward[1])
    if halved:
        sent, mirror, shift = lax.optimization_barrier((sent, mirror, shift))
        extra = (middle.astype(jnp.int32).reshape(1), phase_table(shift[0], devices, slab))
        table = mirrored_weight(scale, *mirror)
    moved = lax.all_to_all(
        sent.reshape(part), ("ty", "tx"), split_axis=0, concat_axis=0, tiled=True
    )
    if halved:
        moved, table, beside = lax.optimization_barrier((moved, table, beside))
        beside = from_neighbours(beside, 1)
        away = (inner, table, inner_t, outer_t)
    spaces = [pltpu.SMEM, pltpu.VMEM][: len(extra)] + [pltpu.VMEM] * 2 + [pl.ANY] * len(away)
    wave = pl.pallas_call(
        functools.partial(column_kernel, halved),
        in_specs=[pl.BlockSpec(memory_space=space) for space in spaces],
        out_shape=jax.ShapeDtypeStruct(part, BF16),
        scratch_shapes=[pltpu.VMEM((devices, 2, slab, slab), BF16)]
        + [pltpu.VMEM(value.shape, BF16) for value in away]
        + [pltpu.SemaphoreType.DMA((len(away),))],
        compiler_params=PARAMS,
    )(*extra, moved, outer, *away)
    if halved:
        wave, beside = lax.optimization_barrier((wave, beside))
    returned = lax.all_to_all(wave, ("ty", "tx"), split_axis=0, concat_axis=0, tiled=True)
    if not halved:
        returned, beside = lax.optimization_barrier((returned, beside))
    slabs = pl.pallas_call(
        backward[0],
        out_shape=[jax.ShapeDtypeStruct((own, cols, PIXELS), BF16)] * lanes,
        compiler_params=PARAMS,
    )(returned.reshape(split), *backward[1])
    return swap_pieces(slabs), beside


def layer_norm(values, gain):
    centre = jnp.mean(values, axis=-1, keepdims=True)
    shifted = values - centre
    spread = jnp.mean(shifted * shifted, axis=-1, keepdims=True)
    return (shifted * lax.rsqrt(spread + EPSILON) * gain).astype(BF16)


def to_windows(band):
    rows, cols, feats = band.shape
    pieces = [
        band[n : n + WIN, k : k + WIN, :].reshape(SPAN, feats)
        for n in range(0, rows, WIN)
        for k in range(0, cols, WIN)
    ]
    return jnp.concatenate(pieces, axis=0)


def from_windows(tokens, cols):
    feats = tokens.shape[-1]
    size = SPAN * cols // WIN
    bands = []
    for top in range(0, tokens.shape[0], size):
        pieces = [
            tokens[n : n + SPAN].reshape(WIN, WIN, feats) for n in range(top, top + size, SPAN)
        ]
        bands.append(jnp.concatenate(pieces, axis=1))
    return jnp.concatenate(bands, axis=0)


def gelu_twice(value):
    value = value.astype(BF16)
    inside = value * (BF16(GELU_IN) + BF16(GELU_CUBE) * (value * value))
    return value + value * jnp.tanh(inside)


def load_weights(j, sources, targets, sems):
    copies = [
        pltpu.make_async_copy(source.at[j], target, sems.at[n])
        for n, (source, target) in enumerate(zip(sources, targets))
    ]

    @pl.when(pl.program_id(0) == 0)
    def _():
        for copy in copies:
            copy.start()

    def wait(which):
        @pl.when(pl.program_id(0) == 0)
        def _():
            for n in which:
                copies[n].wait()

    return wait


def swin_band(flow, wait, bias_ref, gain_ref, weight_refs, scratch):
    qkv_ref, proj_ref, up_ref, down_ref = weight_refs
    mixed_ref, score_ref, prob_ref, active_ref = scratch
    count = flow.shape[0] // SPAN
    pairs = HEADS // 2
    depth = D // HEADS
    wide = 2 * depth
    normed = layer_norm(flow, gain_ref[0:1, :])
    scale = 1.0 / math.sqrt(depth)
    wait((0,))
    mixed_ref[:, :D] = (mm(normed, qkv_ref[:, :D]) * scale).astype(BF16)
    mixed_ref[:, D : 2 * D] = mm(normed, qkv_ref[:, D : 2 * D]).astype(BF16)
    mixed_ref[:, 2 * D :] = mm(normed, qkv_ref[:, 2 * D :]).astype(BF16)
    lower = lax.broadcasted_iota(jnp.int32, (SPAN, wide), 1) < depth

    def scores_of(w):
        rows = slice(w * SPAN, (w + 1) * SPAN)
        for p in range(pairs):
            query = mixed_ref[rows, p * wide : (p + 1) * wide]
            key = mixed_ref[rows, D + p * wide : D + (p + 1) * wide]
            zero = jnp.zeros_like(query)
            split = jnp.concatenate(
                [jnp.where(lower, query, zero), jnp.where(lower, zero, query)], axis=0
            )
            score_ref[w, :, p * wide : (p + 1) * wide] = mm(key, split, NT)

    def probs_of(w):
        bias = bias_ref[w]
        for p in range(pairs):
            lanes = slice(p * wide, (p + 1) * wide)
            scores = score_ref[w, :, lanes] + bias
            weights = jnp.exp(scores - jnp.max(scores, axis=0, keepdims=True))
            share = 1.0 / jnp.sum(weights, axis=0, keepdims=True)
            prob_ref[w, :, lanes] = (weights * share).astype(BF16)

    def mixture_of(w):
        rows = slice(w * SPAN, (w + 1) * SPAN)
        for p in range(pairs):
            lanes = slice(p * wide, (p + 1) * wide)
            value = mixed_ref[rows, 2 * D + p * wide : 2 * D + (p + 1) * wide]
            mixture = mm(prob_ref[w, :, lanes], value, TN)
            mixed_ref[rows, lanes] = jnp.where(lower, mixture[:SPAN], mixture[SPAN:]).astype(BF16)

    for turn in range(count + 2):
        if turn < count:
            scores_of(turn)
        if 0 <= turn - 1 < count:
            probs_of(turn - 1)
        if 0 <= turn - 2:
            mixture_of(turn - 2)
    wait((1, 2, 3))
    flow = flow + mm(mixed_ref[:, :D], proj_ref[...])
    normed = layer_norm(flow, gain_ref[1:2, :])
    chunks = up_ref.shape[1] // D
    for c in range(chunks):
        part = slice(c * D, (c + 1) * D)
        active_ref[:, part] = gelu_twice(mm(normed, up_ref[:, part]))
    return flow + 0.5 * mm(active_ref[...], down_ref[...])


def row_of(refs, row):
    size = refs[0].shape[0]
    value = refs[-1][jnp.clip(row - size * (len(refs) - 1), 0, size - 1)]
    for n in range(len(refs) - 2, -1, -1):
        here = refs[n][jnp.clip(row - size * n, 0, size - 1)]
        value = jnp.where(row < size * (n + 1), here, value)
    return value


def rolled_band(sign, top, shift_ref, refs, rows, count):
    *refs, edge_ref, corner_ref = refs
    main_refs, side_refs = refs[: len(refs) // 2], refs[len(refs) // 2 :]
    cols = main_refs[0].shape[1]
    top = top + sign * shift_ref[0]
    behind = -rows if sign > 0 else WIN
    beside = -cols if sign > 0 else WIN

    def pick(width, offset):
        source = lax.broadcasted_iota(jnp.int32, (cols, width), 1)
        wanted = lax.broadcasted_iota(jnp.int32, (cols, width), 0) + sign * shift_ref[1] + offset
        return jnp.where(source == wanted, 1.0, 0.0).astype(BF16)

    pick_main, pick_side = pick(cols, 0), pick(WIN, beside)
    band = []
    for j in range(count):
        row = top + j
        inside = (row >= 0) & (row < rows)
        there = jnp.clip(row + behind, 0, WIN - 1)
        main = jnp.where(inside, row_of(main_refs, row), edge_ref[there])
        side = jnp.where(inside, row_of(side_refs, row), corner_ref[there])
        band.append(mm(pick_main, main) + mm(pick_side, side))
    return jnp.stack(band)


def first_kernel(begin, zeta, sigma, count, parts, rows, before, backs, *refs):
    shift_ref, state_ref, *refs = refs
    if before is not None:
        back_refs, refs = refs[:backs], refs[backs:]
    grad_refs, refs = refs[: count * parts], refs[count * parts :]
    if sigma is not None:
        noise_ref, *refs = refs
    bias_ref, embed_ref, gain_ref, *sources = refs[:7]
    base_ref, out_ref, side_ref, *scratch = refs[7:]
    if begin == 0:
        edge_ref, corner_ref, *scratch = scratch
    targets, sems, scratch = scratch[:4], scratch[4], scratch[5:]
    wait = load_weights(0, sources, targets, sems)
    state = state_ref[...]
    if before is not None:
        top = begin * state.shape[0]
        state = state - before * rolled_band(-1, top, shift_ref, back_refs, rows, state.shape[0])
    height = state.shape[0]
    if parts == 1:
        grad = grad_refs[0][...].astype(F32)
    else:
        bands = []
        for k in range(height // WIN):
            turn = (begin * (height // WIN) + k) ^ shift_ref[2]
            band = 0.0
            for n in range(0, count * parts, parts):
                piece = grad_refs[n][...]
                for m in range(1, parts):
                    piece = jnp.where(turn == m, grad_refs[n + m][...], piece)
                band = band + piece.astype(F32)
            bands.append(band)
        grad = jnp.concatenate(bands, axis=0)
    step = zeta * grad
    half = state - step
    tokens = mm(to_windows(half).astype(BF16), embed_ref[...]).astype(BF16).astype(F32)
    flow = swin_band(tokens, wait, bias_ref, gain_ref, targets, scratch)
    result = from_windows(flow, half.shape[1]).astype(BF16)
    out_ref[:, :, :D] = result
    side_ref[:, :, :D] = result[:, :WIN]
    if sigma is None:
        base_ref[...] = half
    else:
        noise = sigma * noise_ref[...]
        base_ref[...] = half + noise
        change = (noise - step).astype(BF16)
        out_ref[:, :, D:] = change
        side_ref[:, :, D:] = change[:, :WIN]

    if begin == 0:
        edge_ref[...] = out_ref[:WIN]
        corner_ref[...] = side_ref[:WIN]


def write_pieces(turn, refs, value):
    for m, ref in enumerate(refs):

        def write(ref=ref):
            ref[...] = value

        pl.when(turn == m)(write)


def second_kernel(begin, edged, sigma, rows, tiles, parts, *refs):
    shift_ref, *refs = refs
    tile_refs, refs = refs[:tiles], refs[tiles:]
    bias_ref, unembed_ref, gain_ref, *sources = refs[:7]
    out_ref, side_ref, *scratch = refs[7:]
    if edged:
        edge_ref, corner_ref, *scratch = scratch
    state_refs, scratch = scratch[:parts], scratch[parts:]
    targets, sems, scratch = scratch[:4], scratch[4], scratch[5:]
    wait = load_weights(1, sources, targets, sems)
    height, cols, _ = out_ref.shape
    here = pl.program_id(0) + begin
    band = rolled_band(1, here * height, shift_ref, tile_refs, rows, height)
    tokens = to_windows(band[:, :, :D])
    flow = swin_band(tokens, wait, bias_ref, gain_ref, targets, scratch)
    estimate = from_windows(mm(flow.astype(BF16), unembed_ref[...]), cols)
    narrow = estimate.astype(BF16)
    out_ref[...] = narrow
    side_ref[...] = narrow[:, cols - WIN :]
    if edged:
        edge_ref[...] = narrow[height - WIN :]
        corner_ref[...] = narrow[height - WIN :, cols - WIN :]
    if parts > 0:
        change = (band[:, :, D:] - sigma * estimate).astype(BF16)
        for n in range(height // WIN):
            turn = (here * (height // WIN) + n) ^ shift_ref[2]
            write_pieces(turn, state_refs, change[n * WIN : (n + 1) * WIN])


def whole(array):
    zeros = (0,) * array.ndim
    return pl.BlockSpec(array.shape, lambda *_: zeros)


def member(array, j):
    place = (j,) + (0,) * (array.ndim - 1)
    return pl.BlockSpec((None,) + array.shape[1:], lambda *_: place)


def band_spec(cols, feats, height=WIN, begin=0):
    return pl.BlockSpec((height, cols, feats), lambda n, *_: (n + begin, 0, 0))


def bias_spec(cols, height, begin):
    count = height * cols // SPAN
    return pl.BlockSpec((count, SPAN, 2 * SPAN), lambda n, *_: (n + begin, 0, 0))


def band_scratch(cols, weights, height):
    count = height * cols // SPAN
    return [pltpu.VMEM(value.shape[1:], BF16) for value in weights] + [
        pltpu.SemaphoreType.DMA((len(weights),)),
        pltpu.VMEM((height * cols, 3 * D), BF16),
        pltpu.VMEM((count, SPAN, HEADS * SPAN), F32),
        pltpu.VMEM((count, SPAN, HEADS * SPAN), BF16),
        pltpu.VMEM((height * cols, weights[2].shape[2]), BF16),
    ]


def strip_outs(rows, cols, feats, height, edged):
    specs = [band_spec(cols, feats, height), band_spec(WIN, feats, height)]
    shapes = [(rows, cols), (rows, WIN)]
    if edged:
        specs += [
            pl.BlockSpec((WIN, width, feats), lambda *_: (0, 0, 0)) for width in (cols, WIN)
        ]
        shapes += [(WIN, cols), (WIN, WIN)]
    return specs, [jax.ShapeDtypeStruct(shape + (feats,), BF16) for shape in shapes]


def flat(tile):
    return [*tile[0], *tile[1], *tile[2:]]


def first_block(
    begin, rows, zeta, sigma, state, before, shift, back, grads, noise, bias, w_embed, weights
):
    *weights, gains = weights
    height, cols = HEIGHT, state.shape[1]
    parts = len(grads[0])
    pieces = [piece for grad in grads for piece in grad]
    fields = [] if sigma is None else [noise]
    feats = D if sigma is None else D + PIXELS
    specs, shapes = strip_outs(height, cols, feats, height, begin == 0)
    back = flat(back) if back else []
    band = band_spec(cols, PIXELS, height, begin)
    alone = band_spec(cols, PIXELS, height)
    return pl.pallas_call(
        functools.partial(
            first_kernel, begin, zeta, sigma, len(grads), parts, rows, before, len(back)
        ),
        grid_spec=pltpu.PrefetchScalarGridSpec(
            num_scalar_prefetch=1,
            grid=(1,),
            in_specs=[alone if state.shape[0] == height else band]
            + [whole(value) for value in back]
            + [band if parts == 1 else whole(value) for value in pieces]
            + [band] * len(fields)
            + [bias_spec(cols, height, begin), whole(w_embed), member(gains, 0)]
            + [pl.BlockSpec(memory_space=pl.ANY)] * len(weights),
            out_specs=[alone] + specs,
            scratch_shapes=band_scratch(cols, weights, height),
        ),
        out_shape=[jax.ShapeDtypeStruct((height, cols, PIXELS), F32)] + shapes,
        compiler_params=PARAMS,
    )(shift, state, *back, *pieces, *fields, bias, w_embed, gains, *weights)


def second_block(begin, steps, rows, sigma, shift, tile, bias, w_unembed, weights, parts):
    *weights, gains = weights
    height, cols = HEIGHT, tile[0][0].shape[1]
    tile = flat(tile)
    edged = (begin + steps) * height == rows
    specs, shapes = strip_outs(steps * height, cols, PIXELS, height, edged)
    specs += [pl.BlockSpec((WIN, cols, PIXELS), lambda *_: (0, 0, 0))] * parts
    shapes += [jax.ShapeDtypeStruct((WIN, cols, PIXELS), BF16)] * parts
    return pl.pallas_call(
        functools.partial(second_kernel, begin, edged, sigma, rows, len(tile), parts),
        grid_spec=pltpu.PrefetchScalarGridSpec(
            num_scalar_prefetch=1,
            grid=(steps,),
            in_specs=[whole(value) for value in tile]
            + [bias_spec(cols, height, begin), whole(w_unembed), member(gains, 1)]
            + [pl.BlockSpec(memory_space=pl.ANY)] * len(weights),
            out_specs=specs,
            scratch_shapes=band_scratch(cols, weights, height),
        ),
        out_shape=shapes,
        compiler_params=PARAMS,
    )(shift, *tile, bias, w_unembed, gains, *weights)


def from_neighbours(tile, by):
    mains, sides, edge, corner = tile
    ty, tx = lax.axis_size("ty"), lax.axis_size("tx")
    down = [(i, (i + by) % ty) for i in range(ty)]
    along = [(k, (k + by) % tx) for k in range(tx)]
    across = [(i * tx + k, i_to * tx + k_to) for i, i_to in down for k, k_to in along]
    return (
        mains,
        [lax.ppermute(side, "tx", along) for side in sides],
        lax.ppermute(edge, "ty", down),
        lax.ppermute(corner, ("ty", "tx"), across),
    )


def windows_of(grid):
    rows, cols = grid.shape
    shaped = grid.reshape(rows // WIN, WIN, cols // WIN, WIN).transpose(0, 2, 1, 3)
    return shaped.reshape(rows // WIN * (cols // WIN), SPAN)


def bias_of(labels, keep):
    allowed = jnp.ones((1, SPAN, SPAN), bool)
    if labels is not None:
        label = windows_of(labels)
        allowed = label[:, :, None] == label[:, None, :]
    if keep is not None:
        kept = windows_of(keep)[:, :, None] == 1
        allowed = allowed & (kept | jnp.eye(SPAN, dtype=bool)[None])
    bias = jnp.where(allowed, 0.0, -1e30).astype(F32)
    return jnp.concatenate([bias, bias], axis=2)


def region(index, shift):
    return jnp.where(index < TOK - WIN, 0, jnp.where(index < TOK - shift, 1, 2)).astype(jnp.int32)


@functools.lru_cache(maxsize=None)
def lane_order(cols):
    parts = LANES // cols
    groups = PATCH // parts
    lane = np.arange(PATCH * cols)
    g, h, k = lane // LANES, lane % LANES // cols, lane % cols
    source = PATCH * k + h * groups + g
    matrix = np.zeros((PATCH * cols, PATCH * cols), np.float32)
    matrix[source, lane] = 1.0
    return matrix.astype(ml_dtypes.bfloat16), np.ascontiguousarray(matrix.T).astype(
        ml_dtypes.bfloat16
    )


def move_lanes(values, matrix):
    high = values.astype(BF16)
    low = (values - high.astype(F32)).astype(BF16)
    return mm(high, matrix) + mm(low, matrix)


def to_patches_kernel(narrow, place_ref, tile_ref, order_ref, *out_refs):
    count, cols, _ = out_refs[0].shape
    parts = LANES // cols
    groups = PATCH // parts
    if narrow:
        ordered = mm(tile_ref[...].astype(BF16), order_ref[...])
    else:
        ordered = move_lanes(tile_ref[...], order_ref[...])
    patches = []
    for i in range(count):
        band = ordered[i * PATCH : (i + 1) * PATCH]
        stacked = jnp.concatenate(
            [band[:, g * LANES : (g + 1) * LANES] for g in range(groups)], axis=0
        )
        turned = stacked.T
        patches.append(
            jnp.concatenate([turned[h * cols : (h + 1) * cols] for h in range(parts)], axis=1)
        )
    result = jnp.stack(patches).astype(out_refs[0].dtype)
    if len(out_refs) == 1:
        out_refs[0][...] = result
    else:
        write_pieces(pl.program_id(0) ^ place_ref[0], out_refs, result)


def to_tile_kernel(sigma, scale, rows, bases, *refs):
    shift_ref, *refs = refs
    base_refs, refs = refs[:bases], refs[bases:]
    *back_refs, noise_ref, order_ref, out_ref = refs
    count, cols, _ = base_refs[0].shape
    here = pl.program_id(0)
    base = base_refs[0][...]
    for n in range(1, bases):
        base = jnp.where(here * count < n * (rows // bases), base, base_refs[n][...])
    parts = LANES // cols
    groups = PATCH // parts
    width = groups * PATCH
    state = base - sigma * rolled_band(-1, here * count, shift_ref, back_refs, rows, count)
    bands = []
    for i in range(count):
        stacked = jnp.concatenate(
            [state[i, :, h * width : (h + 1) * width] for h in range(parts)], axis=0
        )
        turned = stacked.T
        bands.append(
            jnp.concatenate([turned[g * PATCH : (g + 1) * PATCH] for g in range(groups)], axis=1)
        )
    moved = move_lanes(jnp.concatenate(bands, axis=0), order_ref[...])
    out_ref[...] = moved + scale * noise_ref[...]


def patches_of(tiles, j, place, kind=F32, parts=1):
    rows, cols = tiles.shape[1] // PATCH, tiles.shape[2] // PATCH
    order = jnp.asarray(lane_order(cols)[0])
    spec, shape = band_spec(cols, PIXELS), (rows, cols, PIXELS)
    if parts > 1:
        spec = pl.BlockSpec((WIN, cols, PIXELS), lambda *_: (0, 0, 0))
        shape = (WIN, cols, PIXELS)
    return pl.pallas_call(
        functools.partial(to_patches_kernel, kind == BF16),
        grid_spec=pltpu.PrefetchScalarGridSpec(
            num_scalar_prefetch=1,
            grid=(rows // WIN,),
            in_specs=[
                pl.BlockSpec((None, WIN * PATCH, cols * PATCH), lambda n, *_: (j, n, 0)),
                whole(order),
            ],
            out_specs=[spec] * parts,
        ),
        out_shape=[jax.ShapeDtypeStruct(shape, kind)] * parts,
        compiler_params=PARAMS,
    )(place, tiles, order)


def tile_of(bases, sigma, shift, back, scale, noise, j):
    size, cols, _ = bases[0].shape
    rows, steps = size * len(bases), size // WIN
    order = jnp.asarray(lane_order(cols)[1])
    back = flat(back)

    def part(m):
        return pl.BlockSpec(
            (WIN, cols, PIXELS), lambda n, *_: (jnp.clip(n - m * steps, 0, steps - 1), 0, 0)
        )

    return pl.pallas_call(
        functools.partial(to_tile_kernel, sigma, scale, rows, len(bases)),
        grid_spec=pltpu.PrefetchScalarGridSpec(
            num_scalar_prefetch=1,
            grid=(rows // WIN,),
            in_specs=[part(m) for m in range(len(bases))]
            + [whole(value) for value in back]
            + [
                pl.BlockSpec((None, WIN * PATCH, cols * PATCH), lambda n, *_: (j, n, 0)),
                whole(order),
            ],
            out_specs=pl.BlockSpec((WIN * PATCH, cols * PATCH), lambda n, *_: (n, 0)),
        ),
        out_shape=jax.ShapeDtypeStruct((rows * PATCH, cols * PATCH), F32),
        compiler_params=PARAMS,
    )(shift, *bases, *back, noise, order)


def per_device(
    image, noise, offsets, key_mask, gains, observed, vis_weight,
    w_embed, w_qkv, w_proj, w_up, w_down, w_unembed, norm_gains,
):
    rows = image.shape[0] // PATCH
    cols = image.shape[1] // PATCH
    devices = lax.axis_size("ty") * lax.axis_size("tx")
    lanes = lax.axis_size("tx")
    fast = N // devices == TOK // 2 and rows == lanes * WIN and lanes & (lanes - 1) == 0
    column = lax.axis_index("tx").astype(jnp.int32)[None]
    places = [jnp.concatenate([offsets[step], column]) for step in range(STEPS)]
    row_index = lax.axis_index("ty") * rows + counting(rows)
    col_index = lax.axis_index("tx") * cols + counting(cols)
    weights = (w_qkv, w_proj, w_up, w_down, norm_gains)
    w_embed = w_embed.reshape(PATCH, PATCH, D).transpose(1, 0, 2).reshape(PIXELS, D)
    w_unembed = w_unembed.reshape(D, PATCH, PATCH).transpose(0, 2, 1).reshape(D, PIXELS)
    state = patches_of(image[None], 0, column)[0]
    extras = [patches_of(noise, step, column)[0] for step in range(STEPS - 1)] + [None]
    first_bias = bias_of(None, key_mask)
    biases = []
    for step in range(STEPS):
        labels = (
            3 * region(row_index, offsets[step, 0])[:, None]
            + region(col_index, offsets[step, 1])[None, :]
        )
        biases.append(bias_of(labels, None))
    beside = (state, extras, first_bias, biases, w_embed, w_unembed)
    shift, before, back, moving, mirror = places[0], None, None, None, None
    halves = rows // HEIGHT
    grads = []
    if fast:
        weight, scale, data = spectrum_inputs(gains, observed, vis_weight, devices)
        half = weight.shape[0] // 2
        lines = (weight[half:], weight[:1])
        grad, (beside, lines) = patch_gradient(
            patches_of(image[None], 0, column, BF16, lanes), scale, data, None, None,
            (beside, lines),
        )
        grad, lines = lax.optimization_barrier((grad, lines))
        mirror = mirrored_exchange(*lines, devices)
        grads = [grad]
        state, extras, first_bias, biases, w_embed, w_unembed = beside
    state = [state] * halves
    for step in range(STEPS):
        if not fast:
            tile = image if step == 0 else tile_of(state, before, shift, back, 0.0, noise, 0)
            grad = plain_gradient(tile, gains, observed, vis_weight)
            grad = patches_of(grad.astype(F32)[None], 0, column, BF16)[0]
            grads = [[grad]]
        elif step > 0:
            grad, back = patch_gradient(moving, scale, None, shift, mirror, back)
            grads = grads + [grad]
        last = step + 1 == STEPS
        sigma = None if last else SIGMAS[step + 1]
        blocks = [
            first_block(
                m, rows, STEP_SIZES[step], sigma, state[m], before, shift, back, grads,
                extras[step], first_bias, w_embed, weights,
            )
            for m in range(halves)
        ]
        state, mains, sides = zip(*(block[:3] for block in blocks))
        shift, before = places[step], SIGMAS[step]
        if fast and step == 0:
            sides, mirror = lax.optimization_barrier((sides, mirror))
        first = from_neighbours((mains, sides, *blocks[0][3:]), -1)
        spans = [(m, 1) for m in range(halves)] if last else [(0, halves)]
        rolled = [
            second_block(
                m, steps, rows, before, shift, first, biases[step], w_unembed, weights,
                lanes if fast and not last else 0,
            )
            for m, steps in spans
        ]
        back = ([part[0] for part in rolled], [part[1] for part in rolled], *rolled[-1][2:4])
        moving = rolled[-1][4:]
        if last or not fast:
            back = from_neighbours(back, 1)
    return tile_of(state, before, shift, back, SIGMAS[STEPS], noise, STEPS - 1)


def solution(mesh):
    in_specs = (
        P("ty", "tx"),
        P(None, "ty", "tx"),
        P(),
        P("ty", "tx"),
        P(None, ("ty", "tx"), None),
        P(None, ("ty", "tx"), None),
        P(("ty", "tx"), None),
        P(),
        P(),
        P(),
        P(),
        P(),
        P(),
        P(),
    )
    out_specs = P("ty", "tx")
    return jax.shard_map(
        per_device, mesh=mesh, in_specs=in_specs, out_specs=out_specs, check_vma=False
    )
```

```python
import functools
import math

import jax
import jax.numpy as jnp
import ml_dtypes
import numpy as np
from jax import lax
from jax.experimental import pallas as pl
from jax.experimental.pallas import tpu as pltpu
from jax.sharding import PartitionSpec as P

N = 4096
PATCH = 16
PIXELS = PATCH * PATCH
WIN = 8
D = 512
HEADS = 8
STEPS = 2
SPAN = WIN * WIN
LANES = 128
GROUP = 8
TOK = N // PATCH

SIGMAS = (0.8, 0.5, 0.3)
STEP_SIZES = (0.9, 0.7)
EPSILON = 1e-05
HIGHEST = lax.Precision.HIGHEST
BF16 = jnp.bfloat16
F32 = jnp.float32
GELU_IN = math.sqrt(2.0 / math.pi)
GELU_CUBE = 0.044715 * GELU_IN
VMEM_LIMIT = 56 * 1024 * 1024
PARAMS = pltpu.CompilerParams(vmem_limit_bytes=VMEM_LIMIT)
TN = (((0,), (0,)), ((), ()))
NT = (((1,), (1,)), ((), ()))
NN = (((1,), (0,)), ((), ()))


def mm(left, right, dims=NN):
    return lax.dot_general(left, right, dims, preferred_element_type=F32)


def counting(length):
    return jnp.arange(length, dtype=jnp.int32)


def roots(length, outer, inner, sign):
    product = outer[:, None] * inner[None, :] % length
    angle = 2.0 * math.pi / length * product.astype(F32)
    return (jnp.cos(angle), sign * jnp.sin(angle))


def complex_einsum(form, left, right):
    real = jnp.einsum(form, left[0], right[0], precision=HIGHEST) - jnp.einsum(
        form, left[1], right[1], precision=HIGHEST
    )
    imag = jnp.einsum(form, left[0], right[1], precision=HIGHEST) + jnp.einsum(
        form, left[1], right[0], precision=HIGHEST
    )
    return (real, imag)


def complex_times(left, right):
    return (left[0] * right[0] - left[1] * right[1], left[0] * right[1] + left[1] * right[0])


def along_last(real_part, imag_part, groups, sign):
    rows, length = real_part.shape
    inner = length // groups
    first = roots(groups, counting(groups), counting(groups), sign)
    twist = roots(length, counting(inner), counting(groups), sign)
    second = roots(inner, counting(inner), counting(inner), sign)
    shaped = real_part.reshape(rows, groups, inner)
    if imag_part is None:
        partial_value = (
            jnp.einsum("mab,ka->mbk", shaped, first[0], precision=HIGHEST),
            jnp.einsum("mab,ka->mbk", shaped, first[1], precision=HIGHEST),
        )
    else:
        partial_value = complex_einsum(
            "mab,ka->mbk", (shaped, imag_part.reshape(rows, groups, inner)), first
        )
    partial_value = complex_times(partial_value, twist)
    result = complex_einsum("jb,mbk->mjk", second, partial_value)
    return (result[0].reshape(rows, length), result[1].reshape(rows, length))


def across_groups(pair, groups, sign):
    inner, cols = pair[0].shape
    width = cols // groups
    length = groups * inner
    first = roots(groups, counting(groups), counting(groups), sign)
    twist = roots(length, counting(inner), counting(groups), sign)
    second = roots(inner, counting(inner), counting(inner), sign)
    shaped = (pair[0].reshape(inner, groups, width), pair[1].reshape(inner, groups, width))
    partial_value = complex_einsum("bhc,kh->cbk", shaped, first)
    partial_value = complex_times(partial_value, twist)
    result = complex_einsum("jb,cbk->cjk", second, partial_value)
    return (result[0].reshape(width, length), result[1].reshape(width, length))


def exchange_pair(pair):
    return tuple(
        lax.all_to_all(
            part.astype(BF16), ("ty", "tx"), split_axis=1, concat_axis=1, tiled=True
        ).astype(F32)
        for part in pair
    )


def plain_gradient(tile, gains, observed, vis_weight):
    devices = lax.axis_size("ty") * lax.axis_size("tx")
    slab = lax.all_to_all(tile.astype(BF16), "tx", split_axis=0, concat_axis=1, tiled=True)
    moved = exchange_pair(along_last(slab.astype(F32), None, devices, -1.0))
    spectrum = across_groups(moved, devices, -1.0)
    spectrum = (spectrum[0] * (1.0 / N), spectrum[1] * (1.0 / N))
    model = complex_times((gains[0], gains[1]), spectrum)
    misfit = (vis_weight * (model[0] - observed[0]), vis_weight * (model[1] - observed[1]))
    back = complex_times((gains[0], -gains[1]), misfit)
    returned = exchange_pair(along_last(back[0], back[1], devices, 1.0))
    slab_grad = across_groups(returned, devices, 1.0)[0] * (1.0 / N)
    return lax.all_to_all(slab_grad.astype(BF16), "tx", split_axis=1, concat_axis=0, tiled=True)


def embed_complex(angle, row_axis, col_axis):
    cos, sin = np.cos(angle), np.sin(angle)
    top = np.stack([cos, sin], axis=col_axis)
    bottom = np.stack([-sin, cos], axis=col_axis)
    return np.stack([top, bottom], axis=row_axis)


def wheel(length, product):
    return 2.0 * math.pi / length * (product % length)


@functools.lru_cache(maxsize=None)
def row_constants():
    k = np.arange(TOK)
    angle = wheel(TOK, k[:, None] * k[None, :])
    first = np.concatenate([np.cos(angle), -np.sin(angle)], axis=1)
    b = np.repeat(np.arange(PATCH), PATCH)
    angle = wheel(N, b[:, None] * k[None, :])
    twist = np.stack([np.cos(angle), -np.sin(angle)])
    p = np.arange(PATCH)
    small = embed_complex(wheel(PATCH, p[:, None] * p[None, :]), 1, 1)
    second = np.einsum("kpqb,xy->kpxqby", small, np.eye(PATCH)).reshape(2 * PIXELS, 2 * PIXELS)
    return (
        first.astype(ml_dtypes.bfloat16),
        twist.astype(np.float32),
        second.astype(ml_dtypes.bfloat16),
        np.ascontiguousarray(second.T).astype(ml_dtypes.bfloat16),
    )


@functools.lru_cache(maxsize=None)
def half_constants():
    _, twist, second, _ = row_constants()
    half, quarter = TOK // 2, TOK // 4
    low = np.concatenate([1 + np.arange(quarter), 1 + half + np.arange(quarter)])
    digits = np.concatenate([low, low - 1])
    k = np.arange(TOK)
    angle = wheel(TOK, k[:, None] * digits[None, :])
    first = np.concatenate([np.cos(angle), -np.sin(angle)], axis=1)
    zero_line = np.concatenate([np.tile(np.eye(PATCH), PATCH), np.zeros((PATCH, PIXELS))], axis=1)
    upper = np.concatenate([second[PIXELS:].astype(np.float32), zero_line])
    lower = second[:PIXELS].astype(np.float32)
    return (first.astype(ml_dtypes.bfloat16), np.ascontiguousarray(twist[:, :, digits])) + tuple(
        np.ascontiguousarray(value).astype(ml_dtypes.bfloat16)
        for value in (lower, upper, lower.T, upper.T)
    )


@functools.lru_cache(maxsize=None)
def column_constants(devices, rows):
    s = np.arange(devices)
    small = embed_complex(wheel(devices, s[:, None] * s[None, :]), 1, 2)
    wide = devices * 2 * GROUP
    outer = np.einsum("qpsr,xy->qpxsry", small, np.eye(GROUP)).reshape(wide, wide)
    kr = s[:, None] + devices * np.arange(rows)[None, :]
    angle = wheel(N, kr[:, :, None] * np.arange(rows)[None, None, :])
    inner = embed_complex(angle, 1, 2).reshape(devices, 2 * rows, 2 * rows) / N
    return tuple(
        np.ascontiguousarray(value).astype(ml_dtypes.bfloat16)
        for value in (outer, outer.T, inner, inner.transpose(0, 2, 1))
    )


def row_forward(*refs):
    *x_refs, first_ref, twist_ref, second_ref, out_ref = refs
    count = x_refs[0].shape[0]

    def step(i, carry):
        band = jnp.concatenate([x_ref[i] for x_ref in x_refs], axis=0)
        mixed = mm(band, first_ref[...], TN)
        real, imag = mixed[:, :TOK], mixed[:, TOK:]
        tr, ti = twist_ref[0], twist_ref[1]
        turned = jnp.concatenate(
            [(real * tr - imag * ti).astype(BF16), (real * ti + imag * tr).astype(BF16)], axis=0
        )
        result = mm(second_ref[...], turned).astype(BF16).reshape(PATCH, 2, PATCH, TOK)
        half = TOK // 2
        rows = pl.ds(pl.multiple_of(i * PATCH, PATCH), PATCH)
        out_ref[:, 0, :, rows, :] = result[..., :half]
        out_ref[:, 1, :, rows, :] = result[..., half:]
        return carry

    lax.fori_loop(0, count, step, 0, unroll=8)


def row_inverse(v_ref, first_ref, twist_ref, second_ref, *out_refs):
    count, cols, _ = out_refs[0].shape

    def step(i, carry):
        rows = pl.ds(pl.multiple_of(i * PATCH, PATCH), PATCH)
        wide = jnp.concatenate(
            [
                v_ref[:, 0, :, rows, :].reshape(2 * PIXELS, TOK // 2),
                v_ref[:, 1, :, rows, :].reshape(2 * PIXELS, TOK // 2),
            ],
            axis=1,
        )
        mixed = mm(second_ref[...], wide)
        real, imag = mixed[:PIXELS], mixed[PIXELS:]
        tr, ti = twist_ref[0], twist_ref[1]
        turned = jnp.concatenate(
            [(real * tr + imag * ti).astype(BF16), (imag * tr - real * ti).astype(BF16)], axis=1
        )
        result = mm(first_ref[...], turned, NT).astype(BF16)
        for m, out_ref in enumerate(out_refs):
            out_ref[i] = result[m * cols : (m + 1) * cols]
        return carry

    lax.fori_loop(0, count, step, 0, unroll=8)


def lane_index(shape):
    return lax.broadcasted_iota(jnp.int32, shape, len(shape) - 1)


def swap_halves(values):
    return pltpu.roll(values, values.shape[-1] // 2, len(values.shape) - 1)


def row_forward_half(*refs):
    *x_refs, first_ref, twist_ref, lower_ref, upper_ref, out_ref = refs
    count = x_refs[0].shape[0]
    half = TOK // 2

    def packed(real, imag, rows, high):
        left = lane_index(real.shape) < half // 2
        out_ref[high, 0, rows, :] = jnp.where(left, real, swap_halves(imag)).astype(BF16)
        out_ref[high, 1, rows, :] = jnp.where(left, swap_halves(real), imag).astype(BF16)

    def step(i, carry):
        band = jnp.concatenate([x_ref[i] for x_ref in x_refs], axis=0)
        mixed = mm(band, first_ref[...], TN)
        real, imag = mixed[:, :TOK], mixed[:, TOK:]
        tr, ti = twist_ref[0], twist_ref[1]
        turned = jnp.concatenate(
            [(real * tr - imag * ti).astype(BF16), (real * ti + imag * tr).astype(BF16)], axis=0
        )
        rows = pl.ds(pl.multiple_of(i * PATCH, PATCH), PATCH)
        lower = mm(lower_ref[...], turned[:, :half]).reshape(PATCH // 2, 2, PATCH, half)
        packed(lower[:, 0], lower[:, 1], rows, slice(0, PATCH // 2))
        upper = mm(upper_ref[...], turned[:, half:])
        line = upper[PIXELS:]
        upper = upper[:PIXELS].reshape(PATCH // 2, 2, PATCH, half)
        imag = upper[:, 1]
        head = jnp.where(lane_index(line.shape) == 0, line, imag[0])
        imag = jnp.concatenate([head[None], imag[1:]], axis=0)
        packed(upper[:, 0], imag, rows, slice(PATCH // 2, PATCH))
        return carry

    lax.fori_loop(0, count, step, 0, unroll=8)


def row_inverse_half(v_ref, first_ref, twist_ref, lower_ref, upper_ref, *out_refs):
    count, cols, _ = out_refs[0].shape
    half = TOK // 2

    def unpacked(rows, high):
        even = v_ref[high, 0, rows, :].astype(F32)
        odd = v_ref[high, 1, rows, :].astype(F32)
        left = lane_index(even.shape) < half // 2
        return jnp.where(left, even, swap_halves(odd)), jnp.where(left, swap_halves(even), odd)

    def step(i, carry):
        rows = pl.ds(pl.multiple_of(i * PATCH, PATCH), PATCH)
        real, imag = unpacked(rows, slice(0, PATCH // 2))
        lower = jnp.stack([real, imag], axis=1).reshape(PIXELS, half)
        real, imag = unpacked(rows, slice(PATCH // 2, PATCH))
        head = imag[0]
        at_zero = lane_index(head.shape) == 0
        nothing = jnp.zeros_like(head)
        imag = jnp.concatenate([jnp.where(at_zero, nothing, head)[None], imag[1:]], axis=0)
        upper = jnp.stack([real, imag], axis=1).reshape(PIXELS, half)
        upper = jnp.concatenate([upper, jnp.where(at_zero, head, nothing)], axis=0)
        mixed = jnp.concatenate(
            [mm(lower_ref[...], lower.astype(BF16)), mm(upper_ref[...], upper.astype(BF16))], axis=1
        )
        real, imag = mixed[:PIXELS], mixed[PIXELS:]
        tr, ti = twist_ref[0], twist_ref[1]
        turned = jnp.concatenate(
            [(real * tr + imag * ti).astype(BF16), (imag * tr - real * ti).astype(BF16)], axis=1
        )
        result = mm(first_ref[...], turned, NT).astype(BF16)
        for m, out_ref in enumerate(out_refs):
            out_ref[i] = result[m * cols : (m + 1) * cols]
        return carry

    lax.fori_loop(0, count, step, 0, unroll=8)


def column_kernel(halved, *refs):
    if halved:
        flag_ref, phase_ref, refs = refs[0], refs[1], refs[2:]
    x_ref, outer_ref, *refs = refs
    count = 4 if halved else 5
    sources, out_ref = refs[:count], refs[count]
    mid_ref, *targets, sems = refs[count + 1 :]
    copies = [
        pltpu.make_async_copy(source, target, sems.at[n])
        for n, (source, target) in enumerate(zip(sources, targets))
    ]
    for copy in copies:
        copy.start()
    inner_ref, scale_ref, inner_t_ref, outer_t_ref = targets[:4]
    devices, _, rows, width = mid_ref.shape
    wide = devices * 2 * GROUP
    if halved:
        lane = lane_index((devices, PATCH, width))
        centre = flag_ref[0] == 1
        half = width // 2
        hidden = (lane == half) | (centre & (lane == 0))
        real_lane = (lane < half) | (centre & (lane == half))

    def load(place):
        if not halved:
            return x_ref[:, :, place, :].astype(F32)
        piece = x_ref[:, place, :].astype(F32)
        other = swap_halves(piece)
        return jnp.stack([piece, jnp.where(hidden, jnp.zeros_like(other), other)], axis=1)

    def store(place, value):
        if halved:
            value = jnp.where(real_lane, value[:, 0], swap_halves(value[:, 1])).astype(BF16)
            out_ref[:, place, :] = value
        else:
            out_ref[:, :, place, :] = value.astype(BF16)

    def outer(matrix_ref, value):
        groups = [
            value[:, :, n : n + GROUP, :].reshape(wide, width) for n in range(0, PATCH, GROUP)
        ]
        result = mm(matrix_ref[...], jnp.concatenate(groups, axis=1).astype(BF16))
        parts = [
            result[:, n : n + width].reshape(devices, 2, GROUP, width)
            for n in range(0, result.shape[1], width)
        ]
        return jnp.concatenate(parts, axis=2)

    for top in range(0, rows, PATCH):
        place = slice(top, top + PATCH)
        mid_ref[:, :, place, :] = outer(outer_ref, load(place)).astype(BF16)

    for n, copy in enumerate(copies):
        if n != 3:
            copy.wait()

    def step(q, carry):
        spectrum = mm(inner_ref[q], mid_ref[q].reshape(2 * rows, width))
        real, imag = spectrum[:rows], spectrum[rows:]
        scale = scale_ref[q].astype(F32)
        if halved:
            pr, pi = phase_ref[q, 0], phase_ref[q, 1]
            real = real.reshape(rows // 8, 8, width)
            imag = imag.reshape(rows // 8, 8, width)
            real, imag = real * pr - imag * pi, real * pi + imag * pr
            real, imag = real.reshape(rows, width) * scale, imag.reshape(rows, width) * scale
        else:
            data_ref = targets[4]
            real = real * scale - data_ref[0, q].astype(F32)
            imag = imag * scale - data_ref[1, q].astype(F32)
        back = jnp.concatenate([real.astype(BF16), imag.astype(BF16)], axis=0)
        mid_ref[q] = mm(inner_t_ref[q], back).astype(BF16).reshape(2, rows, width)
        return carry

    lax.fori_loop(0, devices, step, 0, unroll=8)
    copies[3].wait()

    for top in range(0, rows, PATCH):
        place = slice(top, top + PATCH)
        store(place, outer(outer_t_ref, mid_ref[:, :, place, :].astype(F32)))


def turned(value, devices):
    lines = value.shape[0]
    return value.astype(BF16).reshape(lines, N // devices, devices).transpose(2, 1, 0)


def spectrum_inputs(gains, observed, vis_weight, devices):
    gr, gi = gains[0], gains[1]
    weight = (vis_weight * (gr * gr + gi * gi)).astype(BF16)
    data = jnp.stack(
        [
            turned(vis_weight * (gr * observed[0] + gi * observed[1]), devices),
            turned(vis_weight * (gr * observed[1] - gi * observed[0]), devices),
        ]
    )
    return weight, turned(weight, devices), data


def mirror_kernel(scale_ref, got_ref, pick_ref, flip_ref, out_ref):
    devices = out_ref.shape[0]
    for q in range(devices):
        facing = mm(flip_ref[min(q, 1)], got_ref[(devices - q) % devices]).astype(BF16)
        total = mm(scale_ref[q], pick_ref[0]) + mm(facing, pick_ref[1])
        out_ref[q] = total.astype(BF16)


def mirrored_exchange(upper, line, devices):
    middle = devices // 2
    facing = [(e, devices - 1 - e) for e in range(devices)]
    partner = [(e, devices - e) for e in range(1, devices) if e != middle]
    partner = partner + [(0, middle), (middle, 0)]
    upper = lax.ppermute(upper, ("ty", "tx"), facing)
    line = lax.ppermute(line, ("ty", "tx"), partner)
    return upper, line


def mirrored_weight(scale, upper, line):
    devices, slab, _ = scale.shape
    half, middle = slab // 2, devices // 2
    me = lax.axis_index(("ty", "tx"))
    got = jnp.concatenate([upper, jnp.broadcast_to(line, (half, N))], axis=0)
    source = lax.broadcasted_iota(jnp.int32, (slab, slab), 0)
    slot = lax.broadcasted_iota(jnp.int32, (slab, slab), 1)
    low = (me < middle).astype(jnp.int32)
    own = (slot < half) & (source == slot + low)
    other = (slot < half) & (source == half - low - slot)
    other = other & ((me != middle) | (slot > 0))
    other = other | ((me == middle) & (slot == half) & (source == half))
    picks = jnp.stack([own, other]).astype(BF16)
    q2 = np.arange(slab)
    flips = np.stack([q2[:, None] == (slab - q2) % slab, q2[:, None] == slab - 1 - q2])
    return pl.pallas_call(
        mirror_kernel,
        out_shape=jax.ShapeDtypeStruct(scale.shape, BF16),
        compiler_params=PARAMS,
    )(scale, turned(got, devices), picks, jnp.asarray(flips.astype(ml_dtypes.bfloat16)))


def row_matrix(first, cols, lanes, shift):
    twice = jnp.asarray(np.concatenate([first, first[: 2 * WIN]], axis=0))
    me = lax.axis_index("tx")
    zero = jnp.zeros((), jnp.int32)
    starts = [(me ^ m) * cols + (0 if shift is None else shift) for m in range(lanes)]
    rows = [lax.dynamic_slice(twice, (start, zero), (cols, first.shape[1])) for start in starts]
    return jnp.concatenate(rows, axis=0)


def swap_pieces(pieces):
    lanes = len(pieces)
    return [pieces[0]] + [
        lax.ppermute(pieces[m], "tx", [(k, k ^ m) for k in range(lanes)]) for m in range(1, lanes)
    ]


def phase_table(shift, devices, width):
    kr = counting(devices)[:, None] + devices * counting(8)[None, :]
    angle = 2.0 * math.pi / TOK * (kr * shift % TOK).astype(F32)
    table = jnp.stack([jnp.cos(angle), -jnp.sin(angle)], axis=1)
    return jnp.broadcast_to(table[..., None], (devices, 2, 8, width))


def patch_gradient(pieces, scale, data, shift, mirror, beside):
    lanes = lax.axis_size("tx")
    devices = lax.axis_size("ty") * lanes
    own, cols, _ = pieces[0].shape
    slab = N // devices
    halved = data is None
    outer, outer_t, inner, inner_t = (
        jnp.asarray(value) for value in column_constants(devices, slab)
    )
    if halved:
        first = half_constants()[0]
        twist, low, high, low_t, high_t = (jnp.asarray(value) for value in half_constants()[1:])
        part = (devices, slab, slab)
        onward = (row_forward_half, (row_matrix(first, cols, lanes, shift[1]), twist, low, high))
        backward = (row_inverse_half, (row_matrix(first, cols, lanes, None), twist, low_t, high_t))
        middle = lax.axis_index(("ty", "tx")) == devices // 2
    else:
        first = row_matrix(row_constants()[0], cols, lanes, None)
        twist, second, second_t = (jnp.asarray(value) for value in row_constants()[1:])
        part = (devices, 2, slab, slab)
        onward = (row_forward, (first, twist, second))
        backward = (row_inverse, (first, twist, second_t))
        extra = ()
        away = (inner, scale, inner_t, outer_t, data)
    split = (PATCH, devices // PATCH) + part[1:]
    sent = pl.pallas_call(
        onward[0], out_shape=jax.ShapeDtypeStruct(split, BF16), compiler_params=PARAMS
    )(*swap_pieces(pieces), *onward[1])
    if halved:
        sent, mirror, shift = lax.optimization_barrier((sent, mirror, shift))
        extra = (middle.astype(jnp.int32).reshape(1), phase_table(shift[0], devices, slab))
        table = mirrored_weight(scale, *mirror)
    moved = lax.all_to_all(
        sent.reshape(part), ("ty", "tx"), split_axis=0, concat_axis=0, tiled=True
    )
    if halved:
        moved, table, beside = lax.optimization_barrier((moved, table, beside))
        beside = from_neighbours(beside, 1)
        away = (inner, table, inner_t, outer_t)
    spaces = [pltpu.SMEM, pltpu.VMEM][: len(extra)] + [pltpu.VMEM] * 2 + [pl.ANY] * len(away)
    wave = pl.pallas_call(
        functools.partial(column_kernel, halved),
        in_specs=[pl.BlockSpec(memory_space=space) for space in spaces],
        out_shape=jax.ShapeDtypeStruct(part, BF16),
        scratch_shapes=[pltpu.VMEM((devices, 2, slab, slab), BF16)]
        + [pltpu.VMEM(value.shape, BF16) for value in away]
        + [pltpu.SemaphoreType.DMA((len(away),))],
        compiler_params=PARAMS,
    )(*extra, moved, outer, *away)
    if halved:
        wave, beside = lax.optimization_barrier((wave, beside))
    returned = lax.all_to_all(wave, ("ty", "tx"), split_axis=0, concat_axis=0, tiled=True)
    if not halved:
        returned, beside = lax.optimization_barrier((returned, beside))
    slabs = pl.pallas_call(
        backward[0],
        out_shape=[jax.ShapeDtypeStruct((own, cols, PIXELS), BF16)] * lanes,
        compiler_params=PARAMS,
    )(returned.reshape(split), *backward[1])
    return swap_pieces(slabs), beside


def layer_norm(values, gain):
    centre = jnp.mean(values, axis=-1, keepdims=True)
    shifted = values - centre
    spread = jnp.mean(shifted * shifted, axis=-1, keepdims=True)
    return (shifted * lax.rsqrt(spread + EPSILON) * gain).astype(BF16)


def to_windows(band):
    rows, cols, feats = band.shape
    pieces = [
        band[n : n + WIN, k : k + WIN, :].reshape(SPAN, feats)
        for n in range(0, rows, WIN)
        for k in range(0, cols, WIN)
    ]
    return jnp.concatenate(pieces, axis=0)


def from_windows(tokens, cols):
    feats = tokens.shape[-1]
    size = SPAN * cols // WIN
    bands = []
    for top in range(0, tokens.shape[0], size):
        pieces = [
            tokens[n : n + SPAN].reshape(WIN, WIN, feats) for n in range(top, top + size, SPAN)
        ]
        bands.append(jnp.concatenate(pieces, axis=1))
    return jnp.concatenate(bands, axis=0)


def gelu_twice(value):
    value = value.astype(BF16)
    inside = value * (BF16(GELU_IN) + BF16(GELU_CUBE) * (value * value))
    return value + value * jnp.tanh(inside)


def load_weights(j, sources, targets, sems):
    copies = [
        pltpu.make_async_copy(source.at[j], target, sems.at[n])
        for n, (source, target) in enumerate(zip(sources, targets))
    ]

    @pl.when(pl.program_id(0) == 0)
    def _():
        for copy in copies:
            copy.start()

    def wait(which):
        @pl.when(pl.program_id(0) == 0)
        def _():
            for n in which:
                copies[n].wait()

    return wait


def swin_band(flow, wait, bias_ref, gain_ref, weight_refs, scratch, staggered):
    qkv_ref, proj_ref, up_ref, down_ref = weight_refs
    mixed_ref, score_ref, prob_ref, active_ref = scratch
    count = flow.shape[0] // SPAN
    pairs = HEADS // 2
    depth = D // HEADS
    wide = 2 * depth
    normed = layer_norm(flow, gain_ref[0:1, :])
    scale = 1.0 / math.sqrt(depth)
    wait((0,))
    mixed_ref[:, :D] = (mm(normed, qkv_ref[:, :D]) * scale).astype(BF16)
    mixed_ref[:, D : 2 * D] = mm(normed, qkv_ref[:, D : 2 * D]).astype(BF16)
    mixed_ref[:, 2 * D :] = mm(normed, qkv_ref[:, 2 * D :]).astype(BF16)
    lower = lax.broadcasted_iota(jnp.int32, (SPAN, wide), 1) < depth

    def scores_of(w):
        rows = slice(w * SPAN, (w + 1) * SPAN)
        for p in range(pairs):
            query = mixed_ref[rows, p * wide : (p + 1) * wide]
            key = mixed_ref[rows, D + p * wide : D + (p + 1) * wide]
            zero = jnp.zeros_like(query)
            split = jnp.concatenate(
                [jnp.where(lower, query, zero), jnp.where(lower, zero, query)], axis=0
            )
            score_ref[w, :, p * wide : (p + 1) * wide] = mm(key, split, NT)

    def probs_of(w):
        bias = bias_ref[w]
        for p in range(pairs):
            lanes = slice(p * wide, (p + 1) * wide)
            scores = score_ref[w, :, lanes] + bias
            weights = jnp.exp(scores - jnp.max(scores, axis=0, keepdims=True))
            share = 1.0 / jnp.sum(weights, axis=0, keepdims=True)
            prob_ref[w, :, lanes] = (weights * share).astype(BF16)

    def mixture_of(w):
        rows = slice(w * SPAN, (w + 1) * SPAN)
        for p in range(pairs):
            lanes = slice(p * wide, (p + 1) * wide)
            value = mixed_ref[rows, 2 * D + p * wide : 2 * D + (p + 1) * wide]
            mixture = mm(prob_ref[w, :, lanes], value, TN)
            mixed_ref[rows, lanes] = jnp.where(lower, mixture[:SPAN], mixture[SPAN:]).astype(BF16)

    passes = (scores_of, probs_of, mixture_of)
    if staggered:
        for turn in range(count + 2):
            for n, run in enumerate(passes):
                if 0 <= turn - n < count:
                    run(turn - n)
    else:
        for run in passes:
            for w in range(count):
                run(w)
    wait((1, 2, 3))
    flow = flow + mm(mixed_ref[:, :D], proj_ref[...])
    normed = layer_norm(flow, gain_ref[1:2, :])
    chunks = up_ref.shape[1] // D
    for c in range(chunks):
        part = slice(c * D, (c + 1) * D)
        active_ref[:, part] = gelu_twice(mm(normed, up_ref[:, part]))
    return flow + 0.5 * mm(active_ref[...], down_ref[...])


def rolled_band(sign, shift_ref, refs, rows, count=WIN):
    main_ref, side_ref, edge_ref, corner_ref = refs
    cols = main_ref.shape[1]
    top = pl.program_id(0) * count + sign * shift_ref[0]
    behind = -rows if sign > 0 else WIN
    beside = -cols if sign > 0 else WIN

    source = lax.broadcasted_iota(jnp.int32, (cols, cols + WIN), 1)
    wanted = lax.broadcasted_iota(jnp.int32, (cols, cols + WIN), 0) + sign * shift_ref[1]
    found = (source < cols) & (source == wanted)
    found = found | (source >= cols) & (source - cols == wanted + beside)
    pick = jnp.where(found, 1.0, 0.0).astype(BF16)
    band = []
    for j in range(count):
        row = top + j
        inside = (row >= 0) & (row < rows)
        here, there = jnp.clip(row, 0, rows - 1), jnp.clip(row + behind, 0, WIN - 1)
        main = jnp.where(inside, main_ref[here], edge_ref[there])
        side = jnp.where(inside, side_ref[here], corner_ref[there])
        band.append(mm(pick, jnp.concatenate([main, side], axis=0)))
    return jnp.stack(band)


def first_kernel(zeta, sigma, count, parts, rows, before, *refs):
    shift_ref, state_ref, *refs = refs
    if before is not None:
        back_refs, refs = refs[:4], refs[4:]
    grad_refs, refs = refs[: count * parts], refs[count * parts :]
    if sigma is not None:
        noise_ref, *refs = refs
    bias_ref, embed_ref, gain_ref, *sources = refs[:7]
    base_ref, out_ref, side_ref, edge_ref, corner_ref, *scratch = refs[7:]
    targets, sems, scratch = scratch[:4], scratch[4], scratch[5:]
    wait = load_weights(0, sources, targets, sems)
    state = state_ref[...]
    if before is not None:
        state = state - before * rolled_band(-1, shift_ref, back_refs, rows, state.shape[0])
    height = state.shape[0]
    if parts == 1:
        grad = grad_refs[0][...].astype(F32)
    else:
        bands = []
        for k in range(height // WIN):
            turn = (pl.program_id(0) * (height // WIN) + k) ^ shift_ref[2]
            band = 0.0
            for n in range(0, count * parts, parts):
                piece = grad_refs[n][...]
                for m in range(1, parts):
                    piece = jnp.where(turn == m, grad_refs[n + m][...], piece)
                band = band + piece.astype(F32)
            bands.append(band)
        grad = jnp.concatenate(bands, axis=0)
    step = zeta * grad
    half = state - step
    tokens = mm(to_windows(half).astype(BF16), embed_ref[...]).astype(BF16).astype(F32)
    flow = swin_band(tokens, wait, bias_ref, gain_ref, targets, scratch, True)
    result = from_windows(flow, half.shape[1]).astype(BF16)
    out_ref[:, :, :D] = result
    side_ref[:, :, :D] = result[:, :WIN]
    if sigma is None:
        base_ref[...] = half
    else:
        noise = sigma * noise_ref[...]
        base_ref[...] = half + noise
        change = (noise - step).astype(BF16)
        out_ref[:, :, D:] = change
        side_ref[:, :, D:] = change[:, :WIN]

    @pl.when(pl.program_id(0) == 0)
    def _():
        edge_ref[...] = out_ref[:WIN]
        corner_ref[...] = side_ref[:WIN]


def write_pieces(turn, refs, value):
    for m, ref in enumerate(refs):

        def write(ref=ref):
            ref[...] = value

        pl.when(turn == m)(write)


def second_kernel(sigma, rows, parts, *refs):
    shift_ref, *refs = refs
    tile_refs, refs = refs[:4], refs[4:]
    bias_ref, unembed_ref, gain_ref, *sources = refs[:7]
    out_ref, side_ref, edge_ref, corner_ref, *scratch = refs[7:]
    state_refs, scratch = scratch[:parts], scratch[parts:]
    targets, sems, scratch = scratch[:4], scratch[4], scratch[5:]
    wait = load_weights(1, sources, targets, sems)
    height, cols, _ = out_ref.shape
    band = rolled_band(1, shift_ref, tile_refs, rows, height)
    tokens = to_windows(band[:, :, :D])
    flow = swin_band(tokens, wait, bias_ref, gain_ref, targets, scratch, False)
    estimate = from_windows(mm(flow.astype(BF16), unembed_ref[...]), cols)
    narrow = estimate.astype(BF16)
    out_ref[...] = narrow
    side_ref[...] = narrow[:, cols - WIN :]
    edge_ref[...] = narrow[height - WIN :]
    corner_ref[...] = narrow[height - WIN :, cols - WIN :]
    if parts > 0:
        change = (band[:, :, D:] - sigma * estimate).astype(BF16)
        for n in range(height // WIN):
            turn = (pl.program_id(0) * (height // WIN) + n) ^ shift_ref[2]
            write_pieces(turn, state_refs, change[n * WIN : (n + 1) * WIN])


def whole(array):
    zeros = (0,) * array.ndim
    return pl.BlockSpec(array.shape, lambda *_: zeros)


def member(array, j):
    place = (j,) + (0,) * (array.ndim - 1)
    return pl.BlockSpec((None,) + array.shape[1:], lambda *_: place)


def band_spec(cols, feats, height=WIN):
    return pl.BlockSpec((height, cols, feats), lambda n, *_: (n, 0, 0))


def bias_spec(cols, height=WIN):
    count = height * cols // SPAN
    return pl.BlockSpec((count, SPAN, 2 * SPAN), lambda n, *_: (n, 0, 0))


def band_scratch(cols, weights, height=WIN):
    count = height * cols // SPAN
    return [pltpu.VMEM(value.shape[1:], BF16) for value in weights] + [
        pltpu.SemaphoreType.DMA((len(weights),)),
        pltpu.VMEM((height * cols, 3 * D), BF16),
        pltpu.VMEM((count, SPAN, HEADS * SPAN), F32),
        pltpu.VMEM((count, SPAN, HEADS * SPAN), BF16),
    ]


def strip_outs(rows, cols, feats, height=WIN):
    specs = [band_spec(cols, feats, height), band_spec(WIN, feats, height)]
    specs += [
        pl.BlockSpec((WIN, width, feats), lambda *_: (0, 0, 0)) for width in (cols, WIN)
    ]
    shapes = [(rows, cols), (rows, WIN), (WIN, cols), (WIN, WIN)]
    return specs, [jax.ShapeDtypeStruct(shape + (feats,), BF16) for shape in shapes]


def first_block(zeta, sigma, state, before, shift, back, grads, noise, bias, w_embed, weights):
    *weights, gains = weights
    rows, cols, _ = state.shape
    parts = len(grads[0])
    pieces = [piece for grad in grads for piece in grad]
    fields = [] if sigma is None else [noise]
    feats = D if sigma is None else D + PIXELS
    height = 2 * WIN
    specs, shapes = strip_outs(rows, cols, feats, height)
    band = band_spec(cols, PIXELS, height)
    return pl.pallas_call(
        functools.partial(first_kernel, zeta, sigma, len(grads), parts, rows, before),
        grid_spec=pltpu.PrefetchScalarGridSpec(
            num_scalar_prefetch=1,
            grid=(rows // height,),
            in_specs=[band]
            + [whole(value) for value in back]
            + [band if parts == 1 else whole(value) for value in pieces]
            + [band] * len(fields)
            + [bias_spec(cols, height), whole(w_embed), member(gains, 0)]
            + [pl.BlockSpec(memory_space=pl.ANY)] * len(weights),
            out_specs=[band] + specs,
            scratch_shapes=band_scratch(cols, weights, height)
            + [pltpu.VMEM((height * cols, weights[2].shape[2]), BF16)],
        ),
        out_shape=[jax.ShapeDtypeStruct((rows, cols, PIXELS), F32)] + shapes,
        compiler_params=PARAMS,
    )(shift, state, *back, *pieces, *fields, bias, w_embed, gains, *weights)


def second_block(sigma, shift, tile, bias, w_unembed, weights, parts):
    *weights, gains = weights
    rows, cols, _ = tile[0].shape
    height = 2 * WIN
    specs, shapes = strip_outs(rows, cols, PIXELS, height)
    specs += [pl.BlockSpec((WIN, cols, PIXELS), lambda *_: (0, 0, 0))] * parts
    shapes += [jax.ShapeDtypeStruct((WIN, cols, PIXELS), BF16)] * parts
    return pl.pallas_call(
        functools.partial(second_kernel, sigma, rows, parts),
        grid_spec=pltpu.PrefetchScalarGridSpec(
            num_scalar_prefetch=1,
            grid=(rows // height,),
            in_specs=[whole(value) for value in tile]
            + [bias_spec(cols, height), whole(w_unembed), member(gains, 1)]
            + [pl.BlockSpec(memory_space=pl.ANY)] * len(weights),
            out_specs=specs,
            scratch_shapes=band_scratch(cols, weights, height)
            + [pltpu.VMEM((height * cols, weights[2].shape[2]), BF16)],
        ),
        out_shape=shapes,
        compiler_params=PARAMS,
    )(shift, *tile, bias, w_unembed, gains, *weights)


def from_neighbours(tile, by):
    main, side, edge, corner = tile
    ty, tx = lax.axis_size("ty"), lax.axis_size("tx")
    across = [
        (i * tx + k, (i + by) % ty * tx + (k + by) % tx) for i in range(ty) for k in range(tx)
    ]
    return (
        main,
        lax.ppermute(side, "tx", [(k, (k + by) % tx) for k in range(tx)]),
        lax.ppermute(edge, "ty", [(i, (i + by) % ty) for i in range(ty)]),
        lax.ppermute(corner, ("ty", "tx"), across),
    )


def windows_of(grid):
    rows, cols = grid.shape
    shaped = grid.reshape(rows // WIN, WIN, cols // WIN, WIN).transpose(0, 2, 1, 3)
    return shaped.reshape(rows // WIN * (cols // WIN), SPAN)


def bias_of(labels, keep):
    allowed = jnp.ones((1, SPAN, SPAN), bool)
    if labels is not None:
        label = windows_of(labels)
        allowed = label[:, :, None] == label[:, None, :]
    if keep is not None:
        kept = windows_of(keep)[:, :, None] == 1
        allowed = allowed & (kept | jnp.eye(SPAN, dtype=bool)[None])
    bias = jnp.where(allowed, 0.0, -1e30).astype(F32)
    return jnp.concatenate([bias, bias], axis=2)


def region(index, shift):
    return jnp.where(index < TOK - WIN, 0, jnp.where(index < TOK - shift, 1, 2)).astype(jnp.int32)


@functools.lru_cache(maxsize=None)
def lane_order(cols):
    parts = LANES // cols
    groups = PATCH // parts
    lane = np.arange(PATCH * cols)
    g, h, k = lane // LANES, lane % LANES // cols, lane % cols
    source = PATCH * k + h * groups + g
    matrix = np.zeros((PATCH * cols, PATCH * cols), np.float32)
    matrix[source, lane] = 1.0
    return matrix.astype(ml_dtypes.bfloat16), np.ascontiguousarray(matrix.T).astype(
        ml_dtypes.bfloat16
    )


def move_lanes(values, matrix):
    high = values.astype(BF16)
    low = (values - high.astype(F32)).astype(BF16)
    return mm(high, matrix) + mm(low, matrix)


def to_patches_kernel(narrow, place_ref, tile_ref, order_ref, *out_refs):
    count, cols, _ = out_refs[0].shape
    parts = LANES // cols
    groups = PATCH // parts
    if narrow:
        ordered = mm(tile_ref[...].astype(BF16), order_ref[...])
    else:
        ordered = move_lanes(tile_ref[...], order_ref[...])
    patches = []
    for i in range(count):
        band = ordered[i * PATCH : (i + 1) * PATCH]
        stacked = jnp.concatenate(
            [band[:, g * LANES : (g + 1) * LANES] for g in range(groups)], axis=0
        )
        turned = stacked.T
        patches.append(
            jnp.concatenate([turned[h * cols : (h + 1) * cols] for h in range(parts)], axis=1)
        )
    result = jnp.stack(patches).astype(out_refs[0].dtype)
    if len(out_refs) == 1:
        out_refs[0][...] = result
    else:
        write_pieces(pl.program_id(0) ^ place_ref[0], out_refs, result)


def to_tile_kernel(sigma, scale, rows, *refs):
    shift_ref, base_ref, *refs = refs
    noise_ref, order_ref, out_ref = refs[4:]
    count, cols, _ = base_ref.shape
    parts = LANES // cols
    groups = PATCH // parts
    width = groups * PATCH
    state = base_ref[...] - sigma * rolled_band(-1, shift_ref, refs[:4], rows)
    bands = []
    for i in range(count):
        stacked = jnp.concatenate(
            [state[i, :, h * width : (h + 1) * width] for h in range(parts)], axis=0
        )
        turned = stacked.T
        bands.append(
            jnp.concatenate([turned[g * PATCH : (g + 1) * PATCH] for g in range(groups)], axis=1)
        )
    moved = move_lanes(jnp.concatenate(bands, axis=0), order_ref[...])
    out_ref[...] = moved + scale * noise_ref[...]


def patches_of(tiles, j, place, kind=F32, parts=1):
    rows, cols = tiles.shape[1] // PATCH, tiles.shape[2] // PATCH
    order = jnp.asarray(lane_order(cols)[0])
    spec, shape = band_spec(cols, PIXELS), (rows, cols, PIXELS)
    if parts > 1:
        spec = pl.BlockSpec((WIN, cols, PIXELS), lambda *_: (0, 0, 0))
        shape = (WIN, cols, PIXELS)
    return pl.pallas_call(
        functools.partial(to_patches_kernel, kind == BF16),
        grid_spec=pltpu.PrefetchScalarGridSpec(
            num_scalar_prefetch=1,
            grid=(rows // WIN,),
            in_specs=[
                pl.BlockSpec((None, WIN * PATCH, cols * PATCH), lambda n, *_: (j, n, 0)),
                whole(order),
            ],
            out_specs=[spec] * parts,
        ),
        out_shape=[jax.ShapeDtypeStruct(shape, kind)] * parts,
        compiler_params=PARAMS,
    )(place, tiles, order)


def tile_of(base, sigma, shift, back, scale, noise, j):
    rows, cols, _ = base.shape
    order = jnp.asarray(lane_order(cols)[1])
    return pl.pallas_call(
        functools.partial(to_tile_kernel, sigma, scale, rows),
        grid_spec=pltpu.PrefetchScalarGridSpec(
            num_scalar_prefetch=1,
            grid=(rows // WIN,),
            in_specs=[band_spec(cols, PIXELS)]
            + [whole(value) for value in back]
            + [
                pl.BlockSpec((None, WIN * PATCH, cols * PATCH), lambda n, *_: (j, n, 0)),
                whole(order),
            ],
            out_specs=pl.BlockSpec((WIN * PATCH, cols * PATCH), lambda n, *_: (n, 0)),
        ),
        out_shape=jax.ShapeDtypeStruct((rows * PATCH, cols * PATCH), F32),
        compiler_params=PARAMS,
    )(shift, base, *back, noise, order)


def per_device(
    image, noise, offsets, key_mask, gains, observed, vis_weight,
    w_embed, w_qkv, w_proj, w_up, w_down, w_unembed, norm_gains,
):
    rows = image.shape[0] // PATCH
    cols = image.shape[1] // PATCH
    devices = lax.axis_size("ty") * lax.axis_size("tx")
    lanes = lax.axis_size("tx")
    fast = N // devices == TOK // 2 and rows == lanes * WIN and lanes & (lanes - 1) == 0
    column = lax.axis_index("tx").astype(jnp.int32)[None]
    places = [jnp.concatenate([offsets[step], column]) for step in range(STEPS)]
    row_index = lax.axis_index("ty") * rows + counting(rows)
    col_index = lax.axis_index("tx") * cols + counting(cols)
    weights = (w_qkv, w_proj, w_up, w_down, norm_gains)
    w_embed = w_embed.reshape(PATCH, PATCH, D).transpose(1, 0, 2).reshape(PIXELS, D)
    w_unembed = w_unembed.reshape(D, PATCH, PATCH).transpose(0, 2, 1).reshape(D, PIXELS)
    state = patches_of(image[None], 0, column)[0]
    extras = [patches_of(noise, step, column)[0] for step in range(STEPS - 1)] + [None]
    first_bias = bias_of(None, key_mask)
    biases = []
    for step in range(STEPS):
        labels = (
            3 * region(row_index, offsets[step, 0])[:, None]
            + region(col_index, offsets[step, 1])[None, :]
        )
        biases.append(bias_of(labels, None))
    beside = (state, extras, first_bias, biases, w_embed, w_unembed)
    shift, before, back, moving, mirror = places[0], None, (), None, None
    grads = []
    if fast:
        weight, scale, data = spectrum_inputs(gains, observed, vis_weight, devices)
        half = weight.shape[0] // 2
        lines = (weight[half:], weight[:1])
        grad, (beside, lines) = patch_gradient(
            patches_of(image[None], 0, column, BF16, lanes), scale, data, None, None,
            (beside, lines),
        )
        grad, lines = lax.optimization_barrier((grad, lines))
        mirror = mirrored_exchange(*lines, devices)
        grads = [grad]
        state, extras, first_bias, biases, w_embed, w_unembed = beside
    for step in range(STEPS):
        if not fast:
            tile = image if step == 0 else tile_of(state, before, shift, back, 0.0, noise, 0)
            grad = plain_gradient(tile, gains, observed, vis_weight)
            grad = patches_of(grad.astype(F32)[None], 0, column, BF16)[0]
            grads = [[grad]]
        elif step > 0:
            grad, back = patch_gradient(moving, scale, None, shift, mirror, back)
            grads = grads + [grad]
        last = step + 1 == STEPS
        sigma = None if last else SIGMAS[step + 1]
        state, *first = first_block(
            STEP_SIZES[step], sigma, state, before, shift, back, grads, extras[step], first_bias,
            w_embed, weights,
        )
        shift, before = places[step], SIGMAS[step]
        if fast and step == 0:
            first, mirror = lax.optimization_barrier((first, mirror))
        rolled = second_block(
            before, shift, from_neighbours(first, -1), biases[step], w_unembed, weights,
            lanes if fast and not last else 0,
        )
        back, moving = rolled[:4], rolled[4:]
        if last or not fast:
            back = from_neighbours(back, 1)
    return tile_of(state, before, shift, back, SIGMAS[STEPS], noise, STEPS - 1)


def solution(mesh):
    in_specs = (
        P("ty", "tx"),
        P(None, "ty", "tx"),
        P(),
        P("ty", "tx"),
        P(None, ("ty", "tx"), None),
        P(None, ("ty", "tx"), None),
        P(("ty", "tx"), None),
        P(),
        P(),
        P(),
        P(),
        P(),
        P(),
        P(),
    )
    out_specs = P("ty", "tx")
    return jax.shard_map(
        per_device, mesh=mesh, in_specs=in_specs, out_specs=out_specs, check_vma=False
    )
```

```python
import functools
import math

import jax
import jax.numpy as jnp
import ml_dtypes
import numpy as np
from jax import lax
from jax.experimental import pallas as pl
from jax.experimental.pallas import tpu as pltpu
from jax.sharding import PartitionSpec as P

N = 4096
PATCH = 16
PIXELS = PATCH * PATCH
WIN = 8
D = 512
HEADS = 8
STEPS = 2
SPAN = WIN * WIN
LANES = 128
GROUP = 8
TOK = N // PATCH

SIGMAS = (0.8, 0.5, 0.3)
STEP_SIZES = (0.9, 0.7)
EPSILON = 1e-05
HIGHEST = lax.Precision.HIGHEST
BF16 = jnp.bfloat16
F32 = jnp.float32
GELU_IN = math.sqrt(2.0 / math.pi)
GELU_CUBE = 0.044715 * GELU_IN
VMEM_LIMIT = 56 * 1024 * 1024
PARAMS = pltpu.CompilerParams(vmem_limit_bytes=VMEM_LIMIT)
TN = (((0,), (0,)), ((), ()))
NT = (((1,), (1,)), ((), ()))
NN = (((1,), (0,)), ((), ()))


def mm(left, right, dims=NN):
    return lax.dot_general(left, right, dims, preferred_element_type=F32)


def counting(length):
    return jnp.arange(length, dtype=jnp.int32)


def roots(length, outer, inner, sign):
    product = outer[:, None] * inner[None, :] % length
    angle = 2.0 * math.pi / length * product.astype(F32)
    return (jnp.cos(angle), sign * jnp.sin(angle))


def complex_einsum(form, left, right):
    real = jnp.einsum(form, left[0], right[0], precision=HIGHEST) - jnp.einsum(
        form, left[1], right[1], precision=HIGHEST
    )
    imag = jnp.einsum(form, left[0], right[1], precision=HIGHEST) + jnp.einsum(
        form, left[1], right[0], precision=HIGHEST
    )
    return (real, imag)


def complex_times(left, right):
    return (left[0] * right[0] - left[1] * right[1], left[0] * right[1] + left[1] * right[0])


def along_last(real_part, imag_part, groups, sign):
    rows, length = real_part.shape
    inner = length // groups
    first = roots(groups, counting(groups), counting(groups), sign)
    twist = roots(length, counting(inner), counting(groups), sign)
    second = roots(inner, counting(inner), counting(inner), sign)
    shaped = real_part.reshape(rows, groups, inner)
    if imag_part is None:
        partial_value = (
            jnp.einsum("mab,ka->mbk", shaped, first[0], precision=HIGHEST),
            jnp.einsum("mab,ka->mbk", shaped, first[1], precision=HIGHEST),
        )
    else:
        partial_value = complex_einsum(
            "mab,ka->mbk", (shaped, imag_part.reshape(rows, groups, inner)), first
        )
    partial_value = complex_times(partial_value, twist)
    result = complex_einsum("jb,mbk->mjk", second, partial_value)
    return (result[0].reshape(rows, length), result[1].reshape(rows, length))


def across_groups(pair, groups, sign):
    inner, cols = pair[0].shape
    width = cols // groups
    length = groups * inner
    first = roots(groups, counting(groups), counting(groups), sign)
    twist = roots(length, counting(inner), counting(groups), sign)
    second = roots(inner, counting(inner), counting(inner), sign)
    shaped = (pair[0].reshape(inner, groups, width), pair[1].reshape(inner, groups, width))
    partial_value = complex_einsum("bhc,kh->cbk", shaped, first)
    partial_value = complex_times(partial_value, twist)
    result = complex_einsum("jb,cbk->cjk", second, partial_value)
    return (result[0].reshape(width, length), result[1].reshape(width, length))


def exchange_pair(pair):
    return tuple(
        lax.all_to_all(
            part.astype(BF16), ("ty", "tx"), split_axis=1, concat_axis=1, tiled=True
        ).astype(F32)
        for part in pair
    )


def plain_gradient(tile, gains, observed, vis_weight):
    devices = lax.axis_size("ty") * lax.axis_size("tx")
    slab = lax.all_to_all(tile.astype(BF16), "tx", split_axis=0, concat_axis=1, tiled=True)
    moved = exchange_pair(along_last(slab.astype(F32), None, devices, -1.0))
    spectrum = across_groups(moved, devices, -1.0)
    spectrum = (spectrum[0] * (1.0 / N), spectrum[1] * (1.0 / N))
    model = complex_times((gains[0], gains[1]), spectrum)
    misfit = (vis_weight * (model[0] - observed[0]), vis_weight * (model[1] - observed[1]))
    back = complex_times((gains[0], -gains[1]), misfit)
    returned = exchange_pair(along_last(back[0], back[1], devices, 1.0))
    slab_grad = across_groups(returned, devices, 1.0)[0] * (1.0 / N)
    return lax.all_to_all(slab_grad.astype(BF16), "tx", split_axis=1, concat_axis=0, tiled=True)


def embed_complex(angle, row_axis, col_axis):
    cos, sin = np.cos(angle), np.sin(angle)
    top = np.stack([cos, sin], axis=col_axis)
    bottom = np.stack([-sin, cos], axis=col_axis)
    return np.stack([top, bottom], axis=row_axis)


def wheel(length, product):
    return 2.0 * math.pi / length * (product % length)


@functools.lru_cache(maxsize=None)
def row_constants():
    k = np.arange(TOK)
    angle = wheel(TOK, k[:, None] * k[None, :])
    first = np.concatenate([np.cos(angle), -np.sin(angle)], axis=1)
    b = np.repeat(np.arange(PATCH), PATCH)
    angle = wheel(N, b[:, None] * k[None, :])
    twist = np.stack([np.cos(angle), -np.sin(angle)])
    p = np.arange(PATCH)
    small = embed_complex(wheel(PATCH, p[:, None] * p[None, :]), 1, 1)
    second = np.einsum("kpqb,xy->kpxqby", small, np.eye(PATCH)).reshape(2 * PIXELS, 2 * PIXELS)
    return (
        first.astype(ml_dtypes.bfloat16),
        twist.astype(np.float32),
        second.astype(ml_dtypes.bfloat16),
        np.ascontiguousarray(second.T).astype(ml_dtypes.bfloat16),
    )


@functools.lru_cache(maxsize=None)
def half_constants():
    _, twist, second, _ = row_constants()
    half, quarter = TOK // 2, TOK // 4
    low = np.concatenate([1 + np.arange(quarter), 1 + half + np.arange(quarter)])
    digits = np.concatenate([low, low - 1])
    k = np.arange(TOK)
    angle = wheel(TOK, k[:, None] * digits[None, :])
    first = np.concatenate([np.cos(angle), -np.sin(angle)], axis=1)
    zero_line = np.concatenate([np.tile(np.eye(PATCH), PATCH), np.zeros((PATCH, PIXELS))], axis=1)
    upper = np.concatenate([second[PIXELS:].astype(np.float32), zero_line])
    lower = second[:PIXELS].astype(np.float32)
    return (first.astype(ml_dtypes.bfloat16), np.ascontiguousarray(twist[:, :, digits])) + tuple(
        np.ascontiguousarray(value).astype(ml_dtypes.bfloat16)
        for value in (lower, upper, lower.T, upper.T)
    )


@functools.lru_cache(maxsize=None)
def column_constants(devices, rows):
    s = np.arange(devices)
    small = embed_complex(wheel(devices, s[:, None] * s[None, :]), 1, 2)
    wide = devices * 2 * GROUP
    outer = np.einsum("qpsr,xy->qpxsry", small, np.eye(GROUP)).reshape(wide, wide)
    kr = s[:, None] + devices * np.arange(rows)[None, :]
    angle = wheel(N, kr[:, :, None] * np.arange(rows)[None, None, :])
    inner = embed_complex(angle, 1, 2).reshape(devices, 2 * rows, 2 * rows) / N
    return tuple(
        np.ascontiguousarray(value).astype(ml_dtypes.bfloat16)
        for value in (outer, outer.T, inner, inner.transpose(0, 2, 1))
    )


def row_forward(*refs):
    *x_refs, first_ref, twist_ref, second_ref, out_ref = refs
    count = x_refs[0].shape[0]

    def step(i, carry):
        band = jnp.concatenate([x_ref[i] for x_ref in x_refs], axis=0)
        mixed = mm(band, first_ref[...], TN)
        real, imag = mixed[:, :TOK], mixed[:, TOK:]
        tr, ti = twist_ref[0], twist_ref[1]
        turned = jnp.concatenate(
            [(real * tr - imag * ti).astype(BF16), (real * ti + imag * tr).astype(BF16)], axis=0
        )
        result = mm(second_ref[...], turned).astype(BF16).reshape(PATCH, 2, PATCH, TOK)
        half = TOK // 2
        rows = pl.ds(pl.multiple_of(i * PATCH, PATCH), PATCH)
        out_ref[:, 0, :, rows, :] = result[..., :half]
        out_ref[:, 1, :, rows, :] = result[..., half:]
        return carry

    lax.fori_loop(0, count, step, 0, unroll=8)


def row_inverse(v_ref, first_ref, twist_ref, second_ref, *out_refs):
    count, cols, _ = out_refs[0].shape

    def step(i, carry):
        rows = pl.ds(pl.multiple_of(i * PATCH, PATCH), PATCH)
        wide = jnp.concatenate(
            [
                v_ref[:, 0, :, rows, :].reshape(2 * PIXELS, TOK // 2),
                v_ref[:, 1, :, rows, :].reshape(2 * PIXELS, TOK // 2),
            ],
            axis=1,
        )
        mixed = mm(second_ref[...], wide)
        real, imag = mixed[:PIXELS], mixed[PIXELS:]
        tr, ti = twist_ref[0], twist_ref[1]
        turned = jnp.concatenate(
            [(real * tr + imag * ti).astype(BF16), (imag * tr - real * ti).astype(BF16)], axis=1
        )
        result = mm(first_ref[...], turned, NT).astype(BF16)
        for m, out_ref in enumerate(out_refs):
            out_ref[i] = result[m * cols : (m + 1) * cols]
        return carry

    lax.fori_loop(0, count, step, 0, unroll=8)


def lane_index(shape):
    return lax.broadcasted_iota(jnp.int32, shape, len(shape) - 1)


def swap_halves(values):
    return pltpu.roll(values, values.shape[-1] // 2, len(values.shape) - 1)


def row_forward_half(*refs):
    *x_refs, first_ref, twist_ref, lower_ref, upper_ref, out_ref = refs
    count = x_refs[0].shape[0]
    half = TOK // 2

    def packed(real, imag, rows, high):
        left = lane_index(real.shape) < half // 2
        out_ref[high, 0, rows, :] = jnp.where(left, real, swap_halves(imag)).astype(BF16)
        out_ref[high, 1, rows, :] = jnp.where(left, swap_halves(real), imag).astype(BF16)

    def step(i, carry):
        band = jnp.concatenate([x_ref[i] for x_ref in x_refs], axis=0)
        mixed = mm(band, first_ref[...], TN)
        real, imag = mixed[:, :TOK], mixed[:, TOK:]
        tr, ti = twist_ref[0], twist_ref[1]
        turned = jnp.concatenate(
            [(real * tr - imag * ti).astype(BF16), (real * ti + imag * tr).astype(BF16)], axis=0
        )
        rows = pl.ds(pl.multiple_of(i * PATCH, PATCH), PATCH)
        lower = mm(lower_ref[...], turned[:, :half]).reshape(PATCH // 2, 2, PATCH, half)
        packed(lower[:, 0], lower[:, 1], rows, slice(0, PATCH // 2))
        upper = mm(upper_ref[...], turned[:, half:])
        line = upper[PIXELS:]
        upper = upper[:PIXELS].reshape(PATCH // 2, 2, PATCH, half)
        imag = upper[:, 1]
        head = jnp.where(lane_index(line.shape) == 0, line, imag[0])
        imag = jnp.concatenate([head[None], imag[1:]], axis=0)
        packed(upper[:, 0], imag, rows, slice(PATCH // 2, PATCH))
        return carry

    lax.fori_loop(0, count, step, 0, unroll=8)


def row_inverse_half(v_ref, first_ref, twist_ref, lower_ref, upper_ref, *out_refs):
    count, cols, _ = out_refs[0].shape
    half = TOK // 2

    def unpacked(rows, high):
        even = v_ref[high, 0, rows, :].astype(F32)
        odd = v_ref[high, 1, rows, :].astype(F32)
        left = lane_index(even.shape) < half // 2
        return jnp.where(left, even, swap_halves(odd)), jnp.where(left, swap_halves(even), odd)

    def step(i, carry):
        rows = pl.ds(pl.multiple_of(i * PATCH, PATCH), PATCH)
        real, imag = unpacked(rows, slice(0, PATCH // 2))
        lower = jnp.stack([real, imag], axis=1).reshape(PIXELS, half)
        real, imag = unpacked(rows, slice(PATCH // 2, PATCH))
        head = imag[0]
        at_zero = lane_index(head.shape) == 0
        nothing = jnp.zeros_like(head)
        imag = jnp.concatenate([jnp.where(at_zero, nothing, head)[None], imag[1:]], axis=0)
        upper = jnp.stack([real, imag], axis=1).reshape(PIXELS, half)
        upper = jnp.concatenate([upper, jnp.where(at_zero, head, nothing)], axis=0)
        mixed = jnp.concatenate(
            [mm(lower_ref[...], lower.astype(BF16)), mm(upper_ref[...], upper.astype(BF16))], axis=1
        )
        real, imag = mixed[:PIXELS], mixed[PIXELS:]
        tr, ti = twist_ref[0], twist_ref[1]
        turned = jnp.concatenate(
            [(real * tr + imag * ti).astype(BF16), (imag * tr - real * ti).astype(BF16)], axis=1
        )
        result = mm(first_ref[...], turned, NT).astype(BF16)
        for m, out_ref in enumerate(out_refs):
            out_ref[i] = result[m * cols : (m + 1) * cols]
        return carry

    lax.fori_loop(0, count, step, 0, unroll=8)


def column_kernel(halved, *refs):
    if halved:
        flag_ref, phase_ref, refs = refs[0], refs[1], refs[2:]
    x_ref, outer_ref, *refs = refs
    count = 4 if halved else 5
    sources, out_ref = refs[:count], refs[count]
    mid_ref, *targets, sems = refs[count + 1 :]
    copies = [
        pltpu.make_async_copy(source, target, sems.at[n])
        for n, (source, target) in enumerate(zip(sources, targets))
    ]
    for copy in copies:
        copy.start()
    inner_ref, scale_ref, inner_t_ref, outer_t_ref = targets[:4]
    devices, _, rows, width = mid_ref.shape
    wide = devices * 2 * GROUP
    if halved:
        lane = lane_index((devices, PATCH, width))
        centre = flag_ref[0] == 1
        half = width // 2
        hidden = (lane == half) | (centre & (lane == 0))
        real_lane = (lane < half) | (centre & (lane == half))

    def load(place):
        if not halved:
            return x_ref[:, :, place, :].astype(F32)
        piece = x_ref[:, place, :].astype(F32)
        other = swap_halves(piece)
        return jnp.stack([piece, jnp.where(hidden, jnp.zeros_like(other), other)], axis=1)

    def store(place, value):
        if halved:
            value = jnp.where(real_lane, value[:, 0], swap_halves(value[:, 1])).astype(BF16)
            out_ref[:, place, :] = value
        else:
            out_ref[:, :, place, :] = value.astype(BF16)

    def outer(matrix_ref, value):
        groups = [
            value[:, :, n : n + GROUP, :].reshape(wide, width) for n in range(0, PATCH, GROUP)
        ]
        result = mm(matrix_ref[...], jnp.concatenate(groups, axis=1).astype(BF16))
        parts = [
            result[:, n : n + width].reshape(devices, 2, GROUP, width)
            for n in range(0, result.shape[1], width)
        ]
        return jnp.concatenate(parts, axis=2)

    for top in range(0, rows, PATCH):
        place = slice(top, top + PATCH)
        mid_ref[:, :, place, :] = outer(outer_ref, load(place)).astype(BF16)

    for n, copy in enumerate(copies):
        if n != 3:
            copy.wait()

    def step(q, carry):
        spectrum = mm(inner_ref[q], mid_ref[q].reshape(2 * rows, width))
        real, imag = spectrum[:rows], spectrum[rows:]
        scale = scale_ref[q].astype(F32)
        if halved:
            pr, pi = phase_ref[q, 0], phase_ref[q, 1]
            real = real.reshape(rows // 8, 8, width)
            imag = imag.reshape(rows // 8, 8, width)
            real, imag = real * pr - imag * pi, real * pi + imag * pr
            real, imag = real.reshape(rows, width) * scale, imag.reshape(rows, width) * scale
        else:
            data_ref = targets[4]
            real = real * scale - data_ref[0, q].astype(F32)
            imag = imag * scale - data_ref[1, q].astype(F32)
        back = jnp.concatenate([real.astype(BF16), imag.astype(BF16)], axis=0)
        mid_ref[q] = mm(inner_t_ref[q], back).astype(BF16).reshape(2, rows, width)
        return carry

    lax.fori_loop(0, devices, step, 0, unroll=16)
    copies[3].wait()

    for top in range(0, rows, PATCH):
        place = slice(top, top + PATCH)
        store(place, outer(outer_t_ref, mid_ref[:, :, place, :].astype(F32)))


def turned(value, devices):
    lines = value.shape[0]
    return value.astype(BF16).reshape(lines, N // devices, devices).transpose(2, 1, 0)


def spectrum_inputs(gains, observed, vis_weight, devices):
    gr, gi = gains[0], gains[1]
    weight = (vis_weight * (gr * gr + gi * gi)).astype(BF16)
    data = jnp.stack(
        [
            turned(vis_weight * (gr * observed[0] + gi * observed[1]), devices),
            turned(vis_weight * (gr * observed[1] - gi * observed[0]), devices),
        ]
    )
    return weight, turned(weight, devices), data


def mirror_kernel(scale_ref, got_ref, pick_ref, flip_ref, out_ref):
    devices = out_ref.shape[0]
    for q in range(devices):
        facing = mm(flip_ref[min(q, 1)], got_ref[(devices - q) % devices]).astype(BF16)
        total = mm(scale_ref[q], pick_ref[0]) + mm(facing, pick_ref[1])
        out_ref[q] = total.astype(BF16)


def mirrored_exchange(upper, line, devices):
    middle = devices // 2
    facing = [(e, devices - 1 - e) for e in range(devices)]
    partner = [(e, devices - e) for e in range(1, devices) if e != middle]
    partner = partner + [(0, middle), (middle, 0)]
    upper = lax.ppermute(upper, ("ty", "tx"), facing)
    line = lax.ppermute(line, ("ty", "tx"), partner)
    return upper, line


def mirrored_weight(scale, upper, line):
    devices, slab, _ = scale.shape
    half, middle = slab // 2, devices // 2
    me = lax.axis_index(("ty", "tx"))
    got = jnp.concatenate([upper, jnp.broadcast_to(line, (half, N))], axis=0)
    source = lax.broadcasted_iota(jnp.int32, (slab, slab), 0)
    slot = lax.broadcasted_iota(jnp.int32, (slab, slab), 1)
    low = (me < middle).astype(jnp.int32)
    own = (slot < half) & (source == slot + low)
    other = (slot < half) & (source == half - low - slot)
    other = other & ((me != middle) | (slot > 0))
    other = other | ((me == middle) & (slot == half) & (source == half))
    picks = jnp.stack([own, other]).astype(BF16)
    q2 = np.arange(slab)
    flips = np.stack([q2[:, None] == (slab - q2) % slab, q2[:, None] == slab - 1 - q2])
    return pl.pallas_call(
        mirror_kernel,
        out_shape=jax.ShapeDtypeStruct(scale.shape, BF16),
        compiler_params=PARAMS,
    )(scale, turned(got, devices), picks, jnp.asarray(flips.astype(ml_dtypes.bfloat16)))


def row_matrix(first, cols, lanes, shift):
    twice = jnp.asarray(np.concatenate([first, first[: 2 * WIN]], axis=0))
    me = lax.axis_index("tx")
    zero = jnp.zeros((), jnp.int32)
    starts = [(me ^ m) * cols + (0 if shift is None else shift) for m in range(lanes)]
    rows = [lax.dynamic_slice(twice, (start, zero), (cols, first.shape[1])) for start in starts]
    return jnp.concatenate(rows, axis=0)


def swap_pieces(pieces):
    lanes = len(pieces)
    return [pieces[0]] + [
        lax.ppermute(pieces[m], "tx", [(k, k ^ m) for k in range(lanes)]) for m in range(1, lanes)
    ]


def phase_table(shift, devices, width):
    kr = counting(devices)[:, None] + devices * counting(8)[None, :]
    angle = 2.0 * math.pi / TOK * (kr * shift % TOK).astype(F32)
    table = jnp.stack([jnp.cos(angle), -jnp.sin(angle)], axis=1)
    return jnp.broadcast_to(table[..., None], (devices, 2, 8, width))


def patch_gradient(pieces, scale, data, shift, mirror, beside):
    lanes = lax.axis_size("tx")
    devices = lax.axis_size("ty") * lanes
    own, cols, _ = pieces[0].shape
    slab = N // devices
    halved = data is None
    outer, outer_t, inner, inner_t = (
        jnp.asarray(value) for value in column_constants(devices, slab)
    )
    if halved:
        first = half_constants()[0]
        twist, low, high, low_t, high_t = (jnp.asarray(value) for value in half_constants()[1:])
        part = (devices, slab, slab)
        onward = (row_forward_half, (row_matrix(first, cols, lanes, shift[1]), twist, low, high))
        backward = (row_inverse_half, (row_matrix(first, cols, lanes, None), twist, low_t, high_t))
        middle = lax.axis_index(("ty", "tx")) == devices // 2
    else:
        first = row_matrix(row_constants()[0], cols, lanes, None)
        twist, second, second_t = (jnp.asarray(value) for value in row_constants()[1:])
        part = (devices, 2, slab, slab)
        onward = (row_forward, (first, twist, second))
        backward = (row_inverse, (first, twist, second_t))
        extra = ()
        away = (inner, scale, inner_t, outer_t, data)
    split = (PATCH, devices // PATCH) + part[1:]
    sent = pl.pallas_call(
        onward[0], out_shape=jax.ShapeDtypeStruct(split, BF16), compiler_params=PARAMS
    )(*swap_pieces(pieces), *onward[1])
    if halved:
        sent, mirror, shift = lax.optimization_barrier((sent, mirror, shift))
        extra = (middle.astype(jnp.int32).reshape(1), phase_table(shift[0], devices, slab))
        table = mirrored_weight(scale, *mirror)
    moved = lax.all_to_all(
        sent.reshape(part), ("ty", "tx"), split_axis=0, concat_axis=0, tiled=True
    )
    if halved:
        moved, table, beside = lax.optimization_barrier((moved, table, beside))
        beside = from_neighbours(beside, 1)
        away = (inner, table, inner_t, outer_t)
    spaces = [pltpu.SMEM, pltpu.VMEM][: len(extra)] + [pltpu.VMEM] * 2 + [pl.ANY] * len(away)
    wave = pl.pallas_call(
        functools.partial(column_kernel, halved),
        in_specs=[pl.BlockSpec(memory_space=space) for space in spaces],
        out_shape=jax.ShapeDtypeStruct(part, BF16),
        scratch_shapes=[pltpu.VMEM((devices, 2, slab, slab), BF16)]
        + [pltpu.VMEM(value.shape, BF16) for value in away]
        + [pltpu.SemaphoreType.DMA((len(away),))],
        compiler_params=PARAMS,
    )(*extra, moved, outer, *away)
    if halved:
        wave, beside = lax.optimization_barrier((wave, beside))
    returned = lax.all_to_all(wave, ("ty", "tx"), split_axis=0, concat_axis=0, tiled=True)
    if not halved:
        returned, beside = lax.optimization_barrier((returned, beside))
    slabs = pl.pallas_call(
        backward[0],
        out_shape=[jax.ShapeDtypeStruct((own, cols, PIXELS), BF16)] * lanes,
        compiler_params=PARAMS,
    )(returned.reshape(split), *backward[1])
    return swap_pieces(slabs), beside


def layer_norm(values, gain):
    centre = jnp.mean(values, axis=-1, keepdims=True)
    shifted = values - centre
    spread = jnp.mean(shifted * shifted, axis=-1, keepdims=True)
    return (shifted * lax.rsqrt(spread + EPSILON) * gain).astype(BF16)


def to_windows(band):
    rows, cols, feats = band.shape
    pieces = [
        band[n : n + WIN, k : k + WIN, :].reshape(SPAN, feats)
        for n in range(0, rows, WIN)
        for k in range(0, cols, WIN)
    ]
    return jnp.concatenate(pieces, axis=0)


def from_windows(tokens, cols):
    feats = tokens.shape[-1]
    size = SPAN * cols // WIN
    bands = []
    for top in range(0, tokens.shape[0], size):
        pieces = [
            tokens[n : n + SPAN].reshape(WIN, WIN, feats) for n in range(top, top + size, SPAN)
        ]
        bands.append(jnp.concatenate(pieces, axis=1))
    return jnp.concatenate(bands, axis=0)


def gelu_twice(value):
    value = value.astype(BF16)
    inside = value * (BF16(GELU_IN) + BF16(GELU_CUBE) * (value * value))
    return value + value * jnp.tanh(inside)


def load_weights(j, sources, targets, sems):
    copies = [
        pltpu.make_async_copy(source.at[j], target, sems.at[n])
        for n, (source, target) in enumerate(zip(sources, targets))
    ]

    @pl.when(pl.program_id(0) == 0)
    def _():
        for copy in copies:
            copy.start()

    def wait(which):
        @pl.when(pl.program_id(0) == 0)
        def _():
            for n in which:
                copies[n].wait()

    return wait


def swin_band(flow, wait, bias_ref, gain_ref, weight_refs, scratch):
    qkv_ref, proj_ref, up_ref, down_ref = weight_refs
    mixed_ref, score_ref, prob_ref, active_ref = scratch
    count = flow.shape[0] // SPAN
    pairs = HEADS // 2
    depth = D // HEADS
    wide = 2 * depth
    normed = layer_norm(flow, gain_ref[0:1, :])
    scale = 1.0 / math.sqrt(depth)
    wait((0,))
    mixed_ref[:, :D] = (mm(normed, qkv_ref[:, :D]) * scale).astype(BF16)
    mixed_ref[:, D : 2 * D] = mm(normed, qkv_ref[:, D : 2 * D]).astype(BF16)
    mixed_ref[:, 2 * D :] = mm(normed, qkv_ref[:, 2 * D :]).astype(BF16)
    lower = lax.broadcasted_iota(jnp.int32, (SPAN, wide), 1) < depth

    def scores_of(w):
        rows = slice(w * SPAN, (w + 1) * SPAN)
        for p in range(pairs):
            query = mixed_ref[rows, p * wide : (p + 1) * wide]
            key = mixed_ref[rows, D + p * wide : D + (p + 1) * wide]
            zero = jnp.zeros_like(query)
            split = jnp.concatenate(
                [jnp.where(lower, query, zero), jnp.where(lower, zero, query)], axis=0
            )
            score_ref[w, :, p * wide : (p + 1) * wide] = mm(key, split, NT)

    def probs_of(w):
        bias = bias_ref[w]
        for p in range(pairs):
            lanes = slice(p * wide, (p + 1) * wide)
            scores = score_ref[w, :, lanes] + bias
            weights = jnp.exp(scores - jnp.max(scores, axis=0, keepdims=True))
            share = 1.0 / jnp.sum(weights, axis=0, keepdims=True)
            prob_ref[w, :, lanes] = (weights * share).astype(BF16)

    def mixture_of(w):
        rows = slice(w * SPAN, (w + 1) * SPAN)
        for p in range(pairs):
            lanes = slice(p * wide, (p + 1) * wide)
            value = mixed_ref[rows, 2 * D + p * wide : 2 * D + (p + 1) * wide]
            mixture = mm(prob_ref[w, :, lanes], value, TN)
            mixed_ref[rows, lanes] = jnp.where(lower, mixture[:SPAN], mixture[SPAN:]).astype(BF16)

    for run in (scores_of, probs_of, mixture_of):
        for w in range(count):
            run(w)
    wait((1, 2, 3))
    flow = flow + mm(mixed_ref[:, :D], proj_ref[...])
    normed = layer_norm(flow, gain_ref[1:2, :])
    chunks = up_ref.shape[1] // D
    for c in range(chunks):
        part = slice(c * D, (c + 1) * D)
        active_ref[:, part] = gelu_twice(mm(normed, up_ref[:, part]))
    return flow + 0.5 * mm(active_ref[...], down_ref[...])


def rolled_band(sign, shift_ref, refs, rows, count=WIN):
    main_ref, side_ref, edge_ref, corner_ref = refs
    cols = main_ref.shape[1]
    top = pl.program_id(0) * count + sign * shift_ref[0]
    behind = -rows if sign > 0 else WIN
    beside = -cols if sign > 0 else WIN

    source = lax.broadcasted_iota(jnp.int32, (cols, cols + WIN), 1)
    wanted = lax.broadcasted_iota(jnp.int32, (cols, cols + WIN), 0) + sign * shift_ref[1]
    found = (source < cols) & (source == wanted)
    found = found | (source >= cols) & (source - cols == wanted + beside)
    pick = jnp.where(found, 1.0, 0.0).astype(BF16)
    band = []
    for j in range(count):
        row = top + j
        inside = (row >= 0) & (row < rows)
        here, there = jnp.clip(row, 0, rows - 1), jnp.clip(row + behind, 0, WIN - 1)
        main = jnp.where(inside, main_ref[here], edge_ref[there])
        side = jnp.where(inside, side_ref[here], corner_ref[there])
        band.append(mm(pick, jnp.concatenate([main, side], axis=0)))
    return jnp.stack(band)


def first_kernel(zeta, sigma, count, parts, rows, before, *refs):
    shift_ref, state_ref, *refs = refs
    if before is not None:
        back_refs, refs = refs[:4], refs[4:]
    grad_refs, refs = refs[: count * parts], refs[count * parts :]
    if sigma is not None:
        noise_ref, *refs = refs
    bias_ref, embed_ref, gain_ref, *sources = refs[:7]
    base_ref, out_ref, side_ref, edge_ref, corner_ref, *scratch = refs[7:]
    targets, sems, scratch = scratch[:4], scratch[4], scratch[5:]
    wait = load_weights(0, sources, targets, sems)
    state = state_ref[...]
    if before is not None:
        state = state - before * rolled_band(-1, shift_ref, back_refs, rows, state.shape[0])
    height = state.shape[0]
    if parts == 1:
        grad = grad_refs[0][...].astype(F32)
    else:
        bands = []
        for k in range(height // WIN):
            turn = (pl.program_id(0) * (height // WIN) + k) ^ shift_ref[2]
            band = 0.0
            for n in range(0, count * parts, parts):
                piece = grad_refs[n][...]
                for m in range(1, parts):
                    piece = jnp.where(turn == m, grad_refs[n + m][...], piece)
                band = band + piece.astype(F32)
            bands.append(band)
        grad = jnp.concatenate(bands, axis=0)
    step = zeta * grad
    half = state - step
    tokens = mm(to_windows(half).astype(BF16), embed_ref[...]).astype(BF16).astype(F32)
    flow = swin_band(tokens, wait, bias_ref, gain_ref, targets, scratch)
    result = from_windows(flow, half.shape[1]).astype(BF16)
    out_ref[:, :, :D] = result
    side_ref[:, :, :D] = result[:, :WIN]
    if sigma is None:
        base_ref[...] = half
    else:
        noise = sigma * noise_ref[...]
        base_ref[...] = half + noise
        change = (noise - step).astype(BF16)
        out_ref[:, :, D:] = change
        side_ref[:, :, D:] = change[:, :WIN]

    @pl.when(pl.program_id(0) == 0)
    def _():
        edge_ref[...] = out_ref[:WIN]
        corner_ref[...] = side_ref[:WIN]


def write_pieces(turn, refs, value):
    for m, ref in enumerate(refs):

        def write(ref=ref):
            ref[...] = value

        pl.when(turn == m)(write)


def second_kernel(sigma, rows, parts, *refs):
    shift_ref, *refs = refs
    tile_refs, refs = refs[:4], refs[4:]
    bias_ref, unembed_ref, gain_ref, *sources = refs[:7]
    out_ref, side_ref, edge_ref, corner_ref, *scratch = refs[7:]
    state_refs, scratch = scratch[:parts], scratch[parts:]
    targets, sems, scratch = scratch[:4], scratch[4], scratch[5:]
    wait = load_weights(1, sources, targets, sems)
    height, cols, _ = out_ref.shape
    band = rolled_band(1, shift_ref, tile_refs, rows, height)
    tokens = to_windows(band[:, :, :D])
    flow = swin_band(tokens, wait, bias_ref, gain_ref, targets, scratch)
    estimate = from_windows(mm(flow.astype(BF16), unembed_ref[...]), cols)
    narrow = estimate.astype(BF16)
    out_ref[...] = narrow
    side_ref[...] = narrow[:, cols - WIN :]
    edge_ref[...] = narrow[height - WIN :]
    corner_ref[...] = narrow[height - WIN :, cols - WIN :]
    if parts > 0:
        change = (band[:, :, D:] - sigma * estimate).astype(BF16)
        for n in range(height // WIN):
            turn = (pl.program_id(0) * (height // WIN) + n) ^ shift_ref[2]
            write_pieces(turn, state_refs, change[n * WIN : (n + 1) * WIN])


def whole(array):
    zeros = (0,) * array.ndim
    return pl.BlockSpec(array.shape, lambda *_: zeros)


def member(array, j):
    place = (j,) + (0,) * (array.ndim - 1)
    return pl.BlockSpec((None,) + array.shape[1:], lambda *_: place)


def band_spec(cols, feats, height=WIN):
    return pl.BlockSpec((height, cols, feats), lambda n, *_: (n, 0, 0))


def bias_spec(cols, height=WIN):
    count = height * cols // SPAN
    return pl.BlockSpec((count, SPAN, 2 * SPAN), lambda n, *_: (n, 0, 0))


def band_scratch(cols, weights, height=WIN):
    count = height * cols // SPAN
    return [pltpu.VMEM(value.shape[1:], BF16) for value in weights] + [
        pltpu.SemaphoreType.DMA((len(weights),)),
        pltpu.VMEM((height * cols, 3 * D), BF16),
        pltpu.VMEM((count, SPAN, HEADS * SPAN), F32),
        pltpu.VMEM((count, SPAN, HEADS * SPAN), BF16),
    ]


def strip_outs(rows, cols, feats, height=WIN):
    specs = [band_spec(cols, feats, height), band_spec(WIN, feats, height)]
    specs += [
        pl.BlockSpec((WIN, width, feats), lambda *_: (0, 0, 0)) for width in (cols, WIN)
    ]
    shapes = [(rows, cols), (rows, WIN), (WIN, cols), (WIN, WIN)]
    return specs, [jax.ShapeDtypeStruct(shape + (feats,), BF16) for shape in shapes]


def first_block(zeta, sigma, state, before, shift, back, grads, noise, bias, w_embed, weights):
    *weights, gains = weights
    rows, cols, _ = state.shape
    parts = len(grads[0])
    pieces = [piece for grad in grads for piece in grad]
    fields = [] if sigma is None else [noise]
    feats = D if sigma is None else D + PIXELS
    height = 2 * WIN
    specs, shapes = strip_outs(rows, cols, feats, height)
    band = band_spec(cols, PIXELS, height)
    return pl.pallas_call(
        functools.partial(first_kernel, zeta, sigma, len(grads), parts, rows, before),
        grid_spec=pltpu.PrefetchScalarGridSpec(
            num_scalar_prefetch=1,
            grid=(rows // height,),
            in_specs=[band]
            + [whole(value) for value in back]
            + [band if parts == 1 else whole(value) for value in pieces]
            + [band] * len(fields)
            + [bias_spec(cols, height), whole(w_embed), member(gains, 0)]
            + [pl.BlockSpec(memory_space=pl.ANY)] * len(weights),
            out_specs=[band] + specs,
            scratch_shapes=band_scratch(cols, weights, height)
            + [pltpu.VMEM((height * cols, weights[2].shape[2]), BF16)],
        ),
        out_shape=[jax.ShapeDtypeStruct((rows, cols, PIXELS), F32)] + shapes,
        compiler_params=PARAMS,
    )(shift, state, *back, *pieces, *fields, bias, w_embed, gains, *weights)


def second_block(sigma, shift, tile, bias, w_unembed, weights, parts):
    *weights, gains = weights
    rows, cols, _ = tile[0].shape
    height = 2 * WIN
    specs, shapes = strip_outs(rows, cols, PIXELS, height)
    specs += [pl.BlockSpec((WIN, cols, PIXELS), lambda *_: (0, 0, 0))] * parts
    shapes += [jax.ShapeDtypeStruct((WIN, cols, PIXELS), BF16)] * parts
    return pl.pallas_call(
        functools.partial(second_kernel, sigma, rows, parts),
        grid_spec=pltpu.PrefetchScalarGridSpec(
            num_scalar_prefetch=1,
            grid=(rows // height,),
            in_specs=[whole(value) for value in tile]
            + [bias_spec(cols, height), whole(w_unembed), member(gains, 1)]
            + [pl.BlockSpec(memory_space=pl.ANY)] * len(weights),
            out_specs=specs,
            scratch_shapes=band_scratch(cols, weights, height)
            + [pltpu.VMEM((height * cols, weights[2].shape[2]), BF16)],
        ),
        out_shape=shapes,
        compiler_params=PARAMS,
    )(shift, *tile, bias, w_unembed, gains, *weights)


def from_neighbours(tile, by):
    main, side, edge, corner = tile
    ty, tx = lax.axis_size("ty"), lax.axis_size("tx")
    across = [
        (i * tx + k, (i + by) % ty * tx + (k + by) % tx) for i in range(ty) for k in range(tx)
    ]
    return (
        main,
        lax.ppermute(side, "tx", [(k, (k + by) % tx) for k in range(tx)]),
        lax.ppermute(edge, "ty", [(i, (i + by) % ty) for i in range(ty)]),
        lax.ppermute(corner, ("ty", "tx"), across),
    )


def windows_of(grid):
    rows, cols = grid.shape
    shaped = grid.reshape(rows // WIN, WIN, cols // WIN, WIN).transpose(0, 2, 1, 3)
    return shaped.reshape(rows // WIN * (cols // WIN), SPAN)


def bias_of(labels, keep):
    allowed = jnp.ones((1, SPAN, SPAN), bool)
    if labels is not None:
        label = windows_of(labels)
        allowed = label[:, :, None] == label[:, None, :]
    if keep is not None:
        kept = windows_of(keep)[:, :, None] == 1
        allowed = allowed & (kept | jnp.eye(SPAN, dtype=bool)[None])
    bias = jnp.where(allowed, 0.0, -1e30).astype(F32)
    return jnp.concatenate([bias, bias], axis=2)


def region(index, shift):
    return jnp.where(index < TOK - WIN, 0, jnp.where(index < TOK - shift, 1, 2)).astype(jnp.int32)


@functools.lru_cache(maxsize=None)
def lane_order(cols):
    parts = LANES // cols
    groups = PATCH // parts
    lane = np.arange(PATCH * cols)
    g, h, k = lane // LANES, lane % LANES // cols, lane % cols
    source = PATCH * k + h * groups + g
    matrix = np.zeros((PATCH * cols, PATCH * cols), np.float32)
    matrix[source, lane] = 1.0
    return matrix.astype(ml_dtypes.bfloat16), np.ascontiguousarray(matrix.T).astype(
        ml_dtypes.bfloat16
    )


def move_lanes(values, matrix):
    high = values.astype(BF16)
    low = (values - high.astype(F32)).astype(BF16)
    return mm(high, matrix) + mm(low, matrix)


def to_patches_kernel(narrow, place_ref, tile_ref, order_ref, *out_refs):
    count, cols, _ = out_refs[0].shape
    parts = LANES // cols
    groups = PATCH // parts
    if narrow:
        ordered = mm(tile_ref[...].astype(BF16), order_ref[...])
    else:
        ordered = move_lanes(tile_ref[...], order_ref[...])
    patches = []
    for i in range(count):
        band = ordered[i * PATCH : (i + 1) * PATCH]
        stacked = jnp.concatenate(
            [band[:, g * LANES : (g + 1) * LANES] for g in range(groups)], axis=0
        )
        turned = stacked.T
        patches.append(
            jnp.concatenate([turned[h * cols : (h + 1) * cols] for h in range(parts)], axis=1)
        )
    result = jnp.stack(patches).astype(out_refs[0].dtype)
    if len(out_refs) == 1:
        out_refs[0][...] = result
    else:
        write_pieces(pl.program_id(0) ^ place_ref[0], out_refs, result)


def lanes_of(patches):
    count, cols, _ = patches.shape
    parts = LANES // cols
    groups = PATCH // parts
    width = groups * PATCH
    bands = []
    for i in range(count):
        stacked = jnp.concatenate(
            [patches[i, :, h * width : (h + 1) * width] for h in range(parts)], axis=0
        )
        turned = stacked.T
        bands.append(
            jnp.concatenate([turned[g * PATCH : (g + 1) * PATCH] for g in range(groups)], axis=1)
        )
    return jnp.concatenate(bands, axis=0)


def base_tile_kernel(scale, base_ref, noise_ref, order_ref, out_ref):
    moved = move_lanes(lanes_of(base_ref[...]), order_ref[...])
    out_ref[...] = moved + scale * noise_ref[...]


def last_tile_kernel(sigma, rows, shift_ref, tile_ref, *refs):
    *back_refs, order_ref, out_ref = refs
    estimate = rolled_band(-1, shift_ref, back_refs, rows)
    moved = mm(lanes_of(estimate).astype(BF16), order_ref[...])
    out_ref[...] = tile_ref[...] - sigma * moved


def patches_of(tiles, j, place, kind=F32, parts=1):
    rows, cols = tiles.shape[1] // PATCH, tiles.shape[2] // PATCH
    order = jnp.asarray(lane_order(cols)[0])
    spec, shape = band_spec(cols, PIXELS), (rows, cols, PIXELS)
    if parts > 1:
        spec = pl.BlockSpec((WIN, cols, PIXELS), lambda *_: (0, 0, 0))
        shape = (WIN, cols, PIXELS)
    return pl.pallas_call(
        functools.partial(to_patches_kernel, kind == BF16),
        grid_spec=pltpu.PrefetchScalarGridSpec(
            num_scalar_prefetch=1,
            grid=(rows // WIN,),
            in_specs=[
                pl.BlockSpec((None, WIN * PATCH, cols * PATCH), lambda n, *_: (j, n, 0)),
                whole(order),
            ],
            out_specs=[spec] * parts,
        ),
        out_shape=[jax.ShapeDtypeStruct(shape, kind)] * parts,
        compiler_params=PARAMS,
    )(place, tiles, order)


def tile_of(base, sigma, shift, back, scale, noise, j):
    rows, cols, _ = base.shape
    order = jnp.asarray(lane_order(cols)[1])
    tile_spec = pl.BlockSpec((WIN * PATCH, cols * PATCH), lambda n, *_: (n, 0))
    shape = jax.ShapeDtypeStruct((rows * PATCH, cols * PATCH), F32)
    tile = pl.pallas_call(
        functools.partial(base_tile_kernel, scale),
        grid=(rows // WIN,),
        in_specs=[
            band_spec(cols, PIXELS),
            pl.BlockSpec((None, WIN * PATCH, cols * PATCH), lambda n, *_: (j, n, 0)),
            whole(order),
        ],
        out_specs=tile_spec,
        out_shape=shape,
        compiler_params=PARAMS,
    )(base, noise, order)
    return pl.pallas_call(
        functools.partial(last_tile_kernel, sigma, rows),
        grid_spec=pltpu.PrefetchScalarGridSpec(
            num_scalar_prefetch=1,
            grid=(rows // WIN,),
            in_specs=[tile_spec] + [whole(value) for value in back] + [whole(order)],
            out_specs=tile_spec,
        ),
        out_shape=shape,
        compiler_params=PARAMS,
    )(shift, tile, *back, order)


def per_device(
    image, noise, offsets, key_mask, gains, observed, vis_weight,
    w_embed, w_qkv, w_proj, w_up, w_down, w_unembed, norm_gains,
):
    rows = image.shape[0] // PATCH
    cols = image.shape[1] // PATCH
    devices = lax.axis_size("ty") * lax.axis_size("tx")
    lanes = lax.axis_size("tx")
    fast = N // devices == TOK // 2 and rows == lanes * WIN and lanes & (lanes - 1) == 0
    column = lax.axis_index("tx").astype(jnp.int32)[None]
    places = [jnp.concatenate([offsets[step], column]) for step in range(STEPS)]
    row_index = lax.axis_index("ty") * rows + counting(rows)
    col_index = lax.axis_index("tx") * cols + counting(cols)
    weights = (w_qkv, w_proj, w_up, w_down, norm_gains)
    w_embed = w_embed.reshape(PATCH, PATCH, D).transpose(1, 0, 2).reshape(PIXELS, D)
    w_unembed = w_unembed.reshape(D, PATCH, PATCH).transpose(0, 2, 1).reshape(D, PIXELS)
    state = patches_of(image[None], 0, column)[0]
    extras = [patches_of(noise, step, column)[0] for step in range(STEPS - 1)] + [None]
    first_bias = bias_of(None, key_mask)
    biases = []
    for step in range(STEPS):
        labels = (
            3 * region(row_index, offsets[step, 0])[:, None]
            + region(col_index, offsets[step, 1])[None, :]
        )
        biases.append(bias_of(labels, None))
    beside = (state, extras, first_bias, biases, w_embed, w_unembed)
    shift, before, back, moving, mirror = places[0], None, (), None, None
    grads = []
    if fast:
        weight, scale, data = spectrum_inputs(gains, observed, vis_weight, devices)
        half = weight.shape[0] // 2
        lines = (weight[half:], weight[:1])
        grad, (beside, lines) = patch_gradient(
            patches_of(image[None], 0, column, BF16, lanes), scale, data, None, None,
            (beside, lines),
        )
        grads = [grad]
        state, extras, first_bias, biases, w_embed, w_unembed = beside
    for step in range(STEPS):
        if not fast:
            tile = image if step == 0 else tile_of(state, before, shift, back, 0.0, noise, 0)
            grad = plain_gradient(tile, gains, observed, vis_weight)
            grad = patches_of(grad.astype(F32)[None], 0, column, BF16)[0]
            grads = [[grad]]
        elif step > 0:
            grad, back = patch_gradient(moving, scale, None, shift, mirror, back)
            grads = grads + [grad]
        last = step + 1 == STEPS
        sigma = None if last else SIGMAS[step + 1]
        state, *first = first_block(
            STEP_SIZES[step], sigma, state, before, shift, back, grads, extras[step], first_bias,
            w_embed, weights,
        )
        shift, before = places[step], SIGMAS[step]
        first = from_neighbours(first, -1)
        if fast and step == 0:
            first, lines = lax.optimization_barrier((first, lines))
            mirror = mirrored_exchange(*lines, devices)
        rolled = second_block(
            before, shift, first, biases[step], w_unembed, weights,
            lanes if fast and not last else 0,
        )
        back, moving = rolled[:4], rolled[4:]
        if fast and step == 0:
            moving, mirror = lax.optimization_barrier((moving, mirror))
        if last or not fast:
            back = from_neighbours(back, 1)
    return tile_of(state, before, shift, back, SIGMAS[STEPS], noise, STEPS - 1)


def solution(mesh):
    in_specs = (
        P("ty", "tx"),
        P(None, "ty", "tx"),
        P(),
        P("ty", "tx"),
        P(None, ("ty", "tx"), None),
        P(None, ("ty", "tx"), None),
        P(("ty", "tx"), None),
        P(),
        P(),
        P(),
        P(),
        P(),
        P(),
        P(),
    )
    out_specs = P("ty", "tx")
    return jax.shard_map(
        per_device, mesh=mesh, in_specs=in_specs, out_specs=out_specs, check_vma=False
    )
```

```python
import functools
import math

import jax
import jax.numpy as jnp
import ml_dtypes
import numpy as np
from jax import lax
from jax.experimental import pallas as pl
from jax.experimental.pallas import tpu as pltpu
from jax.sharding import PartitionSpec as P

N = 4096
PATCH = 16
PIXELS = PATCH * PATCH
WIN = 8
D = 512
HEADS = 8
STEPS = 2
SPAN = WIN * WIN
LANES = 128
GROUP = 8
TOK = N // PATCH

SIGMAS = (0.8, 0.5, 0.3)
STEP_SIZES = (0.9, 0.7)
EPSILON = 1e-05
HIGHEST = lax.Precision.HIGHEST
BF16 = jnp.bfloat16
F32 = jnp.float32
GELU_IN = math.sqrt(2.0 / math.pi)
GELU_CUBE = 0.044715 * GELU_IN
VMEM_LIMIT = 56 * 1024 * 1024
PARAMS = pltpu.CompilerParams(vmem_limit_bytes=VMEM_LIMIT)
TN = (((0,), (0,)), ((), ()))
NT = (((1,), (1,)), ((), ()))
NN = (((1,), (0,)), ((), ()))


def mm(left, right, dims=NN):
    return lax.dot_general(left, right, dims, preferred_element_type=F32)


def counting(length):
    return jnp.arange(length, dtype=jnp.int32)


def roots(length, outer, inner, sign):
    product = outer[:, None] * inner[None, :] % length
    angle = 2.0 * math.pi / length * product.astype(F32)
    return (jnp.cos(angle), sign * jnp.sin(angle))


def complex_einsum(form, left, right):
    real = jnp.einsum(form, left[0], right[0], precision=HIGHEST) - jnp.einsum(
        form, left[1], right[1], precision=HIGHEST
    )
    imag = jnp.einsum(form, left[0], right[1], precision=HIGHEST) + jnp.einsum(
        form, left[1], right[0], precision=HIGHEST
    )
    return (real, imag)


def complex_times(left, right):
    return (left[0] * right[0] - left[1] * right[1], left[0] * right[1] + left[1] * right[0])


def along_last(real_part, imag_part, groups, sign):
    rows, length = real_part.shape
    inner = length // groups
    first = roots(groups, counting(groups), counting(groups), sign)
    twist = roots(length, counting(inner), counting(groups), sign)
    second = roots(inner, counting(inner), counting(inner), sign)
    shaped = real_part.reshape(rows, groups, inner)
    if imag_part is None:
        partial_value = (
            jnp.einsum("mab,ka->mbk", shaped, first[0], precision=HIGHEST),
            jnp.einsum("mab,ka->mbk", shaped, first[1], precision=HIGHEST),
        )
    else:
        partial_value = complex_einsum(
            "mab,ka->mbk", (shaped, imag_part.reshape(rows, groups, inner)), first
        )
    partial_value = complex_times(partial_value, twist)
    result = complex_einsum("jb,mbk->mjk", second, partial_value)
    return (result[0].reshape(rows, length), result[1].reshape(rows, length))


def across_groups(pair, groups, sign):
    inner, cols = pair[0].shape
    width = cols // groups
    length = groups * inner
    first = roots(groups, counting(groups), counting(groups), sign)
    twist = roots(length, counting(inner), counting(groups), sign)
    second = roots(inner, counting(inner), counting(inner), sign)
    shaped = (pair[0].reshape(inner, groups, width), pair[1].reshape(inner, groups, width))
    partial_value = complex_einsum("bhc,kh->cbk", shaped, first)
    partial_value = complex_times(partial_value, twist)
    result = complex_einsum("jb,cbk->cjk", second, partial_value)
    return (result[0].reshape(width, length), result[1].reshape(width, length))


def exchange_pair(pair):
    return tuple(
        lax.all_to_all(
            part.astype(BF16), ("ty", "tx"), split_axis=1, concat_axis=1, tiled=True
        ).astype(F32)
        for part in pair
    )


def plain_gradient(tile, gains, observed, vis_weight):
    devices = lax.axis_size("ty") * lax.axis_size("tx")
    slab = lax.all_to_all(tile.astype(BF16), "tx", split_axis=0, concat_axis=1, tiled=True)
    moved = exchange_pair(along_last(slab.astype(F32), None, devices, -1.0))
    spectrum = across_groups(moved, devices, -1.0)
    spectrum = (spectrum[0] * (1.0 / N), spectrum[1] * (1.0 / N))
    model = complex_times((gains[0], gains[1]), spectrum)
    misfit = (vis_weight * (model[0] - observed[0]), vis_weight * (model[1] - observed[1]))
    back = complex_times((gains[0], -gains[1]), misfit)
    returned = exchange_pair(along_last(back[0], back[1], devices, 1.0))
    slab_grad = across_groups(returned, devices, 1.0)[0] * (1.0 / N)
    return lax.all_to_all(slab_grad.astype(BF16), "tx", split_axis=1, concat_axis=0, tiled=True)


def embed_complex(angle, row_axis, col_axis):
    cos, sin = np.cos(angle), np.sin(angle)
    top = np.stack([cos, sin], axis=col_axis)
    bottom = np.stack([-sin, cos], axis=col_axis)
    return np.stack([top, bottom], axis=row_axis)


def wheel(length, product):
    return 2.0 * math.pi / length * (product % length)


@functools.lru_cache(maxsize=None)
def row_constants():
    k = np.arange(TOK)
    angle = wheel(TOK, k[:, None] * k[None, :])
    first = np.concatenate([np.cos(angle), -np.sin(angle)], axis=1)
    b = np.repeat(np.arange(PATCH), PATCH)
    angle = wheel(N, b[:, None] * k[None, :])
    twist = np.stack([np.cos(angle), -np.sin(angle)])
    p = np.arange(PATCH)
    small = embed_complex(wheel(PATCH, p[:, None] * p[None, :]), 1, 1)
    second = np.einsum("kpqb,xy->kpxqby", small, np.eye(PATCH)).reshape(2 * PIXELS, 2 * PIXELS)
    return (
        first.astype(ml_dtypes.bfloat16),
        twist.astype(np.float32),
        second.astype(ml_dtypes.bfloat16),
        np.ascontiguousarray(second.T).astype(ml_dtypes.bfloat16),
    )


@functools.lru_cache(maxsize=None)
def half_constants():
    _, twist, second, _ = row_constants()
    half, quarter = TOK // 2, TOK // 4
    low = np.concatenate([1 + np.arange(quarter), 1 + half + np.arange(quarter)])
    digits = np.concatenate([low, low - 1])
    k = np.arange(TOK)
    angle = wheel(TOK, k[:, None] * digits[None, :])
    first = np.concatenate([np.cos(angle), -np.sin(angle)], axis=1)
    zero_line = np.concatenate([np.tile(np.eye(PATCH), PATCH), np.zeros((PATCH, PIXELS))], axis=1)
    upper = np.concatenate([second[PIXELS:].astype(np.float32), zero_line])
    lower = second[:PIXELS].astype(np.float32)
    return (first.astype(ml_dtypes.bfloat16), np.ascontiguousarray(twist[:, :, digits])) + tuple(
        np.ascontiguousarray(value).astype(ml_dtypes.bfloat16)
        for value in (lower, upper, lower.T, upper.T)
    )


@functools.lru_cache(maxsize=None)
def column_constants(devices, rows):
    s = np.arange(devices)
    small = embed_complex(wheel(devices, s[:, None] * s[None, :]), 1, 2)
    wide = devices * 2 * GROUP
    outer = np.einsum("qpsr,xy->qpxsry", small, np.eye(GROUP)).reshape(wide, wide)
    kr = s[:, None] + devices * np.arange(rows)[None, :]
    angle = wheel(N, kr[:, :, None] * np.arange(rows)[None, None, :])
    inner = embed_complex(angle, 1, 2).reshape(devices, 2 * rows, 2 * rows) / N
    return tuple(
        np.ascontiguousarray(value).astype(ml_dtypes.bfloat16)
        for value in (outer, outer.T, inner, inner.transpose(0, 2, 1))
    )


def row_forward(*refs):
    *x_refs, first_ref, twist_ref, second_ref, out_ref = refs
    count = x_refs[0].shape[0]

    def step(i, carry):
        band = jnp.concatenate([x_ref[i] for x_ref in x_refs], axis=0)
        mixed = mm(band, first_ref[...], TN)
        real, imag = mixed[:, :TOK], mixed[:, TOK:]
        tr, ti = twist_ref[0], twist_ref[1]
        turned = jnp.concatenate(
            [(real * tr - imag * ti).astype(BF16), (real * ti + imag * tr).astype(BF16)], axis=0
        )
        result = mm(second_ref[...], turned).astype(BF16).reshape(PATCH, 2, PATCH, TOK)
        half = TOK // 2
        rows = pl.ds(pl.multiple_of(i * PATCH, PATCH), PATCH)
        out_ref[:, 0, :, rows, :] = result[..., :half]
        out_ref[:, 1, :, rows, :] = result[..., half:]
        return carry

    lax.fori_loop(0, count, step, 0, unroll=8)


def load_bands(source, target, sems, count):
    def copy(i):
        rows = pl.ds(pl.multiple_of(i * PATCH, PATCH), PATCH)
        return pltpu.make_async_copy(
            source.at[..., rows, :], target.at[..., rows, :], sems.at[i]
        )

    for i in range(count):
        copy(i).start()
    return lambda i: copy(i).wait()


def row_inverse(v_hbm, first_ref, twist_ref, second_ref, *refs):
    *out_refs, v_ref, sems = refs
    count, cols, _ = out_refs[0].shape
    wait = load_bands(v_hbm, v_ref, sems, count)

    def step(i, carry):
        wait(i)
        rows = pl.ds(pl.multiple_of(i * PATCH, PATCH), PATCH)
        wide = jnp.concatenate(
            [
                v_ref[:, 0, :, rows, :].reshape(2 * PIXELS, TOK // 2),
                v_ref[:, 1, :, rows, :].reshape(2 * PIXELS, TOK // 2),
            ],
            axis=1,
        )
        mixed = mm(second_ref[...], wide)
        real, imag = mixed[:PIXELS], mixed[PIXELS:]
        tr, ti = twist_ref[0], twist_ref[1]
        turned = jnp.concatenate(
            [(real * tr + imag * ti).astype(BF16), (imag * tr - real * ti).astype(BF16)], axis=1
        )
        result = mm(first_ref[...], turned, NT).astype(BF16)
        for m, out_ref in enumerate(out_refs):
            out_ref[i] = result[m * cols : (m + 1) * cols]
        return carry

    lax.fori_loop(0, count, step, 0, unroll=8)


def lane_index(shape):
    return lax.broadcasted_iota(jnp.int32, shape, len(shape) - 1)


def swap_halves(values):
    return pltpu.roll(values, values.shape[-1] // 2, len(values.shape) - 1)


def row_forward_half(*refs):
    *x_refs, first_ref, twist_ref, lower_ref, upper_ref, out_ref = refs
    count = x_refs[0].shape[0]
    half = TOK // 2

    def packed(real, imag, rows, high):
        left = lane_index(real.shape) < half // 2
        out_ref[high, 0, rows, :] = jnp.where(left, real, swap_halves(imag)).astype(BF16)
        out_ref[high, 1, rows, :] = jnp.where(left, swap_halves(real), imag).astype(BF16)

    def step(i, carry):
        band = jnp.concatenate([x_ref[i] for x_ref in x_refs], axis=0)
        mixed = mm(band, first_ref[...], TN)
        real, imag = mixed[:, :TOK], mixed[:, TOK:]
        tr, ti = twist_ref[0], twist_ref[1]
        turned = jnp.concatenate(
            [(real * tr - imag * ti).astype(BF16), (real * ti + imag * tr).astype(BF16)], axis=0
        )
        rows = pl.ds(pl.multiple_of(i * PATCH, PATCH), PATCH)
        lower = mm(lower_ref[...], turned[:, :half]).reshape(PATCH // 2, 2, PATCH, half)
        packed(lower[:, 0], lower[:, 1], rows, slice(0, PATCH // 2))
        upper = mm(upper_ref[...], turned[:, half:])
        line = upper[PIXELS:]
        upper = upper[:PIXELS].reshape(PATCH // 2, 2, PATCH, half)
        imag = upper[:, 1]
        head = jnp.where(lane_index(line.shape) == 0, line, imag[0])
        imag = jnp.concatenate([head[None], imag[1:]], axis=0)
        packed(upper[:, 0], imag, rows, slice(PATCH // 2, PATCH))
        return carry

    lax.fori_loop(0, count, step, 0, unroll=8)


def row_inverse_half(v_hbm, first_ref, twist_ref, lower_ref, upper_ref, *refs):
    *out_refs, v_ref, sems = refs
    count, cols, _ = out_refs[0].shape
    wait = load_bands(v_hbm, v_ref, sems, count)
    half = TOK // 2

    def unpacked(rows, high):
        even = v_ref[high, 0, rows, :].astype(F32)
        odd = v_ref[high, 1, rows, :].astype(F32)
        left = lane_index(even.shape) < half // 2
        return jnp.where(left, even, swap_halves(odd)), jnp.where(left, swap_halves(even), odd)

    def step(i, carry):
        wait(i)
        rows = pl.ds(pl.multiple_of(i * PATCH, PATCH), PATCH)
        real, imag = unpacked(rows, slice(0, PATCH // 2))
        lower = jnp.stack([real, imag], axis=1).reshape(PIXELS, half)
        real, imag = unpacked(rows, slice(PATCH // 2, PATCH))
        head = imag[0]
        at_zero = lane_index(head.shape) == 0
        nothing = jnp.zeros_like(head)
        imag = jnp.concatenate([jnp.where(at_zero, nothing, head)[None], imag[1:]], axis=0)
        upper = jnp.stack([real, imag], axis=1).reshape(PIXELS, half)
        upper = jnp.concatenate([upper, jnp.where(at_zero, head, nothing)], axis=0)
        mixed = jnp.concatenate(
            [mm(lower_ref[...], lower.astype(BF16)), mm(upper_ref[...], upper.astype(BF16))], axis=1
        )
        real, imag = mixed[:PIXELS], mixed[PIXELS:]
        tr, ti = twist_ref[0], twist_ref[1]
        turned = jnp.concatenate(
            [(real * tr + imag * ti).astype(BF16), (imag * tr - real * ti).astype(BF16)], axis=1
        )
        result = mm(first_ref[...], turned, NT).astype(BF16)
        for m, out_ref in enumerate(out_refs):
            out_ref[i] = result[m * cols : (m + 1) * cols]
        return carry

    lax.fori_loop(0, count, step, 0, unroll=8)


def column_kernel(halved, *refs):
    if halved:
        flag_ref, phase_ref, refs = refs[0], refs[1], refs[2:]
    x_ref, outer_ref, *refs = refs
    count = 4 if halved else 5
    sources, out_ref = refs[:count], refs[count]
    mid_ref, *targets, sems = refs[count + 1 :]
    copies = [
        pltpu.make_async_copy(source, target, sems.at[n])
        for n, (source, target) in enumerate(zip(sources, targets))
    ]
    for copy in copies:
        copy.start()
    inner_ref, scale_ref, inner_t_ref, outer_t_ref = targets[:4]
    devices, _, rows, width = mid_ref.shape
    wide = devices * 2 * GROUP
    if halved:
        lane = lane_index((devices, PATCH, width))
        centre = flag_ref[0] == 1
        half = width // 2
        hidden = (lane == half) | (centre & (lane == 0))
        real_lane = (lane < half) | (centre & (lane == half))

    def load(place):
        if not halved:
            return x_ref[:, :, place, :].astype(F32)
        piece = x_ref[:, place, :].astype(F32)
        other = swap_halves(piece)
        return jnp.stack([piece, jnp.where(hidden, jnp.zeros_like(other), other)], axis=1)

    def store(place, value):
        if halved:
            value = jnp.where(real_lane, value[:, 0], swap_halves(value[:, 1])).astype(BF16)
            out_ref[:, place, :] = value
        else:
            out_ref[:, :, place, :] = value.astype(BF16)

    def outer(matrix_ref, value):
        groups = [
            value[:, :, n : n + GROUP, :].reshape(wide, width) for n in range(0, PATCH, GROUP)
        ]
        result = mm(matrix_ref[...], jnp.concatenate(groups, axis=1).astype(BF16))
        parts = [
            result[:, n : n + width].reshape(devices, 2, GROUP, width)
            for n in range(0, result.shape[1], width)
        ]
        return jnp.concatenate(parts, axis=2)

    for top in range(0, rows, PATCH):
        place = slice(top, top + PATCH)
        mid_ref[:, :, place, :] = outer(outer_ref, load(place)).astype(BF16)

    for n, copy in enumerate(copies):
        if n != 3:
            copy.wait()

    def step(q, carry):
        spectrum = mm(inner_ref[q], mid_ref[q].reshape(2 * rows, width))
        real, imag = spectrum[:rows], spectrum[rows:]
        scale = scale_ref[q].astype(F32)
        if halved:
            pr, pi = phase_ref[q, 0], phase_ref[q, 1]
            real = real.reshape(rows // 8, 8, width)
            imag = imag.reshape(rows // 8, 8, width)
            real, imag = real * pr - imag * pi, real * pi + imag * pr
            real, imag = real.reshape(rows, width) * scale, imag.reshape(rows, width) * scale
        else:
            data_ref = targets[4]
            real = real * scale - data_ref[0, q].astype(F32)
            imag = imag * scale - data_ref[1, q].astype(F32)
        back = jnp.concatenate([real.astype(BF16), imag.astype(BF16)], axis=0)
        mid_ref[q] = mm(inner_t_ref[q], back).astype(BF16).reshape(2, rows, width)
        return carry

    lax.fori_loop(0, devices, step, 0, unroll=32)
    copies[3].wait()

    for top in range(0, rows, PATCH):
        place = slice(top, top + PATCH)
        store(place, outer(outer_t_ref, mid_ref[:, :, place, :].astype(F32)))


def turned(value, devices):
    lines = value.shape[0]
    return value.astype(BF16).reshape(lines, N // devices, devices).transpose(2, 1, 0)


def spectrum_inputs(gains, observed, vis_weight, devices):
    gr, gi = gains[0], gains[1]
    weight = (vis_weight * (gr * gr + gi * gi)).astype(BF16)
    data = jnp.stack(
        [
            turned(vis_weight * (gr * observed[0] + gi * observed[1]), devices),
            turned(vis_weight * (gr * observed[1] - gi * observed[0]), devices),
        ]
    )
    return weight, turned(weight, devices), data


def mirror_kernel(scale_ref, got_ref, pick_ref, flip_ref, out_ref):
    devices = out_ref.shape[0]
    for q in range(devices):
        facing = mm(flip_ref[min(q, 1)], got_ref[(devices - q) % devices]).astype(BF16)
        total = mm(scale_ref[q], pick_ref[0]) + mm(facing, pick_ref[1])
        out_ref[q] = total.astype(BF16)


def mirrored_exchange(upper, line, devices):
    middle = devices // 2
    facing = [(e, devices - 1 - e) for e in range(devices)]
    partner = [(e, devices - e) for e in range(1, devices) if e != middle]
    partner = partner + [(0, middle), (middle, 0)]
    upper = lax.ppermute(upper, ("ty", "tx"), facing)
    line = lax.ppermute(line, ("ty", "tx"), partner)
    return upper, line


def mirrored_weight(scale, upper, line):
    devices, slab, _ = scale.shape
    half, middle = slab // 2, devices // 2
    me = lax.axis_index(("ty", "tx"))
    got = jnp.concatenate([upper, jnp.broadcast_to(line, (half, N))], axis=0)
    source = lax.broadcasted_iota(jnp.int32, (slab, slab), 0)
    slot = lax.broadcasted_iota(jnp.int32, (slab, slab), 1)
    low = (me < middle).astype(jnp.int32)
    own = (slot < half) & (source == slot + low)
    other = (slot < half) & (source == half - low - slot)
    other = other & ((me != middle) | (slot > 0))
    other = other | ((me == middle) & (slot == half) & (source == half))
    picks = jnp.stack([own, other]).astype(BF16)
    q2 = np.arange(slab)
    flips = np.stack([q2[:, None] == (slab - q2) % slab, q2[:, None] == slab - 1 - q2])
    return pl.pallas_call(
        mirror_kernel,
        out_shape=jax.ShapeDtypeStruct(scale.shape, BF16),
        compiler_params=PARAMS,
    )(scale, turned(got, devices), picks, jnp.asarray(flips.astype(ml_dtypes.bfloat16)))


def row_matrix(first, cols, lanes, shift):
    twice = jnp.asarray(np.concatenate([first, first[: 2 * WIN]], axis=0))
    me = lax.axis_index("tx")
    zero = jnp.zeros((), jnp.int32)
    starts = [(me ^ m) * cols + (0 if shift is None else shift) for m in range(lanes)]
    rows = [lax.dynamic_slice(twice, (start, zero), (cols, first.shape[1])) for start in starts]
    return jnp.concatenate(rows, axis=0)


def swap_pieces(pieces):
    lanes = len(pieces)
    return [pieces[0]] + [
        lax.ppermute(pieces[m], "tx", [(k, k ^ m) for k in range(lanes)]) for m in range(1, lanes)
    ]


def phase_table(shift, devices, width):
    kr = counting(devices)[:, None] + devices * counting(8)[None, :]
    angle = 2.0 * math.pi / TOK * (kr * shift % TOK).astype(F32)
    table = jnp.stack([jnp.cos(angle), -jnp.sin(angle)], axis=1)
    return jnp.broadcast_to(table[..., None], (devices, 2, 8, width))


def patch_gradient(pieces, scale, data, shift, mirror, beside):
    lanes = lax.axis_size("tx")
    devices = lax.axis_size("ty") * lanes
    own, cols, _ = pieces[0].shape
    slab = N // devices
    halved = data is None
    outer, outer_t, inner, inner_t = (
        jnp.asarray(value) for value in column_constants(devices, slab)
    )
    if halved:
        first = half_constants()[0]
        twist, low, high, low_t, high_t = (jnp.asarray(value) for value in half_constants()[1:])
        part = (devices, slab, slab)
        onward = (row_forward_half, (row_matrix(first, cols, lanes, shift[1]), twist, low, high))
        backward = (row_inverse_half, (row_matrix(first, cols, lanes, None), twist, low_t, high_t))
        middle = lax.axis_index(("ty", "tx")) == devices // 2
    else:
        first = row_matrix(row_constants()[0], cols, lanes, None)
        twist, second, second_t = (jnp.asarray(value) for value in row_constants()[1:])
        part = (devices, 2, slab, slab)
        onward = (row_forward, (first, twist, second))
        backward = (row_inverse, (first, twist, second_t))
        extra = ()
        away = (inner, scale, inner_t, outer_t, data)
    split = (PATCH, devices // PATCH) + part[1:]
    sent = pl.pallas_call(
        onward[0], out_shape=jax.ShapeDtypeStruct(split, BF16), compiler_params=PARAMS
    )(*swap_pieces(pieces), *onward[1])
    if halved:
        sent, mirror, shift = lax.optimization_barrier((sent, mirror, shift))
        extra = (middle.astype(jnp.int32).reshape(1), phase_table(shift[0], devices, slab))
        table = mirrored_weight(scale, *mirror)
    moved = lax.all_to_all(
        sent.reshape(part), ("ty", "tx"), split_axis=0, concat_axis=0, tiled=True
    )
    if halved:
        moved, table, beside = lax.optimization_barrier((moved, table, beside))
        beside = from_neighbours(beside, 1)
        away = (inner, table, inner_t, outer_t)
    spaces = [pltpu.SMEM, pltpu.VMEM][: len(extra)] + [pltpu.VMEM] * 2 + [pl.ANY] * len(away)
    wave = pl.pallas_call(
        functools.partial(column_kernel, halved),
        in_specs=[pl.BlockSpec(memory_space=space) for space in spaces],
        out_shape=jax.ShapeDtypeStruct(part, BF16),
        scratch_shapes=[pltpu.VMEM((devices, 2, slab, slab), BF16)]
        + [pltpu.VMEM(value.shape, BF16) for value in away]
        + [pltpu.SemaphoreType.DMA((len(away),))],
        compiler_params=PARAMS,
    )(*extra, moved, outer, *away)
    if halved:
        wave, beside = lax.optimization_barrier((wave, beside))
    returned = lax.all_to_all(wave, ("ty", "tx"), split_axis=0, concat_axis=0, tiled=True)
    if not halved:
        returned, beside = lax.optimization_barrier((returned, beside))
    slabs = pl.pallas_call(
        backward[0],
        in_specs=[pl.BlockSpec(memory_space=pltpu.HBM)]
        + [pl.BlockSpec(memory_space=pltpu.VMEM)] * len(backward[1]),
        out_shape=[jax.ShapeDtypeStruct((own, cols, PIXELS), BF16)] * lanes,
        scratch_shapes=[pltpu.VMEM(split, BF16), pltpu.SemaphoreType.DMA((own,))],
        compiler_params=PARAMS,
    )(returned.reshape(split), *backward[1])
    return swap_pieces(slabs), beside


def layer_norm(values, gain):
    centre = jnp.mean(values, axis=-1, keepdims=True)
    shifted = values - centre
    spread = jnp.mean(shifted * shifted, axis=-1, keepdims=True)
    return (shifted * lax.rsqrt(spread + EPSILON) * gain).astype(BF16)


def to_windows(band):
    rows, cols, feats = band.shape
    pieces = [
        band[n : n + WIN, k : k + WIN, :].reshape(SPAN, feats)
        for n in range(0, rows, WIN)
        for k in range(0, cols, WIN)
    ]
    return jnp.concatenate(pieces, axis=0)


def from_windows(tokens, cols):
    feats = tokens.shape[-1]
    size = SPAN * cols // WIN
    bands = []
    for top in range(0, tokens.shape[0], size):
        pieces = [
            tokens[n : n + SPAN].reshape(WIN, WIN, feats) for n in range(top, top + size, SPAN)
        ]
        bands.append(jnp.concatenate(pieces, axis=1))
    return jnp.concatenate(bands, axis=0)


def gelu_twice(value):
    value = value.astype(BF16)
    inside = value * (BF16(GELU_IN) + BF16(GELU_CUBE) * (value * value))
    return value + value * jnp.tanh(inside)


def load_weights(j, sources, targets, sems):
    copies = [
        pltpu.make_async_copy(source.at[j], target, sems.at[n])
        for n, (source, target) in enumerate(zip(sources, targets))
    ]

    @pl.when(pl.program_id(0) == 0)
    def _():
        for copy in copies:
            copy.start()

    def wait(which):
        @pl.when(pl.program_id(0) == 0)
        def _():
            for n in which:
                copies[n].wait()

    return wait


def swin_band(flow, wait, bias_ref, gain_ref, weight_refs, scratch):
    qkv_ref, proj_ref, up_ref, down_ref = weight_refs
    mixed_ref, score_ref, prob_ref, active_ref = scratch
    count = flow.shape[0] // SPAN
    pairs = HEADS // 2
    depth = D // HEADS
    wide = 2 * depth
    normed = layer_norm(flow, gain_ref[0:1, :])
    scale = 1.0 / math.sqrt(depth)
    wait((0,))
    mixed_ref[:, :D] = (mm(normed, qkv_ref[:, :D]) * scale).astype(BF16)
    mixed_ref[:, D : 2 * D] = mm(normed, qkv_ref[:, D : 2 * D]).astype(BF16)
    mixed_ref[:, 2 * D :] = mm(normed, qkv_ref[:, 2 * D :]).astype(BF16)
    lower = lax.broadcasted_iota(jnp.int32, (SPAN, wide), 1) < depth

    def scores_of(w):
        rows = slice(w * SPAN, (w + 1) * SPAN)
        for p in range(pairs):
            query = mixed_ref[rows, p * wide : (p + 1) * wide]
            key = mixed_ref[rows, D + p * wide : D + (p + 1) * wide]
            zero = jnp.zeros_like(query)
            split = jnp.concatenate(
                [jnp.where(lower, query, zero), jnp.where(lower, zero, query)], axis=0
            )
            score_ref[w, :, p * wide : (p + 1) * wide] = mm(key, split, NT)

    def probs_of(w):
        bias = bias_ref[w]
        for p in range(pairs):
            lanes = slice(p * wide, (p + 1) * wide)
            scores = score_ref[w, :, lanes] + bias
            weights = jnp.exp(scores - jnp.max(scores, axis=0, keepdims=True))
            share = 1.0 / jnp.sum(weights, axis=0, keepdims=True)
            prob_ref[w, :, lanes] = (weights * share).astype(BF16)

    def mixture_of(w):
        rows = slice(w * SPAN, (w + 1) * SPAN)
        for p in range(pairs):
            lanes = slice(p * wide, (p + 1) * wide)
            value = mixed_ref[rows, 2 * D + p * wide : 2 * D + (p + 1) * wide]
            mixture = mm(prob_ref[w, :, lanes], value, TN)
            mixed_ref[rows, lanes] = jnp.where(lower, mixture[:SPAN], mixture[SPAN:]).astype(BF16)

    for run in (scores_of, probs_of, mixture_of):
        for w in range(count):
            run(w)
    wait((1, 2, 3))
    flow = flow + mm(mixed_ref[:, :D], proj_ref[...])
    normed = layer_norm(flow, gain_ref[1:2, :])
    chunks = up_ref.shape[1] // D
    for c in range(chunks):
        part = slice(c * D, (c + 1) * D)
        active_ref[:, part] = gelu_twice(mm(normed, up_ref[:, part]))
    return flow + 0.5 * mm(active_ref[...], down_ref[...])


def rolled_band(sign, shift_ref, refs, rows, count=WIN):
    main_ref, side_ref, edge_ref, corner_ref = refs
    cols = main_ref.shape[1]
    top = pl.program_id(0) * count + sign * shift_ref[0]
    behind = -rows if sign > 0 else WIN
    beside = -cols if sign > 0 else WIN

    source = lax.broadcasted_iota(jnp.int32, (cols, cols + WIN), 1)
    wanted = lax.broadcasted_iota(jnp.int32, (cols, cols + WIN), 0) + sign * shift_ref[1]
    found = (source < cols) & (source == wanted)
    found = found | (source >= cols) & (source - cols == wanted + beside)
    pick = jnp.where(found, 1.0, 0.0).astype(BF16)
    band = []
    for j in range(count):
        row = top + j
        inside = (row >= 0) & (row < rows)
        here, there = jnp.clip(row, 0, rows - 1), jnp.clip(row + behind, 0, WIN - 1)
        main = jnp.where(inside, main_ref[here], edge_ref[there])
        side = jnp.where(inside, side_ref[here], corner_ref[there])
        band.append(mm(pick, jnp.concatenate([main, side], axis=0)))
    return jnp.stack(band)


def first_kernel(zeta, sigma, count, parts, rows, before, *refs):
    shift_ref, state_ref, *refs = refs
    if before is not None:
        back_refs, refs = refs[:4], refs[4:]
    grad_refs, refs = refs[: count * parts], refs[count * parts :]
    if sigma is not None:
        noise_ref, *refs = refs
    bias_ref, embed_ref, gain_ref, *sources = refs[:7]
    base_ref, out_ref, side_ref, edge_ref, corner_ref, *scratch = refs[7:]
    targets, sems, scratch = scratch[:4], scratch[4], scratch[5:]
    wait = load_weights(0, sources, targets, sems)
    state = state_ref[...]
    if before is not None:
        state = state - before * rolled_band(-1, shift_ref, back_refs, rows, state.shape[0])
    height = state.shape[0]
    if parts == 1:
        grad = grad_refs[0][...].astype(F32)
    else:
        bands = []
        for k in range(height // WIN):
            turn = (pl.program_id(0) * (height // WIN) + k) ^ shift_ref[2]
            band = 0.0
            for n in range(0, count * parts, parts):
                piece = grad_refs[n][...]
                for m in range(1, parts):
                    piece = jnp.where(turn == m, grad_refs[n + m][...], piece)
                band = band + piece.astype(F32)
            bands.append(band)
        grad = jnp.concatenate(bands, axis=0)
    step = zeta * grad
    half = state - step
    tokens = mm(to_windows(half).astype(BF16), embed_ref[...]).astype(BF16).astype(F32)
    flow = swin_band(tokens, wait, bias_ref, gain_ref, targets, scratch)
    result = from_windows(flow, half.shape[1]).astype(BF16)
    out_ref[:, :, :D] = result
    side_ref[:, :, :D] = result[:, :WIN]
    if sigma is None:
        base_ref[...] = half
    else:
        noise = sigma * noise_ref[...]
        base_ref[...] = half + noise
        change = (noise - step).astype(BF16)
        out_ref[:, :, D:] = change
        side_ref[:, :, D:] = change[:, :WIN]

    @pl.when(pl.program_id(0) == 0)
    def _():
        edge_ref[...] = out_ref[:WIN]
        corner_ref[...] = side_ref[:WIN]


def write_pieces(turn, refs, value):
    for m, ref in enumerate(refs):

        def write(ref=ref):
            ref[...] = value

        pl.when(turn == m)(write)


def second_kernel(sigma, rows, parts, *refs):
    shift_ref, *refs = refs
    tile_refs, refs = refs[:4], refs[4:]
    bias_ref, unembed_ref, gain_ref, *sources = refs[:7]
    out_ref, side_ref, edge_ref, corner_ref, *scratch = refs[7:]
    state_refs, scratch = scratch[:parts], scratch[parts:]
    targets, sems, scratch = scratch[:4], scratch[4], scratch[5:]
    wait = load_weights(1, sources, targets, sems)
    height, cols, _ = out_ref.shape
    band = rolled_band(1, shift_ref, tile_refs, rows, height)
    tokens = to_windows(band[:, :, :D])
    flow = swin_band(tokens, wait, bias_ref, gain_ref, targets, scratch)
    estimate = from_windows(mm(flow.astype(BF16), unembed_ref[...]), cols)
    narrow = estimate.astype(BF16)
    out_ref[...] = narrow
    side_ref[...] = narrow[:, cols - WIN :]
    edge_ref[...] = narrow[height - WIN :]
    corner_ref[...] = narrow[height - WIN :, cols - WIN :]
    if parts > 0:
        change = (band[:, :, D:] - sigma * estimate).astype(BF16)
        for n in range(height // WIN):
            turn = (pl.program_id(0) * (height // WIN) + n) ^ shift_ref[2]
            write_pieces(turn, state_refs, change[n * WIN : (n + 1) * WIN])


def whole(array):
    zeros = (0,) * array.ndim
    return pl.BlockSpec(array.shape, lambda *_: zeros)


def member(array, j):
    place = (j,) + (0,) * (array.ndim - 1)
    return pl.BlockSpec((None,) + array.shape[1:], lambda *_: place)


def band_spec(cols, feats, height=WIN):
    return pl.BlockSpec((height, cols, feats), lambda n, *_: (n, 0, 0))


def bias_spec(cols, height=WIN):
    count = height * cols // SPAN
    return pl.BlockSpec((count, SPAN, 2 * SPAN), lambda n, *_: (n, 0, 0))


def band_scratch(cols, weights, height=WIN):
    count = height * cols // SPAN
    return [pltpu.VMEM(value.shape[1:], BF16) for value in weights] + [
        pltpu.SemaphoreType.DMA((len(weights),)),
        pltpu.VMEM((height * cols, 3 * D), BF16),
        pltpu.VMEM((count, SPAN, HEADS * SPAN), F32),
        pltpu.VMEM((count, SPAN, HEADS * SPAN), BF16),
    ]


def strip_outs(rows, cols, feats, height=WIN):
    specs = [band_spec(cols, feats, height), band_spec(WIN, feats, height)]
    specs += [
        pl.BlockSpec((WIN, width, feats), lambda *_: (0, 0, 0)) for width in (cols, WIN)
    ]
    shapes = [(rows, cols), (rows, WIN), (WIN, cols), (WIN, WIN)]
    return specs, [jax.ShapeDtypeStruct(shape + (feats,), BF16) for shape in shapes]


def first_block(zeta, sigma, state, before, shift, back, grads, noise, bias, w_embed, weights):
    *weights, gains = weights
    rows, cols, _ = state.shape
    parts = len(grads[0])
    pieces = [piece for grad in grads for piece in grad]
    fields = [] if sigma is None else [noise]
    feats = D if sigma is None else D + PIXELS
    height = 2 * WIN
    specs, shapes = strip_outs(rows, cols, feats, height)
    band = band_spec(cols, PIXELS, height)
    return pl.pallas_call(
        functools.partial(first_kernel, zeta, sigma, len(grads), parts, rows, before),
        grid_spec=pltpu.PrefetchScalarGridSpec(
            num_scalar_prefetch=1,
            grid=(rows // height,),
            in_specs=[band]
            + [whole(value) for value in back]
            + [band if parts == 1 else whole(value) for value in pieces]
            + [band] * len(fields)
            + [bias_spec(cols, height), whole(w_embed), member(gains, 0)]
            + [pl.BlockSpec(memory_space=pl.ANY)] * len(weights),
            out_specs=[band] + specs,
            scratch_shapes=band_scratch(cols, weights, height)
            + [pltpu.VMEM((height * cols, weights[2].shape[2]), BF16)],
        ),
        out_shape=[jax.ShapeDtypeStruct((rows, cols, PIXELS), F32)] + shapes,
        compiler_params=PARAMS,
    )(shift, state, *back, *pieces, *fields, bias, w_embed, gains, *weights)


def second_block(sigma, shift, tile, bias, w_unembed, weights, parts):
    *weights, gains = weights
    rows, cols, _ = tile[0].shape
    height = 2 * WIN
    specs, shapes = strip_outs(rows, cols, PIXELS, height)
    specs += [pl.BlockSpec((WIN, cols, PIXELS), lambda *_: (0, 0, 0))] * parts
    shapes += [jax.ShapeDtypeStruct((WIN, cols, PIXELS), BF16)] * parts
    return pl.pallas_call(
        functools.partial(second_kernel, sigma, rows, parts),
        grid_spec=pltpu.PrefetchScalarGridSpec(
            num_scalar_prefetch=1,
            grid=(rows // height,),
            in_specs=[whole(value) for value in tile]
            + [bias_spec(cols, height), whole(w_unembed), member(gains, 1)]
            + [pl.BlockSpec(memory_space=pl.ANY)] * len(weights),
            out_specs=specs,
            scratch_shapes=band_scratch(cols, weights, height)
            + [pltpu.VMEM((height * cols, weights[2].shape[2]), BF16)],
        ),
        out_shape=shapes,
        compiler_params=PARAMS,
    )(shift, *tile, bias, w_unembed, gains, *weights)


def from_neighbours(tile, by):
    main, side, edge, corner = tile
    ty, tx = lax.axis_size("ty"), lax.axis_size("tx")
    across = [
        (i * tx + k, (i + by) % ty * tx + (k + by) % tx) for i in range(ty) for k in range(tx)
    ]
    return (
        main,
        lax.ppermute(side, "tx", [(k, (k + by) % tx) for k in range(tx)]),
        lax.ppermute(edge, "ty", [(i, (i + by) % ty) for i in range(ty)]),
        lax.ppermute(corner, ("ty", "tx"), across),
    )


def windows_of(grid):
    rows, cols = grid.shape
    shaped = grid.reshape(rows // WIN, WIN, cols // WIN, WIN).transpose(0, 2, 1, 3)
    return shaped.reshape(rows // WIN * (cols // WIN), SPAN)


def bias_of(labels, keep):
    allowed = jnp.ones((1, SPAN, SPAN), bool)
    if labels is not None:
        label = windows_of(labels)
        allowed = label[:, :, None] == label[:, None, :]
    if keep is not None:
        kept = windows_of(keep)[:, :, None] == 1
        allowed = allowed & (kept | jnp.eye(SPAN, dtype=bool)[None])
    bias = jnp.where(allowed, 0.0, -1e30).astype(F32)
    return jnp.concatenate([bias, bias], axis=2)


def region(index, shift):
    return jnp.where(index < TOK - WIN, 0, jnp.where(index < TOK - shift, 1, 2)).astype(jnp.int32)


@functools.lru_cache(maxsize=None)
def lane_order(cols):
    parts = LANES // cols
    groups = PATCH // parts
    lane = np.arange(PATCH * cols)
    g, h, k = lane // LANES, lane % LANES // cols, lane % cols
    source = PATCH * k + h * groups + g
    matrix = np.zeros((PATCH * cols, PATCH * cols), np.float32)
    matrix[source, lane] = 1.0
    return matrix.astype(ml_dtypes.bfloat16), np.ascontiguousarray(matrix.T).astype(
        ml_dtypes.bfloat16
    )


def move_lanes(values, matrix):
    high = values.astype(BF16)
    low = (values - high.astype(F32)).astype(BF16)
    return mm(high, matrix) + mm(low, matrix)


def to_patches_kernel(narrow, place_ref, tile_ref, order_ref, *out_refs):
    count, cols, _ = out_refs[0].shape
    parts = LANES // cols
    groups = PATCH // parts
    if narrow:
        ordered = mm(tile_ref[...].astype(BF16), order_ref[...])
    else:
        ordered = move_lanes(tile_ref[...], order_ref[...])
    patches = []
    for i in range(count):
        band = ordered[i * PATCH : (i + 1) * PATCH]
        stacked = jnp.concatenate(
            [band[:, g * LANES : (g + 1) * LANES] for g in range(groups)], axis=0
        )
        turned = stacked.T
        patches.append(
            jnp.concatenate([turned[h * cols : (h + 1) * cols] for h in range(parts)], axis=1)
        )
    result = jnp.stack(patches).astype(out_refs[0].dtype)
    if len(out_refs) == 1:
        out_refs[0][...] = result
    else:
        write_pieces(pl.program_id(0) ^ place_ref[0], out_refs, result)


def lanes_of(patches):
    count, cols, _ = patches.shape
    parts = LANES // cols
    groups = PATCH // parts
    width = groups * PATCH
    bands = []
    for i in range(count):
        stacked = jnp.concatenate(
            [patches[i, :, h * width : (h + 1) * width] for h in range(parts)], axis=0
        )
        turned = stacked.T
        bands.append(
            jnp.concatenate([turned[g * PATCH : (g + 1) * PATCH] for g in range(groups)], axis=1)
        )
    return jnp.concatenate(bands, axis=0)


def base_tile_kernel(scale, base_ref, noise_ref, order_ref, out_ref):
    moved = move_lanes(lanes_of(base_ref[...]), order_ref[...])
    out_ref[...] = moved + scale * noise_ref[...]


def last_tile_kernel(sigma, rows, shift_ref, tile_ref, *refs):
    *back_refs, order_ref, out_ref = refs
    estimate = rolled_band(-1, shift_ref, back_refs, rows)
    moved = mm(lanes_of(estimate).astype(BF16), order_ref[...])
    out_ref[...] = tile_ref[...] - sigma * moved


def patches_of(tiles, j, place, kind=F32, parts=1):
    rows, cols = tiles.shape[1] // PATCH, tiles.shape[2] // PATCH
    order = jnp.asarray(lane_order(cols)[0])
    spec, shape = band_spec(cols, PIXELS), (rows, cols, PIXELS)
    if parts > 1:
        spec = pl.BlockSpec((WIN, cols, PIXELS), lambda *_: (0, 0, 0))
        shape = (WIN, cols, PIXELS)
    return pl.pallas_call(
        functools.partial(to_patches_kernel, kind == BF16),
        grid_spec=pltpu.PrefetchScalarGridSpec(
            num_scalar_prefetch=1,
            grid=(rows // WIN,),
            in_specs=[
                pl.BlockSpec((None, WIN * PATCH, cols * PATCH), lambda n, *_: (j, n, 0)),
                whole(order),
            ],
            out_specs=[spec] * parts,
        ),
        out_shape=[jax.ShapeDtypeStruct(shape, kind)] * parts,
        compiler_params=PARAMS,
    )(place, tiles, order)


def tile_of(base, sigma, shift, back, scale, noise, j):
    rows, cols, _ = base.shape
    order = jnp.asarray(lane_order(cols)[1])
    tile_spec = pl.BlockSpec((WIN * PATCH, cols * PATCH), lambda n, *_: (n, 0))
    shape = jax.ShapeDtypeStruct((rows * PATCH, cols * PATCH), F32)
    tile = pl.pallas_call(
        functools.partial(base_tile_kernel, scale),
        grid=(rows // WIN,),
        in_specs=[
            band_spec(cols, PIXELS),
            pl.BlockSpec((None, WIN * PATCH, cols * PATCH), lambda n, *_: (j, n, 0)),
            whole(order),
        ],
        out_specs=tile_spec,
        out_shape=shape,
        compiler_params=PARAMS,
    )(base, noise, order)
    return pl.pallas_call(
        functools.partial(last_tile_kernel, sigma, rows),
        grid_spec=pltpu.PrefetchScalarGridSpec(
            num_scalar_prefetch=1,
            grid=(rows // WIN,),
            in_specs=[tile_spec] + [whole(value) for value in back] + [whole(order)],
            out_specs=tile_spec,
        ),
        out_shape=shape,
        compiler_params=PARAMS,
    )(shift, tile, *back, order)


def per_device(
    image, noise, offsets, key_mask, gains, observed, vis_weight,
    w_embed, w_qkv, w_proj, w_up, w_down, w_unembed, norm_gains,
):
    rows = image.shape[0] // PATCH
    cols = image.shape[1] // PATCH
    devices = lax.axis_size("ty") * lax.axis_size("tx")
    lanes = lax.axis_size("tx")
    fast = N // devices == TOK // 2 and rows == lanes * WIN and lanes & (lanes - 1) == 0
    column = lax.axis_index("tx").astype(jnp.int32)[None]
    places = [jnp.concatenate([offsets[step], column]) for step in range(STEPS)]
    row_index = lax.axis_index("ty") * rows + counting(rows)
    col_index = lax.axis_index("tx") * cols + counting(cols)
    weights = (w_qkv, w_proj, w_up, w_down, norm_gains)
    w_embed = w_embed.reshape(PATCH, PATCH, D).transpose(1, 0, 2).reshape(PIXELS, D)
    w_unembed = w_unembed.reshape(D, PATCH, PATCH).transpose(0, 2, 1).reshape(D, PIXELS)
    state = patches_of(image[None], 0, column)[0]
    extras = [patches_of(noise, step, column)[0] for step in range(STEPS - 1)] + [None]
    first_bias = bias_of(None, key_mask)
    biases = []
    for step in range(STEPS):
        labels = (
            3 * region(row_index, offsets[step, 0])[:, None]
            + region(col_index, offsets[step, 1])[None, :]
        )
        biases.append(bias_of(labels, None))
    beside = (state, extras, first_bias, biases, w_embed, w_unembed)
    shift, before, back, moving, mirror = places[0], None, (), None, None
    grads = []
    if fast:
        weight, scale, data = spectrum_inputs(gains, observed, vis_weight, devices)
        half = weight.shape[0] // 2
        lines = (weight[half:], weight[:1])
        grad, (beside, lines) = patch_gradient(
            patches_of(image[None], 0, column, BF16, lanes), scale, data, None, None,
            (beside, lines),
        )
        grads = [grad]
        state, extras, first_bias, biases, w_embed, w_unembed = beside
    for step in range(STEPS):
        if not fast:
            tile = image if step == 0 else tile_of(state, before, shift, back, 0.0, noise, 0)
            grad = plain_gradient(tile, gains, observed, vis_weight)
            grad = patches_of(grad.astype(F32)[None], 0, column, BF16)[0]
            grads = [[grad]]
        elif step > 0:
            grad, back = patch_gradient(moving, scale, None, shift, mirror, back)
            grads = grads + [grad]
        last = step + 1 == STEPS
        sigma = None if last else SIGMAS[step + 1]
        state, *first = first_block(
            STEP_SIZES[step], sigma, state, before, shift, back, grads, extras[step], first_bias,
            w_embed, weights,
        )
        shift, before = places[step], SIGMAS[step]
        first = from_neighbours(first, -1)
        if fast and step == 0:
            first, lines = lax.optimization_barrier((first, lines))
            mirror = mirrored_exchange(*lines, devices)
        rolled = second_block(
            before, shift, first, biases[step], w_unembed, weights,
            lanes if fast and not last else 0,
        )
        back, moving = rolled[:4], rolled[4:]
        if fast and step == 0:
            moving, mirror = lax.optimization_barrier((moving, mirror))
        if last or not fast:
            back = from_neighbours(back, 1)
    return tile_of(state, before, shift, back, SIGMAS[STEPS], noise, STEPS - 1)


def solution(mesh):
    in_specs = (
        P("ty", "tx"),
        P(None, "ty", "tx"),
        P(),
        P("ty", "tx"),
        P(None, ("ty", "tx"), None),
        P(None, ("ty", "tx"), None),
        P(("ty", "tx"), None),
        P(),
        P(),
        P(),
        P(),
        P(),
        P(),
        P(),
    )
    out_specs = P("ty", "tx")
    return jax.shard_map(
        per_device, mesh=mesh, in_specs=in_specs, out_specs=out_specs, check_vma=False
    )
```

```python
import functools
import math

import jax
import jax.numpy as jnp
import ml_dtypes
import numpy as np
from jax import lax
from jax.experimental import pallas as pl
from jax.experimental.pallas import tpu as pltpu
from jax.sharding import PartitionSpec as P

N = 4096
PATCH = 16
PIXELS = PATCH * PATCH
WIN = 8
D = 512
HEADS = 8
STEPS = 2
SPAN = WIN * WIN
LANES = 128
GROUP = 8
TOK = N // PATCH

SIGMAS = (0.8, 0.5, 0.3)
STEP_SIZES = (0.9, 0.7)
EPSILON = 1e-05
HIGHEST = lax.Precision.HIGHEST
BF16 = jnp.bfloat16
F32 = jnp.float32
GELU_IN = math.sqrt(2.0 / math.pi)
GELU_CUBE = 0.044715 * GELU_IN
VMEM_LIMIT = 56 * 1024 * 1024
PARAMS = pltpu.CompilerParams(vmem_limit_bytes=VMEM_LIMIT)
TN = (((0,), (0,)), ((), ()))
NT = (((1,), (1,)), ((), ()))
NN = (((1,), (0,)), ((), ()))


def mm(left, right, dims=NN):
    return lax.dot_general(left, right, dims, preferred_element_type=F32)


def counting(length):
    return jnp.arange(length, dtype=jnp.int32)


def roots(length, outer, inner, sign):
    product = outer[:, None] * inner[None, :] % length
    angle = 2.0 * math.pi / length * product.astype(F32)
    return (jnp.cos(angle), sign * jnp.sin(angle))


def complex_einsum(form, left, right):
    real = jnp.einsum(form, left[0], right[0], precision=HIGHEST) - jnp.einsum(
        form, left[1], right[1], precision=HIGHEST
    )
    imag = jnp.einsum(form, left[0], right[1], precision=HIGHEST) + jnp.einsum(
        form, left[1], right[0], precision=HIGHEST
    )
    return (real, imag)


def complex_times(left, right):
    return (left[0] * right[0] - left[1] * right[1], left[0] * right[1] + left[1] * right[0])


def along_last(real_part, imag_part, groups, sign):
    rows, length = real_part.shape
    inner = length // groups
    first = roots(groups, counting(groups), counting(groups), sign)
    twist = roots(length, counting(inner), counting(groups), sign)
    second = roots(inner, counting(inner), counting(inner), sign)
    shaped = real_part.reshape(rows, groups, inner)
    if imag_part is None:
        partial_value = (
            jnp.einsum("mab,ka->mbk", shaped, first[0], precision=HIGHEST),
            jnp.einsum("mab,ka->mbk", shaped, first[1], precision=HIGHEST),
        )
    else:
        partial_value = complex_einsum(
            "mab,ka->mbk", (shaped, imag_part.reshape(rows, groups, inner)), first
        )
    partial_value = complex_times(partial_value, twist)
    result = complex_einsum("jb,mbk->mjk", second, partial_value)
    return (result[0].reshape(rows, length), result[1].reshape(rows, length))


def across_groups(pair, groups, sign):
    inner, cols = pair[0].shape
    width = cols // groups
    length = groups * inner
    first = roots(groups, counting(groups), counting(groups), sign)
    twist = roots(length, counting(inner), counting(groups), sign)
    second = roots(inner, counting(inner), counting(inner), sign)
    shaped = (pair[0].reshape(inner, groups, width), pair[1].reshape(inner, groups, width))
    partial_value = complex_einsum("bhc,kh->cbk", shaped, first)
    partial_value = complex_times(partial_value, twist)
    result = complex_einsum("jb,cbk->cjk", second, partial_value)
    return (result[0].reshape(width, length), result[1].reshape(width, length))


def exchange_pair(pair):
    return tuple(
        lax.all_to_all(
            part.astype(BF16), ("ty", "tx"), split_axis=1, concat_axis=1, tiled=True
        ).astype(F32)
        for part in pair
    )


def plain_gradient(tile, gains, observed, vis_weight):
    devices = lax.axis_size("ty") * lax.axis_size("tx")
    slab = lax.all_to_all(tile.astype(BF16), "tx", split_axis=0, concat_axis=1, tiled=True)
    moved = exchange_pair(along_last(slab.astype(F32), None, devices, -1.0))
    spectrum = across_groups(moved, devices, -1.0)
    spectrum = (spectrum[0] * (1.0 / N), spectrum[1] * (1.0 / N))
    model = complex_times((gains[0], gains[1]), spectrum)
    misfit = (vis_weight * (model[0] - observed[0]), vis_weight * (model[1] - observed[1]))
    back = complex_times((gains[0], -gains[1]), misfit)
    returned = exchange_pair(along_last(back[0], back[1], devices, 1.0))
    slab_grad = across_groups(returned, devices, 1.0)[0] * (1.0 / N)
    return lax.all_to_all(slab_grad.astype(BF16), "tx", split_axis=1, concat_axis=0, tiled=True)


def embed_complex(angle, row_axis, col_axis):
    cos, sin = np.cos(angle), np.sin(angle)
    top = np.stack([cos, sin], axis=col_axis)
    bottom = np.stack([-sin, cos], axis=col_axis)
    return np.stack([top, bottom], axis=row_axis)


def wheel(length, product):
    return 2.0 * math.pi / length * (product % length)


@functools.lru_cache(maxsize=None)
def row_constants():
    k = np.arange(TOK)
    angle = wheel(TOK, k[:, None] * k[None, :])
    first = np.concatenate([np.cos(angle), -np.sin(angle)], axis=1)
    b = np.repeat(np.arange(PATCH), PATCH)
    angle = wheel(N, b[:, None] * k[None, :])
    twist = np.stack([np.cos(angle), -np.sin(angle)])
    p = np.arange(PATCH)
    small = embed_complex(wheel(PATCH, p[:, None] * p[None, :]), 1, 1)
    second = np.einsum("kpqb,xy->kpxqby", small, np.eye(PATCH)).reshape(2 * PIXELS, 2 * PIXELS)
    return (
        first.astype(ml_dtypes.bfloat16),
        twist.astype(np.float32),
        second.astype(ml_dtypes.bfloat16),
        np.ascontiguousarray(second.T).astype(ml_dtypes.bfloat16),
    )


@functools.lru_cache(maxsize=None)
def half_constants():
    _, twist, second, _ = row_constants()
    half, quarter = TOK // 2, TOK // 4
    low = np.concatenate([1 + np.arange(quarter), 1 + half + np.arange(quarter)])
    digits = np.concatenate([low, low - 1])
    k = np.arange(TOK)
    angle = wheel(TOK, k[:, None] * digits[None, :])
    first = np.concatenate([np.cos(angle), -np.sin(angle)], axis=1)
    zero_line = np.concatenate([np.tile(np.eye(PATCH), PATCH), np.zeros((PATCH, PIXELS))], axis=1)
    upper = np.concatenate([second[PIXELS:].astype(np.float32), zero_line])
    lower = second[:PIXELS].astype(np.float32)
    return (first.astype(ml_dtypes.bfloat16), np.ascontiguousarray(twist[:, :, digits])) + tuple(
        np.ascontiguousarray(value).astype(ml_dtypes.bfloat16)
        for value in (lower, upper, lower.T, upper.T)
    )


@functools.lru_cache(maxsize=None)
def column_constants(devices, rows):
    s = np.arange(devices)
    small = embed_complex(wheel(devices, s[:, None] * s[None, :]), 1, 2)
    wide = devices * 2 * GROUP
    outer = np.einsum("qpsr,xy->qpxsry", small, np.eye(GROUP)).reshape(wide, wide)
    kr = s[:, None] + devices * np.arange(rows)[None, :]
    angle = wheel(N, kr[:, :, None] * np.arange(rows)[None, None, :])
    inner = embed_complex(angle, 1, 2).reshape(devices, 2 * rows, 2 * rows) / N
    return tuple(
        np.ascontiguousarray(value).astype(ml_dtypes.bfloat16)
        for value in (outer, outer.T, inner, inner.transpose(0, 2, 1))
    )


def row_forward(*refs):
    *x_refs, first_ref, twist_ref, second_ref, out_ref = refs
    count = x_refs[0].shape[0]

    def step(i, carry):
        band = jnp.concatenate([x_ref[i] for x_ref in x_refs], axis=0)
        mixed = mm(band, first_ref[...], TN)
        real, imag = mixed[:, :TOK], mixed[:, TOK:]
        tr, ti = twist_ref[0], twist_ref[1]
        turned = jnp.concatenate(
            [(real * tr - imag * ti).astype(BF16), (real * ti + imag * tr).astype(BF16)], axis=0
        )
        result = mm(second_ref[...], turned).astype(BF16).reshape(PATCH, 2, PATCH, TOK)
        half = TOK // 2
        rows = pl.ds(pl.multiple_of(i * PATCH, PATCH), PATCH)
        out_ref[:, 0, :, rows, :] = result[..., :half]
        out_ref[:, 1, :, rows, :] = result[..., half:]
        return carry

    lax.fori_loop(0, count, step, 0, unroll=8)


def row_inverse(v_ref, first_ref, twist_ref, second_ref, *out_refs):
    count, cols, _ = out_refs[0].shape

    def step(i, carry):
        rows = pl.ds(pl.multiple_of(i * PATCH, PATCH), PATCH)
        wide = jnp.concatenate(
            [
                v_ref[:, 0, :, rows, :].reshape(2 * PIXELS, TOK // 2),
                v_ref[:, 1, :, rows, :].reshape(2 * PIXELS, TOK // 2),
            ],
            axis=1,
        )
        mixed = mm(second_ref[...], wide)
        real, imag = mixed[:PIXELS], mixed[PIXELS:]
        tr, ti = twist_ref[0], twist_ref[1]
        turned = jnp.concatenate(
            [(real * tr + imag * ti).astype(BF16), (imag * tr - real * ti).astype(BF16)], axis=1
        )
        result = mm(first_ref[...], turned, NT).astype(BF16)
        for m, out_ref in enumerate(out_refs):
            out_ref[i] = result[m * cols : (m + 1) * cols]
        return carry

    lax.fori_loop(0, count, step, 0, unroll=8)


def lane_index(shape):
    return lax.broadcasted_iota(jnp.int32, shape, len(shape) - 1)


def swap_halves(values):
    return pltpu.roll(values, values.shape[-1] // 2, len(values.shape) - 1)


def row_forward_half(*refs):
    *x_refs, first_ref, twist_ref, lower_ref, upper_ref, out_ref = refs
    count = x_refs[0].shape[0]
    half = TOK // 2

    def packed(real, imag, rows, high):
        left = lane_index(real.shape) < half // 2
        out_ref[high, 0, rows, :] = jnp.where(left, real, swap_halves(imag)).astype(BF16)
        out_ref[high, 1, rows, :] = jnp.where(left, swap_halves(real), imag).astype(BF16)

    def step(i, carry):
        band = jnp.concatenate([x_ref[i] for x_ref in x_refs], axis=0)
        mixed = mm(band, first_ref[...], TN)
        real, imag = mixed[:, :TOK], mixed[:, TOK:]
        tr, ti = twist_ref[0], twist_ref[1]
        turned = jnp.concatenate(
            [(real * tr - imag * ti).astype(BF16), (real * ti + imag * tr).astype(BF16)], axis=0
        )
        rows = pl.ds(pl.multiple_of(i * PATCH, PATCH), PATCH)
        lower = mm(lower_ref[...], turned[:, :half]).reshape(PATCH // 2, 2, PATCH, half)
        packed(lower[:, 0], lower[:, 1], rows, slice(0, PATCH // 2))
        upper = mm(upper_ref[...], turned[:, half:])
        line = upper[PIXELS:]
        upper = upper[:PIXELS].reshape(PATCH // 2, 2, PATCH, half)
        imag = upper[:, 1]
        head = jnp.where(lane_index(line.shape) == 0, line, imag[0])
        imag = jnp.concatenate([head[None], imag[1:]], axis=0)
        packed(upper[:, 0], imag, rows, slice(PATCH // 2, PATCH))
        return carry

    lax.fori_loop(0, count, step, 0, unroll=8)


def row_inverse_half(v_ref, first_ref, twist_ref, lower_ref, upper_ref, *out_refs):
    count, cols, _ = out_refs[0].shape
    half = TOK // 2

    def unpacked(rows, high):
        even = v_ref[high, 0, rows, :].astype(F32)
        odd = v_ref[high, 1, rows, :].astype(F32)
        left = lane_index(even.shape) < half // 2
        return jnp.where(left, even, swap_halves(odd)), jnp.where(left, swap_halves(even), odd)

    def step(i, carry):
        rows = pl.ds(pl.multiple_of(i * PATCH, PATCH), PATCH)
        real, imag = unpacked(rows, slice(0, PATCH // 2))
        lower = jnp.stack([real, imag], axis=1).reshape(PIXELS, half)
        real, imag = unpacked(rows, slice(PATCH // 2, PATCH))
        head = imag[0]
        at_zero = lane_index(head.shape) == 0
        nothing = jnp.zeros_like(head)
        imag = jnp.concatenate([jnp.where(at_zero, nothing, head)[None], imag[1:]], axis=0)
        upper = jnp.stack([real, imag], axis=1).reshape(PIXELS, half)
        upper = jnp.concatenate([upper, jnp.where(at_zero, head, nothing)], axis=0)
        mixed = jnp.concatenate(
            [mm(lower_ref[...], lower.astype(BF16)), mm(upper_ref[...], upper.astype(BF16))], axis=1
        )
        real, imag = mixed[:PIXELS], mixed[PIXELS:]
        tr, ti = twist_ref[0], twist_ref[1]
        turned = jnp.concatenate(
            [(real * tr + imag * ti).astype(BF16), (imag * tr - real * ti).astype(BF16)], axis=1
        )
        result = mm(first_ref[...], turned, NT).astype(BF16)
        for m, out_ref in enumerate(out_refs):
            out_ref[i] = result[m * cols : (m + 1) * cols]
        return carry

    lax.fori_loop(0, count, step, 0, unroll=8)


def column_kernel(halved, *refs):
    if halved:
        flag_ref, phase_ref, refs = refs[0], refs[1], refs[2:]
    x_ref, outer_ref, *refs = refs
    count = 4 if halved else 5
    sources, out_ref = refs[:count], refs[count]
    mid_ref, *targets, sems = refs[count + 1 :]
    copies = [
        pltpu.make_async_copy(source, target, sems.at[n])
        for n, (source, target) in enumerate(zip(sources, targets))
    ]
    for copy in copies:
        copy.start()
    inner_ref, scale_ref, inner_t_ref, outer_t_ref = targets[:4]
    devices, _, rows, width = mid_ref.shape
    wide = devices * 2 * GROUP
    if halved:
        lane = lane_index((devices, PATCH, width))
        centre = flag_ref[0] == 1
        half = width // 2
        hidden = (lane == half) | (centre & (lane == 0))
        real_lane = (lane < half) | (centre & (lane == half))

    def load(place):
        if not halved:
            return x_ref[:, :, place, :].astype(F32)
        piece = x_ref[:, place, :].astype(F32)
        other = swap_halves(piece)
        return jnp.stack([piece, jnp.where(hidden, jnp.zeros_like(other), other)], axis=1)

    def store(place, value):
        if halved:
            value = jnp.where(real_lane, value[:, 0], swap_halves(value[:, 1])).astype(BF16)
            out_ref[:, place, :] = value
        else:
            out_ref[:, :, place, :] = value.astype(BF16)

    def outer(matrix_ref, value):
        groups = [
            value[:, :, n : n + GROUP, :].reshape(wide, width) for n in range(0, PATCH, GROUP)
        ]
        result = mm(matrix_ref[...], jnp.concatenate(groups, axis=1).astype(BF16))
        parts = [
            result[:, n : n + width].reshape(devices, 2, GROUP, width)
            for n in range(0, result.shape[1], width)
        ]
        return jnp.concatenate(parts, axis=2)

    for top in range(0, rows, PATCH):
        place = slice(top, top + PATCH)
        mid_ref[:, :, place, :] = outer(outer_ref, load(place)).astype(BF16)

    for n, copy in enumerate(copies):
        if n != 3:
            copy.wait()

    def step(q, carry):
        spectrum = mm(inner_ref[q], mid_ref[q].reshape(2 * rows, width))
        real, imag = spectrum[:rows], spectrum[rows:]
        scale = scale_ref[q].astype(F32)
        if halved:
            pr, pi = phase_ref[q, 0], phase_ref[q, 1]
            real = real.reshape(rows // 8, 8, width)
            imag = imag.reshape(rows // 8, 8, width)
            real, imag = real * pr - imag * pi, real * pi + imag * pr
            real, imag = real.reshape(rows, width) * scale, imag.reshape(rows, width) * scale
        else:
            data_ref = targets[4]
            real = real * scale - data_ref[0, q].astype(F32)
            imag = imag * scale - data_ref[1, q].astype(F32)
        back = jnp.concatenate([real.astype(BF16), imag.astype(BF16)], axis=0)
        mid_ref[q] = mm(inner_t_ref[q], back).astype(BF16).reshape(2, rows, width)
        return carry

    lax.fori_loop(0, devices, step, 0, unroll=32)
    copies[3].wait()

    for top in range(0, rows, PATCH):
        place = slice(top, top + PATCH)
        store(place, outer(outer_t_ref, mid_ref[:, :, place, :].astype(F32)))


def turned(value, devices):
    lines = value.shape[0]
    return value.astype(BF16).reshape(lines, N // devices, devices).transpose(2, 1, 0)


def spectrum_inputs(gains, observed, vis_weight, devices):
    gr, gi = gains[0], gains[1]
    weight = (vis_weight * (gr * gr + gi * gi)).astype(BF16)
    data = jnp.stack(
        [
            turned(vis_weight * (gr * observed[0] + gi * observed[1]), devices),
            turned(vis_weight * (gr * observed[1] - gi * observed[0]), devices),
        ]
    )
    return weight, turned(weight, devices), data


def mirror_kernel(scale_ref, got_ref, pick_ref, flip_ref, out_ref):
    devices = out_ref.shape[0]
    for q in range(devices):
        facing = mm(flip_ref[min(q, 1)], got_ref[(devices - q) % devices]).astype(BF16)
        total = mm(scale_ref[q], pick_ref[0]) + mm(facing, pick_ref[1])
        out_ref[q] = total.astype(BF16)


def mirrored_exchange(upper, line, devices):
    middle = devices // 2
    facing = [(e, devices - 1 - e) for e in range(devices)]
    partner = [(e, devices - e) for e in range(1, devices) if e != middle]
    partner = partner + [(0, middle), (middle, 0)]
    upper = lax.ppermute(upper, ("ty", "tx"), facing)
    line = lax.ppermute(line, ("ty", "tx"), partner)
    return upper, line


def mirrored_weight(scale, upper, line):
    devices, slab, _ = scale.shape
    half, middle = slab // 2, devices // 2
    me = lax.axis_index(("ty", "tx"))
    got = jnp.concatenate([upper, jnp.broadcast_to(line, (half, N))], axis=0)
    source = lax.broadcasted_iota(jnp.int32, (slab, slab), 0)
    slot = lax.broadcasted_iota(jnp.int32, (slab, slab), 1)
    low = (me < middle).astype(jnp.int32)
    own = (slot < half) & (source == slot + low)
    other = (slot < half) & (source == half - low - slot)
    other = other & ((me != middle) | (slot > 0))
    other = other | ((me == middle) & (slot == half) & (source == half))
    picks = jnp.stack([own, other]).astype(BF16)
    q2 = np.arange(slab)
    flips = np.stack([q2[:, None] == (slab - q2) % slab, q2[:, None] == slab - 1 - q2])
    return pl.pallas_call(
        mirror_kernel,
        out_shape=jax.ShapeDtypeStruct(scale.shape, BF16),
        compiler_params=PARAMS,
    )(scale, turned(got, devices), picks, jnp.asarray(flips.astype(ml_dtypes.bfloat16)))


def row_matrix(first, cols, lanes, shift):
    twice = jnp.asarray(np.concatenate([first, first[: 2 * WIN]], axis=0))
    me = lax.axis_index("tx")
    zero = jnp.zeros((), jnp.int32)
    starts = [(me ^ m) * cols + (0 if shift is None else shift) for m in range(lanes)]
    rows = [lax.dynamic_slice(twice, (start, zero), (cols, first.shape[1])) for start in starts]
    return jnp.concatenate(rows, axis=0)


def swap_pieces(pieces):
    lanes = len(pieces)
    return [pieces[0]] + [
        lax.ppermute(pieces[m], "tx", [(k, k ^ m) for k in range(lanes)]) for m in range(1, lanes)
    ]


def phase_table(shift, devices, width):
    kr = counting(devices)[:, None] + devices * counting(8)[None, :]
    angle = 2.0 * math.pi / TOK * (kr * shift % TOK).astype(F32)
    table = jnp.stack([jnp.cos(angle), -jnp.sin(angle)], axis=1)
    return jnp.broadcast_to(table[..., None], (devices, 2, 8, width))


def patch_gradient(pieces, scale, data, shift, mirror, beside):
    lanes = lax.axis_size("tx")
    devices = lax.axis_size("ty") * lanes
    own, cols, _ = pieces[0].shape
    slab = N // devices
    halved = data is None
    outer, outer_t, inner, inner_t = (
        jnp.asarray(value) for value in column_constants(devices, slab)
    )
    if halved:
        first = half_constants()[0]
        twist, low, high, low_t, high_t = (jnp.asarray(value) for value in half_constants()[1:])
        part = (devices, slab, slab)
        onward = (row_forward_half, (row_matrix(first, cols, lanes, shift[1]), twist, low, high))
        backward = (row_inverse_half, (row_matrix(first, cols, lanes, None), twist, low_t, high_t))
        middle = lax.axis_index(("ty", "tx")) == devices // 2
    else:
        first = row_matrix(row_constants()[0], cols, lanes, None)
        twist, second, second_t = (jnp.asarray(value) for value in row_constants()[1:])
        part = (devices, 2, slab, slab)
        onward = (row_forward, (first, twist, second))
        backward = (row_inverse, (first, twist, second_t))
        extra = ()
        away = (inner, scale, inner_t, outer_t, data)
    split = (PATCH, devices // PATCH) + part[1:]
    sent = pl.pallas_call(
        onward[0], out_shape=jax.ShapeDtypeStruct(split, BF16), compiler_params=PARAMS
    )(*swap_pieces(pieces), *onward[1])
    if halved:
        sent, mirror, shift = lax.optimization_barrier((sent, mirror, shift))
        extra = (middle.astype(jnp.int32).reshape(1), phase_table(shift[0], devices, slab))
        table = mirrored_weight(scale, *mirror)
    moved = lax.all_to_all(
        sent.reshape(part), ("ty", "tx"), split_axis=0, concat_axis=0, tiled=True
    )
    if halved:
        moved, table, beside = lax.optimization_barrier((moved, table, beside))
        beside = from_neighbours(beside, 1)
        away = (inner, table, inner_t, outer_t)
    spaces = [pltpu.SMEM, pltpu.VMEM][: len(extra)] + [pltpu.VMEM] * 2 + [pl.ANY] * len(away)
    wave = pl.pallas_call(
        functools.partial(column_kernel, halved),
        in_specs=[pl.BlockSpec(memory_space=space) for space in spaces],
        out_shape=jax.ShapeDtypeStruct(part, BF16),
        scratch_shapes=[pltpu.VMEM((devices, 2, slab, slab), BF16)]
        + [pltpu.VMEM(value.shape, BF16) for value in away]
        + [pltpu.SemaphoreType.DMA((len(away),))],
        compiler_params=PARAMS,
    )(*extra, moved, outer, *away)
    if halved:
        wave, beside = lax.optimization_barrier((wave, beside))
    returned = lax.all_to_all(wave, ("ty", "tx"), split_axis=0, concat_axis=0, tiled=True)
    if not halved:
        returned, beside = lax.optimization_barrier((returned, beside))
    slabs = pl.pallas_call(
        backward[0],
        out_shape=[jax.ShapeDtypeStruct((own, cols, PIXELS), BF16)] * lanes,
        compiler_params=PARAMS,
    )(returned.reshape(split), *backward[1])
    return swap_pieces(slabs), beside


def layer_norm(values, gain):
    centre = jnp.mean(values, axis=-1, keepdims=True)
    shifted = values - centre
    spread = jnp.mean(shifted * shifted, axis=-1, keepdims=True)
    return (shifted * lax.rsqrt(spread + EPSILON) * gain).astype(BF16)


def to_windows(band):
    rows, cols, feats = band.shape
    pieces = [
        band[n : n + WIN, k : k + WIN, :].reshape(SPAN, feats)
        for n in range(0, rows, WIN)
        for k in range(0, cols, WIN)
    ]
    return jnp.concatenate(pieces, axis=0)


def from_windows(tokens, cols):
    feats = tokens.shape[-1]
    size = SPAN * cols // WIN
    bands = []
    for top in range(0, tokens.shape[0], size):
        pieces = [
            tokens[n : n + SPAN].reshape(WIN, WIN, feats) for n in range(top, top + size, SPAN)
        ]
        bands.append(jnp.concatenate(pieces, axis=1))
    return jnp.concatenate(bands, axis=0)


def gelu_twice(value):
    value = value.astype(BF16)
    inside = value * (BF16(GELU_IN) + BF16(GELU_CUBE) * (value * value))
    return value + value * jnp.tanh(inside)


def load_weights(j, sources, targets, sems):
    copies = [
        pltpu.make_async_copy(source.at[j], target, sems.at[n])
        for n, (source, target) in enumerate(zip(sources, targets))
    ]

    @pl.when(pl.program_id(0) == 0)
    def _():
        for copy in copies:
            copy.start()

    def wait(which):
        @pl.when(pl.program_id(0) == 0)
        def _():
            for n in which:
                copies[n].wait()

    return wait


def swin_band(flow, wait, bias_ref, gain_ref, weight_refs, scratch):
    qkv_ref, proj_ref, up_ref, down_ref = weight_refs
    mixed_ref, score_ref, prob_ref, active_ref = scratch
    count = flow.shape[0] // SPAN
    pairs = HEADS // 2
    depth = D // HEADS
    wide = 2 * depth
    normed = layer_norm(flow, gain_ref[0:1, :])
    scale = 1.0 / math.sqrt(depth)
    wait((0,))
    mixed_ref[:, :D] = (mm(normed, qkv_ref[:, :D]) * scale).astype(BF16)
    mixed_ref[:, D : 2 * D] = mm(normed, qkv_ref[:, D : 2 * D]).astype(BF16)
    mixed_ref[:, 2 * D :] = mm(normed, qkv_ref[:, 2 * D :]).astype(BF16)
    lower = lax.broadcasted_iota(jnp.int32, (SPAN, wide), 1) < depth

    def scores_of(w):
        rows = slice(w * SPAN, (w + 1) * SPAN)
        for p in range(pairs):
            query = mixed_ref[rows, p * wide : (p + 1) * wide]
            key = mixed_ref[rows, D + p * wide : D + (p + 1) * wide]
            zero = jnp.zeros_like(query)
            split = jnp.concatenate(
                [jnp.where(lower, query, zero), jnp.where(lower, zero, query)], axis=0
            )
            score_ref[w, :, p * wide : (p + 1) * wide] = mm(key, split, NT)

    def probs_of(w):
        bias = bias_ref[w]
        for p in range(pairs):
            lanes = slice(p * wide, (p + 1) * wide)
            scores = score_ref[w, :, lanes] + bias
            weights = jnp.exp(scores - jnp.max(scores, axis=0, keepdims=True))
            share = 1.0 / jnp.sum(weights, axis=0, keepdims=True)
            prob_ref[w, :, lanes] = (weights * share).astype(BF16)

    def mixture_of(w):
        rows = slice(w * SPAN, (w + 1) * SPAN)
        for p in range(pairs):
            lanes = slice(p * wide, (p + 1) * wide)
            value = mixed_ref[rows, 2 * D + p * wide : 2 * D + (p + 1) * wide]
            mixture = mm(prob_ref[w, :, lanes], value, TN)
            mixed_ref[rows, lanes] = jnp.where(lower, mixture[:SPAN], mixture[SPAN:]).astype(BF16)

    for run in (scores_of, probs_of, mixture_of):
        for w in range(count):
            run(w)
    wait((1, 2, 3))
    flow = flow + mm(mixed_ref[:, :D], proj_ref[...])
    normed = layer_norm(flow, gain_ref[1:2, :])
    chunks = up_ref.shape[1] // D
    for c in range(chunks):
        part = slice(c * D, (c + 1) * D)
        active_ref[:, part] = gelu_twice(mm(normed, up_ref[:, part]))
    return flow + 0.5 * mm(active_ref[...], down_ref[...])


def rolled_band(sign, shift_ref, refs, rows, count=WIN):
    main_ref, side_ref, edge_ref, corner_ref = refs
    cols = main_ref.shape[1]
    top = pl.program_id(0) * count + sign * shift_ref[0]
    behind = -rows if sign > 0 else WIN
    beside = -cols if sign > 0 else WIN

    source = lax.broadcasted_iota(jnp.int32, (cols, cols + WIN), 1)
    wanted = lax.broadcasted_iota(jnp.int32, (cols, cols + WIN), 0) + sign * shift_ref[1]
    found = (source < cols) & (source == wanted)
    found = found | (source >= cols) & (source - cols == wanted + beside)
    pick = jnp.where(found, 1.0, 0.0).astype(BF16)
    band = []
    for j in range(count):
        row = top + j
        inside = (row >= 0) & (row < rows)
        here, there = jnp.clip(row, 0, rows - 1), jnp.clip(row + behind, 0, WIN - 1)
        main = jnp.where(inside, main_ref[here], edge_ref[there])
        side = jnp.where(inside, side_ref[here], corner_ref[there])
        band.append(mm(pick, jnp.concatenate([main, side], axis=0)))
    return jnp.stack(band)


def first_kernel(zeta, sigma, count, parts, rows, before, *refs):
    shift_ref, state_ref, *refs = refs
    if before is not None:
        back_refs, refs = refs[:4], refs[4:]
    grad_refs, refs = refs[: count * parts], refs[count * parts :]
    if sigma is not None:
        noise_ref, *refs = refs
    bias_ref, embed_ref, gain_ref, *sources = refs[:7]
    base_ref, out_ref, side_ref, edge_ref, corner_ref, *scratch = refs[7:]
    targets, sems, scratch = scratch[:4], scratch[4], scratch[5:]
    wait = load_weights(0, sources, targets, sems)
    state = state_ref[...]
    if before is not None:
        state = state - before * rolled_band(-1, shift_ref, back_refs, rows, state.shape[0])
    height = state.shape[0]
    if parts == 1:
        grad = grad_refs[0][...].astype(F32)
    else:
        bands = []
        for k in range(height // WIN):
            turn = (pl.program_id(0) * (height // WIN) + k) ^ shift_ref[2]
            band = 0.0
            for n in range(0, count * parts, parts):
                piece = grad_refs[n][...]
                for m in range(1, parts):
                    piece = jnp.where(turn == m, grad_refs[n + m][...], piece)
                band = band + piece.astype(F32)
            bands.append(band)
        grad = jnp.concatenate(bands, axis=0)
    step = zeta * grad
    half = state - step
    tokens = mm(to_windows(half).astype(BF16), embed_ref[...]).astype(BF16).astype(F32)
    flow = swin_band(tokens, wait, bias_ref, gain_ref, targets, scratch)
    result = from_windows(flow, half.shape[1]).astype(BF16)
    out_ref[:, :, :D] = result
    side_ref[:, :, :D] = result[:, :WIN]
    if sigma is None:
        base_ref[...] = half
    else:
        noise = sigma * noise_ref[...]
        base_ref[...] = half + noise
        change = (noise - step).astype(BF16)
        out_ref[:, :, D:] = change
        side_ref[:, :, D:] = change[:, :WIN]

    @pl.when(pl.program_id(0) == 0)
    def _():
        edge_ref[...] = out_ref[:WIN]
        corner_ref[...] = side_ref[:WIN]


def write_pieces(turn, refs, value):
    for m, ref in enumerate(refs):

        def write(ref=ref):
            ref[...] = value

        pl.when(turn == m)(write)


def second_kernel(sigma, rows, parts, *refs):
    shift_ref, *refs = refs
    tile_refs, refs = refs[:4], refs[4:]
    bias_ref, unembed_ref, gain_ref, *sources = refs[:7]
    out_ref, side_ref, edge_ref, corner_ref, *scratch = refs[7:]
    state_refs, scratch = scratch[:parts], scratch[parts:]
    targets, sems, scratch = scratch[:4], scratch[4], scratch[5:]
    wait = load_weights(1, sources, targets, sems)
    height, cols, _ = out_ref.shape
    band = rolled_band(1, shift_ref, tile_refs, rows, height)
    tokens = to_windows(band[:, :, :D])
    flow = swin_band(tokens, wait, bias_ref, gain_ref, targets, scratch)
    estimate = from_windows(mm(flow.astype(BF16), unembed_ref[...]), cols)
    narrow = estimate.astype(BF16)
    out_ref[...] = narrow
    side_ref[...] = narrow[:, cols - WIN :]
    edge_ref[...] = narrow[height - WIN :]
    corner_ref[...] = narrow[height - WIN :, cols - WIN :]
    if parts > 0:
        change = (band[:, :, D:] - sigma * estimate).astype(BF16)
        for n in range(height // WIN):
            turn = (pl.program_id(0) * (height // WIN) + n) ^ shift_ref[2]
            write_pieces(turn, state_refs, change[n * WIN : (n + 1) * WIN])


def whole(array):
    zeros = (0,) * array.ndim
    return pl.BlockSpec(array.shape, lambda *_: zeros)


def member(array, j):
    place = (j,) + (0,) * (array.ndim - 1)
    return pl.BlockSpec((None,) + array.shape[1:], lambda *_: place)


def band_spec(cols, feats, height=WIN):
    return pl.BlockSpec((height, cols, feats), lambda n, *_: (n, 0, 0))


def bias_spec(cols, height=WIN):
    count = height * cols // SPAN
    return pl.BlockSpec((count, SPAN, 2 * SPAN), lambda n, *_: (n, 0, 0))


def band_scratch(cols, weights, height=WIN):
    count = height * cols // SPAN
    return [pltpu.VMEM(value.shape[1:], BF16) for value in weights] + [
        pltpu.SemaphoreType.DMA((len(weights),)),
        pltpu.VMEM((height * cols, 3 * D), BF16),
        pltpu.VMEM((count, SPAN, HEADS * SPAN), F32),
        pltpu.VMEM((count, SPAN, HEADS * SPAN), BF16),
    ]


def strip_outs(rows, cols, feats, height=WIN):
    specs = [band_spec(cols, feats, height), band_spec(WIN, feats, height)]
    specs += [
        pl.BlockSpec((WIN, width, feats), lambda *_: (0, 0, 0)) for width in (cols, WIN)
    ]
    shapes = [(rows, cols), (rows, WIN), (WIN, cols), (WIN, WIN)]
    return specs, [jax.ShapeDtypeStruct(shape + (feats,), BF16) for shape in shapes]


def first_block(zeta, sigma, state, before, shift, back, grads, noise, bias, w_embed, weights):
    *weights, gains = weights
    rows, cols, _ = state.shape
    parts = len(grads[0])
    pieces = [piece for grad in grads for piece in grad]
    fields = [] if sigma is None else [noise]
    feats = D if sigma is None else D + PIXELS
    height = 2 * WIN
    specs, shapes = strip_outs(rows, cols, feats, height)
    band = band_spec(cols, PIXELS, height)
    return pl.pallas_call(
        functools.partial(first_kernel, zeta, sigma, len(grads), parts, rows, before),
        grid_spec=pltpu.PrefetchScalarGridSpec(
            num_scalar_prefetch=1,
            grid=(rows // height,),
            in_specs=[band]
            + [whole(value) for value in back]
            + [band if parts == 1 else whole(value) for value in pieces]
            + [band] * len(fields)
            + [bias_spec(cols, height), whole(w_embed), member(gains, 0)]
            + [pl.BlockSpec(memory_space=pl.ANY)] * len(weights),
            out_specs=[band] + specs,
            scratch_shapes=band_scratch(cols, weights, height)
            + [pltpu.VMEM((height * cols, weights[2].shape[2]), BF16)],
        ),
        out_shape=[jax.ShapeDtypeStruct((rows, cols, PIXELS), F32)] + shapes,
        compiler_params=PARAMS,
    )(shift, state, *back, *pieces, *fields, bias, w_embed, gains, *weights)


def second_block(sigma, shift, tile, bias, w_unembed, weights, parts):
    *weights, gains = weights
    rows, cols, _ = tile[0].shape
    height = 2 * WIN
    specs, shapes = strip_outs(rows, cols, PIXELS, height)
    specs += [pl.BlockSpec((WIN, cols, PIXELS), lambda *_: (0, 0, 0))] * parts
    shapes += [jax.ShapeDtypeStruct((WIN, cols, PIXELS), BF16)] * parts
    return pl.pallas_call(
        functools.partial(second_kernel, sigma, rows, parts),
        grid_spec=pltpu.PrefetchScalarGridSpec(
            num_scalar_prefetch=1,
            grid=(rows // height,),
            in_specs=[whole(value) for value in tile]
            + [bias_spec(cols, height), whole(w_unembed), member(gains, 1)]
            + [pl.BlockSpec(memory_space=pl.ANY)] * len(weights),
            out_specs=specs,
            scratch_shapes=band_scratch(cols, weights, height)
            + [pltpu.VMEM((height * cols, weights[2].shape[2]), BF16)],
        ),
        out_shape=shapes,
        compiler_params=PARAMS,
    )(shift, *tile, bias, w_unembed, gains, *weights)


def from_neighbours(tile, by):
    main, side, edge, corner = tile
    ty, tx = lax.axis_size("ty"), lax.axis_size("tx")
    across = [
        (i * tx + k, (i + by) % ty * tx + (k + by) % tx) for i in range(ty) for k in range(tx)
    ]
    return (
        main,
        lax.ppermute(side, "tx", [(k, (k + by) % tx) for k in range(tx)]),
        lax.ppermute(edge, "ty", [(i, (i + by) % ty) for i in range(ty)]),
        lax.ppermute(corner, ("ty", "tx"), across),
    )


def windows_of(grid):
    rows, cols = grid.shape
    shaped = grid.reshape(rows // WIN, WIN, cols // WIN, WIN).transpose(0, 2, 1, 3)
    return shaped.reshape(rows // WIN * (cols // WIN), SPAN)


def bias_of(labels, keep):
    allowed = jnp.ones((1, SPAN, SPAN), bool)
    if labels is not None:
        label = windows_of(labels)
        allowed = label[:, :, None] == label[:, None, :]
    if keep is not None:
        kept = windows_of(keep)[:, :, None] == 1
        allowed = allowed & (kept | jnp.eye(SPAN, dtype=bool)[None])
    bias = jnp.where(allowed, 0.0, -1e30).astype(F32)
    return jnp.concatenate([bias, bias], axis=2)


def region(index, shift):
    return jnp.where(index < TOK - WIN, 0, jnp.where(index < TOK - shift, 1, 2)).astype(jnp.int32)


@functools.lru_cache(maxsize=None)
def lane_order(cols):
    parts = LANES // cols
    groups = PATCH // parts
    lane = np.arange(PATCH * cols)
    g, h, k = lane // LANES, lane % LANES // cols, lane % cols
    source = PATCH * k + h * groups + g
    matrix = np.zeros((PATCH * cols, PATCH * cols), np.float32)
    matrix[source, lane] = 1.0
    return matrix.astype(ml_dtypes.bfloat16), np.ascontiguousarray(matrix.T).astype(
        ml_dtypes.bfloat16
    )


def move_lanes(values, matrix):
    high = values.astype(BF16)
    low = (values - high.astype(F32)).astype(BF16)
    return mm(high, matrix) + mm(low, matrix)


def to_patches_kernel(narrow, place_ref, tile_ref, order_ref, *out_refs):
    count, cols, _ = out_refs[0].shape
    parts = LANES // cols
    groups = PATCH // parts
    if narrow:
        ordered = mm(tile_ref[...].astype(BF16), order_ref[...])
    else:
        ordered = move_lanes(tile_ref[...], order_ref[...])
    patches = []
    for i in range(count):
        band = ordered[i * PATCH : (i + 1) * PATCH]
        stacked = jnp.concatenate(
            [band[:, g * LANES : (g + 1) * LANES] for g in range(groups)], axis=0
        )
        turned = stacked.T
        patches.append(
            jnp.concatenate([turned[h * cols : (h + 1) * cols] for h in range(parts)], axis=1)
        )
    result = jnp.stack(patches).astype(out_refs[0].dtype)
    if len(out_refs) == 1:
        out_refs[0][...] = result
    else:
        write_pieces(pl.program_id(0) ^ place_ref[0], out_refs, result)


def lanes_of(patches):
    count, cols, _ = patches.shape
    parts = LANES // cols
    groups = PATCH // parts
    width = groups * PATCH
    bands = []
    for i in range(count):
        stacked = jnp.concatenate(
            [patches[i, :, h * width : (h + 1) * width] for h in range(parts)], axis=0
        )
        turned = stacked.T
        bands.append(
            jnp.concatenate([turned[g * PATCH : (g + 1) * PATCH] for g in range(groups)], axis=1)
        )
    return jnp.concatenate(bands, axis=0)


def base_tile_kernel(scale, base_ref, noise_ref, order_ref, out_ref):
    moved = move_lanes(lanes_of(base_ref[...]), order_ref[...])
    out_ref[...] = moved + scale * noise_ref[...]


def last_tile_kernel(sigma, rows, shift_ref, tile_ref, *refs):
    *back_refs, order_ref, out_ref = refs
    estimate = rolled_band(-1, shift_ref, back_refs, rows)
    moved = mm(lanes_of(estimate).astype(BF16), order_ref[...])
    out_ref[...] = tile_ref[...] - sigma * moved


def patches_of(tiles, j, place, kind=F32, parts=1):
    rows, cols = tiles.shape[1] // PATCH, tiles.shape[2] // PATCH
    order = jnp.asarray(lane_order(cols)[0])
    spec, shape = band_spec(cols, PIXELS), (rows, cols, PIXELS)
    if parts > 1:
        spec = pl.BlockSpec((WIN, cols, PIXELS), lambda *_: (0, 0, 0))
        shape = (WIN, cols, PIXELS)
    return pl.pallas_call(
        functools.partial(to_patches_kernel, kind == BF16),
        grid_spec=pltpu.PrefetchScalarGridSpec(
            num_scalar_prefetch=1,
            grid=(rows // WIN,),
            in_specs=[
                pl.BlockSpec((None, WIN * PATCH, cols * PATCH), lambda n, *_: (j, n, 0)),
                whole(order),
            ],
            out_specs=[spec] * parts,
        ),
        out_shape=[jax.ShapeDtypeStruct(shape, kind)] * parts,
        compiler_params=PARAMS,
    )(place, tiles, order)


def tile_of(base, sigma, shift, back, scale, noise, j):
    rows, cols, _ = base.shape
    order = jnp.asarray(lane_order(cols)[1])
    tile_spec = pl.BlockSpec((WIN * PATCH, cols * PATCH), lambda n, *_: (n, 0))
    shape = jax.ShapeDtypeStruct((rows * PATCH, cols * PATCH), F32)
    tile = pl.pallas_call(
        functools.partial(base_tile_kernel, scale),
        grid=(rows // WIN,),
        in_specs=[
            band_spec(cols, PIXELS),
            pl.BlockSpec((None, WIN * PATCH, cols * PATCH), lambda n, *_: (j, n, 0)),
            whole(order),
        ],
        out_specs=tile_spec,
        out_shape=shape,
        compiler_params=PARAMS,
    )(base, noise, order)
    return pl.pallas_call(
        functools.partial(last_tile_kernel, sigma, rows),
        grid_spec=pltpu.PrefetchScalarGridSpec(
            num_scalar_prefetch=1,
            grid=(rows // WIN,),
            in_specs=[tile_spec] + [whole(value) for value in back] + [whole(order)],
            out_specs=tile_spec,
        ),
        out_shape=shape,
        compiler_params=PARAMS,
    )(shift, tile, *back, order)


def per_device(
    image, noise, offsets, key_mask, gains, observed, vis_weight,
    w_embed, w_qkv, w_proj, w_up, w_down, w_unembed, norm_gains,
):
    rows = image.shape[0] // PATCH
    cols = image.shape[1] // PATCH
    devices = lax.axis_size("ty") * lax.axis_size("tx")
    lanes = lax.axis_size("tx")
    fast = N // devices == TOK // 2 and rows == lanes * WIN and lanes & (lanes - 1) == 0
    column = lax.axis_index("tx").astype(jnp.int32)[None]
    places = [jnp.concatenate([offsets[step], column]) for step in range(STEPS)]
    row_index = lax.axis_index("ty") * rows + counting(rows)
    col_index = lax.axis_index("tx") * cols + counting(cols)
    weights = (w_qkv, w_proj, w_up, w_down, norm_gains)
    w_embed = w_embed.reshape(PATCH, PATCH, D).transpose(1, 0, 2).reshape(PIXELS, D)
    w_unembed = w_unembed.reshape(D, PATCH, PATCH).transpose(0, 2, 1).reshape(D, PIXELS)
    state = patches_of(image[None], 0, column)[0]
    extras = [patches_of(noise, step, column)[0] for step in range(STEPS - 1)] + [None]
    first_bias = bias_of(None, key_mask)
    biases = []
    for step in range(STEPS):
        labels = (
            3 * region(row_index, offsets[step, 0])[:, None]
            + region(col_index, offsets[step, 1])[None, :]
        )
        biases.append(bias_of(labels, None))
    beside = (state, extras, first_bias, biases, w_embed, w_unembed)
    shift, before, back, moving, mirror = places[0], None, (), None, None
    grads = []
    if fast:
        weight, scale, data = spectrum_inputs(gains, observed, vis_weight, devices)
        half = weight.shape[0] // 2
        lines = (weight[half:], weight[:1])
        grad, (beside, lines) = patch_gradient(
            patches_of(image[None], 0, column, BF16, lanes), scale, data, None, None,
            (beside, lines),
        )
        grads = [grad]
        state, extras, first_bias, biases, w_embed, w_unembed = beside
    for step in range(STEPS):
        if not fast:
            tile = image if step == 0 else tile_of(state, before, shift, back, 0.0, noise, 0)
            grad = plain_gradient(tile, gains, observed, vis_weight)
            grad = patches_of(grad.astype(F32)[None], 0, column, BF16)[0]
            grads = [[grad]]
        elif step > 0:
            grad, back = patch_gradient(moving, scale, None, shift, mirror, back)
            grads = grads + [grad]
        last = step + 1 == STEPS
        sigma = None if last else SIGMAS[step + 1]
        state, *first = first_block(
            STEP_SIZES[step], sigma, state, before, shift, back, grads, extras[step], first_bias,
            w_embed, weights,
        )
        shift, before = places[step], SIGMAS[step]
        first = from_neighbours(first, -1)
        if fast and step == 0:
            first, lines = lax.optimization_barrier((first, lines))
            mirror = mirrored_exchange(*lines, devices)
        rolled = second_block(
            before, shift, first, biases[step], w_unembed, weights,
            lanes if fast and not last else 0,
        )
        back, moving = rolled[:4], rolled[4:]
        if fast and step == 0:
            moving, mirror = lax.optimization_barrier((moving, mirror))
        if last or not fast:
            back = from_neighbours(back, 1)
    return tile_of(state, before, shift, back, SIGMAS[STEPS], noise, STEPS - 1)


def solution(mesh):
    in_specs = (
        P("ty", "tx"),
        P(None, "ty", "tx"),
        P(),
        P("ty", "tx"),
        P(None, ("ty", "tx"), None),
        P(None, ("ty", "tx"), None),
        P(("ty", "tx"), None),
        P(),
        P(),
        P(),
        P(),
        P(),
        P(),
        P(),
    )
    out_specs = P("ty", "tx")
    return jax.shard_map(
        per_device, mesh=mesh, in_specs=in_specs, out_specs=out_specs, check_vma=False
    )
```
